128 devices in a mesh: ctx: 32 (over z_hi, x, y), fsdp: 4 (over z_lo, core).
Axes of the slice: x: 4, y: 4, z: 4 (z_hi: 2, z_lo: 2; z = z_hi * 2 + z_lo), core: 2. Of those that a mesh axis runs over, the one named last changes fastest.
Arguments:
- tokens: bfloat16 [4, 4096, 1024], P('fsdp', 'ctx'), may hold values from -6 to 6
- cotangent: bfloat16 [4, 4096, 1024], P('fsdp', 'ctx'), may hold values from -6 to 6
- positions: int32 [4, 4096], P('fsdp'), may hold values from 0 to 3071, as said below
- seq_ids: int32 [4, 4096], P('fsdp'), may hold values from 0 to 1, as said below
- query_weight: float32 [1024, 2048], P(('ctx', 'fsdp')), may hold values from -0.1875 to 0.1875
- keyval_weight: float32 [1024, 2048], P(('ctx', 'fsdp')), may hold values from -0.1875 to 0.1875
- output_weight: float32 [2048, 1024], P(('ctx', 'fsdp')), may hold values from -0.125 to 0.125
- gateup_weight: float32 [1024, 6144], P(('ctx', 'fsdp')), may hold values from -0.1875 to 0.1875
- down_weight: float32 [3072, 1024], P(('ctx', 'fsdp')), may hold values from -0.109375 to 0.109375
- norm_gains: float32 [2304], P(('ctx', 'fsdp')), may hold values from 0.6 to 1.8
- query_mean: float32 [1024, 2048], P(('ctx', 'fsdp')), may hold values from -80 to 80
- keyval_mean: float32 [1024, 2048], P(('ctx', 'fsdp')), may hold values from -80 to 80
- output_mean: float32 [2048, 1024], P(('ctx', 'fsdp')), may hold values from -80 to 80
- gateup_mean: float32 [1024, 6144], P(('ctx', 'fsdp')), may hold values from -80 to 80
- down_mean: float32 [3072, 1024], P(('ctx', 'fsdp')), may hold values from -80 to 80
- gains_mean: float32 [2304], P(('ctx', 'fsdp')), may hold values from -80 to 80
- query_square: float32 [1024, 2048], P(('ctx', 'fsdp')), may hold values from 862 to 3449
- keyval_square: float32 [1024, 2048], P(('ctx', 'fsdp')), may hold values from 862 to 3449
- output_square: float32 [2048, 1024], P(('ctx', 'fsdp')), may hold values from 862 to 3449
- gateup_square: float32 [1024, 6144], P(('ctx', 'fsdp')), may hold values from 862 to 3449
- down_square: float32 [3072, 1024], P(('ctx', 'fsdp')), may hold values from 862 to 3449
- gains_square: float32 [2304], P(('ctx', 'fsdp')), may hold values from 862 to 3449
Outputs:
- block_output: bfloat16 [4, 4096, 1024], P('fsdp', 'ctx')
- token_gradient: float32 [4, 4096, 1024], P('fsdp', 'ctx')
- query_gradient: float32 [1024, 2048], P(('ctx', 'fsdp'))
- keyval_gradient: float32 [1024, 2048], P(('ctx', 'fsdp'))
- output_gradient: float32 [2048, 1024], P(('ctx', 'fsdp'))
- gateup_gradient: float32 [1024, 6144], P(('ctx', 'fsdp'))
- down_gradient: float32 [3072, 1024], P(('ctx', 'fsdp'))
- gains_gradient: float32 [2304], P(('ctx', 'fsdp'))
- query_new: float32 [1024, 2048], P(('ctx', 'fsdp'))
- keyval_new: float32 [1024, 2048], P(('ctx', 'fsdp'))
- output_new: float32 [2048, 1024], P(('ctx', 'fsdp'))
- gateup_new: float32 [1024, 6144], P(('ctx', 'fsdp'))
- down_new: float32 [3072, 1024], P(('ctx', 'fsdp'))
- gains_new: float32 [2304], P(('ctx', 'fsdp'))
- query_mean_new: float32 [1024, 2048], P(('ctx', 'fsdp'))
- keyval_mean_new: float32 [1024, 2048], P(('ctx', 'fsdp'))
- output_mean_new: float32 [2048, 1024], P(('ctx', 'fsdp'))
- gateup_mean_new: float32 [1024, 6144], P(('ctx', 'fsdp'))
- down_mean_new: float32 [3072, 1024], P(('ctx', 'fsdp'))
- gains_mean_new: float32 [2304], P(('ctx', 'fsdp'))
- query_square_new: float32 [1024, 2048], P(('ctx', 'fsdp'))
- keyval_square_new: float32 [1024, 2048], P(('ctx', 'fsdp'))
- output_square_new: float32 [2048, 1024], P(('ctx', 'fsdp'))
- gateup_square_new: float32 [1024, 6144], P(('ctx', 'fsdp'))
- down_square_new: float32 [3072, 1024], P(('ctx', 'fsdp'))
- gains_square_new: float32 [2304], P(('ctx', 'fsdp'))
The draws below stay inside these ranges and needn't reach their ends.
Inputs may be any that keep to these rules, and one draw needn't show every extreme that they name: Each pack holds a sequence of 3072 tokens, then one of 1024, cut in order into 64 blocks of 64 tokens; the 128 rows of the i-th device of ctx hold a block b and then the block 63 - b, with b drawn per device and pack, each b once. positions gives a token's place in its sequence. `seq_ids`: 0 for the first sequence of the pack, 1 for the second, in the layout stated for positions.
All inputs are finite; a program needn't handle non-finite values.
Results may differ from the reference program's by a relative error of at most 0.02.
The reference program's roundings to bfloat16 on the way count: a program that leaves them out, or rounds other values in their place, can miss the bound.
Values may be sent and summed in bfloat16 or wider, within the bound.
A program may use at most 320 MiB of HBM per device.

```python
import math
import jax
import jax.numpy as jnp
from jax import lax

D = 1024
H = 16
KVH = 8
HD = 128
FF = 3072
HQ = 2048
KV = 1024
PACK_TOK = 4096
TOK_DEV = 128
PACKS = 4
TOKENS = 16384
LONG = 3072
STEP = 10


def deal_blocks(key):
    devices = PACK_TOK // TOK_DEV
    halfway = TOK_DEV // 2
    pack_keys = jax.random.split(key, PACKS)
    order = jax.vmap(lambda pack_key: jax.random.permutation(pack_key, devices))(pack_keys)
    offsets = jnp.arange(halfway, dtype=jnp.int32)
    early = order[:, :, None].astype(jnp.int32) * halfway + offsets[None, None, :]
    late = (2 * devices - 1 - order[:, :, None].astype(jnp.int32)) * halfway + offsets[None, None, :]
    slots = jnp.concatenate([early, late], axis=2).reshape(PACKS, PACK_TOK)
    return slots.astype(jnp.int32)


def draw_positions(key, part):
    slots = deal_blocks(key)
    second_seq = (slots >= LONG).astype(jnp.int32)
    return (slots - second_seq * LONG).astype(jnp.int32)


def draw_seq_ids(key, part):
    slots = deal_blocks(key)
    return (slots >= LONG).astype(jnp.int32)


def steps_of(own_key, dims, cuts, least, top_value):
    level, own = 1.0, jax.random.fold_in(own_key, 6)
    for dim, shards_of in cuts:
        draws = jnp.exp(jax.random.uniform(jax.random.fold_in(own, dim), (shards_of,), jnp.float32, least / len(cuts), top_value / len(cuts)))
        level = level * jnp.repeat(draws, dims[dim] // shards_of).reshape([-1 if axis == dim else 1 for axis in range(len(dims))])
    return level


def bell_draw(key, dims, deviation, limit, cuts=(), held_as=jnp.bfloat16):
    array = deviation * jax.random.normal(key, dims, jnp.float32)
    if cuts:
        array = array * steps_of(key, dims, cuts, -0.22, 0.18)
    return jnp.clip(array, -limit, limit).astype(held_as)


def setup_inputs(seed: int = 0) -> dict:
    keys = jax.random.split(jax.random.key(seed), 23)
    tokens = bell_draw(keys[0], (PACKS, PACK_TOK, D), 1.0, 6.0, ((0, 4), (1, 32)))
    cotangent = bell_draw(keys[1], (PACKS, PACK_TOK, D), 1.0, 6.0, ((0, 4), (1, 32)))
    positions = draw_positions(jax.random.fold_in(keys[22], 71), 0)
    seq_ids = draw_seq_ids(jax.random.fold_in(keys[22], 71), 0)
    query_weight = bell_draw(keys[4], (D, HQ), D ** -0.5, 0.1875, ((0, 128),), jnp.float32)
    keyval_weight = bell_draw(keys[5], (D, 2 * KV), D ** -0.5, 0.1875, ((0, 128),), jnp.float32)
    output_weight = bell_draw(keys[6], (HQ, D), HQ ** -0.5, 0.125, ((0, 128),), jnp.float32)
    gateup_weight = bell_draw(keys[7], (D, 2 * FF), D ** -0.5, 0.1875, ((0, 128),), jnp.float32)
    down_weight = bell_draw(keys[8], (FF, D), FF ** -0.5, 0.109375, ((0, 128),), jnp.float32)
    norm_gains = jnp.clip(0.6 + 1.1999999 * jax.random.uniform(keys[9], (2 * D + 2 * HD,), jnp.float32) ** steps_of(keys[9], (2 * D + 2 * HD,), ((0, 128),), -0.2, 0.2), 0.6, 1.8)
    query_mean = bell_draw(keys[10], (D, HQ), ((TOKENS // 81) ** 0.5), 80.0, ((0, 128),), jnp.float32)
    keyval_mean = bell_draw(keys[11], (D, 2 * KV), ((TOKENS // 81) ** 0.5), 80.0, ((0, 128),), jnp.float32)
    output_mean = bell_draw(keys[12], (HQ, D), ((TOKENS // 81) ** 0.5), 80.0, ((0, 128),), jnp.float32)
    gateup_mean = bell_draw(keys[13], (D, 2 * FF), ((TOKENS // 81) ** 0.5), 80.0, ((0, 128),), jnp.float32)
    down_mean = bell_draw(keys[14], (FF, D), ((TOKENS // 81) ** 0.5), 80.0, ((0, 128),), jnp.float32)
    gains_mean = bell_draw(keys[15], (2 * D + 2 * HD,), ((TOKENS // 81) ** 0.5), 80.0, ((0, 128),), jnp.float32)
    query_square = jnp.clip(jnp.exp(math.log(3449.0) - 1.3865843422731479 * jax.random.uniform(keys[16], (D, HQ), jnp.float32) ** steps_of(keys[16], (D, HQ), ((0, 128),), -0.2, 0.2)), 862.0, 3449.0)
    keyval_square = jnp.clip(jnp.exp(math.log(3449.0) - 1.3865843422731479 * jax.random.uniform(keys[17], (D, 2 * KV), jnp.float32) ** steps_of(keys[17], (D, 2 * KV), ((0, 128),), -0.2, 0.2)), 862.0, 3449.0)
    output_square = jnp.clip(jnp.exp(math.log(3449.0) - 1.3865843422731479 * jax.random.uniform(keys[18], (HQ, D), jnp.float32) ** steps_of(keys[18], (HQ, D), ((0, 128),), -0.2, 0.2)), 862.0, 3449.0)
    gateup_square = jnp.clip(jnp.exp(math.log(3449.0) - 1.3865843422731479 * jax.random.uniform(keys[19], (D, 2 * FF), jnp.float32) ** steps_of(keys[19], (D, 2 * FF), ((0, 128),), -0.2, 0.2)), 862.0, 3449.0)
    down_square = jnp.clip(jnp.exp(math.log(3449.0) - 1.3865843422731479 * jax.random.uniform(keys[20], (FF, D), jnp.float32) ** steps_of(keys[20], (FF, D), ((0, 128),), -0.2, 0.2)), 862.0, 3449.0)
    gains_square = jnp.clip(jnp.exp(math.log(3449.0) - 1.3865843422731479 * jax.random.uniform(keys[21], (2 * D + 2 * HD,), jnp.float32) ** steps_of(keys[21], (2 * D + 2 * HD,), ((0, 128),), -0.2, 0.2)), 862.0, 3449.0)
    return {"tokens": tokens, "cotangent": cotangent, "positions": positions, "seq_ids": seq_ids, "query_weight": query_weight, "keyval_weight": keyval_weight, "output_weight": output_weight, "gateup_weight": gateup_weight, "down_weight": down_weight, "norm_gains": norm_gains, "query_mean": query_mean, "keyval_mean": keyval_mean, "output_mean": output_mean, "gateup_mean": gateup_mean, "down_mean": down_mean, "gains_mean": gains_mean, "query_square": query_square, "keyval_square": keyval_square, "output_square": output_square, "gateup_square": gateup_square, "down_square": down_square, "gains_square": gains_square}


NORM_EPS = 1e-06
ROPE_BASE = 1000000.0
BETA_ONE = 0.9
BETA_TWO = 0.95
ADAM_EPS = 1e-08
DECAY = 0.1
RATE_MATRIX = 0.1
RATE_GAIN = 0.3

@jax.custom_vjp
def low(v):
    return lax.optimization_barrier(v.astype(jnp.bfloat16)).astype(jnp.float32)

@jax.custom_vjp
def low_back(v):
    return v

def low_keep(v):
    return (low(v), None)

def low_pass(kept, grad):
    return (grad,)

def back_keep(v):
    return (v, None)

def back_low(kept, grad):
    return (low(grad),)
low.defvjp(low_keep, low_pass)
low_back.defvjp(back_keep, back_low)

def matmul(left, right):
    return jnp.dot(left, right, precision=lax.Precision.HIGHEST, preferred_element_type=jnp.float32)

def rms_norm(values, norm_gain):
    factor = lax.rsqrt(lax.optimization_barrier(jnp.mean(values * values, axis=-1, keepdims=True)) + NORM_EPS)
    return values * factor * norm_gain

def rotate(values, places):
    halfway = values.shape[-1] // 2
    frequency = ROPE_BASE ** (-jnp.arange(halfway, dtype=jnp.float32) * 2.0 / values.shape[-1])
    angles = places.astype(jnp.float32)[:, None] * frequency[None, :]
    cosine = jnp.cos(angles)[:, None, :]
    sine_part = jnp.sin(angles)[:, None, :]
    leading = values[..., :halfway]
    trailing = values[..., halfway:]
    return jnp.concatenate([leading * cosine - trailing * sine_part, trailing * cosine + leading * sine_part], axis=-1)

def head_prepare(projected, norm_gain, places):
    row_count = projected.shape[0]
    heads = projected.shape[1] // HD
    shaped = projected.reshape(row_count, heads, HD)
    return rotate(rms_norm(shaped, norm_gain), places).reshape(row_count, heads * HD)

def attention(query, key_heads, value_heads, places, labels):
    row_count = query.shape[0]
    per_group = H // KVH
    key_wide = jnp.repeat(key_heads.reshape(row_count, KVH, HD), per_group, axis=1)
    value_wide = jnp.repeat(value_heads.reshape(row_count, KVH, HD), per_group, axis=1)
    block_rows = min(512, row_count)
    blocks = row_count // block_rows

    @jax.checkpoint
    def one_block(block_items):
        query_part, place_part, label_part = block_items
        scores = jnp.einsum('qhd,khd->hqk', query_part, key_wide, precision=lax.Precision.HIGHEST) * HD ** (-0.5)
        scores = low_back(scores)
        allowed = (label_part[:, None] == labels[None, :]) & (places[None, :] <= place_part[:, None])
        scores = jnp.where(allowed[None], scores, -1e+30)
        weights = low(jax.nn.softmax(scores, axis=-1))
        mixed = jnp.einsum('hqk,khd->qhd', weights, value_wide, precision=lax.Precision.HIGHEST)
        return mixed.reshape(block_rows, H * HD)
    outcome = lax.map(one_block, (query.reshape(blocks, block_rows, H, HD), places.reshape(blocks, block_rows), labels.reshape(blocks, block_rows)))
    return outcome.reshape(row_count, H * HD)

def layer(params, inputs, places, labels):
    query_w, keyval_w, output_w, gateup_w, down_w, gains_w = [low(weight) for weight in params]
    attn_gain = gains_w[:D]
    ffn_gain = gains_w[D:2 * D]
    query_gain = gains_w[2 * D:2 * D + HD]
    key_gain = gains_w[2 * D + HD:]
    query_proj = low_back(matmul(inputs, query_w))
    keyval_proj = low_back(matmul(inputs, keyval_w))
    query_use = low(head_prepare(query_proj, query_gain, places))
    key_use = low(head_prepare(keyval_proj[:, :KV], key_gain, places))
    value_use = low(keyval_proj[:, KV:])
    attended = low(low_back(attention(query_use, key_use, value_use, places, labels)))
    branch = low_back(matmul(attended, output_w))
    hidden = inputs + rms_norm(branch, attn_gain)
    hidden_low = low(hidden)
    gate_up = low_back(matmul(hidden_low, gateup_w))
    activated = low(jax.nn.silu(gate_up[:, :FF]) * gate_up[:, FF:])
    ffn_out = low_back(matmul(activated, down_w))
    return hidden + rms_norm(ffn_out, ffn_gain)

def adam_update(weight, gradient, mean_old, square_old, rate, decay):
    mean_new = BETA_ONE * mean_old + (1.0 - BETA_ONE) * gradient
    square_new = BETA_TWO * square_old + (1.0 - BETA_TWO) * gradient * gradient
    mean_hat = mean_new / (1.0 - BETA_ONE ** STEP)
    square_hat = square_new / (1.0 - BETA_TWO ** STEP)
    weight_new = weight - rate * (mean_hat / (jnp.sqrt(square_hat) + ADAM_EPS) + decay * weight)
    return (weight_new, mean_new, square_new)

def reference(tokens, cotangent, positions, seq_ids, query_weight, keyval_weight, output_weight, gateup_weight, down_weight, norm_gains, query_mean, keyval_mean, output_mean, gateup_mean, down_mean, gains_mean, query_square, keyval_square, output_square, gateup_square, down_square, gains_square):
    params = (query_weight, keyval_weight, output_weight, gateup_weight, down_weight, norm_gains)

    def per_pack(totals, pack_items):
        inputs, upstream, places, labels = pack_items

        def forward(weights, values):
            return layer(weights, values, places, labels)
        result, pullback = jax.vjp(forward, params, inputs.astype(jnp.float32))
        weight_grads, token_grad = pullback(upstream.astype(jnp.float32))
        totals = jax.tree.map(jnp.add, totals, weight_grads)
        return (totals, (result.astype(jnp.bfloat16), token_grad))
    zero_grads = jax.tree.map(jnp.zeros_like, params)
    weight_sums, (outputs, token_grads) = lax.scan(per_pack, zero_grads, (tokens, cotangent, positions, seq_ids))
    query_new, query_mean_new, query_square_new = adam_update(query_weight, weight_sums[0], query_mean, query_square, RATE_MATRIX, DECAY)
    keyval_new, keyval_mean_new, keyval_square_new = adam_update(keyval_weight, weight_sums[1], keyval_mean, keyval_square, RATE_MATRIX, DECAY)
    output_new, output_mean_new, output_square_new = adam_update(output_weight, weight_sums[2], output_mean, output_square, RATE_MATRIX, DECAY)
    gateup_new, gateup_mean_new, gateup_square_new = adam_update(gateup_weight, weight_sums[3], gateup_mean, gateup_square, RATE_MATRIX, DECAY)
    down_new, down_mean_new, down_square_new = adam_update(down_weight, weight_sums[4], down_mean, down_square, RATE_MATRIX, DECAY)
    gains_new, gains_mean_new, gains_square_new = adam_update(norm_gains, weight_sums[5], gains_mean, gains_square, RATE_GAIN, 0.0)
    return (outputs, token_grads, weight_sums[0], weight_sums[1], weight_sums[2], weight_sums[3], weight_sums[4], weight_sums[5], query_new, keyval_new, output_new, gateup_new, down_new, gains_new, query_mean_new, keyval_mean_new, output_mean_new, gateup_mean_new, down_mean_new, gains_mean_new, query_square_new, keyval_square_new, output_square_new, gateup_square_new, down_square_new, gains_square_new)
```

```python
import functools
import math

import jax
import jax.numpy as jnp
from jax import lax
from jax.experimental import pallas as pl
from jax.experimental.pallas import tpu as pltpu
from jax.sharding import Mesh
from jax.sharding import PartitionSpec as P

D = 1024
H = 16
KVH = 8
HD = 128
FF = 3072
KV = 1024
STEP = 10
LONG = 3072
ROWS = 128
BLOCK = 64
CHUNK = 512
PACK_TOK = 4096
RANKS = 8
PLANE = 16


NORM_EPS = 1e-06
ROPE_BASE = 1000000.0
BETA_ONE = 0.9
BETA_TWO = 0.95
ADAM_EPS = 1e-08
DECAY = 0.1
RATE_MATRIX = 0.1
RATE_GAIN = 0.3

SCALE = HD**-0.5
LOG2E = math.log2(math.e)

AXES = ("zh", "x", "y", "zl", "co")
SIZE = {"zh": 2, "x": 4, "y": 4, "zl": 2, "co": 2}
COLUMN = ("zh", "zl", "co")
SURFACE = ("x", "y")
MESH = pl.DeviceIdType.MESH
F32 = jnp.float32
BF16 = jnp.bfloat16
VMEM_LIMIT = 50 * 1024 * 1024


def where_am_i():
    return {a: lax.axis_index(a) for a in AXES}


def address(place):
    return tuple(place[a] for a in AXES)


def flat_index(place, axes):
    at = 0
    for a in axes:
        at = at * SIZE[a] + place[a]
    return at


def shifted(place, axes, k, sign):
    to = dict(place)
    for a in reversed(axes):
        step = lax.rem(k, SIZE[a])
        k = lax.div(k, SIZE[a])
        to[a] = lax.rem(place[a] + sign * step + SIZE[a], SIZE[a])
    return to


def push_kernel(channels, n_in, n_out, *refs):
    ins, outs = refs[:n_in], refs[n_in : n_in + n_out]
    sems = refs[n_in + n_out :]
    me = where_am_i()
    barrier = pltpu.get_barrier_semaphore()
    greeted = max((c[2] for c in channels), key=len)
    peers = math.prod(SIZE[a] for a in greeted)

    def greet(k, carry):
        pl.semaphore_signal(
            barrier, inc=1, device_id=address(shifted(me, greeted, k, 1)), device_id_type=MESH
        )
        return carry

    lax.fori_loop(1, peers, greet, 0)
    own = []
    for i, (src, dst, axes, take, put) in enumerate(channels):
        copy = pltpu.make_async_copy(take(ins[src], me), put(outs[dst], me), sems[3 * i + 2])
        copy.start()
        own.append(copy)
    pl.semaphore_wait(barrier, peers - 1)
    for i, (src, dst, axes, take, put) in enumerate(channels):
        n = math.prod(SIZE[a] for a in axes)
        mix = {4: 1, 8: 3, 16: 7}[n]

        def begin(j, carry):
            k = lax.rem(j * mix, n)
            to = shifted(me, axes, k, 1)
            pltpu.make_async_remote_copy(
                src_ref=take(ins[src], to),
                dst_ref=put(outs[dst], me),
                send_sem=sems[3 * i].at[k],
                recv_sem=sems[3 * i + 1].at[k],
                device_id=address(to),
                device_id_type=MESH,
            ).start()
            return carry

        lax.fori_loop(1, n, begin, 0)
    for copy in own:
        copy.wait()
    for i, (src, dst, axes, take, put) in enumerate(channels):
        n = math.prod(SIZE[a] for a in axes)
        mix = {4: 1, 8: 3, 16: 7}[n]

        def finish(j, carry):
            k = lax.rem(j * mix, n)
            to, back = shifted(me, axes, k, 1), shifted(me, axes, k, -1)
            copy = pltpu.make_async_remote_copy(
                src_ref=take(ins[src], to),
                dst_ref=put(outs[dst], back),
                send_sem=sems[3 * i].at[k],
                recv_sem=sems[3 * i + 1].at[k],
                device_id=address(to),
                device_id_type=MESH,
            )
            copy.wait_send()
            copy.wait_recv()
            return carry

        lax.fori_loop(1, n, finish, 0)


def push(name, number, arrays, out_shapes, channels):
    scratch = []
    for _, _, axes, _, _ in channels:
        n = math.prod(SIZE[a] for a in axes)
        scratch += [
            pltpu.SemaphoreType.DMA((n,)),
            pltpu.SemaphoreType.DMA((n,)),
            pltpu.SemaphoreType.DMA,
        ]
    return pl.pallas_call(
        functools.partial(push_kernel, channels, len(arrays), len(out_shapes)),
        out_shape=tuple(jax.ShapeDtypeStruct(s, t) for s, t in out_shapes),
        in_specs=[pl.BlockSpec(memory_space=pl.ANY)] * len(arrays),
        out_specs=tuple([pl.BlockSpec(memory_space=pl.ANY)] * len(out_shapes)),
        scratch_shapes=scratch,
        compiler_params=pltpu.CompilerParams(collective_id=number, has_side_effects=True),
        name=name,
    )(*arrays)


def column_place(me, z, core):
    return dict(me, zh=lax.div(z, 2), zl=lax.rem(z, 2), co=core)


def greet_column(me, z, core):
    barrier = pltpu.get_barrier_semaphore()
    for off in (1, 2, 3):
        to = column_place(me, lax.rem(z + off, 4), core)
        pl.semaphore_signal(barrier, inc=1, device_id=address(to), device_id_type=MESH)
    sibling = column_place(me, z, 1 - core)
    pl.semaphore_signal(barrier, inc=1, device_id=address(sibling), device_id_type=MESH)
    pl.semaphore_wait(barrier, 4)


def gather_kernel(x_ref, out_ref, far_send, far_recv, near_send, near_recv, own_sem):
    me = where_am_i()
    z, core = me["zh"] * 2 + me["zl"], me["co"]
    sibling = address(column_place(me, z, 1 - core))
    own = pltpu.make_async_copy(x_ref, out_ref.at[z * 2 + core], own_sem)
    own.start()
    greet_column(me, z, core)

    def far(off):
        return pltpu.make_async_remote_copy(
            src_ref=x_ref,
            dst_ref=out_ref.at[z * 2 + core],
            send_sem=far_send.at[off],
            recv_sem=far_recv.at[off],
            device_id=address(column_place(me, lax.rem(z + off, 4), core)),
            device_id_type=MESH,
        )

    def near(off, core_of):
        slot = lax.rem(z + 4 - off, 4) * 2 + core_of
        return pltpu.make_async_remote_copy(
            src_ref=x_ref if off == 0 else out_ref.at[slot],
            dst_ref=out_ref.at[slot],
            send_sem=near_send.at[off],
            recv_sem=near_recv.at[off],
            device_id=sibling,
            device_id_type=MESH,
        )

    for off in (1, 3, 2):
        far(off).start()
    near(0, core).start()
    for off in (1, 3, 2):
        slot = lax.rem(z + 4 - off, 4) * 2 + core
        pltpu.make_async_remote_copy(
            src_ref=x_ref,
            dst_ref=out_ref.at[slot],
            send_sem=far_send.at[off],
            recv_sem=far_recv.at[off],
            device_id=address(column_place(me, lax.rem(z + off, 4), core)),
            device_id_type=MESH,
        ).wait_recv()
        near(off, core).start()
    own.wait()
    for off in (1, 3, 2):
        far(off).wait_send()
    for off in (0, 1, 3, 2):
        near(off, core).wait_send()
        near(off, 1 - core).wait_recv()


def gather_column(name, number, x):
    return pl.pallas_call(
        gather_kernel,
        out_shape=jax.ShapeDtypeStruct((RANKS,) + x.shape, x.dtype),
        in_specs=[pl.BlockSpec(memory_space=pl.ANY)],
        out_specs=pl.BlockSpec(memory_space=pl.ANY),
        scratch_shapes=[pltpu.SemaphoreType.DMA((4,))] * 4 + [pltpu.SemaphoreType.DMA],
        compiler_params=pltpu.CompilerParams(collective_id=number, has_side_effects=True),
        name=name,
    )(x)


def sum_kernel(
    part_ref, out_ref, paired, sending, landed, near_send, near_recv, far_send, far_recv
):
    me = where_am_i()
    z, core = me["zh"] * 2 + me["zl"], me["co"]
    sibling = address(column_place(me, z, 1 - core))
    greet_column(me, z, core)

    def near(off):
        to_z = lax.rem(z + off, 4)
        return pltpu.make_async_remote_copy(
            src_ref=part_ref.at[to_z * 2 + (1 - core)],
            dst_ref=paired.at[off],
            send_sem=near_send.at[off],
            recv_sem=near_recv.at[off],
            device_id=sibling,
            device_id_type=MESH,
        )

    def far(off):
        return pltpu.make_async_remote_copy(
            src_ref=sending.at[off],
            dst_ref=landed.at[off],
            send_sem=far_send.at[off],
            recv_sem=far_recv.at[off],
            device_id=address(column_place(me, lax.rem(z + off, 4), core)),
            device_id_type=MESH,
        )

    for off in (2, 1, 3, 0):
        near(off).start()
    for off in (2, 1, 3):
        near(off).wait_recv()
        mine = part_ref[lax.rem(z + off, 4) * 2 + core].astype(F32)
        sending[off] = (mine + paired[off].astype(F32)).astype(BF16)
        far(off).start()
    near(0).wait_recv()
    out_ref[...] = part_ref[z * 2 + core].astype(F32) + paired[0].astype(F32)
    for off in (1, 3, 2):
        far(off).wait_recv()
        out_ref[...] += landed[off].astype(F32)
    for off in (2, 1, 3):
        near(off).wait_send()
        far(off).wait_send()
    near(0).wait_send()


def sum_column(name, number, parts):
    block = parts.shape[1:]
    return pl.pallas_call(
        sum_kernel,
        out_shape=jax.ShapeDtypeStruct(block, F32),
        in_specs=[pl.BlockSpec(memory_space=pltpu.VMEM)],
        out_specs=pl.BlockSpec(memory_space=pltpu.VMEM),
        scratch_shapes=[pltpu.VMEM((4,) + block, BF16)] * 3
        + [pltpu.SemaphoreType.DMA((4,))] * 4,
        compiler_params=pltpu.CompilerParams(
            collective_id=number, has_side_effects=True, vmem_limit_bytes=VMEM_LIMIT
        ),
        name=name,
    )(parts)


def dot_nn(a, b):
    return lax.dot_general(a, b, (((1,), (0,)), ((), ())), preferred_element_type=F32)


def dot_nt(a, b):
    return lax.dot_general(a, b, (((1,), (1,)), ((), ())), preferred_element_type=F32)


def dot_tn(a, b):
    return lax.dot_general(a, b, (((0,), (0,)), ((), ())), preferred_element_type=F32)


def stacked_heads(ref, tile):
    rows = ref[pl.ds(tile * BLOCK, BLOCK), :]
    return jnp.concatenate([rows[:, :HD], rows[:, HD:]], axis=0)


def allowed_keys(block, chunk):
    keys = chunk * CHUNK + lax.broadcasted_iota(jnp.int32, (CHUNK, 2 * BLOCK), 0)
    lanes = lax.broadcasted_iota(jnp.int32, (CHUNK, 2 * BLOCK), 1)
    return keys <= block * BLOCK + lax.rem(lanes, BLOCK)


def first_chunk(block):
    return jnp.where(block >= LONG // BLOCK, LONG // CHUNK, 0)


def attend_kernel(q_blocks, k_blocks, q_ref, kv_ref, out_ref, lse_ref, keys, values, values_t):
    def sort(i, carry):
        to = pl.multiple_of(k_blocks[i] * BLOCK, BLOCK)
        here = pl.multiple_of(i * BLOCK, BLOCK)
        keys[pl.ds(to, BLOCK), :] = kv_ref[pl.ds(here, BLOCK), :HD]
        values[pl.ds(to, BLOCK), :] = kv_ref[pl.ds(here, BLOCK), HD:]
        return carry

    lax.fori_loop(0, PACK_TOK // BLOCK, sort, 0)
    for c in range(PACK_TOK // CHUNK):
        part = values[c * CHUNK : (c + 1) * CHUNK, :].astype(F32)
        values_t[c] = part.T.astype(BF16)

    def one_tile(tile, carry):
        block = q_blocks[tile]
        query = stacked_heads(q_ref, tile)
        last = lax.div(block, CHUNK // BLOCK)

        def one_chunk(c, state, masked):
            total, mixed = state
            chunk_keys = keys[pl.ds(pl.multiple_of(c * CHUNK, CHUNK), CHUNK), :]
            weights = jnp.exp2(dot_nt(chunk_keys, query) * (SCALE * LOG2E))
            if masked:
                weights = jnp.where(allowed_keys(block, c), weights, 0.0)
            total = total + jnp.sum(weights, axis=0, keepdims=True)
            mixed = mixed + dot_nn(values_t[c], weights.astype(BF16))
            return total, mixed

        state = (jnp.zeros((1, 2 * BLOCK), F32), jnp.zeros((HD, 2 * BLOCK), F32))
        state = lax.fori_loop(
            first_chunk(block), last, lambda c, s: one_chunk(c, s, False), state
        )
        total, mixed = one_chunk(last, state, True)
        result = (mixed / total).T.astype(BF16)
        rows = pl.ds(pl.multiple_of(tile * BLOCK, BLOCK), BLOCK)
        out_ref[rows, :HD] = result[:BLOCK]
        out_ref[rows, HD:] = result[BLOCK:]
        lse_ref[pl.ds(tile, 1), :] = jnp.log2(total)
        return carry

    lax.fori_loop(0, q_ref.shape[0] // BLOCK, one_tile, 0)


def attend(q_blocks, k_blocks, q, kv):
    smem = pl.BlockSpec(memory_space=pltpu.SMEM)
    vmem = pl.BlockSpec(memory_space=pltpu.VMEM)
    tiles = q.shape[0] // BLOCK
    return pl.pallas_call(
        attend_kernel,
        out_shape=(
            jax.ShapeDtypeStruct(q.shape, BF16),
            jax.ShapeDtypeStruct((tiles, 2 * BLOCK), F32),
        ),
        in_specs=[smem, smem, vmem, vmem],
        out_specs=(vmem, vmem),
        scratch_shapes=[
            pltpu.VMEM((PACK_TOK, HD), BF16),
            pltpu.VMEM((PACK_TOK, HD), BF16),
            pltpu.VMEM((PACK_TOK // CHUNK, HD, CHUNK), BF16),
        ],
        compiler_params=pltpu.CompilerParams(vmem_limit_bytes=VMEM_LIMIT),
        cost_estimate=pl.CostEstimate(
            flops=4 * 10**9, bytes_accessed=4 * 10**6, transcendentals=8 * 10**6
        ),
        name="attend",
    )(q_blocks, k_blocks, q, kv)


def attend_back_kernel(
    q_blocks,
    k_blocks,
    q_ref,
    kv_ref,
    grad_ref,
    out_ref,
    lse_ref,
    dq_ref,
    dkv_ref,
    keys,
    values,
    keys_t,
    dk,
    dv,
):
    def sort(i, carry):
        to = pl.multiple_of(k_blocks[i] * BLOCK, BLOCK)
        here = pl.multiple_of(i * BLOCK, BLOCK)
        keys[pl.ds(to, BLOCK), :] = kv_ref[pl.ds(here, BLOCK), :HD]
        values[pl.ds(to, BLOCK), :] = kv_ref[pl.ds(here, BLOCK), HD:]
        return carry

    lax.fori_loop(0, PACK_TOK // BLOCK, sort, 0)
    for c in range(PACK_TOK // CHUNK):
        part = keys[c * CHUNK : (c + 1) * CHUNK, :].astype(F32)
        keys_t[c] = part.T.astype(BF16)
    dk[...] = jnp.zeros_like(dk)
    dv[...] = jnp.zeros_like(dv)

    def one_tile(tile, carry):
        block = q_blocks[tile]
        query = stacked_heads(q_ref, tile)
        grad = stacked_heads(grad_ref, tile)
        out = stacked_heads(out_ref, tile)
        inner = jnp.sum((grad.astype(F32) * out.astype(F32)).T, axis=0, keepdims=True)
        lse = lse_ref[pl.ds(tile, 1), :]
        last = lax.div(block, CHUNK // BLOCK)

        def one_chunk(c, dq, masked):
            rows = pl.ds(pl.multiple_of(c * CHUNK, CHUNK), CHUNK)
            probs = jnp.exp2(dot_nt(keys[rows, :], query) * (SCALE * LOG2E) - lse)
            if masked:
                probs = jnp.where(allowed_keys(block, c), probs, 0.0)
            grad_probs = dot_nt(values[rows, :], grad)
            grad_scores = (probs * (grad_probs - inner)).astype(BF16)
            dv[rows, :] += dot_nn(probs.astype(BF16), grad)
            dk[rows, :] += dot_nn(grad_scores, query)
            return dq + dot_nn(keys_t[c], grad_scores)

        dq = lax.fori_loop(
            first_chunk(block),
            last,
            lambda c, s: one_chunk(c, s, False),
            jnp.zeros((HD, 2 * BLOCK), F32),
        )
        dq = (one_chunk(last, dq, True) * SCALE).T.astype(BF16)
        rows = pl.ds(pl.multiple_of(tile * BLOCK, BLOCK), BLOCK)
        dq_ref[rows, :HD] = dq[:BLOCK]
        dq_ref[rows, HD:] = dq[BLOCK:]
        return carry

    lax.fori_loop(0, q_ref.shape[0] // BLOCK, one_tile, 0)

    def unsort(i, carry):
        at = pl.multiple_of(k_blocks[i] * BLOCK, BLOCK)
        here = pl.multiple_of(i * BLOCK, BLOCK)
        dkv_ref[pl.ds(here, BLOCK), :HD] = (dk[pl.ds(at, BLOCK), :] * SCALE).astype(BF16)
        dkv_ref[pl.ds(here, BLOCK), HD:] = dv[pl.ds(at, BLOCK), :].astype(BF16)
        return carry

    lax.fori_loop(0, PACK_TOK // BLOCK, unsort, 0)


def attend_back(q_blocks, k_blocks, q, kv, grad, out, lse):
    smem = pl.BlockSpec(memory_space=pltpu.SMEM)
    vmem = pl.BlockSpec(memory_space=pltpu.VMEM)
    return pl.pallas_call(
        attend_back_kernel,
        out_shape=(
            jax.ShapeDtypeStruct(q.shape, BF16),
            jax.ShapeDtypeStruct(kv.shape, BF16),
        ),
        in_specs=[smem, smem] + [vmem] * 5,
        out_specs=(vmem, vmem),
        scratch_shapes=[
            pltpu.VMEM((PACK_TOK, HD), BF16),
            pltpu.VMEM((PACK_TOK, HD), BF16),
            pltpu.VMEM((PACK_TOK // CHUNK, HD, CHUNK), BF16),
            pltpu.VMEM((PACK_TOK, HD), F32),
            pltpu.VMEM((PACK_TOK, HD), F32),
        ],
        compiler_params=pltpu.CompilerParams(vmem_limit_bytes=VMEM_LIMIT),
        cost_estimate=pl.CostEstimate(
            flops=10**10, bytes_accessed=8 * 10**6, transcendentals=8 * 10**6
        ),
        name="attend_back",
    )(q_blocks, k_blocks, q, kv, grad, out, lse)


def rms_norm(values, norm_gain):
    factor = lax.rsqrt(jnp.mean(values * values, axis=-1, keepdims=True) + NORM_EPS)
    return values * factor * norm_gain


def head_prepare(projected, norm_gain, cosine, sine_part):
    normed = rms_norm(projected, norm_gain)
    halfway = HD // 2
    leading, trailing = normed[..., :halfway], normed[..., halfway:]
    return jnp.concatenate(
        [leading * cosine - trailing * sine_part, trailing * cosine + leading * sine_part], axis=-1
    )


def swiglu(gate_up):
    half = gate_up.shape[-1] // 2
    return jax.nn.silu(gate_up[:, :half]) * gate_up[:, half:]


def adam_update(weight, gradient, mean_old, square_old, rate, decay):
    mean_new = BETA_ONE * mean_old + (1.0 - BETA_ONE) * gradient
    square_new = BETA_TWO * square_old + (1.0 - BETA_TWO) * gradient * gradient
    mean_hat = mean_new / (1.0 - BETA_ONE**STEP)
    square_hat = square_new / (1.0 - BETA_TWO**STEP)
    weight_new = weight - rate * (mean_hat / (jnp.sqrt(square_hat) + ADAM_EPS) + decay * weight)
    return (weight_new, mean_new, square_new)


def by_rank(array, width):
    return array.reshape(array.shape[0], RANKS, width)


def swap_owner(array):
    pairs = [(a * 4 + b, b * 4 + a) for a in range(4) for b in range(4)]
    return lax.ppermute(array, ("x", "zl", "co"), pairs)


def body(
    tokens,
    cotangent,
    positions,
    seq_ids,
    query_weight,
    keyval_weight,
    output_weight,
    gateup_weight,
    down_weight,
    norm_gains,
    query_mean,
    keyval_mean,
    output_mean,
    gateup_mean,
    down_mean,
    gains_mean,
    query_square,
    keyval_square,
    output_square,
    gateup_square,
    down_square,
    gains_square,
):
    inputs = tokens[0]
    upstream = cotangent[0].astype(F32)
    at_x, at_y = lax.axis_index("x"), lax.axis_index("y")

    own_blocks = (positions[0] + LONG * seq_ids[0]).reshape(-1, BLOCK)[:, 0] // BLOCK
    extra = jnp.zeros((8, HD), F32)
    extra = extra.at[0, : norm_gains.shape[0]].set(norm_gains)
    extra = extra.at[1, :BLOCK].set(own_blocks.astype(F32))
    sent = jnp.concatenate(
        [
            by_rank(query_weight, 256),
            by_rank(keyval_weight[:, :KV], 128),
            by_rank(keyval_weight[:, KV:], 128),
            jnp.broadcast_to(extra[:, None, :], (8, RANKS, HD)),
            by_rank(gateup_weight[:, :FF], 384),
            by_rank(gateup_weight[:, FF:], 384),
        ],
        axis=2,
    ).transpose(1, 0, 2)
    (shares,) = push(
        "weights_column",
        1,
        [sent],
        [(sent.shape, F32)],
        [
            (
                0,
                0,
                COLUMN,
                lambda ref, to: ref.at[flat_index(to, COLUMN)],
                lambda ref, frm: ref.at[flat_index(frm, COLUMN)],
            )
        ],
    )
    shares_low = shares.astype(BF16).reshape(2, 32, 1408)
    all_tokens = gather_column("tokens_column", 2, inputs).reshape(RANKS * ROWS, D)
    (qkv_wide,) = push(
        "weights_plane",
        3,
        [shares_low[..., :640]],
        [((2, PLANE, 32, 640), BF16)],
        [
            (
                0,
                0,
                SURFACE,
                lambda ref, to: ref,
                lambda ref, frm: ref.at[:, flat_index(frm, SURFACE)],
            )
        ],
    )
    row_shares = swap_owner(
        jnp.concatenate(
            [output_weight.astype(BF16), down_weight.astype(BF16).reshape(16, 1536)], axis=1
        )
    )
    row_wide = lax.all_gather(row_shares, ("y", "x"))
    output_part = row_wide[:, :, :D].reshape(256, D)
    down_part = row_wide[:, :, D:].reshape(384, D)
    gateup_part = lax.all_gather(shares_low[..., 640:], SURFACE, axis=1).reshape(D, 768)

    qkv_part = qkv_wide[..., :512].reshape(D, 512)
    gains_all = (
        qkv_wide[..., 512:].reshape(2, PLANE, 4, 8, HD)[:, :, :, 0, :18].reshape(-1).astype(F32)
    )
    attn_gain = gains_all[:D]
    ffn_gain = gains_all[D : 2 * D]
    query_gain = gains_all[2 * D : 2 * D + HD]
    key_gain = gains_all[2 * D + HD :]

    blocks = shares[:4, 1, 512 : 512 + BLOCK].astype(jnp.int32).reshape(4, 2, 4, 4, 2)
    pack_blocks = lax.dynamic_index_in_dim(blocks, at_x, 0, keepdims=False)
    key_blocks = pack_blocks.transpose(1, 2, 0, 3).reshape(-1)
    query_blocks = (
        lax.dynamic_index_in_dim(pack_blocks, at_y, 2, keepdims=False).transpose(1, 0, 2).reshape(-1)
    )
    row_blocks = lax.dynamic_index_in_dim(
        lax.dynamic_index_in_dim(blocks, at_x, 2, keepdims=False), at_y, 2, keepdims=False
    ).transpose(1, 0, 2)
    slots = row_blocks[..., None] * BLOCK + jnp.arange(BLOCK, dtype=jnp.int32)
    places = jnp.where(slots >= LONG, slots - LONG, slots).reshape(-1)
    halfway = HD // 2
    frequency = ROPE_BASE ** (-jnp.arange(halfway, dtype=F32) * 2.0 / HD)
    angles = places.astype(F32)[:, None] * frequency[None, :]
    cosine = jnp.cos(angles)[:, None, :]
    sine_part = jnp.sin(angles)[:, None, :]

    qkv_proj = dot_nn(all_tokens, qkv_part)
    head_gains = jnp.stack([query_gain, query_gain, key_gain])
    heads_in = qkv_proj[:, :384].reshape(-1, 3, HD)
    prepare = functools.partial(head_prepare, cosine=cosine, sine_part=sine_part)
    heads_use, heads_pull = jax.vjp(prepare, heads_in, head_gains)
    qkv = jnp.concatenate(
        [heads_use.reshape(-1, 384).astype(BF16), qkv_proj[:, 384:].astype(BF16)], axis=1
    ).reshape(2, 4, ROWS, 512)

    def to_pack_x(ref, to):
        return ref.at[:, to["x"]]

    def from_x(ref, frm):
        return ref.at[frm["x"]]

    q_mine, kv_mine = push(
        "attention_in",
        4,
        [qkv[..., :256], qkv[..., 256:]],
        [((4, 2, ROWS, 256), BF16), ((PLANE, 2, ROWS, 256), BF16)],
        [
            (1, 1, SURFACE, to_pack_x, lambda ref, frm: ref.at[flat_index(frm, SURFACE)]),
            (0, 0, ("x",), to_pack_x, from_x),
        ],
    )
    q_mine = q_mine.reshape(1024, 256)
    kv_mine = kv_mine.reshape(PACK_TOK, 256)
    out_mine, lse = attend(query_blocks, key_blocks, q_mine, kv_mine)

    def to_x(ref, to):
        return ref.at[to["x"]]

    def from_pack_x(ref, frm):
        return ref.at[:, frm["x"]]

    (attended,) = push(
        "attention_out",
        5,
        [out_mine.reshape(4, 2, ROWS, 256)],
        [((2, 4, ROWS, 256), BF16)],
        [(0, 0, ("x",), to_x, from_pack_x)],
    )
    attended = attended.reshape(RANKS * ROWS, 256)

    branch = sum_column(
        "branch_column", 6, dot_nn(attended, output_part).astype(BF16).reshape(RANKS, ROWS, D)
    )
    hidden = inputs.astype(F32) + rms_norm(branch, attn_gain)

    all_hidden = gather_column("hidden_column", 7, hidden.astype(BF16)).reshape(RANKS * ROWS, D)
    gate_up = dot_nn(all_hidden, gateup_part)
    activated = swiglu(gate_up).astype(BF16)
    ffn_out = sum_column(
        "ffn_column", 8, dot_nn(activated, down_part).astype(BF16).reshape(RANKS, ROWS, D)
    )
    ffn_norm_out, ffn_pull = jax.vjp(rms_norm, ffn_out, ffn_gain)
    result = hidden + ffn_norm_out
    grad_ffn_out, grad_ffn_gain = ffn_pull(upstream)

    grad_ffn = gather_column("grad_ffn_column", 9, grad_ffn_out.astype(BF16)).reshape(
        RANKS * ROWS, D
    )
    down_grad = dot_tn(activated, grad_ffn)
    grad_act = dot_nt(grad_ffn, down_part)
    act_out, act_pull = jax.vjp(swiglu, gate_up)
    grad_gate_low = act_pull(grad_act)[0].astype(BF16)
    gateup_grad = dot_tn(all_hidden, grad_gate_low)
    grad_hidden = upstream + sum_column(
        "grad_hidden_column",
        10,
        dot_nt(grad_gate_low, gateup_part).astype(BF16).reshape(RANKS, ROWS, D),
    )
    attn_norm_out, attn_pull = jax.vjp(rms_norm, branch, attn_gain)
    grad_branch_own, grad_attn_gain = attn_pull(grad_hidden)
    grad_branch = gather_column("grad_branch_column", 11, grad_branch_own.astype(BF16)).reshape(
        RANKS * ROWS, D
    )
    output_grad = dot_tn(attended, grad_branch)
    grad_attended = dot_nt(grad_branch, output_part).astype(BF16)

    (grad_mine,) = push(
        "attention_grad_in",
        12,
        [grad_attended.reshape(2, 4, ROWS, 256)],
        [((4, 2, ROWS, 256), BF16)],
        [(0, 0, ("x",), to_pack_x, from_x)],
    )
    dq_mine, dkv_mine = attend_back(
        query_blocks, key_blocks, q_mine, kv_mine, grad_mine.reshape(1024, 256), out_mine, lse
    )
    dq, dkv_parts = push(
        "attention_grad_out",
        13,
        [dq_mine.reshape(4, 2, ROWS, 256), dkv_mine.reshape(PLANE, 2, ROWS, 256)],
        [((2, 4, ROWS, 256), BF16), ((4, 2, 4, ROWS, 256), BF16)],
        [
            (
                1,
                1,
                SURFACE,
                lambda ref, to: ref.at[flat_index(to, SURFACE)],
                lambda ref, frm: ref.at[frm["y"], :, frm["x"]],
            ),
            (0, 0, ("x",), to_x, from_pack_x),
        ],
    )
    dkv = jnp.sum(dkv_parts.astype(F32), axis=0).reshape(RANKS * ROWS, 256)
    grad_heads = jnp.concatenate([dq.reshape(RANKS * ROWS, 256).astype(F32), dkv[:, :HD]], axis=1)
    grad_heads_in, grad_head_gains = heads_pull(grad_heads.reshape(-1, 3, HD))
    grad_qkv = jnp.concatenate(
        [grad_heads_in.reshape(-1, 384).astype(BF16), dkv[:, HD:].astype(BF16)], axis=1
    )
    qkv_grad = dot_tn(all_tokens, grad_qkv)
    token_grad = grad_hidden + sum_column(
        "grad_token_column",
        14,
        dot_nt(grad_qkv, qkv_part).astype(BF16).reshape(RANKS, ROWS, D),
    )

    gains_grad = jnp.concatenate(
        [
            grad_attn_gain,
            grad_ffn_gain,
            grad_head_gains[0] + grad_head_gains[1],
            grad_head_gains[2],
        ]
    )
    gains_lines = jnp.pad(
        gains_grad.reshape(2, PLANE, 4, 18).transpose(1, 0, 2, 3).reshape(PLANE, RANKS, 18),
        ((0, 0), (0, 0), (0, HD - 18)),
    )

    def to_surface_inner(ref, to):
        return ref.at[:, flat_index(to, SURFACE)]

    def to_surface(ref, to):
        return ref.at[flat_index(to, SURFACE)]

    def to_surface_swapped(ref, to):
        return ref.at[flat_index(to, ("y", "x"))]

    gateup_lines = gateup_grad.astype(BF16).reshape(2, PLANE, 32, 768)
    qkv_lines = qkv_grad.astype(BF16).reshape(2, PLANE, 32, 512)
    row_lines = jnp.concatenate(
        [
            output_grad.astype(BF16).reshape(PLANE, 16, D),
            down_grad.astype(BF16).reshape(PLANE, 16, 1536),
        ],
        axis=2,
    )
    gateup_parts, row_parts, qkv_parts, gains_parts = push(
        "grads_plane",
        15,
        [gateup_lines, row_lines, qkv_lines, gains_lines],
        [
            ((PLANE, 2, 32, 768), BF16),
            ((PLANE, 16, D + 1536), BF16),
            ((PLANE, 2, 32, 512), BF16),
            ((PLANE, RANKS, HD), F32),
        ],
        [
            (0, 0, SURFACE, to_surface_inner, to_surface),
            (1, 1, SURFACE, to_surface_swapped, to_surface),
            (2, 2, SURFACE, to_surface_inner, to_surface),
            (3, 3, SURFACE, to_surface, to_surface),
        ],
    )
    row_sum = swap_owner(jnp.sum(row_parts.astype(F32), axis=0))
    output_sum = row_sum[:, :D]
    down_sum = row_sum[:, D:].reshape(24, D)
    gains_sums = jnp.sum(gains_parts, axis=0).reshape(RANKS, 1, HD)
    column_sums = jnp.concatenate(
        [
            jnp.sum(qkv_parts.astype(F32), axis=0).reshape(RANKS, 8, 512),
            jnp.pad(gains_sums, ((0, 0), (0, 7), (0, 0))),
            jnp.sum(gateup_parts.astype(F32), axis=0).reshape(RANKS, 8, 768),
        ],
        axis=2,
    )
    (summed,) = push(
        "grads_column",
        16,
        [column_sums],
        [((RANKS, 8, 1408), F32)],
        [
            (
                0,
                0,
                COLUMN,
                lambda ref, to: ref.at[flat_index(to, COLUMN)],
                lambda ref, frm: ref.at[flat_index(frm, COLUMN)],
            )
        ],
    )
    gains_sum = jnp.sum(summed[:, 0, 512 : 512 + 18], axis=0)
    wide = summed.transpose(1, 0, 2)
    query_sum = wide[:, :, :256].reshape(8, 2048)
    keyval_sum = jnp.concatenate(
        [wide[:, :, 256:384].reshape(8, KV), wide[:, :, 384:512].reshape(8, KV)], axis=1
    )
    gateup_sum = jnp.concatenate(
        [wide[:, :, 640:1024].reshape(8, FF), wide[:, :, 1024:].reshape(8, FF)], axis=1
    )

    query_new, query_mean_new, query_square_new = adam_update(
        query_weight, query_sum, query_mean, query_square, RATE_MATRIX, DECAY
    )
    keyval_new, keyval_mean_new, keyval_square_new = adam_update(
        keyval_weight, keyval_sum, keyval_mean, keyval_square, RATE_MATRIX, DECAY
    )
    output_new, output_mean_new, output_square_new = adam_update(
        output_weight, output_sum, output_mean, output_square, RATE_MATRIX, DECAY
    )
    gateup_new, gateup_mean_new, gateup_square_new = adam_update(
        gateup_weight, gateup_sum, gateup_mean, gateup_square, RATE_MATRIX, DECAY
    )
    down_new, down_mean_new, down_square_new = adam_update(
        down_weight, down_sum, down_mean, down_square, RATE_MATRIX, DECAY
    )
    gains_new, gains_mean_new, gains_square_new = adam_update(
        norm_gains, gains_sum, gains_mean, gains_square, RATE_GAIN, 0.0
    )
    return (
        result.astype(BF16)[None],
        token_grad[None],
        query_sum,
        keyval_sum,
        output_sum,
        gateup_sum,
        down_sum,
        gains_sum,
        query_new,
        keyval_new,
        output_new,
        gateup_new,
        down_new,
        gains_new,
        query_mean_new,
        keyval_mean_new,
        output_mean_new,
        gateup_mean_new,
        down_mean_new,
        gains_mean_new,
        query_square_new,
        keyval_square_new,
        output_square_new,
        gateup_square_new,
        down_square_new,
        gains_square_new,
    )


def solution(mesh):
    fine = Mesh(mesh.devices.reshape([SIZE[a] for a in AXES]), AXES)
    rows = P(("zl", "co"), ("zh", "x", "y"), None)
    packs = P(("zl", "co"), None)
    matrix = P(AXES, None)
    vector = P(AXES)
    params = [matrix] * 5 + [vector]
    return jax.shard_map(
        body,
        mesh=fine,
        in_specs=(rows, rows, packs, packs, *params, *params, *params),
        out_specs=(rows, rows, *params, *params, *params, *params),
        check_vma=False,
    )
```

```python
import functools
import math

import jax
import jax.numpy as jnp
from jax import lax
from jax.experimental import pallas as pl
from jax.experimental.pallas import tpu as pltpu
from jax.sharding import Mesh
from jax.sharding import PartitionSpec as P

D = 1024
H = 16
KVH = 8
HD = 128
FF = 3072
KV = 1024
STEP = 10
LONG = 3072
ROWS = 128
BLOCK = 64
CHUNK = 512
PACK_TOK = 4096
RANKS = 8
PLANE = 16


NORM_EPS = 1e-06
ROPE_BASE = 1000000.0
BETA_ONE = 0.9
BETA_TWO = 0.95
ADAM_EPS = 1e-08
DECAY = 0.1
RATE_MATRIX = 0.1
RATE_GAIN = 0.3

SCALE = HD**-0.5
LOG2E = math.log2(math.e)

AXES = ("zh", "x", "y", "zl", "co")
SIZE = {"zh": 2, "x": 4, "y": 4, "zl": 2, "co": 2}
COLUMN = ("zh", "zl", "co")
SURFACE = ("x", "y")
MESH = pl.DeviceIdType.MESH
F32 = jnp.float32
BF16 = jnp.bfloat16
VMEM_LIMIT = 50 * 1024 * 1024


def where_am_i():
    return {a: lax.axis_index(a) for a in AXES}


def address(place):
    return tuple(place[a] for a in AXES)


def flat_index(place, axes):
    at = 0
    for a in axes:
        at = at * SIZE[a] + place[a]
    return at


def shifted(place, axes, k, sign):
    to = dict(place)
    for a in reversed(axes):
        step = lax.rem(k, SIZE[a])
        k = lax.div(k, SIZE[a])
        to[a] = lax.rem(place[a] + sign * step + SIZE[a], SIZE[a])
    return to


def push_kernel(channels, n_in, n_out, *refs):
    ins, outs = refs[:n_in], refs[n_in : n_in + n_out]
    sems = refs[n_in + n_out :]
    me = where_am_i()
    barrier = pltpu.get_barrier_semaphore()
    greeted = max((c[2] for c in channels), key=len)
    peers = math.prod(SIZE[a] for a in greeted)

    def greet(k, carry):
        pl.semaphore_signal(
            barrier, inc=1, device_id=address(shifted(me, greeted, k, 1)), device_id_type=MESH
        )
        return carry

    lax.fori_loop(1, peers, greet, 0)
    own = []
    for i, (src, dst, axes, take, put) in enumerate(channels):
        copy = pltpu.make_async_copy(take(ins[src], me), put(outs[dst], me), sems[3 * i + 2])
        copy.start()
        own.append(copy)
    pl.semaphore_wait(barrier, peers - 1)
    for i, (src, dst, axes, take, put) in enumerate(channels):
        n = math.prod(SIZE[a] for a in axes)
        mix = {4: 1, 8: 3, 16: 7}[n]

        def begin(j, carry):
            k = lax.rem(j * mix, n)
            to = shifted(me, axes, k, 1)
            pltpu.make_async_remote_copy(
                src_ref=take(ins[src], to),
                dst_ref=put(outs[dst], me),
                send_sem=sems[3 * i].at[k],
                recv_sem=sems[3 * i + 1].at[k],
                device_id=address(to),
                device_id_type=MESH,
            ).start()
            return carry

        lax.fori_loop(1, n, begin, 0)
    for copy in own:
        copy.wait()
    for i, (src, dst, axes, take, put) in enumerate(channels):
        n = math.prod(SIZE[a] for a in axes)
        mix = {4: 1, 8: 3, 16: 7}[n]

        def finish(j, carry):
            k = lax.rem(j * mix, n)
            to, back = shifted(me, axes, k, 1), shifted(me, axes, k, -1)
            copy = pltpu.make_async_remote_copy(
                src_ref=take(ins[src], to),
                dst_ref=put(outs[dst], back),
                send_sem=sems[3 * i].at[k],
                recv_sem=sems[3 * i + 1].at[k],
                device_id=address(to),
                device_id_type=MESH,
            )
            copy.wait_send()
            copy.wait_recv()
            return carry

        lax.fori_loop(1, n, finish, 0)


def push(name, number, arrays, out_shapes, channels):
    scratch = []
    for _, _, axes, _, _ in channels:
        n = math.prod(SIZE[a] for a in axes)
        scratch += [
            pltpu.SemaphoreType.DMA((n,)),
            pltpu.SemaphoreType.DMA((n,)),
            pltpu.SemaphoreType.DMA,
        ]
    return pl.pallas_call(
        functools.partial(push_kernel, channels, len(arrays), len(out_shapes)),
        out_shape=tuple(jax.ShapeDtypeStruct(s, t) for s, t in out_shapes),
        in_specs=[pl.BlockSpec(memory_space=pl.ANY)] * len(arrays),
        out_specs=tuple([pl.BlockSpec(memory_space=pl.ANY)] * len(out_shapes)),
        scratch_shapes=scratch,
        compiler_params=pltpu.CompilerParams(collective_id=number, has_side_effects=True),
        name=name,
    )(*arrays)


def column_place(me, z, core):
    return dict(me, zh=lax.div(z, 2), zl=lax.rem(z, 2), co=core)


def greet_column(me, z, core):
    barrier = pltpu.get_barrier_semaphore()
    for off in (1, 2, 3):
        to = column_place(me, lax.rem(z + off, 4), core)
        pl.semaphore_signal(barrier, inc=1, device_id=address(to), device_id_type=MESH)
    sibling = column_place(me, z, 1 - core)
    pl.semaphore_signal(barrier, inc=1, device_id=address(sibling), device_id_type=MESH)
    pl.semaphore_wait(barrier, 4)


def gather_kernel(x_ref, out_ref, far_send, far_recv, near_send, near_recv, own_sem):
    me = where_am_i()
    z, core = me["zh"] * 2 + me["zl"], me["co"]
    sibling = address(column_place(me, z, 1 - core))
    own = pltpu.make_async_copy(x_ref, out_ref.at[z * 2 + core], own_sem)
    own.start()
    greet_column(me, z, core)

    def far(off):
        return pltpu.make_async_remote_copy(
            src_ref=x_ref,
            dst_ref=out_ref.at[z * 2 + core],
            send_sem=far_send.at[off],
            recv_sem=far_recv.at[off],
            device_id=address(column_place(me, lax.rem(z + off, 4), core)),
            device_id_type=MESH,
        )

    def near(off, core_of):
        slot = lax.rem(z + 4 - off, 4) * 2 + core_of
        return pltpu.make_async_remote_copy(
            src_ref=x_ref if off == 0 else out_ref.at[slot],
            dst_ref=out_ref.at[slot],
            send_sem=near_send.at[off],
            recv_sem=near_recv.at[off],
            device_id=sibling,
            device_id_type=MESH,
        )

    for off in (1, 3, 2):
        far(off).start()
    near(0, core).start()
    for off in (1, 3, 2):
        slot = lax.rem(z + 4 - off, 4) * 2 + core
        pltpu.make_async_remote_copy(
            src_ref=x_ref,
            dst_ref=out_ref.at[slot],
            send_sem=far_send.at[off],
            recv_sem=far_recv.at[off],
            device_id=address(column_place(me, lax.rem(z + off, 4), core)),
            device_id_type=MESH,
        ).wait_recv()
        near(off, core).start()
    own.wait()
    for off in (1, 3, 2):
        far(off).wait_send()
    for off in (0, 1, 3, 2):
        near(off, core).wait_send()
        near(off, 1 - core).wait_recv()


def gather_column(name, number, x):
    return pl.pallas_call(
        gather_kernel,
        out_shape=jax.ShapeDtypeStruct((RANKS,) + x.shape, x.dtype),
        in_specs=[pl.BlockSpec(memory_space=pl.ANY)],
        out_specs=pl.BlockSpec(memory_space=pl.ANY),
        scratch_shapes=[pltpu.SemaphoreType.DMA((4,))] * 4 + [pltpu.SemaphoreType.DMA],
        compiler_params=pltpu.CompilerParams(collective_id=number, has_side_effects=True),
        name=name,
    )(x)


def sum_kernel(
    part_ref, out_ref, paired, sending, landed, near_send, near_recv, far_send, far_recv
):
    me = where_am_i()
    z, core = me["zh"] * 2 + me["zl"], me["co"]
    sibling = address(column_place(me, z, 1 - core))
    greet_column(me, z, core)

    def near(off):
        to_z = lax.rem(z + off, 4)
        return pltpu.make_async_remote_copy(
            src_ref=part_ref.at[to_z * 2 + (1 - core)],
            dst_ref=paired.at[off],
            send_sem=near_send.at[off],
            recv_sem=near_recv.at[off],
            device_id=sibling,
            device_id_type=MESH,
        )

    def far(off):
        return pltpu.make_async_remote_copy(
            src_ref=sending.at[off],
            dst_ref=landed.at[off],
            send_sem=far_send.at[off],
            recv_sem=far_recv.at[off],
            device_id=address(column_place(me, lax.rem(z + off, 4), core)),
            device_id_type=MESH,
        )

    for off in (2, 1, 3, 0):
        near(off).start()
    for off in (2, 1, 3):
        near(off).wait_recv()
        mine = part_ref[lax.rem(z + off, 4) * 2 + core].astype(F32)
        sending[off] = (mine + paired[off].astype(F32)).astype(BF16)
        far(off).start()
    near(0).wait_recv()
    out_ref[...] = part_ref[z * 2 + core].astype(F32) + paired[0].astype(F32)
    for off in (1, 3, 2):
        far(off).wait_recv()
        out_ref[...] += landed[off].astype(F32)
    for off in (2, 1, 3):
        near(off).wait_send()
        far(off).wait_send()
    near(0).wait_send()


def sum_column(name, number, parts):
    block = parts.shape[1:]
    return pl.pallas_call(
        sum_kernel,
        out_shape=jax.ShapeDtypeStruct(block, F32),
        in_specs=[pl.BlockSpec(memory_space=pltpu.VMEM)],
        out_specs=pl.BlockSpec(memory_space=pltpu.VMEM),
        scratch_shapes=[pltpu.VMEM((4,) + block, BF16)] * 3
        + [pltpu.SemaphoreType.DMA((4,))] * 4,
        compiler_params=pltpu.CompilerParams(
            collective_id=number, has_side_effects=True, vmem_limit_bytes=VMEM_LIMIT
        ),
        name=name,
    )(parts)


def dot_nn(a, b):
    return lax.dot_general(a, b, (((1,), (0,)), ((), ())), preferred_element_type=F32)


def dot_nt(a, b):
    return lax.dot_general(a, b, (((1,), (1,)), ((), ())), preferred_element_type=F32)


def dot_tn(a, b):
    return lax.dot_general(a, b, (((0,), (0,)), ((), ())), preferred_element_type=F32)


def stacked_heads(ref, tile):
    rows = ref[pl.ds(tile * BLOCK, BLOCK), :]
    return jnp.concatenate([rows[:, :HD], rows[:, HD:]], axis=0)


def allowed_keys(block, chunk):
    keys = chunk * CHUNK + lax.broadcasted_iota(jnp.int32, (CHUNK, 2 * BLOCK), 0)
    lanes = lax.broadcasted_iota(jnp.int32, (CHUNK, 2 * BLOCK), 1)
    return keys <= block * BLOCK + lax.rem(lanes, BLOCK)


def first_chunk(block):
    return jnp.where(block >= LONG // BLOCK, LONG // CHUNK, 0)


def attend_kernel(q_blocks, k_blocks, q_ref, kv_ref, out_ref, lse_ref, keys, values, values_t):
    def sort(i, carry):
        to = pl.multiple_of(k_blocks[i] * BLOCK, BLOCK)
        here = pl.multiple_of(i * BLOCK, BLOCK)
        keys[pl.ds(to, BLOCK), :] = kv_ref[pl.ds(here, BLOCK), :HD]
        values[pl.ds(to, BLOCK), :] = kv_ref[pl.ds(here, BLOCK), HD:]
        return carry

    lax.fori_loop(0, PACK_TOK // BLOCK, sort, 0)
    for c in range(PACK_TOK // CHUNK):
        part = values[c * CHUNK : (c + 1) * CHUNK, :].astype(F32)
        values_t[c] = part.T.astype(BF16)

    def one_tile(tile, carry):
        block = q_blocks[tile]
        query = stacked_heads(q_ref, tile)
        last = lax.div(block, CHUNK // BLOCK)

        def one_chunk(c, state, masked):
            total, mixed = state
            chunk_keys = keys[pl.ds(pl.multiple_of(c * CHUNK, CHUNK), CHUNK), :]
            weights = jnp.exp2(dot_nt(chunk_keys, query) * (SCALE * LOG2E))
            if masked:
                weights = jnp.where(allowed_keys(block, c), weights, 0.0)
            total = total + jnp.sum(weights, axis=0, keepdims=True)
            mixed = mixed + dot_nn(values_t[c], weights.astype(BF16))
            return total, mixed

        state = (jnp.zeros((1, 2 * BLOCK), F32), jnp.zeros((HD, 2 * BLOCK), F32))
        state = lax.fori_loop(
            first_chunk(block), last, lambda c, s: one_chunk(c, s, False), state
        )
        total, mixed = one_chunk(last, state, True)
        result = (mixed / total).T.astype(BF16)
        rows = pl.ds(pl.multiple_of(tile * BLOCK, BLOCK), BLOCK)
        out_ref[rows, :HD] = result[:BLOCK]
        out_ref[rows, HD:] = result[BLOCK:]
        lse_ref[pl.ds(tile, 1), :] = jnp.log2(total)
        return carry

    lax.fori_loop(0, q_ref.shape[0] // BLOCK, one_tile, 0)


def attend(q_blocks, k_blocks, q, kv):
    smem = pl.BlockSpec(memory_space=pltpu.SMEM)
    vmem = pl.BlockSpec(memory_space=pltpu.VMEM)
    tiles = q.shape[0] // BLOCK
    return pl.pallas_call(
        attend_kernel,
        out_shape=(
            jax.ShapeDtypeStruct(q.shape, BF16),
            jax.ShapeDtypeStruct((tiles, 2 * BLOCK), F32),
        ),
        in_specs=[smem, smem, vmem, vmem],
        out_specs=(vmem, vmem),
        scratch_shapes=[
            pltpu.VMEM((PACK_TOK, HD), BF16),
            pltpu.VMEM((PACK_TOK, HD), BF16),
            pltpu.VMEM((PACK_TOK // CHUNK, HD, CHUNK), BF16),
        ],
        compiler_params=pltpu.CompilerParams(vmem_limit_bytes=VMEM_LIMIT),
        cost_estimate=pl.CostEstimate(
            flops=4 * 10**9, bytes_accessed=4 * 10**6, transcendentals=8 * 10**6
        ),
        name="attend",
    )(q_blocks, k_blocks, q, kv)


def attend_back_kernel(
    q_blocks,
    k_blocks,
    q_ref,
    kv_ref,
    grad_ref,
    out_ref,
    lse_ref,
    dq_ref,
    dkv_ref,
    keys,
    values,
    keys_t,
    dk,
    dv,
):
    def sort(i, carry):
        to = pl.multiple_of(k_blocks[i] * BLOCK, BLOCK)
        here = pl.multiple_of(i * BLOCK, BLOCK)
        keys[pl.ds(to, BLOCK), :] = kv_ref[pl.ds(here, BLOCK), :HD]
        values[pl.ds(to, BLOCK), :] = kv_ref[pl.ds(here, BLOCK), HD:]
        return carry

    lax.fori_loop(0, PACK_TOK // BLOCK, sort, 0)
    for c in range(PACK_TOK // CHUNK):
        part = keys[c * CHUNK : (c + 1) * CHUNK, :].astype(F32)
        keys_t[c] = part.T.astype(BF16)
    dk[...] = jnp.zeros_like(dk)
    dv[...] = jnp.zeros_like(dv)

    def one_tile(tile, carry):
        block = q_blocks[tile]
        query = stacked_heads(q_ref, tile)
        grad = stacked_heads(grad_ref, tile)
        out = stacked_heads(out_ref, tile)
        inner = jnp.sum((grad.astype(F32) * out.astype(F32)).T, axis=0, keepdims=True)
        lse = lse_ref[pl.ds(tile, 1), :]
        last = lax.div(block, CHUNK // BLOCK)

        def one_chunk(c, dq, masked):
            rows = pl.ds(pl.multiple_of(c * CHUNK, CHUNK), CHUNK)
            probs = jnp.exp2(dot_nt(keys[rows, :], query) * (SCALE * LOG2E) - lse)
            if masked:
                probs = jnp.where(allowed_keys(block, c), probs, 0.0)
            grad_probs = dot_nt(values[rows, :], grad)
            grad_scores = (probs * (grad_probs - inner)).astype(BF16)
            dv[rows, :] += dot_nn(probs.astype(BF16), grad)
            dk[rows, :] += dot_nn(grad_scores, query)
            return dq + dot_nn(keys_t[c], grad_scores)

        dq = lax.fori_loop(
            first_chunk(block),
            last,
            lambda c, s: one_chunk(c, s, False),
            jnp.zeros((HD, 2 * BLOCK), F32),
        )
        dq = (one_chunk(last, dq, True) * SCALE).T.astype(BF16)
        rows = pl.ds(pl.multiple_of(tile * BLOCK, BLOCK), BLOCK)
        dq_ref[rows, :HD] = dq[:BLOCK]
        dq_ref[rows, HD:] = dq[BLOCK:]
        return carry

    lax.fori_loop(0, q_ref.shape[0] // BLOCK, one_tile, 0)

    def unsort(i, carry):
        at = pl.multiple_of(k_blocks[i] * BLOCK, BLOCK)
        here = pl.multiple_of(i * BLOCK, BLOCK)
        dkv_ref[pl.ds(here, BLOCK), :HD] = (dk[pl.ds(at, BLOCK), :] * SCALE).astype(BF16)
        dkv_ref[pl.ds(here, BLOCK), HD:] = dv[pl.ds(at, BLOCK), :].astype(BF16)
        return carry

    lax.fori_loop(0, PACK_TOK // BLOCK, unsort, 0)


def attend_back(q_blocks, k_blocks, q, kv, grad, out, lse):
    smem = pl.BlockSpec(memory_space=pltpu.SMEM)
    vmem = pl.BlockSpec(memory_space=pltpu.VMEM)
    return pl.pallas_call(
        attend_back_kernel,
        out_shape=(
            jax.ShapeDtypeStruct(q.shape, BF16),
            jax.ShapeDtypeStruct(kv.shape, BF16),
        ),
        in_specs=[smem, smem] + [vmem] * 5,
        out_specs=(vmem, vmem),
        scratch_shapes=[
            pltpu.VMEM((PACK_TOK, HD), BF16),
            pltpu.VMEM((PACK_TOK, HD), BF16),
            pltpu.VMEM((PACK_TOK // CHUNK, HD, CHUNK), BF16),
            pltpu.VMEM((PACK_TOK, HD), F32),
            pltpu.VMEM((PACK_TOK, HD), F32),
        ],
        compiler_params=pltpu.CompilerParams(vmem_limit_bytes=VMEM_LIMIT),
        cost_estimate=pl.CostEstimate(
            flops=10**10, bytes_accessed=8 * 10**6, transcendentals=8 * 10**6
        ),
        name="attend_back",
    )(q_blocks, k_blocks, q, kv, grad, out, lse)


class ColumnSums:
    def __init__(self, me, part, paired, sending, landed, near_send, near_recv, far_send, far_recv):
        self.me, self.z, self.core = me, me["zh"] * 2 + me["zl"], me["co"]
        self.part, self.paired, self.sending, self.landed = part, paired, sending, landed
        self.near_sems, self.far_sems = (near_send, near_recv), (far_send, far_recv)

    def near(self, phase, off):
        return pltpu.make_async_remote_copy(
            src_ref=self.part.at[phase, off, 1 - self.core],
            dst_ref=self.paired.at[phase, off],
            send_sem=self.near_sems[0].at[phase, off],
            recv_sem=self.near_sems[1].at[phase, off],
            device_id=address(column_place(self.me, self.z, 1 - self.core)),
            device_id_type=MESH,
        )

    def far(self, phase, off):
        return pltpu.make_async_remote_copy(
            src_ref=self.sending.at[phase, off],
            dst_ref=self.landed.at[phase, off],
            send_sem=self.far_sems[0].at[phase, off],
            recv_sem=self.far_sems[1].at[phase, off],
            device_id=address(column_place(self.me, lax.rem(self.z + off, 4), self.core)),
            device_id_type=MESH,
        )

    def put(self, phase, off, terms):
        self.part[phase, off] = terms.astype(BF16).reshape(2, ROWS, D)
        self.near(phase, off).start()

    def pass_on(self, phase, off):
        self.near(phase, off).wait_recv()
        both = self.part[phase, off, self.core].astype(F32) + self.paired[phase, off].astype(F32)
        self.sending[phase, off] = both.astype(BF16)
        self.far(phase, off).start()

    def total(self, phase):
        self.near(phase, 0).wait_recv()
        total = self.part[phase, 0, self.core].astype(F32) + self.paired[phase, 0].astype(F32)
        for off in (1, 3, 2):
            self.far(phase, off).wait_recv()
            total = total + self.landed[phase, off].astype(F32)
        return total

    def drain(self, phase):
        for off in range(4):
            self.near(phase, off).wait_send()
            if off:
                self.far(phase, off).wait_send()


class ColumnGathers:
    def __init__(self, me, blocks, near_send, near_recv, far_send, far_recv):
        self.me, self.z, self.core = me, me["zh"] * 2 + me["zl"], me["co"]
        self.blocks = blocks
        self.near_sems, self.far_sems = (near_send, near_recv), (far_send, far_recv)

    def far(self, phase, off, arriving):
        z = lax.rem(self.z + 4 - off, 4) if arriving else self.z
        block = self.blocks.at[phase, z * 2 + self.core]
        return pltpu.make_async_remote_copy(
            src_ref=block,
            dst_ref=block,
            send_sem=self.far_sems[0].at[phase, off],
            recv_sem=self.far_sems[1].at[phase, off],
            device_id=address(column_place(self.me, lax.rem(self.z + off, 4), self.core)),
            device_id_type=MESH,
        )

    def near(self, phase, off, arriving):
        core = 1 - self.core if arriving else self.core
        block = self.blocks.at[phase, lax.rem(self.z + 4 - off, 4) * 2 + core]
        return pltpu.make_async_remote_copy(
            src_ref=block,
            dst_ref=block,
            send_sem=self.near_sems[0].at[phase, off],
            recv_sem=self.near_sems[1].at[phase, off],
            device_id=address(column_place(self.me, self.z, 1 - self.core)),
            device_id_type=MESH,
        )

    def begin(self, phase, rows):
        self.blocks[phase, self.z * 2 + self.core] = rows
        for off in (1, 3, 2):
            self.far(phase, off, False).start()
        self.near(phase, 0, False).start()

    def await_chip(self, phase, i):
        off = i + lax.div(i, 2) * (5 - 2 * i)

        @pl.when(i == 1)
        def _():
            for near_by in (1, 3):
                self.far(phase, near_by, True).wait_recv()
                self.near(phase, near_by, False).start()

        @pl.when(i == 3)
        def _():
            self.far(phase, 2, True).wait_recv()
            self.near(phase, 2, False).start()

        self.near(phase, off, True).wait_recv()
        return off, lax.rem(self.z + 4 - off, 4)

    def drain(self, phase):
        for off in range(4):
            self.near(phase, off, False).wait_send()
            if off:
                self.far(phase, off, False).wait_send()


def norm_factor(values):
    return lax.rsqrt(jnp.mean(values * values, axis=-1, keepdims=True) + NORM_EPS)


def norm_back(values, norm_gain, grad):
    factor = norm_factor(values)
    scaled = grad * norm_gain
    inner = jnp.mean(values * scaled, axis=-1, keepdims=True)
    grad_gain = jnp.sum(grad * values * factor, axis=0, keepdims=True)
    return factor * scaled - values * (factor * factor * factor * inner), grad_gain


def quarter(place):
    return place["zl"] * 2 + place["co"]


def at_quarter(place, t):
    return dict(place, zl=lax.div(t, 2), co=lax.rem(t, 2))


def row_user(me, k):
    return at_quarter(shifted(me, SURFACE, k, 1), me["x"])


def row_owner(me, k):
    y, t = lax.div(k, 4), lax.rem(k, 4)
    to = dict(me, x=quarter(me), y=lax.rem(me["y"] + y, 4))
    return at_quarter(to, lax.rem(quarter(me) + t, 4))


def row_slot(owner):
    return owner["y"] * 4 + quarter(owner)


def greet(barrier, place):
    pl.semaphore_signal(barrier, inc=1, device_id=address(place), device_id_type=MESH)


def greet_all(me, column, rows):
    barrier = pltpu.get_barrier_semaphore()

    def greet_surface(k, carry):
        greet(barrier, shifted(me, SURFACE, k, 1))
        return carry

    def greet_column_all(k, carry):
        greet(barrier, shifted(me, COLUMN, k, 1))
        return carry

    lax.fori_loop(1, PLANE, greet_surface, 0)
    expected = PLANE - 1
    if column == "all":
        lax.fori_loop(1, RANKS, greet_column_all, 0)
        expected = expected + RANKS - 1
    else:
        z = me["zh"] * 2 + me["zl"]
        for off in (1, 2, 3):
            greet(barrier, column_place(me, lax.rem(z + off, 4), me["co"]))
        greet(barrier, column_place(me, z, 1 - me["co"]))
        expected = expected + 4
    if rows is not None:
        at_home = me["x"] == quarter(me)

        def greet_rows(k, carry):
            @pl.when(jnp.logical_not(jnp.logical_and(k == 0, at_home)))
            def _():
                if rows != "own":
                    greet(barrier, row_owner(me, k))
                if rows != "use":
                    greet(barrier, row_user(me, k))

            return carry

        lax.fori_loop(0, PLANE, greet_rows, 0)
        count = PLANE - jnp.where(at_home, 1, 0)
        expected = expected + (2 * count if rows == "both" else count)
    pl.semaphore_wait(barrier, expected)


class RowCopies:
    def __init__(self, me, src, dst, send, recv, back):
        self.me, self.src, self.dst, self.send, self.recv, self.back = me, src, dst, send, recv, back
        self.at_home = me["x"] == quarter(me)

    def copy(self, k, arriving):
        me = self.me
        if self.back:
            to = row_owner(me, k)
            frm = row_user(me, k) if arriving else me
            src, slot = self.src.at[row_slot(to)], flat_index(frm, SURFACE)
        else:
            to = row_user(me, k)
            frm = row_owner(me, k) if arriving else me
            src, slot = self.src, row_slot(frm)
        return pltpu.make_async_remote_copy(
            src_ref=src,
            dst_ref=self.dst.at[slot],
            send_sem=self.send.at[k],
            recv_sem=self.recv.at[slot],
            device_id=address(to),
            device_id_type=MESH,
        )

    def own(self):
        me = self.me
        if self.back:
            src, slot = self.src.at[row_slot(me)], flat_index(me, SURFACE)
        else:
            src, slot = self.src, row_slot(me)
        return pltpu.make_async_copy(src, self.dst.at[slot], self.recv.at[slot])

    def each(self, remote, own):
        def one(j, carry):
            k = lax.rem(j * 7, PLANE)
            itself = jnp.logical_and(k == 0, self.at_home)

            @pl.when(itself)
            def _():
                own()

            @pl.when(jnp.logical_not(itself))
            def _():
                remote(k)

            return carry

        lax.fori_loop(0, PLANE, one, 0)

    def begin(self):
        self.each(lambda k: self.copy(k, False).start(), lambda: self.own().start())

    def arrive(self):
        self.each(lambda k: self.copy(k, True).wait_recv(), lambda: self.own().wait())

    def drain(self):
        self.each(lambda k: self.copy(k, False).wait_send(), lambda: None)


class Exchange:
    def __init__(self, me, axes, take, put, send, recv):
        self.me, self.axes, self.take, self.put, self.send, self.recv = me, axes, take, put, send, recv
        self.n = math.prod(SIZE[a] for a in axes)
        self.mix = {4: 1, 8: 3, 16: 7}[self.n]

    def copy(self, k, arriving):
        to = shifted(self.me, self.axes, k, 1)
        frm = shifted(self.me, self.axes, k, -1) if arriving else self.me
        return pltpu.make_async_remote_copy(
            src_ref=self.take(to),
            dst_ref=self.put(frm),
            send_sem=self.send.at[k],
            recv_sem=self.recv.at[k],
            device_id=address(to),
            device_id_type=MESH,
        )

    def each(self, act):
        def one(j, carry):
            act(lax.rem(j * self.mix, self.n))
            return carry

        lax.fori_loop(1, self.n, one, 0)

    def begin(self):
        self.each(lambda k: self.copy(k, False).start())

    def arrive(self):
        self.each(lambda k: self.copy(k, True).wait_recv())

    def drain(self):
        self.each(lambda k: self.copy(k, False).wait_send())


def start_kernel(
    sent_a,
    sent_b,
    tokens,
    output_rows,
    frequency,
    q_mine,
    kv_mine,
    all_tokens,
    output_wide,
    gateup_low,
    extra_out,
    gains_out,
    qkv_part,
    projected,
    cosine,
    sine,
    head_gains,
    shares_a,
    shares_b,
    wide,
    blocks,
    queries,
    keyvals,
    a_send,
    a_recv,
    b_send,
    b_recv,
    w_send,
    w_recv,
    row_send,
    row_recv,
    near_send,
    near_recv,
    far_send,
    far_recv,
    q_send,
    q_recv,
    kv_send,
    kv_recv,
    relay_send,
    relay_recv,
    own_sems,
):
    me = where_am_i()
    x, y = me["x"], me["y"]
    rank, here = flat_index(me, COLUMN), flat_index(me, SURFACE)
    gathers = ColumnGathers(me, blocks, near_send, near_recv, far_send, far_recv)
    to_a = Exchange(
        me,
        COLUMN,
        lambda to: sent_a.at[flat_index(to, COLUMN)],
        lambda frm: shares_a.at[flat_index(frm, COLUMN)],
        a_send,
        a_recv,
    )
    to_b = Exchange(
        me,
        COLUMN,
        lambda to: sent_b.at[flat_index(to, COLUMN)],
        lambda frm: shares_b.at[flat_index(frm, COLUMN)],
        b_send,
        b_recv,
    )
    spread = Exchange(
        me,
        SURFACE,
        lambda to: wide.at[:, here],
        lambda frm: wide.at[:, flat_index(frm, SURFACE)],
        w_send,
        w_recv,
    )
    rows = RowCopies(me, output_rows, output_wide, row_send, row_recv, False)
    own_a = pltpu.make_async_copy(sent_a.at[rank], shares_a.at[rank], own_sems.at[0])
    own_b = pltpu.make_async_copy(sent_b.at[rank], shares_b.at[rank], own_sems.at[1])
    own_a.start()
    own_b.start()
    greet_all(me, "all", "both")
    to_a.begin()
    gathers.begin(0, tokens[...])
    rows.begin()
    to_b.begin()

    own_a.wait()
    to_a.arrive()
    wide[:, here] = shares_a[...].astype(BF16).reshape(2, 32, 640)
    spread.begin()
    extra_out[...] = shares_a[:, :, 512:]

    lanes = lax.broadcasted_iota(jnp.int32, (BLOCK, HD), 1)
    place = lax.broadcasted_iota(jnp.int32, (BLOCK, HD), 0).astype(F32)

    def tables(j, carry):
        for half in range(2):
            first = shares_a[j, 2 + half : 3 + half, 512:]
            angles = (first * float(BLOCK) + place) * frequency[...]
            at = pl.ds(pl.multiple_of(j * ROWS + half * BLOCK, BLOCK), BLOCK)
            cosine[at, :] = jnp.cos(angles)
            sines = jnp.sin(angles)
            sine[at, :] = jnp.where(lanes < HD // 2, -sines, sines)
        return carry

    lax.fori_loop(0, RANKS, tables, 0)
    own_b.wait()
    to_b.arrive()
    gateup_low[...] = shares_b[...].astype(BF16).reshape(2, 32, 768)

    spread.arrive()
    qkv_part[...] = wide[..., :512].reshape(D, 512)
    extra = wide[..., 512:].reshape(D, HD)
    gains_out[...] = extra
    entry = 2 * D + lax.broadcasted_iota(jnp.int32, (HD, 2 * HD), 1)
    pick = (lax.broadcasted_iota(jnp.int32, (HD, 2 * HD), 0) == lax.rem(entry, 18)).astype(BF16)
    entries = 2 * D + lax.broadcasted_iota(jnp.int32, (D, 2 * HD), 1)
    owned = lax.broadcasted_iota(jnp.int32, (D, 2 * HD), 0) == 8 * lax.div(entries, 18)
    gains = jnp.sum(jnp.where(owned, dot_nn(extra, pick), 0.0), axis=0, keepdims=True)
    head_gains[0:1, :] = gains[:, :HD]
    head_gains[1:2, :] = gains[:, HD:]

    def q_copy(row_zh, pack):
        return pltpu.make_async_remote_copy(
            src_ref=queries.at[row_zh, pack],
            dst_ref=q_mine.at[x, row_zh],
            send_sem=q_send.at[row_zh, pack],
            recv_sem=q_recv.at[row_zh, x],
            device_id=address(dict(me, x=pack)),
            device_id_type=MESH,
        )

    def kv_copy(row_zh, pack):
        return pltpu.make_async_remote_copy(
            src_ref=keyvals.at[row_zh, pack],
            dst_ref=kv_mine.at[here, row_zh],
            send_sem=kv_send.at[row_zh, pack],
            recv_sem=kv_recv.at[row_zh, x],
            device_id=address(dict(me, x=pack)),
            device_id_type=MESH,
        )

    def q_own(row_zh):
        return pltpu.make_async_copy(
            queries.at[row_zh, x], q_mine.at[x, row_zh], own_sems.at[2 + row_zh]
        )

    def kv_own(row_zh):
        return pltpu.make_async_copy(
            keyvals.at[row_zh, x], kv_mine.at[here, row_zh], own_sems.at[4 + row_zh]
        )

    def relay(row_zh, from_x, k, arriving):
        to_y = lax.rem(y + k, 4)
        from_y = lax.rem(y + 4 - k, 4) if arriving else y
        block = kv_mine.at[from_x * 4 + from_y, row_zh]
        return pltpu.make_async_remote_copy(
            src_ref=block,
            dst_ref=block,
            send_sem=relay_send.at[row_zh, from_x, k],
            recv_sem=relay_recv.at[row_zh, from_x, k],
            device_id=address(dict(me, y=to_y)),
            device_id_type=MESH,
        )

    def project(i, carry):
        off, at_z = gathers.await_chip(0, i)
        at = pl.ds(pl.multiple_of(at_z * 2 * ROWS, 2 * ROWS), 2 * ROWS)
        both = dot_nn(blocks[0, pl.ds(at_z * 2, 2)].reshape(2 * ROWS, D), qkv_part[...])
        projected[at, :] = both[:, :384]
        row_zh, first = lax.div(at_z, 2), lax.rem(at_z, 2) * 2
        for head in range(3):
            values = both[:, head * HD : (head + 1) * HD]
            gain = head_gains[1:2, :] if head == 2 else head_gains[0:1, :]
            normed = values * norm_factor(values) * gain
            turned = (
                normed * cosine[at, :] + pltpu.roll(normed, HD // 2, 1) * sine[at, :]
            ).astype(BF16)
            turned = turned.reshape(2, ROWS, HD)
            for at_core in range(2):
                if head == 2:
                    keyvals[row_zh, first + at_core, :, :HD] = turned[at_core]
                else:
                    queries[row_zh, first + at_core, :, head * HD : (head + 1) * HD] = turned[
                        at_core
                    ]
        values = both[:, 384:].astype(BF16).reshape(2, ROWS, HD)
        for at_core in range(2):
            pack = first + at_core
            keyvals[row_zh, pack, :, HD:] = values[at_core]

            @pl.when(pack != x)
            def _():
                kv_copy(row_zh, pack).start()
                q_copy(row_zh, pack).start()

            @pl.when(pack == x)
            def _():
                kv_own(row_zh).start()
                q_own(row_zh).start()

        return carry

    lax.fori_loop(0, 4, project, 0)
    for i in range(RANKS):
        slot = pltpu.make_async_copy(blocks.at[0, i], all_tokens.at[i], own_sems.at[6 + i])
        slot.start()
    for row_zh in range(2):
        kv_own(row_zh).wait()
        for k in (2, 1, 3):
            relay(row_zh, x, k, False).start()
    for off in (1, 3, 2):
        from_x = lax.rem(x + 4 - off, 4)
        to_x = lax.rem(x + off, 4)
        for row_zh in range(2):
            pltpu.make_async_remote_copy(
                src_ref=keyvals.at[row_zh, to_x],
                dst_ref=kv_mine.at[from_x * 4 + y, row_zh],
                send_sem=kv_send.at[row_zh, to_x],
                recv_sem=kv_recv.at[row_zh, from_x],
                device_id=address(dict(me, x=to_x)),
                device_id_type=MESH,
            ).wait_recv()
            for k in (2, 1, 3):
                relay(row_zh, from_x, k, False).start()
    for off in (1, 3, 2):
        from_x = lax.rem(x + 4 - off, 4)
        to_x = lax.rem(x + off, 4)
        for row_zh in range(2):
            pltpu.make_async_remote_copy(
                src_ref=queries.at[row_zh, to_x],
                dst_ref=q_mine.at[from_x, row_zh],
                send_sem=q_send.at[row_zh, to_x],
                recv_sem=q_recv.at[row_zh, from_x],
                device_id=address(dict(me, x=to_x)),
                device_id_type=MESH,
            ).wait()
            kv_copy(row_zh, to_x).wait_send()
    for row_zh in range(2):
        q_own(row_zh).wait()

    def finish(j, carry):
        row_zh, from_x = lax.div(j, 4), lax.rem(j, 4)
        for k in (1, 3, 2):
            relay(row_zh, from_x, k, False).wait_send()
            relay(row_zh, from_x, k, True).wait_recv()
        return carry

    lax.fori_loop(0, 8, finish, 0)
    rows.arrive()
    for i in range(RANKS):
        pltpu.make_async_copy(blocks.at[0, i], all_tokens.at[i], own_sems.at[6 + i]).wait()
    for exchange in (to_a, to_b, spread, rows):
        exchange.drain()
    gathers.drain(0)


def start(number, sent_a, sent_b, tokens, output_rows, frequency):
    anywhere = pl.BlockSpec(memory_space=pl.ANY)
    vmem = pl.BlockSpec(memory_space=pltpu.VMEM)
    dma = pltpu.SemaphoreType.DMA
    struct = jax.ShapeDtypeStruct
    return pl.pallas_call(
        start_kernel,
        out_shape=(
            struct((4, 2, ROWS, 256), BF16),
            struct((PLANE, 2, ROWS, 256), BF16),
            struct((RANKS, ROWS, D), BF16),
            struct((PLANE, 16, D), BF16),
            struct((2, 32, 768), BF16),
            struct((RANKS, 8, HD), F32),
            struct((D, HD), BF16),
            struct((D, 512), BF16),
            struct((RANKS * ROWS, 384), F32),
            struct((RANKS * ROWS, HD), F32),
            struct((RANKS * ROWS, HD), F32),
            struct((2, HD), F32),
        ),
        in_specs=[anywhere, anywhere, vmem, anywhere, vmem],
        out_specs=(anywhere, anywhere, anywhere, anywhere) + (vmem,) * 8,
        scratch_shapes=[
            pltpu.VMEM((RANKS, 8, 640), F32),
            pltpu.VMEM((RANKS, 8, 768), F32),
            pltpu.VMEM((2, PLANE, 32, 640), BF16),
            pltpu.VMEM((1, RANKS, ROWS, D), BF16),
            pltpu.VMEM((2, 4, ROWS, 256), BF16),
            pltpu.VMEM((2, 4, ROWS, 256), BF16),
        ]
        + [dma((RANKS,))] * 4
        + [dma((PLANE,))] * 4
        + [dma((1, 4))] * 4
        + [dma((2, 4))] * 4
        + [dma((2, 4, 4)), dma((2, 4, 4)), dma((6 + RANKS,))],
        compiler_params=pltpu.CompilerParams(
            collective_id=number, has_side_effects=True, vmem_limit_bytes=VMEM_LIMIT
        ),
        name="start",
    )(sent_a, sent_b, tokens, output_rows, frequency)


def middle_kernel(
    out_mine,
    wo,
    gateup_low,
    down_rows_low,
    inputs,
    upstream,
    gains,
    result,
    grad_hidden,
    gains_grad,
    grad_mine,
    gateup_parts,
    down_parts,
    output_lines,
    attended,
    blocks,
    part,
    paired,
    sending,
    landed,
    gate_up,
    activated,
    grad_gate,
    grad_attended,
    gateup_lines,
    down_grad,
    down_lines,
    branch,
    hidden,
    wgu,
    down_wide,
    wd,
    near_send,
    near_recv,
    far_send,
    far_recv,
    gnear_send,
    gnear_recv,
    gfar_send,
    gfar_recv,
    att_send,
    att_recv,
    back_send,
    back_recv,
    plane_send,
    plane_recv,
    w_send,
    w_recv,
    row_send,
    row_recv,
    down_send,
    down_recv,
    own_sems,
):
    me = where_am_i()
    x, here = me["x"], flat_index(me, SURFACE)
    z = me["zh"] * 2 + me["zl"]
    sums = ColumnSums(
        me, part, paired, sending, landed, near_send, near_recv, far_send, far_recv
    )
    gathers = ColumnGathers(me, blocks, gnear_send, gnear_recv, gfar_send, gfar_recv)
    own = pltpu.make_async_copy(out_mine.at[x], attended.at[:, x], own_sems.at[0])
    own.start()
    own_wgu = pltpu.make_async_copy(gateup_low, wgu.at[:, here], own_sems.at[2])
    own_wgu.start()
    spread = Exchange(
        me,
        SURFACE,
        lambda to: gateup_low,
        lambda frm: wgu.at[:, flat_index(frm, SURFACE)],
        w_send,
        w_recv,
    )
    rows_in = RowCopies(me, down_rows_low, down_wide, row_send, row_recv, False)
    rows_back = RowCopies(me, down_lines, down_parts, down_send, down_recv, True)
    gateup_back = Exchange(
        me,
        SURFACE,
        lambda to: gateup_lines.at[:, flat_index(to, SURFACE)],
        lambda frm: gateup_parts.at[flat_index(frm, SURFACE)],
        plane_send,
        plane_recv,
    )
    own_gateup = pltpu.make_async_copy(
        gateup_lines.at[:, here], gateup_parts.at[here], own_sems.at[1]
    )
    greet_all(me, "some", "both")

    def attention_out(k, arriving):
        frm = shifted(me, ("x",), k, -1) if arriving else me
        to = shifted(me, ("x",), k, 1)
        return pltpu.make_async_remote_copy(
            src_ref=out_mine.at[to["x"]],
            dst_ref=attended.at[:, frm["x"]],
            send_sem=att_send.at[k],
            recv_sem=att_recv.at[k],
            device_id=address(to),
            device_id_type=MESH,
        )

    for k in (2, 1, 3):
        attention_out(k, False).start()
    spread.begin()
    rows_in.begin()
    own.wait()
    for k in (1, 3, 2):
        attention_out(k, True).wait_recv()

    def project_out(i, carry):
        back = 3 - i
        off = back + lax.div(back, 2) * (5 - 2 * back)
        to_z = lax.rem(z + off, 4)
        rows = attended[lax.div(to_z, 2), pl.ds(lax.rem(to_z, 2) * 2, 2)].reshape(2 * ROWS, 256)
        sums.put(0, off, dot_nn(rows, wo[...]))

        @pl.when(i >= 1)
        def _():
            last = back + 1
            sums.pass_on(0, last + lax.div(last, 2) * (5 - 2 * last))

        return carry

    lax.fori_loop(0, 4, project_out, 0)
    branch[...] = sums.total(0)
    normed = branch[...] * norm_factor(branch[...]) * gains[0:1, :]
    hidden[...] = inputs[...].astype(F32) + normed
    gathers.begin(0, hidden[...].astype(BF16))

    def chip_rows(phase, at_z):
        return blocks[phase, pl.ds(at_z * 2, 2)].reshape(2 * ROWS, D)

    def pass_on_last(phase, i):
        @pl.when(i >= 2)
        def _():
            last = i - 1
            sums.pass_on(phase, last + lax.div(last, 2) * (5 - 2 * last))

    def at_rows(at_z):
        return pl.ds(pl.multiple_of(at_z * 2 * ROWS, 2 * ROWS), 2 * ROWS)

    own_wgu.wait()
    spread.arrive()
    rows_in.arrive()

    def down_line_in(j, carry):
        at = pl.ds(pl.multiple_of(j * 48, 16), 48)
        pair = down_wide[pl.ds(2 * j, 2)].astype(F32)
        for half in range(2):
            part = pair[:, half * 24 : half * 24 + 24].reshape(48, 512)
            wd[at, half * 512 : half * 512 + 512] = part.astype(BF16)
        return carry

    lax.fori_loop(0, PLANE // 2, down_line_in, 0)

    def feed_forward(i, carry):
        off, at_z = gathers.await_chip(0, i)
        both = dot_nn(chip_rows(0, at_z), wgu[...].reshape(D, 768))
        gate_up[at_rows(at_z), :] = both
        gate, up = both[:, :384], both[:, 384:]
        acts = (gate * (1.0 / (1.0 + jnp.exp(-gate))) * up).astype(BF16)
        activated[at_rows(at_z), :] = acts
        sums.put(1, lax.rem(4 - off, 4), dot_nn(acts, wd[...]))

        @pl.when(i >= 2)
        def _():
            last = i - 1
            sums.pass_on(1, 4 - (last + lax.div(last, 2) * (5 - 2 * last)))

        return carry

    lax.fori_loop(0, 4, feed_forward, 0)
    sums.pass_on(1, 2)
    ffn_out = sums.total(1)
    grad = upstream[...].astype(F32)
    result[...] = (hidden[...] + ffn_out * norm_factor(ffn_out) * gains[1:2, :]).astype(BF16)
    grad_ffn, grad_ffn_gain = norm_back(ffn_out, gains[1:2, :], grad)
    gathers.begin(1, grad_ffn.astype(BF16))
    gains_grad[1:2, :] = grad_ffn_gain

    def feed_forward_back(i, carry):
        off, at_z = gathers.await_chip(1, i)
        grad_act = dot_nt(chip_rows(1, at_z), wd[...])
        gate, up = gate_up[at_rows(at_z), :384], gate_up[at_rows(at_z), 384:]
        sig = 1.0 / (1.0 + jnp.exp(-gate))
        grad_gate[at_rows(at_z), :384] = (
            grad_act * up * (sig * (1.0 + gate * (1.0 - sig)))
        ).astype(BF16)
        grad_gate[at_rows(at_z), 384:] = (grad_act * (gate * sig)).astype(BF16)
        sums.put(2, lax.rem(4 - off, 4), dot_nt(grad_gate[at_rows(at_z), :], wgu[...].reshape(D, 768)))

        @pl.when(i >= 2)
        def _():
            last = i - 1
            sums.pass_on(2, 4 - (last + lax.div(last, 2) * (5 - 2 * last)))

        return carry

    lax.fori_loop(0, 4, feed_forward_back, 0)
    sums.pass_on(2, 2)

    def gateup_rows(j, carry):
        cols = pl.ds(pl.multiple_of(j * 256, 256), 256)
        grads = dot_tn(blocks[0, :, :, cols].reshape(RANKS * ROWS, 256), grad_gate[...])
        gateup_lines[lax.div(j, 2), pl.ds(lax.rem(j, 2) * 8, 8)] = grads.astype(BF16).reshape(
            8, 32, 768
        )
        return carry

    lax.fori_loop(0, 4, gateup_rows, 0)
    own_gateup.start()
    gateup_back.begin()

    def down_rows(j, carry):
        cols = pl.ds(pl.multiple_of(j * 128, 128), 128)
        down_grad[cols, :] = dot_tn(activated[:, cols], blocks[1].reshape(RANKS * ROWS, D))
        return carry

    lax.fori_loop(0, 3, down_rows, 0)

    def down_line(s, carry):
        rows = down_grad[pl.ds(pl.multiple_of(s * 24, 8), 24), :].astype(BF16)
        down_lines[s, 0:24, :] = rows[:, :512]
        down_lines[s, 24:48, :] = rows[:, 512:]
        return carry

    lax.fori_loop(0, PLANE, down_line, 0)
    rows_back.begin()

    total = grad + sums.total(2)
    grad_hidden[...] = total
    grad_branch, grad_attn_gain = norm_back(branch[...], gains[0:1, :], total)
    gathers.begin(2, grad_branch.astype(BF16))
    gains_grad[0:1, :] = grad_attn_gain

    def to_attention(row_zh, pack):
        return pltpu.make_async_remote_copy(
            src_ref=grad_attended.at[row_zh, pack],
            dst_ref=grad_mine.at[x, row_zh],
            send_sem=back_send.at[row_zh, pack],
            recv_sem=back_recv.at[row_zh, x],
            device_id=address(dict(me, x=pack)),
            device_id_type=MESH,
        )

    def own_attention(row_zh):
        return pltpu.make_async_copy(
            grad_attended.at[row_zh, x], grad_mine.at[x, row_zh], own_sems.at[3 + row_zh]
        )

    def project_out_back(i, carry):
        off, at_z = gathers.await_chip(2, i)
        grads = dot_nt(chip_rows(2, at_z), wo[...]).astype(BF16).reshape(2, ROWS, 256)
        row_zh = lax.div(at_z, 2)
        for at_core in range(2):
            pack = lax.rem(at_z, 2) * 2 + at_core
            grad_attended[row_zh, pack] = grads[at_core]

            @pl.when(pack != x)
            def _():
                to_attention(row_zh, pack).start()

            @pl.when(pack == x)
            def _():
                own_attention(row_zh).start()

        return carry

    lax.fori_loop(0, 4, project_out_back, 0)

    def output_rows(j, carry):
        cols = pl.ds(pl.multiple_of(j * 128, 128), 128)
        grads = dot_tn(
            attended[:, :, :, cols].reshape(RANKS * ROWS, 128), blocks[2].reshape(RANKS * ROWS, D)
        )
        output_lines[pl.ds(j * 8, 8)] = grads.astype(BF16).reshape(8, 16, D)
        return carry

    lax.fori_loop(0, 2, output_rows, 0)

    for k in (1, 3, 2):
        attention_out(k, False).wait_send()
        frm_x = lax.rem(x + 4 - k, 4)
        to_x = lax.rem(x + k, 4)
        for row_zh in range(2):
            to_attention(row_zh, to_x).wait_send()
            pltpu.make_async_remote_copy(
                src_ref=grad_attended.at[row_zh, to_x],
                dst_ref=grad_mine.at[frm_x, row_zh],
                send_sem=back_send.at[row_zh, to_x],
                recv_sem=back_recv.at[row_zh, frm_x],
                device_id=address(dict(me, x=to_x)),
                device_id_type=MESH,
            ).wait_recv()
    for row_zh in range(2):
        own_attention(row_zh).wait()
    for phase in range(3):
        sums.drain(phase)
        gathers.drain(phase)
    own_gateup.wait()
    gateup_back.arrive()
    rows_back.arrive()
    for exchange in (spread, rows_in, gateup_back, rows_back):
        exchange.drain()


def middle(number, out_mine, wo, gateup_low, down_rows, inputs, upstream, gains):
    anywhere = pl.BlockSpec(memory_space=pl.ANY)
    vmem = pl.BlockSpec(memory_space=pltpu.VMEM)
    block = (ROWS, D)
    dma = pltpu.SemaphoreType.DMA
    return pl.pallas_call(
        middle_kernel,
        out_shape=(
            jax.ShapeDtypeStruct(block, BF16),
            jax.ShapeDtypeStruct(block, F32),
            jax.ShapeDtypeStruct((2, D), F32),
            jax.ShapeDtypeStruct((4, 2, ROWS, 256), BF16),
            jax.ShapeDtypeStruct((PLANE, 2, 32, 768), BF16),
            jax.ShapeDtypeStruct((PLANE, 48, 512), BF16),
            jax.ShapeDtypeStruct((PLANE, 16, D), BF16),
        ),
        in_specs=[anywhere, vmem, anywhere, anywhere, vmem, vmem, vmem],
        out_specs=(vmem, vmem, vmem, anywhere, anywhere, anywhere, vmem),
        scratch_shapes=[
            pltpu.VMEM((2, 4, ROWS, 256), BF16),
            pltpu.VMEM((3, RANKS) + block, BF16),
            pltpu.VMEM((3, 4, 2) + block, BF16),
            pltpu.VMEM((3, 4) + block, BF16),
            pltpu.VMEM((3, 4) + block, BF16),
            pltpu.VMEM((3, 4) + block, BF16),
            pltpu.VMEM((RANKS * ROWS, 768), F32),
            pltpu.VMEM((RANKS * ROWS, 384), BF16),
            pltpu.VMEM((RANKS * ROWS, 768), BF16),
            pltpu.VMEM((2, 4, ROWS, 256), BF16),
            pltpu.VMEM((2, PLANE, 32, 768), BF16),
            pltpu.VMEM((384, D), F32),
            pltpu.VMEM((PLANE, 48, 512), BF16),
            pltpu.VMEM(block, F32),
            pltpu.VMEM(block, F32),
            pltpu.VMEM((2, PLANE, 32, 768), BF16),
            pltpu.VMEM((PLANE, 48, 512), BF16),
            pltpu.VMEM((384, D), BF16),
        ]
        + [dma((3, 4))] * 8
        + [dma((4,)), dma((4,)), dma((2, 4)), dma((2, 4))]
        + [dma((PLANE,))] * 8
        + [dma((5,))],
        compiler_params=pltpu.CompilerParams(
            collective_id=number, has_side_effects=True, vmem_limit_bytes=VMEM_LIMIT
        ),
        name="middle",
    )(out_mine, wo, gateup_low, down_rows, inputs, upstream, gains)


def rms_norm(values, norm_gain):
    factor = lax.rsqrt(jnp.mean(values * values, axis=-1, keepdims=True) + NORM_EPS)
    return values * factor * norm_gain


def head_prepare(projected, norm_gain, cosine, sine_part):
    normed = rms_norm(projected, norm_gain)
    halfway = HD // 2
    leading, trailing = normed[..., :halfway], normed[..., halfway:]
    return jnp.concatenate(
        [leading * cosine - trailing * sine_part, trailing * cosine + leading * sine_part], axis=-1
    )


def swiglu(gate_up):
    half = gate_up.shape[-1] // 2
    return jax.nn.silu(gate_up[:, :half]) * gate_up[:, half:]


def adam_update(weight, gradient, mean_old, square_old, rate, decay):
    mean_new = BETA_ONE * mean_old + (1.0 - BETA_ONE) * gradient
    square_new = BETA_TWO * square_old + (1.0 - BETA_TWO) * gradient * gradient
    mean_hat = mean_new / (1.0 - BETA_ONE**STEP)
    square_hat = square_new / (1.0 - BETA_TWO**STEP)
    weight_new = weight - rate * (mean_hat / (jnp.sqrt(square_hat) + ADAM_EPS) + decay * weight)
    return (weight_new, mean_new, square_new)


def by_rank(array, width):
    return array.reshape(array.shape[0], RANKS, width)


def swap_owner(array):
    pairs = [(a * 4 + b, b * 4 + a) for a in range(4) for b in range(4)]
    return lax.ppermute(array, ("x", "zl", "co"), pairs)


def body(
    tokens,
    cotangent,
    positions,
    seq_ids,
    query_weight,
    keyval_weight,
    output_weight,
    gateup_weight,
    down_weight,
    norm_gains,
    query_mean,
    keyval_mean,
    output_mean,
    gateup_mean,
    down_mean,
    gains_mean,
    query_square,
    keyval_square,
    output_square,
    gateup_square,
    down_square,
    gains_square,
):
    inputs = tokens[0]
    at_x, at_y = lax.axis_index("x"), lax.axis_index("y")

    own_blocks = (positions[0] + LONG * seq_ids[0]).reshape(-1, BLOCK)[:, 0] // BLOCK
    own_pair = lax.dynamic_slice_in_dim(own_blocks, 2 * lax.axis_index(("zh", "x", "y")), 2)
    own_pair = jnp.where(own_pair >= LONG // BLOCK, own_pair - LONG // BLOCK, own_pair)
    extra = jnp.concatenate(
        [
            jnp.pad(norm_gains, (0, HD - norm_gains.shape[0]))[None],
            jnp.pad(own_blocks.astype(F32), (0, HD - BLOCK))[None],
            jnp.broadcast_to(own_pair.astype(F32)[:, None], (2, HD)),
            jnp.zeros((4, HD), F32),
        ]
    )
    sent_a = jnp.concatenate(
        [
            by_rank(query_weight, 256),
            by_rank(keyval_weight[:, :KV], 128),
            by_rank(keyval_weight[:, KV:], 128),
            jnp.broadcast_to(extra[:, None, :], (8, RANKS, HD)),
        ],
        axis=2,
    ).transpose(1, 0, 2)
    sent_b = jnp.concatenate(
        [by_rank(gateup_weight[:, :FF], 384), by_rank(gateup_weight[:, FF:], 384)], axis=2
    ).transpose(1, 0, 2)
    frequency = ROPE_BASE ** (-jnp.arange(HD // 2, dtype=F32) * 2.0 / HD)
    (
        q_mine,
        kv_mine,
        all_tokens,
        output_wide,
        gateup_low,
        extras,
        gains_low,
        qkv_part,
        projected,
        cosine,
        sine,
        head_gains,
    ) = start(
        1,
        sent_a,
        sent_b,
        inputs,
        output_weight.astype(BF16),
        jnp.concatenate([frequency, frequency])[None],
    )
    all_tokens = all_tokens.reshape(RANKS * ROWS, D)
    gains_all = gains_low.reshape(-1, 8, HD)[:, 0, :18].reshape(-1).astype(F32)
    attn_gain = gains_all[:D]
    ffn_gain = gains_all[D : 2 * D]

    blocks = extras[:4, 1, :BLOCK].astype(jnp.int32).reshape(4, 2, 4, 4, 2)
    pack_blocks = lax.dynamic_index_in_dim(blocks, at_x, 0, keepdims=False)
    key_blocks = pack_blocks.transpose(1, 2, 0, 3).reshape(-1)
    query_blocks = (
        lax.dynamic_index_in_dim(pack_blocks, at_y, 2, keepdims=False).transpose(1, 0, 2).reshape(-1)
    )
    q_mine = q_mine.reshape(1024, 256)
    kv_mine = kv_mine.reshape(PACK_TOK, 256)
    out_mine, lse = attend(query_blocks, key_blocks, q_mine, kv_mine)

    def to_x(ref, to):
        return ref.at[to["x"]]

    def from_pack_x(ref, frm):
        return ref.at[:, frm["x"]]

    result, grad_hidden, gains_grad, grad_mine, gateup_parts, down_parts, output_lines = middle(
        5,
        out_mine.reshape(4, 2, ROWS, 256),
        output_wide.reshape(256, D),
        gateup_low,
        jnp.concatenate([down_weight[:, :512], down_weight[:, 512:]], axis=0).astype(BF16),
        inputs,
        cotangent[0],
        jnp.stack([attn_gain, ffn_gain]),
    )
    dq_mine, dkv_mine = attend_back(
        query_blocks, key_blocks, q_mine, kv_mine, grad_mine.reshape(1024, 256), out_mine, lse
    )
    dq, dkv_parts = push(
        "attention_grad_out",
        13,
        [dq_mine.reshape(4, 2, ROWS, 256), dkv_mine.reshape(PLANE, 2, ROWS, 256)],
        [((2, 4, ROWS, 256), BF16), ((4, 2, 4, ROWS, 256), BF16)],
        [
            (
                1,
                1,
                SURFACE,
                lambda ref, to: ref.at[flat_index(to, SURFACE)],
                lambda ref, frm: ref.at[frm["y"], :, frm["x"]],
            ),
            (0, 0, ("x",), to_x, from_pack_x),
        ],
    )
    dkv = jnp.sum(dkv_parts.astype(F32), axis=0).reshape(RANKS * ROWS, 256)
    half = HD // 2
    prepare = functools.partial(
        head_prepare, cosine=cosine[:, None, :half], sine_part=sine[:, None, half:]
    )
    three = jnp.stack([head_gains[0], head_gains[0], head_gains[1]])
    heads_use, heads_pull = jax.vjp(prepare, projected.reshape(-1, 3, HD), three)
    grad_heads = jnp.concatenate([dq.reshape(RANKS * ROWS, 256).astype(F32), dkv[:, :HD]], axis=1)
    grad_heads_in, grad_head_gains = heads_pull(grad_heads.reshape(-1, 3, HD))
    grad_qkv = jnp.concatenate(
        [grad_heads_in.reshape(-1, 384).astype(BF16), dkv[:, HD:].astype(BF16)], axis=1
    )
    qkv_grad = dot_tn(all_tokens, grad_qkv)
    token_grad = grad_hidden + sum_column(
        "grad_token_column",
        14,
        dot_nt(grad_qkv, qkv_part).astype(BF16).reshape(RANKS, ROWS, D),
    )

    gains_grad = jnp.concatenate(
        [
            gains_grad[0],
            gains_grad[1],
            grad_head_gains[0] + grad_head_gains[1],
            grad_head_gains[2],
        ]
    )
    gains_lines = jnp.pad(
        gains_grad.reshape(2, PLANE, 4, 18).transpose(1, 0, 2, 3).reshape(PLANE, RANKS, 18),
        ((0, 0), (0, 0), (0, HD - 18)),
    )

    def to_surface_inner(ref, to):
        return ref.at[:, flat_index(to, SURFACE)]

    def to_surface(ref, to):
        return ref.at[flat_index(to, SURFACE)]

    def to_surface_swapped(ref, to):
        return ref.at[flat_index(to, ("y", "x"))]

    qkv_lines = qkv_grad.astype(BF16).reshape(2, PLANE, 32, 512)
    output_parts, qkv_parts, gains_parts = push(
        "grads_plane",
        15,
        [output_lines, qkv_lines, gains_lines],
        [
            ((PLANE, 16, D), BF16),
            ((PLANE, 2, 32, 512), BF16),
            ((PLANE, RANKS, HD), F32),
        ],
        [
            (0, 0, SURFACE, to_surface_swapped, to_surface),
            (1, 1, SURFACE, to_surface_inner, to_surface),
            (2, 2, SURFACE, to_surface, to_surface),
        ],
    )
    down_wide = jnp.sum(down_parts.astype(F32), axis=0)
    output_sum = swap_owner(jnp.sum(output_parts.astype(F32), axis=0))
    down_sum = jnp.concatenate([down_wide[:24], down_wide[24:]], axis=1)
    gains_sums = jnp.sum(gains_parts, axis=0).reshape(RANKS, 1, HD)
    column_sums = jnp.concatenate(
        [
            jnp.sum(qkv_parts.astype(F32), axis=0).reshape(RANKS, 8, 512),
            jnp.pad(gains_sums, ((0, 0), (0, 7), (0, 0))),
            jnp.sum(gateup_parts.astype(F32), axis=0).reshape(RANKS, 8, 768),
        ],
        axis=2,
    )
    (summed,) = push(
        "grads_column",
        16,
        [column_sums],
        [((RANKS, 8, 1408), F32)],
        [
            (
                0,
                0,
                COLUMN,
                lambda ref, to: ref.at[flat_index(to, COLUMN)],
                lambda ref, frm: ref.at[flat_index(frm, COLUMN)],
            )
        ],
    )
    gains_sum = jnp.sum(summed[:, 0, 512 : 512 + 18], axis=0)
    wide = summed.transpose(1, 0, 2)
    query_sum = wide[:, :, :256].reshape(8, 2048)
    keyval_sum = jnp.concatenate(
        [wide[:, :, 256:384].reshape(8, KV), wide[:, :, 384:512].reshape(8, KV)], axis=1
    )
    gateup_sum = jnp.concatenate(
        [wide[:, :, 640:1024].reshape(8, FF), wide[:, :, 1024:].reshape(8, FF)], axis=1
    )

    query_new, query_mean_new, query_square_new = adam_update(
        query_weight, query_sum, query_mean, query_square, RATE_MATRIX, DECAY
    )
    keyval_new, keyval_mean_new, keyval_square_new = adam_update(
        keyval_weight, keyval_sum, keyval_mean, keyval_square, RATE_MATRIX, DECAY
    )
    output_new, output_mean_new, output_square_new = adam_update(
        output_weight, output_sum, output_mean, output_square, RATE_MATRIX, DECAY
    )
    gateup_new, gateup_mean_new, gateup_square_new = adam_update(
        gateup_weight, gateup_sum, gateup_mean, gateup_square, RATE_MATRIX, DECAY
    )
    down_new, down_mean_new, down_square_new = adam_update(
        down_weight, down_sum, down_mean, down_square, RATE_MATRIX, DECAY
    )
    gains_new, gains_mean_new, gains_square_new = adam_update(
        norm_gains, gains_sum, gains_mean, gains_square, RATE_GAIN, 0.0
    )
    return (
        result[None],
        token_grad[None],
        query_sum,
        keyval_sum,
        output_sum,
        gateup_sum,
        down_sum,
        gains_sum,
        query_new,
        keyval_new,
        output_new,
        gateup_new,
        down_new,
        gains_new,
        query_mean_new,
        keyval_mean_new,
        output_mean_new,
        gateup_mean_new,
        down_mean_new,
        gains_mean_new,
        query_square_new,
        keyval_square_new,
        output_square_new,
        gateup_square_new,
        down_square_new,
        gains_square_new,
    )


def solution(mesh):
    fine = Mesh(mesh.devices.reshape([SIZE[a] for a in AXES]), AXES)
    rows = P(("zl", "co"), ("zh", "x", "y"), None)
    packs = P(("zl", "co"), None)
    matrix = P(AXES, None)
    vector = P(AXES)
    params = [matrix] * 5 + [vector]
    return jax.shard_map(
        body,
        mesh=fine,
        in_specs=(rows, rows, packs, packs, *params, *params, *params),
        out_specs=(rows, rows, *params, *params, *params, *params),
        check_vma=False,
    )
```

```python
import functools
import math

import jax
import jax.numpy as jnp
from jax import lax
from jax.experimental import pallas as pl
from jax.experimental.pallas import tpu as pltpu
from jax.sharding import Mesh
from jax.sharding import PartitionSpec as P

D = 1024
H = 16
KVH = 8
HD = 128
FF = 3072
KV = 1024
STEP = 10
LONG = 3072
ROWS = 128
BLOCK = 64
CHUNK = 512
PACK_TOK = 4096
RANKS = 8
PLANE = 16


NORM_EPS = 1e-06
ROPE_BASE = 1000000.0
BETA_ONE = 0.9
BETA_TWO = 0.95
ADAM_EPS = 1e-08
DECAY = 0.1
RATE_MATRIX = 0.1
RATE_GAIN = 0.3

SCALE = HD**-0.5
LOG2E = math.log2(math.e)

AXES = ("zh", "x", "y", "zl", "co")
SIZE = {"zh": 2, "x": 4, "y": 4, "zl": 2, "co": 2}
COLUMN = ("zh", "zl", "co")
SURFACE = ("x", "y")
MESH = pl.DeviceIdType.MESH
F32 = jnp.float32
BF16 = jnp.bfloat16
VMEM_LIMIT = 50 * 1024 * 1024


def where_am_i():
    return {a: lax.axis_index(a) for a in AXES}


def address(place):
    return tuple(place[a] for a in AXES)


def flat_index(place, axes):
    at = 0
    for a in axes:
        at = at * SIZE[a] + place[a]
    return at


def shifted(place, axes, k, sign):
    to = dict(place)
    for a in reversed(axes):
        step = lax.rem(k, SIZE[a])
        k = lax.div(k, SIZE[a])
        to[a] = lax.rem(place[a] + sign * step + SIZE[a], SIZE[a])
    return to


def column_place(me, z, core):
    return dict(me, zh=lax.div(z, 2), zl=lax.rem(z, 2), co=core)


def dot_nn(a, b):
    return lax.dot_general(a, b, (((1,), (0,)), ((), ())), preferred_element_type=F32)


def dot_nt(a, b):
    return lax.dot_general(a, b, (((1,), (1,)), ((), ())), preferred_element_type=F32)


def dot_tn(a, b):
    return lax.dot_general(a, b, (((0,), (0,)), ((), ())), preferred_element_type=F32)


def stacked_heads(ref, tile):
    rows = ref[pl.ds(tile * BLOCK, BLOCK), :]
    return jnp.concatenate([rows[:, :HD], rows[:, HD:]], axis=0)


def allowed_keys(block, chunk):
    keys = chunk * CHUNK + lax.broadcasted_iota(jnp.int32, (CHUNK, 2 * BLOCK), 0)
    lanes = lax.broadcasted_iota(jnp.int32, (CHUNK, 2 * BLOCK), 1)
    return keys <= block * BLOCK + lax.rem(lanes, BLOCK)


def first_chunk(block):
    return jnp.where(block >= LONG // BLOCK, LONG // CHUNK, 0)


def attend_kernel(q_blocks, k_blocks, q_ref, kv_ref, out_ref, lse_ref, keys, values, values_t):
    def sort(i, carry):
        to = pl.multiple_of(k_blocks[i] * BLOCK, BLOCK)
        here = pl.multiple_of(i * BLOCK, BLOCK)
        keys[pl.ds(to, BLOCK), :] = kv_ref[pl.ds(here, BLOCK), :HD]
        values[pl.ds(to, BLOCK), :] = kv_ref[pl.ds(here, BLOCK), HD:]
        return carry

    lax.fori_loop(0, PACK_TOK // BLOCK, sort, 0)
    for c in range(PACK_TOK // CHUNK):
        part = values[c * CHUNK : (c + 1) * CHUNK, :].astype(F32)
        values_t[c] = part.T.astype(BF16)

    def one_tile(tile, carry):
        block = q_blocks[tile]
        query = stacked_heads(q_ref, tile)
        last = lax.div(block, CHUNK // BLOCK)

        def one_chunk(c, state, masked):
            total, mixed = state
            chunk_keys = keys[pl.ds(pl.multiple_of(c * CHUNK, CHUNK), CHUNK), :]
            weights = jnp.exp2(dot_nt(chunk_keys, query) * (SCALE * LOG2E))
            if masked:
                weights = jnp.where(allowed_keys(block, c), weights, 0.0)
            total = total + jnp.sum(weights, axis=0, keepdims=True)
            mixed = mixed + dot_nn(values_t[c], weights.astype(BF16))
            return total, mixed

        state = (jnp.zeros((1, 2 * BLOCK), F32), jnp.zeros((HD, 2 * BLOCK), F32))
        state = lax.fori_loop(
            first_chunk(block), last, lambda c, s: one_chunk(c, s, False), state
        )
        total, mixed = one_chunk(last, state, True)
        result = (mixed / total).T.astype(BF16)
        rows = pl.ds(pl.multiple_of(tile * BLOCK, BLOCK), BLOCK)
        out_ref[rows, :HD] = result[:BLOCK]
        out_ref[rows, HD:] = result[BLOCK:]
        lse_ref[pl.ds(tile, 1), :] = jnp.log2(total)
        return carry

    lax.fori_loop(0, q_ref.shape[0] // BLOCK, one_tile, 0)


def attend(q_blocks, k_blocks, q, kv):
    smem = pl.BlockSpec(memory_space=pltpu.SMEM)
    vmem = pl.BlockSpec(memory_space=pltpu.VMEM)
    tiles = q.shape[0] // BLOCK
    return pl.pallas_call(
        attend_kernel,
        out_shape=(
            jax.ShapeDtypeStruct(q.shape, BF16),
            jax.ShapeDtypeStruct((tiles, 2 * BLOCK), F32),
        ),
        in_specs=[smem, smem, vmem, vmem],
        out_specs=(vmem, vmem),
        scratch_shapes=[
            pltpu.VMEM((PACK_TOK, HD), BF16),
            pltpu.VMEM((PACK_TOK, HD), BF16),
            pltpu.VMEM((PACK_TOK // CHUNK, HD, CHUNK), BF16),
        ],
        compiler_params=pltpu.CompilerParams(vmem_limit_bytes=VMEM_LIMIT),
        cost_estimate=pl.CostEstimate(
            flops=4 * 10**9, bytes_accessed=4 * 10**6, transcendentals=8 * 10**6
        ),
        name="attend",
    )(q_blocks, k_blocks, q, kv)


def attend_back_kernel(
    q_blocks,
    k_blocks,
    q_ref,
    kv_ref,
    grad_ref,
    out_ref,
    lse_ref,
    dq_ref,
    dkv_ref,
    keys,
    values,
    keys_t,
    dk,
    dv,
):
    def sort(i, carry):
        to = pl.multiple_of(k_blocks[i] * BLOCK, BLOCK)
        here = pl.multiple_of(i * BLOCK, BLOCK)
        keys[pl.ds(to, BLOCK), :] = kv_ref[pl.ds(here, BLOCK), :HD]
        values[pl.ds(to, BLOCK), :] = kv_ref[pl.ds(here, BLOCK), HD:]
        return carry

    lax.fori_loop(0, PACK_TOK // BLOCK, sort, 0)
    for c in range(PACK_TOK // CHUNK):
        part = keys[c * CHUNK : (c + 1) * CHUNK, :].astype(F32)
        keys_t[c] = part.T.astype(BF16)
    dk[...] = jnp.zeros_like(dk)
    dv[...] = jnp.zeros_like(dv)

    def one_tile(tile, carry):
        block = q_blocks[tile]
        query = stacked_heads(q_ref, tile)
        grad = stacked_heads(grad_ref, tile)
        out = stacked_heads(out_ref, tile)
        inner = jnp.sum((grad.astype(F32) * out.astype(F32)).T, axis=0, keepdims=True)
        lse = lse_ref[pl.ds(tile, 1), :]
        last = lax.div(block, CHUNK // BLOCK)

        def one_chunk(c, dq, masked):
            rows = pl.ds(pl.multiple_of(c * CHUNK, CHUNK), CHUNK)
            probs = jnp.exp2(dot_nt(keys[rows, :], query) * (SCALE * LOG2E) - lse)
            if masked:
                probs = jnp.where(allowed_keys(block, c), probs, 0.0)
            grad_probs = dot_nt(values[rows, :], grad)
            grad_scores = (probs * (grad_probs - inner)).astype(BF16)
            dv[rows, :] += dot_nn(probs.astype(BF16), grad)
            dk[rows, :] += dot_nn(grad_scores, query)
            return dq + dot_nn(keys_t[c], grad_scores)

        dq = lax.fori_loop(
            first_chunk(block),
            last,
            lambda c, s: one_chunk(c, s, False),
            jnp.zeros((HD, 2 * BLOCK), F32),
        )
        dq = (one_chunk(last, dq, True) * SCALE).T.astype(BF16)
        rows = pl.ds(pl.multiple_of(tile * BLOCK, BLOCK), BLOCK)
        dq_ref[rows, :HD] = dq[:BLOCK]
        dq_ref[rows, HD:] = dq[BLOCK:]
        return carry

    lax.fori_loop(0, q_ref.shape[0] // BLOCK, one_tile, 0)

    def unsort(i, carry):
        at = pl.multiple_of(k_blocks[i] * BLOCK, BLOCK)
        here = pl.multiple_of(i * BLOCK, BLOCK)
        dkv_ref[pl.ds(here, BLOCK), :HD] = (dk[pl.ds(at, BLOCK), :] * SCALE).astype(BF16)
        dkv_ref[pl.ds(here, BLOCK), HD:] = dv[pl.ds(at, BLOCK), :].astype(BF16)
        return carry

    lax.fori_loop(0, PACK_TOK // BLOCK, unsort, 0)


def attend_back(q_blocks, k_blocks, q, kv, grad, out, lse):
    smem = pl.BlockSpec(memory_space=pltpu.SMEM)
    vmem = pl.BlockSpec(memory_space=pltpu.VMEM)
    return pl.pallas_call(
        attend_back_kernel,
        out_shape=(
            jax.ShapeDtypeStruct(q.shape, BF16),
            jax.ShapeDtypeStruct(kv.shape, BF16),
        ),
        in_specs=[smem, smem] + [vmem] * 5,
        out_specs=(vmem, vmem),
        scratch_shapes=[
            pltpu.VMEM((PACK_TOK, HD), BF16),
            pltpu.VMEM((PACK_TOK, HD), BF16),
            pltpu.VMEM((PACK_TOK // CHUNK, HD, CHUNK), BF16),
            pltpu.VMEM((PACK_TOK, HD), F32),
            pltpu.VMEM((PACK_TOK, HD), F32),
        ],
        compiler_params=pltpu.CompilerParams(vmem_limit_bytes=VMEM_LIMIT),
        cost_estimate=pl.CostEstimate(
            flops=10**10, bytes_accessed=8 * 10**6, transcendentals=8 * 10**6
        ),
        name="attend_back",
    )(q_blocks, k_blocks, q, kv, grad, out, lse)


class ColumnSums:
    def __init__(self, me, part, paired, sending, landed, near_send, near_recv, far_send, far_recv):
        self.me, self.z, self.core = me, me["zh"] * 2 + me["zl"], me["co"]
        self.part, self.paired, self.sending, self.landed = part, paired, sending, landed
        self.near_sems, self.far_sems = (near_send, near_recv), (far_send, far_recv)

    def near(self, phase, off):
        return pltpu.make_async_remote_copy(
            src_ref=self.part.at[phase, off, 1 - self.core],
            dst_ref=self.paired.at[phase, off],
            send_sem=self.near_sems[0].at[phase, off],
            recv_sem=self.near_sems[1].at[phase, off],
            device_id=address(column_place(self.me, self.z, 1 - self.core)),
            device_id_type=MESH,
        )

    def far(self, phase, off):
        return pltpu.make_async_remote_copy(
            src_ref=self.sending.at[phase, off],
            dst_ref=self.landed.at[phase, off],
            send_sem=self.far_sems[0].at[phase, off],
            recv_sem=self.far_sems[1].at[phase, off],
            device_id=address(column_place(self.me, lax.rem(self.z + off, 4), self.core)),
            device_id_type=MESH,
        )

    def put(self, phase, off, terms):
        self.part[phase, off] = terms.astype(BF16).reshape(2, ROWS, D)
        self.near(phase, off).start()

    def pass_on(self, phase, off):
        self.near(phase, off).wait_recv()
        both = self.part[phase, off, self.core].astype(F32) + self.paired[phase, off].astype(F32)
        self.sending[phase, off] = both.astype(BF16)
        self.far(phase, off).start()

    def total(self, phase):
        self.near(phase, 0).wait_recv()
        total = self.part[phase, 0, self.core].astype(F32) + self.paired[phase, 0].astype(F32)
        for off in (1, 3, 2):
            self.far(phase, off).wait_recv()
            total = total + self.landed[phase, off].astype(F32)
        return total

    def drain(self, phase):
        for off in range(4):
            self.near(phase, off).wait_send()
            if off:
                self.far(phase, off).wait_send()


class ColumnGathers:
    def __init__(self, me, blocks, near_send, near_recv, far_send, far_recv):
        self.me, self.z, self.core = me, me["zh"] * 2 + me["zl"], me["co"]
        self.blocks = blocks
        self.near_sems, self.far_sems = (near_send, near_recv), (far_send, far_recv)

    def far(self, phase, off, arriving):
        z = lax.rem(self.z + 4 - off, 4) if arriving else self.z
        block = self.blocks.at[phase, z * 2 + self.core]
        return pltpu.make_async_remote_copy(
            src_ref=block,
            dst_ref=block,
            send_sem=self.far_sems[0].at[phase, off],
            recv_sem=self.far_sems[1].at[phase, off],
            device_id=address(column_place(self.me, lax.rem(self.z + off, 4), self.core)),
            device_id_type=MESH,
        )

    def near(self, phase, off, arriving):
        core = 1 - self.core if arriving else self.core
        block = self.blocks.at[phase, lax.rem(self.z + 4 - off, 4) * 2 + core]
        return pltpu.make_async_remote_copy(
            src_ref=block,
            dst_ref=block,
            send_sem=self.near_sems[0].at[phase, off],
            recv_sem=self.near_sems[1].at[phase, off],
            device_id=address(column_place(self.me, self.z, 1 - self.core)),
            device_id_type=MESH,
        )

    def begin(self, phase, rows):
        self.blocks[phase, self.z * 2 + self.core] = rows
        for off in (1, 3, 2):
            self.far(phase, off, False).start()
        self.near(phase, 0, False).start()

    def await_chip(self, phase, i):
        off = i + lax.div(i, 2) * (5 - 2 * i)

        @pl.when(i == 1)
        def _():
            for near_by in (1, 3):
                self.far(phase, near_by, True).wait_recv()
                self.near(phase, near_by, False).start()

        @pl.when(i == 3)
        def _():
            self.far(phase, 2, True).wait_recv()
            self.near(phase, 2, False).start()

        self.near(phase, off, True).wait_recv()
        return off, lax.rem(self.z + 4 - off, 4)

    def drain(self, phase):
        for off in range(4):
            self.near(phase, off, False).wait_send()
            if off:
                self.far(phase, off, False).wait_send()


def norm_factor(values):
    return lax.rsqrt(jnp.mean(values * values, axis=-1, keepdims=True) + NORM_EPS)


def norm_back(values, norm_gain, grad):
    factor = norm_factor(values)
    scaled = grad * norm_gain
    inner = jnp.mean(values * scaled, axis=-1, keepdims=True)
    grad_gain = jnp.sum(grad * values * factor, axis=0, keepdims=True)
    return factor * scaled - values * (factor * factor * factor * inner), grad_gain


def quarter(place):
    return place["zl"] * 2 + place["co"]


def at_quarter(place, t):
    return dict(place, zl=lax.div(t, 2), co=lax.rem(t, 2))


def row_user(me, k):
    return at_quarter(shifted(me, SURFACE, k, 1), me["x"])


def row_owner(me, k):
    y, t = lax.div(k, 4), lax.rem(k, 4)
    to = dict(me, x=quarter(me), y=lax.rem(me["y"] + y, 4))
    return at_quarter(to, lax.rem(quarter(me) + t, 4))


def row_slot(owner):
    return owner["y"] * 4 + quarter(owner)


def greet(barrier, place):
    pl.semaphore_signal(barrier, inc=1, device_id=address(place), device_id_type=MESH)


def greet_all(me, column, rows):
    barrier = pltpu.get_barrier_semaphore()

    def greet_surface(k, carry):
        greet(barrier, shifted(me, SURFACE, k, 1))
        return carry

    def greet_column_all(k, carry):
        greet(barrier, shifted(me, COLUMN, k, 1))
        return carry

    lax.fori_loop(1, PLANE, greet_surface, 0)
    expected = PLANE - 1
    if column == "all":
        lax.fori_loop(1, RANKS, greet_column_all, 0)
        expected = expected + RANKS - 1
    else:
        z = me["zh"] * 2 + me["zl"]
        for off in (1, 2, 3):
            greet(barrier, column_place(me, lax.rem(z + off, 4), me["co"]))
        greet(barrier, column_place(me, z, 1 - me["co"]))
        expected = expected + 4
    if rows is not None:
        at_home = me["x"] == quarter(me)

        def greet_rows(k, carry):
            @pl.when(jnp.logical_not(jnp.logical_and(k == 0, at_home)))
            def _():
                if rows != "own":
                    greet(barrier, row_owner(me, k))
                if rows != "use":
                    greet(barrier, row_user(me, k))

            return carry

        lax.fori_loop(0, PLANE, greet_rows, 0)
        count = PLANE - jnp.where(at_home, 1, 0)
        expected = expected + (2 * count if rows == "both" else count)
    pl.semaphore_wait(barrier, expected)


class RowCopies:
    def __init__(self, me, src, dst, send, recv, back):
        self.me, self.src, self.dst, self.send, self.recv, self.back = me, src, dst, send, recv, back
        self.at_home = me["x"] == quarter(me)

    def copy(self, k, arriving):
        me = self.me
        if self.back:
            to = row_owner(me, k)
            frm = row_user(me, k) if arriving else me
            src, slot = self.src.at[row_slot(to)], flat_index(frm, SURFACE)
        else:
            to = row_user(me, k)
            frm = row_owner(me, k) if arriving else me
            src, slot = self.src, row_slot(frm)
        return pltpu.make_async_remote_copy(
            src_ref=src,
            dst_ref=self.dst.at[slot],
            send_sem=self.send.at[k],
            recv_sem=self.recv.at[slot],
            device_id=address(to),
            device_id_type=MESH,
        )

    def own(self):
        me = self.me
        if self.back:
            src, slot = self.src.at[row_slot(me)], flat_index(me, SURFACE)
        else:
            src, slot = self.src, row_slot(me)
        return pltpu.make_async_copy(src, self.dst.at[slot], self.recv.at[slot])

    def each(self, remote, own):
        def one(j, carry):
            k = lax.rem(j * 7, PLANE)
            itself = jnp.logical_and(k == 0, self.at_home)

            @pl.when(itself)
            def _():
                own()

            @pl.when(jnp.logical_not(itself))
            def _():
                remote(k)

            return carry

        lax.fori_loop(0, PLANE, one, 0)

    def begin(self):
        self.each(lambda k: self.copy(k, False).start(), lambda: self.own().start())

    def arrive(self):
        self.each(lambda k: self.copy(k, True).wait_recv(), lambda: self.own().wait())

    def drain(self):
        self.each(lambda k: self.copy(k, False).wait_send(), lambda: None)


class Exchange:
    def __init__(self, me, axes, take, put, send, recv):
        self.me, self.axes, self.take, self.put, self.send, self.recv = me, axes, take, put, send, recv
        self.n = math.prod(SIZE[a] for a in axes)
        self.mix = {4: 1, 8: 3, 16: 7}[self.n]

    def copy(self, k, arriving):
        to = shifted(self.me, self.axes, k, 1)
        frm = shifted(self.me, self.axes, k, -1) if arriving else self.me
        return pltpu.make_async_remote_copy(
            src_ref=self.take(to),
            dst_ref=self.put(frm),
            send_sem=self.send.at[k],
            recv_sem=self.recv.at[k],
            device_id=address(to),
            device_id_type=MESH,
        )

    def each(self, act):
        def one(j, carry):
            act(lax.rem(j * self.mix, self.n))
            return carry

        lax.fori_loop(1, self.n, one, 0)

    def begin(self):
        self.each(lambda k: self.copy(k, False).start())

    def arrive(self):
        self.each(lambda k: self.copy(k, True).wait_recv())

    def drain(self):
        self.each(lambda k: self.copy(k, False).wait_send())


def start_kernel(
    sent_a,
    sent_b,
    tokens,
    output_rows,
    frequency,
    q_mine,
    kv_mine,
    all_tokens,
    output_wide,
    gateup_low,
    extra_out,
    gains_out,
    qkv_part,
    projected,
    cosine,
    sine,
    head_gains,
    shares_a,
    shares_b,
    wide,
    blocks,
    queries,
    keyvals,
    a_send,
    a_recv,
    b_send,
    b_recv,
    w_send,
    w_recv,
    row_send,
    row_recv,
    near_send,
    near_recv,
    far_send,
    far_recv,
    q_send,
    q_recv,
    kv_send,
    kv_recv,
    relay_send,
    relay_recv,
    own_sems,
):
    me = where_am_i()
    x, y = me["x"], me["y"]
    rank, here = flat_index(me, COLUMN), flat_index(me, SURFACE)
    gathers = ColumnGathers(me, blocks, near_send, near_recv, far_send, far_recv)
    to_a = Exchange(
        me,
        COLUMN,
        lambda to: sent_a.at[flat_index(to, COLUMN)],
        lambda frm: shares_a.at[flat_index(frm, COLUMN)],
        a_send,
        a_recv,
    )
    to_b = Exchange(
        me,
        COLUMN,
        lambda to: sent_b.at[flat_index(to, COLUMN)],
        lambda frm: shares_b.at[flat_index(frm, COLUMN)],
        b_send,
        b_recv,
    )
    spread = Exchange(
        me,
        SURFACE,
        lambda to: wide.at[:, here],
        lambda frm: wide.at[:, flat_index(frm, SURFACE)],
        w_send,
        w_recv,
    )
    rows = RowCopies(me, output_rows, output_wide, row_send, row_recv, False)
    own_a = pltpu.make_async_copy(sent_a.at[rank], shares_a.at[rank], own_sems.at[0])
    own_b = pltpu.make_async_copy(sent_b.at[rank], shares_b.at[rank], own_sems.at[1])
    own_a.start()
    own_b.start()
    greet_all(me, "all", "use")
    to_a.begin()
    gathers.begin(0, tokens[...])
    rows.begin()
    to_b.begin()

    own_a.wait()
    to_a.arrive()
    wide[:, here] = shares_a[...].astype(BF16).reshape(2, 32, 640)
    spread.begin()
    extra_out[...] = shares_a[:, :, 512:]

    lanes = lax.broadcasted_iota(jnp.int32, (BLOCK, HD), 1)
    place = lax.broadcasted_iota(jnp.int32, (BLOCK, HD), 0).astype(F32)

    def tables(j, carry):
        for half in range(2):
            first = shares_a[j, 2 + half : 3 + half, 512:]
            angles = (first * float(BLOCK) + place) * frequency[...]
            at = pl.ds(pl.multiple_of(j * ROWS + half * BLOCK, BLOCK), BLOCK)
            cosine[at, :] = jnp.cos(angles)
            sines = jnp.sin(angles)
            sine[at, :] = jnp.where(lanes < HD // 2, -sines, sines)
        return carry

    lax.fori_loop(0, RANKS, tables, 0)
    own_b.wait()
    to_b.arrive()
    gateup_low[...] = shares_b[...].astype(BF16).reshape(2, 32, 768)

    spread.arrive()
    qkv_part[...] = wide[..., :512].reshape(D, 512)
    extra = wide[..., 512:].reshape(D, HD)
    gains_out[...] = extra
    entry = 2 * D + lax.broadcasted_iota(jnp.int32, (HD, 2 * HD), 1)
    pick = (lax.broadcasted_iota(jnp.int32, (HD, 2 * HD), 0) == lax.rem(entry, 18)).astype(BF16)
    entries = 2 * D + lax.broadcasted_iota(jnp.int32, (D, 2 * HD), 1)
    owned = lax.broadcasted_iota(jnp.int32, (D, 2 * HD), 0) == 8 * lax.div(entries, 18)
    gains = jnp.sum(jnp.where(owned, dot_nn(extra, pick), 0.0), axis=0, keepdims=True)
    head_gains[0:1, :] = gains[:, :HD]
    head_gains[1:2, :] = gains[:, HD:]

    def q_copy(row_zh, pack):
        return pltpu.make_async_remote_copy(
            src_ref=queries.at[row_zh, pack],
            dst_ref=q_mine.at[x, row_zh],
            send_sem=q_send.at[row_zh, pack],
            recv_sem=q_recv.at[row_zh, x],
            device_id=address(dict(me, x=pack)),
            device_id_type=MESH,
        )

    def kv_copy(row_zh, pack):
        return pltpu.make_async_remote_copy(
            src_ref=keyvals.at[row_zh, pack],
            dst_ref=kv_mine.at[here, row_zh],
            send_sem=kv_send.at[row_zh, pack],
            recv_sem=kv_recv.at[row_zh, x],
            device_id=address(dict(me, x=pack)),
            device_id_type=MESH,
        )

    def q_own(row_zh):
        return pltpu.make_async_copy(
            queries.at[row_zh, x], q_mine.at[x, row_zh], own_sems.at[2 + row_zh]
        )

    def kv_own(row_zh):
        return pltpu.make_async_copy(
            keyvals.at[row_zh, x], kv_mine.at[here, row_zh], own_sems.at[4 + row_zh]
        )

    def relay(row_zh, from_x, k, arriving):
        to_y = lax.rem(y + k, 4)
        from_y = lax.rem(y + 4 - k, 4) if arriving else y
        block = kv_mine.at[from_x * 4 + from_y, row_zh]
        return pltpu.make_async_remote_copy(
            src_ref=block,
            dst_ref=block,
            send_sem=relay_send.at[row_zh, from_x, k],
            recv_sem=relay_recv.at[row_zh, from_x, k],
            device_id=address(dict(me, y=to_y)),
            device_id_type=MESH,
        )

    def project(i, carry):
        off, at_z = gathers.await_chip(0, i)
        at = pl.ds(pl.multiple_of(at_z * 2 * ROWS, 2 * ROWS), 2 * ROWS)
        both = dot_nn(blocks[0, pl.ds(at_z * 2, 2)].reshape(2 * ROWS, D), qkv_part[...])
        projected[at, :] = both[:, :384]
        row_zh, first = lax.div(at_z, 2), lax.rem(at_z, 2) * 2
        for head in range(3):
            values = both[:, head * HD : (head + 1) * HD]
            gain = head_gains[1:2, :] if head == 2 else head_gains[0:1, :]
            normed = values * norm_factor(values) * gain
            turned = (
                normed * cosine[at, :] + pltpu.roll(normed, HD // 2, 1) * sine[at, :]
            ).astype(BF16)
            turned = turned.reshape(2, ROWS, HD)
            for at_core in range(2):
                if head == 2:
                    keyvals[row_zh, first + at_core, :, :HD] = turned[at_core]
                else:
                    queries[row_zh, first + at_core, :, head * HD : (head + 1) * HD] = turned[
                        at_core
                    ]
        values = both[:, 384:].astype(BF16).reshape(2, ROWS, HD)
        for at_core in range(2):
            pack = first + at_core
            keyvals[row_zh, pack, :, HD:] = values[at_core]

            @pl.when(pack != x)
            def _():
                kv_copy(row_zh, pack).start()
                q_copy(row_zh, pack).start()

            @pl.when(pack == x)
            def _():
                kv_own(row_zh).start()
                q_own(row_zh).start()

        return carry

    lax.fori_loop(0, 4, project, 0)
    for i in range(RANKS):
        slot = pltpu.make_async_copy(blocks.at[0, i], all_tokens.at[i], own_sems.at[6 + i])
        slot.start()
    for row_zh in range(2):
        kv_own(row_zh).wait()
        for k in (2, 1, 3):
            relay(row_zh, x, k, False).start()
    for off in (1, 3, 2):
        from_x = lax.rem(x + 4 - off, 4)
        to_x = lax.rem(x + off, 4)
        for row_zh in range(2):
            pltpu.make_async_remote_copy(
                src_ref=keyvals.at[row_zh, to_x],
                dst_ref=kv_mine.at[from_x * 4 + y, row_zh],
                send_sem=kv_send.at[row_zh, to_x],
                recv_sem=kv_recv.at[row_zh, from_x],
                device_id=address(dict(me, x=to_x)),
                device_id_type=MESH,
            ).wait_recv()
            for k in (2, 1, 3):
                relay(row_zh, from_x, k, False).start()
    for off in (1, 3, 2):
        from_x = lax.rem(x + 4 - off, 4)
        to_x = lax.rem(x + off, 4)
        for row_zh in range(2):
            pltpu.make_async_remote_copy(
                src_ref=queries.at[row_zh, to_x],
                dst_ref=q_mine.at[from_x, row_zh],
                send_sem=q_send.at[row_zh, to_x],
                recv_sem=q_recv.at[row_zh, from_x],
                device_id=address(dict(me, x=to_x)),
                device_id_type=MESH,
            ).wait()
            kv_copy(row_zh, to_x).wait_send()
    for row_zh in range(2):
        q_own(row_zh).wait()

    def finish(j, carry):
        row_zh, from_x = lax.div(j, 4), lax.rem(j, 4)
        for k in (1, 3, 2):
            relay(row_zh, from_x, k, False).wait_send()
            relay(row_zh, from_x, k, True).wait_recv()
        return carry

    lax.fori_loop(0, 8, finish, 0)
    rows.arrive()
    for i in range(RANKS):
        pltpu.make_async_copy(blocks.at[0, i], all_tokens.at[i], own_sems.at[6 + i]).wait()
    for exchange in (to_a, to_b, spread, rows):
        exchange.drain()
    gathers.drain(0)


def start(number, sent_a, sent_b, tokens, output_rows, frequency):
    anywhere = pl.BlockSpec(memory_space=pl.ANY)
    vmem = pl.BlockSpec(memory_space=pltpu.VMEM)
    dma = pltpu.SemaphoreType.DMA
    struct = jax.ShapeDtypeStruct
    return pl.pallas_call(
        start_kernel,
        out_shape=(
            struct((4, 2, ROWS, 256), BF16),
            struct((PLANE, 2, ROWS, 256), BF16),
            struct((RANKS, ROWS, D), BF16),
            struct((PLANE, 16, D), BF16),
            struct((2, 32, 768), BF16),
            struct((RANKS, 8, HD), F32),
            struct((D, HD), BF16),
            struct((D, 512), BF16),
            struct((RANKS * ROWS, 384), F32),
            struct((RANKS * ROWS, HD), F32),
            struct((RANKS * ROWS, HD), F32),
            struct((2, HD), F32),
        ),
        in_specs=[anywhere, anywhere, vmem, anywhere, vmem],
        out_specs=(anywhere, anywhere, anywhere, anywhere) + (vmem,) * 8,
        scratch_shapes=[
            pltpu.VMEM((RANKS, 8, 640), F32),
            pltpu.VMEM((RANKS, 8, 768), F32),
            pltpu.VMEM((2, PLANE, 32, 640), BF16),
            pltpu.VMEM((1, RANKS, ROWS, D), BF16),
            pltpu.VMEM((2, 4, ROWS, 256), BF16),
            pltpu.VMEM((2, 4, ROWS, 256), BF16),
        ]
        + [dma((RANKS,))] * 4
        + [dma((PLANE,))] * 4
        + [dma((1, 4))] * 4
        + [dma((2, 4))] * 4
        + [dma((2, 4, 4)), dma((2, 4, 4)), dma((6 + RANKS,))],
        compiler_params=pltpu.CompilerParams(
            collective_id=number, has_side_effects=True, vmem_limit_bytes=VMEM_LIMIT
        ),
        name="start",
    )(sent_a, sent_b, tokens, output_rows, frequency)


def middle_kernel(
    out_mine,
    wo,
    gateup_low,
    down_rows_low,
    inputs,
    upstream,
    gains,
    result,
    grad_hidden,
    gains_grad,
    grad_mine,
    gateup_parts,
    down_parts,
    output_lines,
    attended,
    blocks,
    part,
    paired,
    sending,
    landed,
    gate_up,
    activated,
    grad_gate,
    grad_attended,
    gateup_lines,
    down_grad,
    down_lines,
    branch,
    hidden,
    wgu,
    down_wide,
    wd,
    near_send,
    near_recv,
    far_send,
    far_recv,
    gnear_send,
    gnear_recv,
    gfar_send,
    gfar_recv,
    att_send,
    att_recv,
    back_send,
    back_recv,
    plane_send,
    plane_recv,
    w_send,
    w_recv,
    row_send,
    row_recv,
    down_send,
    down_recv,
    own_sems,
):
    me = where_am_i()
    x, here = me["x"], flat_index(me, SURFACE)
    z = me["zh"] * 2 + me["zl"]
    sums = ColumnSums(
        me, part, paired, sending, landed, near_send, near_recv, far_send, far_recv
    )
    gathers = ColumnGathers(me, blocks, gnear_send, gnear_recv, gfar_send, gfar_recv)
    own = pltpu.make_async_copy(out_mine.at[x], attended.at[:, x], own_sems.at[0])
    own.start()
    own_wgu = pltpu.make_async_copy(gateup_low, wgu.at[:, here], own_sems.at[2])
    own_wgu.start()
    spread = Exchange(
        me,
        SURFACE,
        lambda to: gateup_low,
        lambda frm: wgu.at[:, flat_index(frm, SURFACE)],
        w_send,
        w_recv,
    )
    rows_in = RowCopies(me, down_rows_low, down_wide, row_send, row_recv, False)
    rows_back = RowCopies(me, down_lines, down_parts, down_send, down_recv, True)
    gateup_back = Exchange(
        me,
        SURFACE,
        lambda to: gateup_lines.at[:, flat_index(to, SURFACE)],
        lambda frm: gateup_parts.at[flat_index(frm, SURFACE)],
        plane_send,
        plane_recv,
    )
    own_gateup = pltpu.make_async_copy(
        gateup_lines.at[:, here], gateup_parts.at[here], own_sems.at[1]
    )
    greet_all(me, "some", "both")

    def attention_out(k, arriving):
        frm = shifted(me, ("x",), k, -1) if arriving else me
        to = shifted(me, ("x",), k, 1)
        return pltpu.make_async_remote_copy(
            src_ref=out_mine.at[to["x"]],
            dst_ref=attended.at[:, frm["x"]],
            send_sem=att_send.at[k],
            recv_sem=att_recv.at[k],
            device_id=address(to),
            device_id_type=MESH,
        )

    for k in (2, 1, 3):
        attention_out(k, False).start()
    spread.begin()
    rows_in.begin()
    own.wait()
    for k in (1, 3, 2):
        attention_out(k, True).wait_recv()

    def project_out(i, carry):
        back = 3 - i
        off = back + lax.div(back, 2) * (5 - 2 * back)
        to_z = lax.rem(z + off, 4)
        rows = attended[lax.div(to_z, 2), pl.ds(lax.rem(to_z, 2) * 2, 2)].reshape(2 * ROWS, 256)
        sums.put(0, off, dot_nn(rows, wo[...]))

        @pl.when(i >= 1)
        def _():
            last = back + 1
            sums.pass_on(0, last + lax.div(last, 2) * (5 - 2 * last))

        return carry

    lax.fori_loop(0, 4, project_out, 0)
    branch[...] = sums.total(0)
    normed = branch[...] * norm_factor(branch[...]) * gains[0:1, :]
    hidden[...] = inputs[...].astype(F32) + normed
    gathers.begin(0, hidden[...].astype(BF16))

    def chip_rows(phase, at_z):
        return blocks[phase, pl.ds(at_z * 2, 2)].reshape(2 * ROWS, D)

    def pass_on_last(phase, i):
        @pl.when(i >= 2)
        def _():
            last = i - 1
            sums.pass_on(phase, last + lax.div(last, 2) * (5 - 2 * last))

    def at_rows(at_z):
        return pl.ds(pl.multiple_of(at_z * 2 * ROWS, 2 * ROWS), 2 * ROWS)

    own_wgu.wait()
    spread.arrive()
    rows_in.arrive()

    def down_line_in(j, carry):
        at = pl.ds(pl.multiple_of(j * 48, 16), 48)
        pair = down_wide[pl.ds(2 * j, 2)].astype(F32)
        for half in range(2):
            part = pair[:, half * 24 : half * 24 + 24].reshape(48, 512)
            wd[at, half * 512 : half * 512 + 512] = part.astype(BF16)
        return carry

    lax.fori_loop(0, PLANE // 2, down_line_in, 0)

    def feed_forward(i, carry):
        off, at_z = gathers.await_chip(0, i)
        both = dot_nn(chip_rows(0, at_z), wgu[...].reshape(D, 768))
        gate_up[at_rows(at_z), :] = both
        gate, up = both[:, :384], both[:, 384:]
        acts = (gate * (1.0 / (1.0 + jnp.exp(-gate))) * up).astype(BF16)
        activated[at_rows(at_z), :] = acts
        sums.put(1, lax.rem(4 - off, 4), dot_nn(acts, wd[...]))

        @pl.when(i >= 2)
        def _():
            last = i - 1
            sums.pass_on(1, 4 - (last + lax.div(last, 2) * (5 - 2 * last)))

        return carry

    lax.fori_loop(0, 4, feed_forward, 0)
    sums.pass_on(1, 2)
    ffn_out = sums.total(1)
    grad = upstream[...].astype(F32)
    result[...] = (hidden[...] + ffn_out * norm_factor(ffn_out) * gains[1:2, :]).astype(BF16)
    grad_ffn, grad_ffn_gain = norm_back(ffn_out, gains[1:2, :], grad)
    gathers.begin(1, grad_ffn.astype(BF16))
    gains_grad[1:2, :] = grad_ffn_gain

    def feed_forward_back(i, carry):
        off, at_z = gathers.await_chip(1, i)
        grad_act = dot_nt(chip_rows(1, at_z), wd[...])
        gate, up = gate_up[at_rows(at_z), :384], gate_up[at_rows(at_z), 384:]
        sig = 1.0 / (1.0 + jnp.exp(-gate))
        grad_gate[at_rows(at_z), :384] = (
            grad_act * up * (sig * (1.0 + gate * (1.0 - sig)))
        ).astype(BF16)
        grad_gate[at_rows(at_z), 384:] = (grad_act * (gate * sig)).astype(BF16)
        sums.put(2, lax.rem(4 - off, 4), dot_nt(grad_gate[at_rows(at_z), :], wgu[...].reshape(D, 768)))

        @pl.when(i >= 2)
        def _():
            last = i - 1
            sums.pass_on(2, 4 - (last + lax.div(last, 2) * (5 - 2 * last)))

        return carry

    lax.fori_loop(0, 4, feed_forward_back, 0)
    sums.pass_on(2, 2)

    def gateup_rows(j, carry):
        cols = pl.ds(pl.multiple_of(j * 256, 256), 256)
        grads = dot_tn(blocks[0, :, :, cols].reshape(RANKS * ROWS, 256), grad_gate[...])
        gateup_lines[lax.div(j, 2), pl.ds(lax.rem(j, 2) * 8, 8)] = grads.astype(BF16).reshape(
            8, 32, 768
        )
        return carry

    lax.fori_loop(0, 4, gateup_rows, 0)
    own_gateup.start()
    gateup_back.begin()

    def down_rows(j, carry):
        cols = pl.ds(pl.multiple_of(j * 128, 128), 128)
        down_grad[cols, :] = dot_tn(activated[:, cols], blocks[1].reshape(RANKS * ROWS, D))
        return carry

    lax.fori_loop(0, 3, down_rows, 0)

    def down_line(s, carry):
        rows = down_grad[pl.ds(pl.multiple_of(s * 24, 8), 24), :].astype(BF16)
        down_lines[s, 0:24, :] = rows[:, :512]
        down_lines[s, 24:48, :] = rows[:, 512:]
        return carry

    lax.fori_loop(0, PLANE, down_line, 0)
    rows_back.begin()

    total = grad + sums.total(2)
    grad_hidden[...] = total
    grad_branch, grad_attn_gain = norm_back(branch[...], gains[0:1, :], total)
    gathers.begin(2, grad_branch.astype(BF16))
    gains_grad[0:1, :] = grad_attn_gain

    def to_attention(row_zh, pack):
        return pltpu.make_async_remote_copy(
            src_ref=grad_attended.at[row_zh, pack],
            dst_ref=grad_mine.at[x, row_zh],
            send_sem=back_send.at[row_zh, pack],
            recv_sem=back_recv.at[row_zh, x],
            device_id=address(dict(me, x=pack)),
            device_id_type=MESH,
        )

    def own_attention(row_zh):
        return pltpu.make_async_copy(
            grad_attended.at[row_zh, x], grad_mine.at[x, row_zh], own_sems.at[3 + row_zh]
        )

    def project_out_back(i, carry):
        off, at_z = gathers.await_chip(2, i)
        grads = dot_nt(chip_rows(2, at_z), wo[...]).astype(BF16).reshape(2, ROWS, 256)
        row_zh = lax.div(at_z, 2)
        for at_core in range(2):
            pack = lax.rem(at_z, 2) * 2 + at_core
            grad_attended[row_zh, pack] = grads[at_core]

            @pl.when(pack != x)
            def _():
                to_attention(row_zh, pack).start()

            @pl.when(pack == x)
            def _():
                own_attention(row_zh).start()

        return carry

    lax.fori_loop(0, 4, project_out_back, 0)

    def output_rows(j, carry):
        cols = pl.ds(pl.multiple_of(j * 128, 128), 128)
        grads = dot_tn(
            attended[:, :, :, cols].reshape(RANKS * ROWS, 128), blocks[2].reshape(RANKS * ROWS, D)
        )
        output_lines[pl.ds(j * 8, 8)] = grads.astype(BF16).reshape(8, 16, D)
        return carry

    lax.fori_loop(0, 2, output_rows, 0)

    for k in (1, 3, 2):
        attention_out(k, False).wait_send()
        frm_x = lax.rem(x + 4 - k, 4)
        to_x = lax.rem(x + k, 4)
        for row_zh in range(2):
            to_attention(row_zh, to_x).wait_send()
            pltpu.make_async_remote_copy(
                src_ref=grad_attended.at[row_zh, to_x],
                dst_ref=grad_mine.at[frm_x, row_zh],
                send_sem=back_send.at[row_zh, to_x],
                recv_sem=back_recv.at[row_zh, frm_x],
                device_id=address(dict(me, x=to_x)),
                device_id_type=MESH,
            ).wait_recv()
    for row_zh in range(2):
        own_attention(row_zh).wait()
    for phase in range(3):
        sums.drain(phase)
        gathers.drain(phase)
    own_gateup.wait()
    gateup_back.arrive()
    rows_back.arrive()
    for exchange in (spread, rows_in, gateup_back, rows_back):
        exchange.drain()


def middle(number, out_mine, wo, gateup_low, down_rows, inputs, upstream, gains):
    anywhere = pl.BlockSpec(memory_space=pl.ANY)
    vmem = pl.BlockSpec(memory_space=pltpu.VMEM)
    block = (ROWS, D)
    dma = pltpu.SemaphoreType.DMA
    return pl.pallas_call(
        middle_kernel,
        out_shape=(
            jax.ShapeDtypeStruct(block, BF16),
            jax.ShapeDtypeStruct(block, F32),
            jax.ShapeDtypeStruct((2, D), F32),
            jax.ShapeDtypeStruct((4, 2, ROWS, 256), BF16),
            jax.ShapeDtypeStruct((PLANE, 2, 32, 768), BF16),
            jax.ShapeDtypeStruct((PLANE, 48, 512), BF16),
            jax.ShapeDtypeStruct((PLANE, 16, D), BF16),
        ),
        in_specs=[anywhere, vmem, anywhere, anywhere, vmem, vmem, vmem],
        out_specs=(vmem, vmem, vmem, anywhere, anywhere, anywhere, vmem),
        scratch_shapes=[
            pltpu.VMEM((2, 4, ROWS, 256), BF16),
            pltpu.VMEM((3, RANKS) + block, BF16),
            pltpu.VMEM((3, 4, 2) + block, BF16),
            pltpu.VMEM((3, 4) + block, BF16),
            pltpu.VMEM((3, 4) + block, BF16),
            pltpu.VMEM((3, 4) + block, BF16),
            pltpu.VMEM((RANKS * ROWS, 768), F32),
            pltpu.VMEM((RANKS * ROWS, 384), BF16),
            pltpu.VMEM((RANKS * ROWS, 768), BF16),
            pltpu.VMEM((2, 4, ROWS, 256), BF16),
            pltpu.VMEM((2, PLANE, 32, 768), BF16),
            pltpu.VMEM((384, D), F32),
            pltpu.VMEM((PLANE, 48, 512), BF16),
            pltpu.VMEM(block, F32),
            pltpu.VMEM(block, F32),
            pltpu.VMEM((2, PLANE, 32, 768), BF16),
            pltpu.VMEM((PLANE, 48, 512), BF16),
            pltpu.VMEM((384, D), BF16),
        ]
        + [dma((3, 4))] * 8
        + [dma((4,)), dma((4,)), dma((2, 4)), dma((2, 4))]
        + [dma((PLANE,))] * 8
        + [dma((5,))],
        compiler_params=pltpu.CompilerParams(
            collective_id=number, has_side_effects=True, vmem_limit_bytes=VMEM_LIMIT
        ),
        name="middle",
    )(out_mine, wo, gateup_low, down_rows, inputs, upstream, gains)


def end_kernel(
    dq_mine,
    dkv_mine,
    projected,
    cosine,
    sine,
    head_gains,
    all_tokens,
    qkv_part,
    output_lines,
    gateup_parts,
    grad_hidden,
    gains_grad,
    token_grad,
    summed_a,
    summed_b,
    output_parts,
    gains_sum,
    own_kv,
    stage,
    passing,
    dq_all,
    dkv_all,
    grad_qkv,
    part,
    paired,
    sending,
    landed,
    qkv_lines,
    qkv_parts,
    column_a,
    column_b,
    gains_column,
    gains_plane,
    stage_send,
    stage_recv,
    kv_send,
    kv_recv,
    dq_send,
    dq_recv,
    near_send,
    near_recv,
    far_send,
    far_recv,
    plane_send,
    plane_recv,
    gplane_send,
    gplane_recv,
    row_send,
    row_recv,
    a_send,
    a_recv,
    b_send,
    b_recv,
    gcolumn_send,
    gcolumn_recv,
    own_sems,
):
    me = where_am_i()
    x, y, z = me["x"], me["y"], me["zh"] * 2 + me["zl"]
    rank, here = flat_index(me, COLUMN), flat_index(me, SURFACE)
    sums = ColumnSums(
        me, part, paired, sending, landed, near_send, near_recv, far_send, far_recv
    )

    def by_column(ref, out, send, recv):
        return Exchange(
            me,
            COLUMN,
            lambda to: ref.at[flat_index(to, COLUMN)],
            lambda frm: out.at[flat_index(frm, COLUMN)],
            send,
            recv,
        )

    to_a = by_column(column_a, summed_a, a_send, a_recv)
    to_b = by_column(column_b, summed_b, b_send, b_recv)
    gains_in = Exchange(
        me,
        COLUMN,
        lambda to: gains_column.at[rank],
        lambda frm: gains_column.at[flat_index(frm, COLUMN)],
        gcolumn_send,
        gcolumn_recv,
    )
    gains_over = Exchange(
        me,
        SURFACE,
        lambda to: gains_plane.at[here],
        lambda frm: gains_plane.at[flat_index(frm, SURFACE)],
        gplane_send,
        gplane_recv,
    )
    plane = Exchange(
        me,
        SURFACE,
        lambda to: qkv_lines.at[:, flat_index(to, SURFACE)],
        lambda frm: qkv_parts.at[flat_index(frm, SURFACE)],
        plane_send,
        plane_recv,
    )
    queries = Exchange(
        me,
        ("x",),
        lambda to: dq_mine.at[to["x"]],
        lambda frm: dq_all.at[:, frm["x"]],
        dq_send,
        dq_recv,
    )
    rows = RowCopies(me, output_lines, output_parts, row_send, row_recv, True)
    own_dq = pltpu.make_async_copy(dq_mine.at[x], dq_all.at[:, x], own_sems.at[4])
    own_plane = pltpu.make_async_copy(qkv_lines.at[:, here], qkv_parts.at[here], own_sems.at[5])
    own_a = pltpu.make_async_copy(column_a.at[rank], summed_a.at[rank], own_sems.at[6])
    own_b = pltpu.make_async_copy(column_b.at[rank], summed_b.at[rank], own_sems.at[7])

    def own_copy(j):
        to_x = lax.rem(x + j, 4)
        return pltpu.make_async_copy(dkv_mine.at[to_x * 4 + y], own_kv.at[j], own_sems.at[j])

    def stage_copy(j, k):
        to_x, to_y = lax.rem(x + j, 4), lax.rem(y + k, 4)
        return pltpu.make_async_remote_copy(
            src_ref=dkv_mine.at[to_x * 4 + to_y],
            dst_ref=stage.at[k, j],
            send_sem=stage_send.at[k, j],
            recv_sem=stage_recv.at[k, j],
            device_id=address(dict(me, y=to_y)),
            device_id_type=MESH,
        )

    def kv_copy(j, arriving):
        frm_x = lax.rem(x + 4 - j, 4) if arriving else x
        return pltpu.make_async_remote_copy(
            src_ref=passing.at[j],
            dst_ref=dkv_all.at[:, frm_x],
            send_sem=kv_send.at[j],
            recv_sem=kv_recv.at[j],
            device_id=address(dict(me, x=lax.rem(x + j, 4))),
            device_id_type=MESH,
        )

    own_dq.start()
    for j in (2, 1, 3, 0):
        own_copy(j).start()
    greet_all(me, "all", "own")
    for j in (2, 1, 3, 0):
        for k in (1, 3, 2):
            stage_copy(j, k).start()
    queries.begin()
    rows.begin()

    for row_zh in range(2):

        def add_part(s, total):
            return total + gateup_parts[s, row_zh].astype(F32)

        total = lax.fori_loop(0, PLANE, add_part, jnp.zeros((32, 768), F32))
        column_b[pl.ds(row_zh * 4, 4)] = total.reshape(4, 8, 768)
    own_b.start()
    to_b.begin()

    for j in (2, 1, 3, 0):
        own_copy(j).wait()
        total = own_kv[j].astype(F32)
        for k in (1, 3, 2):
            stage_copy(j, k).wait_recv()
            total = total + stage[k, j].astype(F32)
        if j:
            passing[j] = total.astype(BF16)
            kv_copy(j, False).start()
        else:
            dkv_all[:, x] = total.astype(BF16)
    own_dq.wait()
    queries.arrive()
    for j in (2, 1, 3):
        kv_copy(j, True).wait_recv()

    def project_back(i, carry):
        gain_q, gain_k = carry
        back = 3 - i
        off = back + lax.div(back, 2) * (5 - 2 * back)
        to_z = lax.rem(z + off, 4)
        at = pl.ds(pl.multiple_of(to_z * 2 * ROWS, 2 * ROWS), 2 * ROWS)
        row_zh, first = lax.div(to_z, 2), lax.rem(to_z, 2) * 2
        grad_q = dq_all[row_zh, pl.ds(first, 2)].reshape(2 * ROWS, 256).astype(F32)
        grad_kv = dkv_all[row_zh, pl.ds(first, 2)].reshape(2 * ROWS, 256)
        for head in range(3):
            if head == 2:
                grad, gain = grad_kv[:, :HD].astype(F32), head_gains[1:2, :]
            else:
                grad, gain = grad_q[:, head * HD : (head + 1) * HD], head_gains[0:1, :]
            turned = grad * cosine[at, :] - pltpu.roll(grad, HD // 2, 1) * sine[at, :]
            grad_in, grad_gain = norm_back(
                projected[at, head * HD : (head + 1) * HD], gain, turned
            )
            grad_qkv[at, head * HD : (head + 1) * HD] = grad_in.astype(BF16)
            if head == 2:
                gain_k = gain_k + grad_gain
            else:
                gain_q = gain_q + grad_gain
        grad_qkv[at, 384:] = grad_kv[:, HD:]
        sums.put(0, off, dot_nt(grad_qkv[at, :], qkv_part[...]))

        @pl.when(i >= 1)
        def _():
            last = back + 1
            sums.pass_on(0, last + lax.div(last, 2) * (5 - 2 * last))

        return gain_q, gain_k

    nothing = jnp.zeros((1, HD), F32)
    gain_q, gain_k = lax.fori_loop(0, 4, project_back, (nothing, nothing))

    for j in range(16):
        gains_column[rank, j : j + 1, :] = gains_grad[
            j // 8 : j // 8 + 1, j % 8 * HD : (j % 8 + 1) * HD
        ]
    gains_column[rank, 16:17, :] = gain_q
    gains_column[rank, 17:18, :] = gain_k
    gains_column[rank, 18:24, :] = jnp.zeros((6, HD), F32)
    gains_in.begin()

    def qkv_rows(j, carry):
        cols = pl.ds(pl.multiple_of(j * 256, 256), 256)
        grads = dot_tn(all_tokens[:, :, cols].reshape(RANKS * ROWS, 256), grad_qkv[...])
        qkv_lines[lax.div(j, 2), pl.ds(lax.rem(j, 2) * 8, 8)] = grads.astype(BF16).reshape(
            8, 32, 512
        )
        return carry

    lax.fori_loop(0, 4, qkv_rows, 0)
    own_plane.start()
    plane.begin()

    gains_in.arrive()
    gains_plane[here] = jnp.sum(gains_column[...], axis=0)
    gains_over.begin()
    token_grad[...] = grad_hidden[...] + sums.total(0)

    own_plane.wait()
    plane.arrive()
    for row_zh in range(2):

        def add_qkv(s, total):
            return total + qkv_parts[s, row_zh].astype(F32)

        total = lax.fori_loop(0, PLANE, add_qkv, jnp.zeros((32, 512), F32))
        column_a[pl.ds(row_zh * 4, 4)] = total.reshape(4, 8, 512)
    own_a.start()
    to_a.begin()
    gains_over.arrive()
    gains_sum[...] = jnp.sum(gains_plane[...], axis=0)
    to_b.arrive()
    rows.arrive()
    own_b.wait()
    for j in (2, 1, 3, 0):
        for k in (1, 3, 2):
            stage_copy(j, k).wait_send()
        if j:
            kv_copy(j, False).wait_send()
    sums.drain(0)
    for exchange in (queries, rows, to_b, gains_in, gains_over, plane):
        exchange.drain()
    own_a.wait()
    to_a.arrive()
    to_a.drain()


def end(number, *arrays):
    anywhere = pl.BlockSpec(memory_space=pl.ANY)
    vmem = pl.BlockSpec(memory_space=pltpu.VMEM)
    dma = pltpu.SemaphoreType.DMA
    struct = jax.ShapeDtypeStruct
    block = (ROWS, D)
    quarter_rows = (2, ROWS, 256)
    return pl.pallas_call(
        end_kernel,
        out_shape=(
            struct(block, F32),
            struct((RANKS, 8, 512), F32),
            struct((RANKS, 8, 768), F32),
            struct((PLANE, 16, D), BF16),
            struct((24, HD), F32),
        ),
        in_specs=[anywhere, anywhere] + [vmem] * 6 + [anywhere] + [vmem] * 3,
        out_specs=(vmem, anywhere, anywhere, anywhere, vmem),
        scratch_shapes=[
            pltpu.VMEM((4,) + quarter_rows, BF16),
            pltpu.VMEM((4, 4) + quarter_rows, BF16),
            pltpu.VMEM((4,) + quarter_rows, BF16),
            pltpu.VMEM((2, 4, ROWS, 256), BF16),
            pltpu.VMEM((2, 4, ROWS, 256), BF16),
            pltpu.VMEM((RANKS * ROWS, 512), BF16),
            pltpu.VMEM((1, 4, 2) + block, BF16),
            pltpu.VMEM((1, 4) + block, BF16),
            pltpu.VMEM((1, 4) + block, BF16),
            pltpu.VMEM((1, 4) + block, BF16),
            pltpu.VMEM((2, PLANE, 32, 512), BF16),
            pltpu.VMEM((PLANE, 2, 32, 512), BF16),
            pltpu.VMEM((RANKS, 8, 512), F32),
            pltpu.VMEM((RANKS, 8, 768), F32),
            pltpu.VMEM((RANKS, 24, HD), F32),
            pltpu.VMEM((PLANE, 24, HD), F32),
        ]
        + [dma((4, 4))] * 2
        + [dma((4,))] * 4
        + [dma((1, 4))] * 4
        + [dma((PLANE,))] * 6
        + [dma((RANKS,))] * 6
        + [dma((8,))],
        compiler_params=pltpu.CompilerParams(
            collective_id=number, has_side_effects=True, vmem_limit_bytes=VMEM_LIMIT
        ),
        name="end",
    )(*arrays)


def adam_update(weight, gradient, mean_old, square_old, rate, decay):
    mean_new = BETA_ONE * mean_old + (1.0 - BETA_ONE) * gradient
    square_new = BETA_TWO * square_old + (1.0 - BETA_TWO) * gradient * gradient
    mean_hat = mean_new / (1.0 - BETA_ONE**STEP)
    square_hat = square_new / (1.0 - BETA_TWO**STEP)
    weight_new = weight - rate * (mean_hat / (jnp.sqrt(square_hat) + ADAM_EPS) + decay * weight)
    return (weight_new, mean_new, square_new)


def by_rank(array, width):
    return array.reshape(array.shape[0], RANKS, width)


def body(
    tokens,
    cotangent,
    positions,
    seq_ids,
    query_weight,
    keyval_weight,
    output_weight,
    gateup_weight,
    down_weight,
    norm_gains,
    query_mean,
    keyval_mean,
    output_mean,
    gateup_mean,
    down_mean,
    gains_mean,
    query_square,
    keyval_square,
    output_square,
    gateup_square,
    down_square,
    gains_square,
):
    inputs = tokens[0]
    at_x, at_y = lax.axis_index("x"), lax.axis_index("y")

    own_blocks = (positions[0] + LONG * seq_ids[0]).reshape(-1, BLOCK)[:, 0] // BLOCK
    own_pair = lax.dynamic_slice_in_dim(own_blocks, 2 * lax.axis_index(("zh", "x", "y")), 2)
    own_pair = jnp.where(own_pair >= LONG // BLOCK, own_pair - LONG // BLOCK, own_pair)
    extra = jnp.concatenate(
        [
            jnp.pad(norm_gains, (0, HD - norm_gains.shape[0]))[None],
            jnp.pad(own_blocks.astype(F32), (0, HD - BLOCK))[None],
            jnp.broadcast_to(own_pair.astype(F32)[:, None], (2, HD)),
            jnp.zeros((4, HD), F32),
        ]
    )
    sent_a = jnp.concatenate(
        [
            by_rank(query_weight, 256),
            by_rank(keyval_weight[:, :KV], 128),
            by_rank(keyval_weight[:, KV:], 128),
            jnp.broadcast_to(extra[:, None, :], (8, RANKS, HD)),
        ],
        axis=2,
    ).transpose(1, 0, 2)
    sent_b = jnp.concatenate(
        [by_rank(gateup_weight[:, :FF], 384), by_rank(gateup_weight[:, FF:], 384)], axis=2
    ).transpose(1, 0, 2)
    frequency = ROPE_BASE ** (-jnp.arange(HD // 2, dtype=F32) * 2.0 / HD)
    (
        q_mine,
        kv_mine,
        all_tokens,
        output_wide,
        gateup_low,
        extras,
        gains_low,
        qkv_part,
        projected,
        cosine,
        sine,
        head_gains,
    ) = start(
        1,
        sent_a,
        sent_b,
        inputs,
        output_weight.astype(BF16),
        jnp.concatenate([frequency, frequency])[None],
    )
    gains_all = gains_low.reshape(-1, 8, HD)[:, 0, :18].reshape(-1).astype(F32)
    attn_gain = gains_all[:D]
    ffn_gain = gains_all[D : 2 * D]

    blocks = extras[:4, 1, :BLOCK].astype(jnp.int32).reshape(4, 2, 4, 4, 2)
    pack_blocks = lax.dynamic_index_in_dim(blocks, at_x, 0, keepdims=False)
    key_blocks = pack_blocks.transpose(1, 2, 0, 3).reshape(-1)
    query_blocks = (
        lax.dynamic_index_in_dim(pack_blocks, at_y, 2, keepdims=False).transpose(1, 0, 2).reshape(-1)
    )
    q_mine = q_mine.reshape(1024, 256)
    kv_mine = kv_mine.reshape(PACK_TOK, 256)
    out_mine, lse = attend(query_blocks, key_blocks, q_mine, kv_mine)

    def to_x(ref, to):
        return ref.at[to["x"]]

    def from_pack_x(ref, frm):
        return ref.at[:, frm["x"]]

    result, grad_hidden, gains_grad, grad_mine, gateup_parts, down_parts, output_lines = middle(
        2,
        out_mine.reshape(4, 2, ROWS, 256),
        output_wide.reshape(256, D),
        gateup_low,
        jnp.concatenate([down_weight[:, :512], down_weight[:, 512:]], axis=0).astype(BF16),
        inputs,
        cotangent[0],
        jnp.stack([attn_gain, ffn_gain]),
    )
    dq_mine, dkv_mine = attend_back(
        query_blocks, key_blocks, q_mine, kv_mine, grad_mine.reshape(1024, 256), out_mine, lse
    )
    token_grad, summed_a, summed_b, output_parts, gains_total = end(
        3,
        dq_mine.reshape(4, 2, ROWS, 256),
        dkv_mine.reshape(PLANE, 2, ROWS, 256),
        projected,
        cosine,
        sine,
        head_gains,
        all_tokens,
        qkv_part,
        output_lines,
        gateup_parts,
        grad_hidden,
        gains_grad,
    )
    gains_sum = lax.dynamic_slice_in_dim(
        gains_total.reshape(-1), lax.axis_index(AXES) * norm_gains.shape[0], norm_gains.shape[0]
    )
    output_sum = jnp.sum(output_parts.astype(F32), axis=0)
    down_wide = jnp.sum(down_parts.astype(F32), axis=0)
    down_sum = jnp.concatenate([down_wide[:24], down_wide[24:]], axis=1)
    wide_a, wide_b = summed_a.transpose(1, 0, 2), summed_b.transpose(1, 0, 2)
    query_sum = wide_a[:, :, :256].reshape(8, 2048)
    keyval_sum = jnp.concatenate(
        [wide_a[:, :, 256:384].reshape(8, KV), wide_a[:, :, 384:].reshape(8, KV)], axis=1
    )
    gateup_sum = jnp.concatenate(
        [wide_b[:, :, :384].reshape(8, FF), wide_b[:, :, 384:].reshape(8, FF)], axis=1
    )

    query_new, query_mean_new, query_square_new = adam_update(
        query_weight, query_sum, query_mean, query_square, RATE_MATRIX, DECAY
    )
    keyval_new, keyval_mean_new, keyval_square_new = adam_update(
        keyval_weight, keyval_sum, keyval_mean, keyval_square, RATE_MATRIX, DECAY
    )
    output_new, output_mean_new, output_square_new = adam_update(
        output_weight, output_sum, output_mean, output_square, RATE_MATRIX, DECAY
    )
    gateup_new, gateup_mean_new, gateup_square_new = adam_update(
        gateup_weight, gateup_sum, gateup_mean, gateup_square, RATE_MATRIX, DECAY
    )
    down_new, down_mean_new, down_square_new = adam_update(
        down_weight, down_sum, down_mean, down_square, RATE_MATRIX, DECAY
    )
    gains_new, gains_mean_new, gains_square_new = adam_update(
        norm_gains, gains_sum, gains_mean, gains_square, RATE_GAIN, 0.0
    )
    return (
        result[None],
        token_grad[None],
        query_sum,
        keyval_sum,
        output_sum,
        gateup_sum,
        down_sum,
        gains_sum,
        query_new,
        keyval_new,
        output_new,
        gateup_new,
        down_new,
        gains_new,
        query_mean_new,
        keyval_mean_new,
        output_mean_new,
        gateup_mean_new,
        down_mean_new,
        gains_mean_new,
        query_square_new,
        keyval_square_new,
        output_square_new,
        gateup_square_new,
        down_square_new,
        gains_square_new,
    )


def solution(mesh):
    fine = Mesh(mesh.devices.reshape([SIZE[a] for a in AXES]), AXES)
    rows = P(("zl", "co"), ("zh", "x", "y"), None)
    packs = P(("zl", "co"), None)
    matrix = P(AXES, None)
    vector = P(AXES)
    params = [matrix] * 5 + [vector]
    return jax.shard_map(
        body,
        mesh=fine,
        in_specs=(rows, rows, packs, packs, *params, *params, *params),
        out_specs=(rows, rows, *params, *params, *params, *params),
        check_vma=False,
    )
```

```python
import functools
import math

import jax
import jax.numpy as jnp
from jax import lax
from jax.experimental import pallas as pl
from jax.experimental.pallas import tpu as pltpu
from jax.sharding import Mesh
from jax.sharding import PartitionSpec as P

D = 1024
H = 16
KVH = 8
HD = 128
FF = 3072
KV = 1024
STEP = 10
LONG = 3072
ROWS = 128
BLOCK = 64
CHUNK = 512
PACK_TOK = 4096
RANKS = 8
PLANE = 16


NORM_EPS = 1e-06
ROPE_BASE = 1000000.0
BETA_ONE = 0.9
BETA_TWO = 0.95
ADAM_EPS = 1e-08
DECAY = 0.1
RATE_MATRIX = 0.1
RATE_GAIN = 0.3

SCALE = HD**-0.5
LOG2E = math.log2(math.e)

AXES = ("zh", "x", "y", "zl", "co")
SIZE = {"zh": 2, "x": 4, "y": 4, "zl": 2, "co": 2}
COLUMN = ("zh", "zl", "co")
SURFACE = ("x", "y")
MESH = pl.DeviceIdType.MESH
F32 = jnp.float32
BF16 = jnp.bfloat16
VMEM_LIMIT = 50 * 1024 * 1024


def where_am_i():
    return {a: lax.axis_index(a) for a in AXES}


def address(place):
    return tuple(place[a] for a in AXES)


def flat_index(place, axes):
    at = 0
    for a in axes:
        at = at * SIZE[a] + place[a]
    return at


def shifted(place, axes, k, sign):
    to = dict(place)
    for a in reversed(axes):
        step = lax.rem(k, SIZE[a])
        k = lax.div(k, SIZE[a])
        to[a] = lax.rem(place[a] + sign * step + SIZE[a], SIZE[a])
    return to


def column_place(me, z, core):
    return dict(me, zh=lax.div(z, 2), zl=lax.rem(z, 2), co=core)


def dot_nn(a, b):
    return lax.dot_general(a, b, (((1,), (0,)), ((), ())), preferred_element_type=F32)


def dot_nt(a, b):
    return lax.dot_general(a, b, (((1,), (1,)), ((), ())), preferred_element_type=F32)


def dot_tn(a, b):
    return lax.dot_general(a, b, (((0,), (0,)), ((), ())), preferred_element_type=F32)


def stacked_heads(ref, tile):
    rows = ref[pl.ds(tile * BLOCK, BLOCK), :]
    return jnp.concatenate([rows[:, :HD], rows[:, HD:]], axis=0)


def allowed_keys(block, chunk):
    keys = chunk * CHUNK + lax.broadcasted_iota(jnp.int32, (CHUNK, 2 * BLOCK), 0)
    lanes = lax.broadcasted_iota(jnp.int32, (CHUNK, 2 * BLOCK), 1)
    return keys <= block * BLOCK + lax.rem(lanes, BLOCK)


def first_chunk(block):
    return jnp.where(block >= LONG // BLOCK, LONG // CHUNK, 0)


def attend_kernel(q_blocks, k_blocks, q_ref, kv_ref, out_ref, lse_ref, keys, values, values_t):
    def sort(i, carry):
        to = pl.multiple_of(k_blocks[i] * BLOCK, BLOCK)
        here = pl.multiple_of(i * BLOCK, BLOCK)
        keys[pl.ds(to, BLOCK), :] = kv_ref[pl.ds(here, BLOCK), :HD]
        values[pl.ds(to, BLOCK), :] = kv_ref[pl.ds(here, BLOCK), HD:]
        return carry

    lax.fori_loop(0, PACK_TOK // BLOCK, sort, 0)
    for c in range(PACK_TOK // CHUNK):
        part = values[c * CHUNK : (c + 1) * CHUNK, :].astype(F32)
        values_t[c] = part.T.astype(BF16)

    def one_tile(tile, carry):
        block = q_blocks[tile]
        query = stacked_heads(q_ref, tile)
        last = lax.div(block, CHUNK // BLOCK)

        def one_chunk(c, state, masked):
            total, mixed = state
            chunk_keys = keys[pl.ds(pl.multiple_of(c * CHUNK, CHUNK), CHUNK), :]
            weights = jnp.exp2(dot_nt(chunk_keys, query) * (SCALE * LOG2E))
            if masked:
                weights = jnp.where(allowed_keys(block, c), weights, 0.0)
            total = total + jnp.sum(weights, axis=0, keepdims=True)
            mixed = mixed + dot_nn(values_t[c], weights.astype(BF16))
            return total, mixed

        def two_chunks(j, state):
            c = first + 2 * j
            return one_chunk(c + 1, one_chunk(c, state, False), False)

        first = first_chunk(block)
        pairs = lax.div(last - first, 2)
        state = (jnp.zeros((1, 2 * BLOCK), F32), jnp.zeros((HD, 2 * BLOCK), F32))
        state = lax.fori_loop(0, pairs, two_chunks, state)
        state = lax.fori_loop(
            first + 2 * pairs, last, lambda c, s: one_chunk(c, s, False), state
        )
        total, mixed = one_chunk(last, state, True)
        result = (mixed / total).T.astype(BF16)
        rows = pl.ds(pl.multiple_of(tile * BLOCK, BLOCK), BLOCK)
        out_ref[rows, :HD] = result[:BLOCK]
        out_ref[rows, HD:] = result[BLOCK:]
        lse_ref[pl.ds(tile, 1), :] = jnp.log2(total)
        return carry

    lax.fori_loop(0, q_ref.shape[0] // BLOCK, one_tile, 0)


def attend(q_blocks, k_blocks, q, kv):
    smem = pl.BlockSpec(memory_space=pltpu.SMEM)
    vmem = pl.BlockSpec(memory_space=pltpu.VMEM)
    tiles = q.shape[0] // BLOCK
    return pl.pallas_call(
        attend_kernel,
        out_shape=(
            jax.ShapeDtypeStruct(q.shape, BF16),
            jax.ShapeDtypeStruct((tiles, 2 * BLOCK), F32),
        ),
        in_specs=[smem, smem, vmem, vmem],
        out_specs=(vmem, vmem),
        scratch_shapes=[
            pltpu.VMEM((PACK_TOK, HD), BF16),
            pltpu.VMEM((PACK_TOK, HD), BF16),
            pltpu.VMEM((PACK_TOK // CHUNK, HD, CHUNK), BF16),
        ],
        compiler_params=pltpu.CompilerParams(vmem_limit_bytes=VMEM_LIMIT),
        cost_estimate=pl.CostEstimate(
            flops=4 * 10**9, bytes_accessed=4 * 10**6, transcendentals=8 * 10**6
        ),
        name="attend",
    )(q_blocks, k_blocks, q, kv)


def attend_back_kernel(
    q_blocks,
    k_blocks,
    q_ref,
    kv_ref,
    grad_ref,
    out_ref,
    lse_ref,
    dq_ref,
    dkv_ref,
    keys,
    values,
    keys_t,
    dk,
    dv,
):
    def sort(i, carry):
        to = pl.multiple_of(k_blocks[i] * BLOCK, BLOCK)
        here = pl.multiple_of(i * BLOCK, BLOCK)
        keys[pl.ds(to, BLOCK), :] = kv_ref[pl.ds(here, BLOCK), :HD]
        values[pl.ds(to, BLOCK), :] = kv_ref[pl.ds(here, BLOCK), HD:]
        return carry

    lax.fori_loop(0, PACK_TOK // BLOCK, sort, 0)
    for c in range(PACK_TOK // CHUNK):
        part = keys[c * CHUNK : (c + 1) * CHUNK, :].astype(F32)
        keys_t[c] = part.T.astype(BF16)
    dk[...] = jnp.zeros_like(dk)
    dv[...] = jnp.zeros_like(dv)

    def one_tile(tile, carry):
        block = q_blocks[tile]
        query = stacked_heads(q_ref, tile)
        grad = stacked_heads(grad_ref, tile)
        out = stacked_heads(out_ref, tile)
        inner = jnp.sum((grad.astype(F32) * out.astype(F32)).T, axis=0, keepdims=True)
        lse = lse_ref[pl.ds(tile, 1), :]
        last = lax.div(block, CHUNK // BLOCK)

        def one_chunk(c, dq, masked):
            rows = pl.ds(pl.multiple_of(c * CHUNK, CHUNK), CHUNK)
            probs = jnp.exp2(dot_nt(keys[rows, :], query) * (SCALE * LOG2E) - lse)
            if masked:
                probs = jnp.where(allowed_keys(block, c), probs, 0.0)
            grad_probs = dot_nt(values[rows, :], grad)
            grad_scores = (probs * (grad_probs - inner)).astype(BF16)
            dv[rows, :] += dot_nn(probs.astype(BF16), grad)
            dk[rows, :] += dot_nn(grad_scores, query)
            return dq + dot_nn(keys_t[c], grad_scores)

        def two_chunks(j, dq):
            c = first + 2 * j
            return one_chunk(c + 1, one_chunk(c, dq, False), False)

        first = first_chunk(block)
        pairs = lax.div(last - first, 2)
        dq = lax.fori_loop(0, pairs, two_chunks, jnp.zeros((HD, 2 * BLOCK), F32))
        dq = lax.fori_loop(first + 2 * pairs, last, lambda c, s: one_chunk(c, s, False), dq)
        dq = (one_chunk(last, dq, True) * SCALE).T.astype(BF16)
        rows = pl.ds(pl.multiple_of(tile * BLOCK, BLOCK), BLOCK)
        dq_ref[rows, :HD] = dq[:BLOCK]
        dq_ref[rows, HD:] = dq[BLOCK:]
        return carry

    lax.fori_loop(0, q_ref.shape[0] // BLOCK, one_tile, 0)

    def unsort(i, carry):
        at = pl.multiple_of(k_blocks[i] * BLOCK, BLOCK)
        here = pl.multiple_of(i * BLOCK, BLOCK)
        dkv_ref[pl.ds(here, BLOCK), :HD] = (dk[pl.ds(at, BLOCK), :] * SCALE).astype(BF16)
        dkv_ref[pl.ds(here, BLOCK), HD:] = dv[pl.ds(at, BLOCK), :].astype(BF16)
        return carry

    lax.fori_loop(0, PACK_TOK // BLOCK, unsort, 0)


def attend_back(q_blocks, k_blocks, q, kv, grad, out, lse):
    smem = pl.BlockSpec(memory_space=pltpu.SMEM)
    vmem = pl.BlockSpec(memory_space=pltpu.VMEM)
    return pl.pallas_call(
        attend_back_kernel,
        out_shape=(
            jax.ShapeDtypeStruct(q.shape, BF16),
            jax.ShapeDtypeStruct(kv.shape, BF16),
        ),
        in_specs=[smem, smem] + [vmem] * 5,
        out_specs=(vmem, vmem),
        scratch_shapes=[
            pltpu.VMEM((PACK_TOK, HD), BF16),
            pltpu.VMEM((PACK_TOK, HD), BF16),
            pltpu.VMEM((PACK_TOK // CHUNK, HD, CHUNK), BF16),
            pltpu.VMEM((PACK_TOK, HD), F32),
            pltpu.VMEM((PACK_TOK, HD), F32),
        ],
        compiler_params=pltpu.CompilerParams(vmem_limit_bytes=VMEM_LIMIT),
        cost_estimate=pl.CostEstimate(
            flops=10**10, bytes_accessed=8 * 10**6, transcendentals=8 * 10**6
        ),
        name="attend_back",
    )(q_blocks, k_blocks, q, kv, grad, out, lse)


class ColumnSums:
    def __init__(self, me, part, paired, sending, landed, near_send, near_recv, far_send, far_recv):
        self.me, self.z, self.core = me, me["zh"] * 2 + me["zl"], me["co"]
        self.part, self.paired, self.sending, self.landed = part, paired, sending, landed
        self.near_sems, self.far_sems = (near_send, near_recv), (far_send, far_recv)
        self.rows = part.shape[-2]
        self.top, self.low = pl.ds(0, self.rows // 2), pl.ds(self.rows // 2, self.rows // 2)

    def near(self, phase, off):
        return pltpu.make_async_remote_copy(
            src_ref=self.part.at[phase, lax.rem(self.z + off, 4), 1 - self.core],
            dst_ref=self.paired.at[phase, off],
            send_sem=self.near_sems[0].at[phase, off],
            recv_sem=self.near_sems[1].at[phase, off],
            device_id=address(column_place(self.me, self.z, 1 - self.core)),
            device_id_type=MESH,
        )

    def far(self, phase, which):
        slot = which if which in (1, 3) else 2
        src, dst = self.sending.at[phase, slot], self.landed.at[phase, slot]
        if slot == 2:
            half = self.top if which == 2 else self.low
            src, dst = src.at[half], dst.at[half]
        step = 1 if which in (1, 2) else 3
        return pltpu.make_async_remote_copy(
            src_ref=src,
            dst_ref=dst,
            send_sem=self.far_sems[0].at[phase, which],
            recv_sem=self.far_sems[1].at[phase, which],
            device_id=address(column_place(self.me, lax.rem(self.z + step, 4), self.core)),
            device_id_type=MESH,
        )

    def put(self, phase, off, terms):
        self.part[phase, lax.rem(self.z + off, 4)] = terms.astype(BF16).reshape(2, self.rows, D)
        self.near(phase, off).start()

    def put_all(self, phase, terms):
        self.part[phase] = terms.astype(BF16).reshape(4, 2, self.rows, D)
        for off in (2, 1, 3, 0):
            self.near(phase, off).start()

    def chip_sum(self, phase, off):
        self.near(phase, off).wait_recv()
        mine = self.part[phase, lax.rem(self.z + off, 4), self.core].astype(F32)
        return mine + self.paired[phase, off].astype(F32)

    def first(self, phase):
        self.sending[phase, 2] = self.chip_sum(phase, 2).astype(BF16)
        self.far(phase, 2).start()
        self.far(phase, 0).start()

    def second(self, phase):
        for which, by_way, half in ((1, 2, self.top), (3, 0, self.low)):
            self.sending[phase, which] = self.chip_sum(phase, which).astype(BF16)
            self.far(phase, by_way).wait_recv()
            both = self.sending[phase, which, half].astype(F32)
            both = both + self.landed[phase, 2, half].astype(F32)
            self.sending[phase, which, half] = both.astype(BF16)
            self.far(phase, which).start()

    def total(self, phase):
        total = self.chip_sum(phase, 0)
        for which in (1, 3):
            self.far(phase, which).wait_recv()
            total = total + self.landed[phase, which].astype(F32)
        return total

    def drain(self, phase):
        for off in range(4):
            self.near(phase, off).wait_send()
            self.far(phase, off).wait_send()


class ColumnGathers:
    def __init__(self, me, blocks, near_send, near_recv, far_send, far_recv):
        self.me, self.z, self.core = me, me["zh"] * 2 + me["zl"], me["co"]
        self.blocks = blocks
        self.near_sems, self.far_sems = (near_send, near_recv), (far_send, far_recv)
        self.rows = blocks.shape[-2]

    def far(self, phase, which, arriving):
        step = 1 if which in (1, 2) else 3
        back = (step if which in (1, 3) else 2 * step) if arriving else (0 if which in (1, 3) else step)
        block = self.blocks.at[phase, lax.rem(self.z + 4 * 2 - back, 4) * 2 + self.core]
        if which == 2:
            block = block.at[pl.ds(0, self.rows // 2)]
        if which == 0:
            block = block.at[pl.ds(self.rows // 2, self.rows // 2)]
        return pltpu.make_async_remote_copy(
            src_ref=block,
            dst_ref=block,
            send_sem=self.far_sems[0].at[phase, which],
            recv_sem=self.far_sems[1].at[phase, which],
            device_id=address(column_place(self.me, lax.rem(self.z + step, 4), self.core)),
            device_id_type=MESH,
        )

    def near(self, phase, off, arriving):
        core = 1 - self.core if arriving else self.core
        block = self.blocks.at[phase, lax.rem(self.z + 4 - off, 4) * 2 + core]
        return pltpu.make_async_remote_copy(
            src_ref=block,
            dst_ref=block,
            send_sem=self.near_sems[0].at[phase, off],
            recv_sem=self.near_sems[1].at[phase, off],
            device_id=address(column_place(self.me, self.z, 1 - self.core)),
            device_id_type=MESH,
        )

    def begin(self, phase, rows):
        self.blocks[phase, self.z * 2 + self.core] = rows
        for off in (1, 3):
            self.far(phase, off, False).start()
        self.near(phase, 0, False).start()

    def pass_on(self, phase):
        for off, by_way in ((1, 2), (3, 0)):
            self.far(phase, off, True).wait_recv()
            self.far(phase, by_way, False).start()
            self.near(phase, off, False).start()

    def await_chip(self, phase, i):
        off = i + lax.div(i, 2) * (5 - 2 * i)

        @pl.when(i == 3)
        def _():
            for by_way in (2, 0):
                self.far(phase, by_way, True).wait_recv()
            self.near(phase, 2, False).start()

        self.near(phase, off, True).wait_recv()
        return off, lax.rem(self.z + 4 - off, 4)

    def await_all(self, phase):
        for by_way in (2, 0):
            self.far(phase, by_way, True).wait_recv()
        self.near(phase, 2, False).start()
        for off in range(4):
            self.near(phase, off, True).wait_recv()

    def drain(self, phase):
        for off in range(4):
            self.near(phase, off, False).wait_send()
            self.far(phase, off, False).wait_send()


def norm_factor(values):
    return lax.rsqrt(jnp.mean(values * values, axis=-1, keepdims=True) + NORM_EPS)


def norm_back(values, norm_gain, grad):
    factor = norm_factor(values)
    scaled = grad * norm_gain
    inner = jnp.mean(values * scaled, axis=-1, keepdims=True)
    grad_gain = jnp.sum(grad * values * factor, axis=0, keepdims=True)
    return factor * scaled - values * (factor * factor * factor * inner), grad_gain


def gray(i):
    return i + lax.div(i, 2) * (5 - 2 * i)


def quarter(place):
    return place["zl"] * 2 + place["co"]


def at_quarter(place, t):
    return dict(place, zl=lax.div(t, 2), co=lax.rem(t, 2))


def row_user(me, k):
    return at_quarter(shifted(me, SURFACE, k, 1), me["x"])


def row_owner(me, k):
    y, t = lax.div(k, 4), lax.rem(k, 4)
    to = dict(me, x=quarter(me), y=lax.rem(me["y"] + y, 4))
    return at_quarter(to, lax.rem(quarter(me) + t, 4))


def row_slot(owner):
    return owner["y"] * 4 + quarter(owner)


def greet(barrier, place):
    pl.semaphore_signal(barrier, inc=1, device_id=address(place), device_id_type=MESH)


def greet_all(me, column, rows):
    barrier = pltpu.get_barrier_semaphore()

    def greet_surface(k, carry):
        greet(barrier, shifted(me, SURFACE, k, 1))
        return carry

    def greet_column_all(k, carry):
        greet(barrier, shifted(me, COLUMN, k, 1))
        return carry

    lax.fori_loop(1, PLANE, greet_surface, 0)
    expected = PLANE - 1
    if column == "all":
        lax.fori_loop(1, RANKS, greet_column_all, 0)
        expected = expected + RANKS - 1
    else:
        z = me["zh"] * 2 + me["zl"]
        for off in (1, 2, 3):
            greet(barrier, column_place(me, lax.rem(z + off, 4), me["co"]))
        greet(barrier, column_place(me, z, 1 - me["co"]))
        expected = expected + 4
    at_home = me["x"] == quarter(me)
    if rows == "swap":

        @pl.when(jnp.logical_not(at_home))
        def _():
            greet(barrier, swap_partner(me))

        expected = expected + 1 - jnp.where(at_home, 1, 0)
    elif rows is not None:

        def greet_rows(k, carry):
            @pl.when(jnp.logical_not(jnp.logical_and(k == 0, at_home)))
            def _():
                if rows != "own":
                    greet(barrier, row_owner(me, k))
                if rows != "use":
                    greet(barrier, row_user(me, k))

            return carry

        lax.fori_loop(0, PLANE, greet_rows, 0)
        count = PLANE - jnp.where(at_home, 1, 0)
        expected = expected + (2 * count if rows == "both" else count)
    pl.semaphore_wait(barrier, expected)


def swap_partner(me):
    return at_quarter(dict(me, x=quarter(me)), me["x"])


class Swap:
    def __init__(self, me, src, dst, own_dst, sems):
        self.at_home = me["x"] == quarter(me)
        self.remote = lambda: pltpu.make_async_remote_copy(
            src_ref=src,
            dst_ref=dst,
            send_sem=sems.at[0],
            recv_sem=sems.at[1],
            device_id=address(swap_partner(me)),
            device_id_type=MESH,
        )
        self.own = lambda: pltpu.make_async_copy(src, own_dst, sems.at[0])

    def either(self, remote, own):
        @pl.when(self.at_home)
        def _():
            own()

        @pl.when(jnp.logical_not(self.at_home))
        def _():
            remote()

    def begin(self):
        self.either(lambda: self.remote().start(), lambda: self.own().start())

    def finish(self):
        def both():
            copy = self.remote()
            copy.wait_recv()
            copy.wait_send()

        self.either(both, lambda: self.own().wait())


class RowCopies:
    def __init__(self, me, src, dst, send, recv, back):
        self.me, self.src, self.dst, self.send, self.recv, self.back = me, src, dst, send, recv, back
        self.at_home = me["x"] == quarter(me)

    def copy(self, k, arriving):
        me = self.me
        if self.back:
            to = row_owner(me, k)
            frm = row_user(me, k) if arriving else me
            src, slot = self.src.at[row_slot(to)], flat_index(frm, SURFACE)
        else:
            to = row_user(me, k)
            frm = row_owner(me, k) if arriving else me
            src, slot = self.src, row_slot(frm)
        return pltpu.make_async_remote_copy(
            src_ref=src,
            dst_ref=self.dst.at[slot],
            send_sem=self.send.at[k],
            recv_sem=self.recv.at[slot],
            device_id=address(to),
            device_id_type=MESH,
        )

    def own(self):
        me = self.me
        if self.back:
            src, slot = self.src.at[row_slot(me)], flat_index(me, SURFACE)
        else:
            src, slot = self.src, row_slot(me)
        return pltpu.make_async_copy(src, self.dst.at[slot], self.recv.at[slot])

    def each(self, remote, own):
        def one(j, carry):
            k = lax.rem(j * 7, PLANE)
            itself = jnp.logical_and(k == 0, self.at_home)

            @pl.when(itself)
            def _():
                own()

            @pl.when(jnp.logical_not(itself))
            def _():
                remote(k)

            return carry

        lax.fori_loop(0, PLANE, one, 0)

    def begin(self):
        self.each(lambda k: self.copy(k, False).start(), lambda: self.own().start())

    def arrive(self):
        self.each(lambda k: self.copy(k, True).wait_recv(), lambda: self.own().wait())

    def drain(self):
        self.each(lambda k: self.copy(k, False).wait_send(), lambda: None)


class Exchange:
    def __init__(self, me, axes, take, put, send, recv):
        self.me, self.axes, self.take, self.put, self.send, self.recv = me, axes, take, put, send, recv
        self.n = math.prod(SIZE[a] for a in axes)
        self.mix = {4: 1, 8: 3, 16: 7}[self.n]

    def copy(self, k, arriving):
        to = shifted(self.me, self.axes, k, 1)
        frm = shifted(self.me, self.axes, k, -1) if arriving else self.me
        return pltpu.make_async_remote_copy(
            src_ref=self.take(to),
            dst_ref=self.put(frm),
            send_sem=self.send.at[k],
            recv_sem=self.recv.at[k],
            device_id=address(to),
            device_id_type=MESH,
        )

    def each(self, act):
        def one(j, carry):
            act(lax.rem(j * self.mix, self.n))
            return carry

        lax.fori_loop(1, self.n, one, 0)

    def begin(self):
        self.each(lambda k: self.copy(k, False).start())

    def arrive(self):
        self.each(lambda k: self.copy(k, True).wait_recv())

    def drain(self):
        self.each(lambda k: self.copy(k, False).wait_send())


class PlaneGathers:
    def __init__(self, me, views, first_send, first_recv, second_send, second_recv):
        self.me, self.views = me, views
        self.sems = ((first_send, first_recv), (second_send, second_recv))

    def copy(self, turn, view, half, k, arriving):
        axis = "xy"[half] if turn == 0 else "yx"[half]
        to = shifted(self.me, (axis,), k, 1)
        frm = shifted(self.me, (axis,), k, -1) if arriving else self.me
        one, many = self.views[view]
        block = one(half, frm["x"], frm["y"]) if turn == 0 else many(half, frm["yx"[half]])
        return pltpu.make_async_remote_copy(
            src_ref=block,
            dst_ref=block,
            send_sem=self.sems[turn][0].at[view, half, k],
            recv_sem=self.sems[turn][1].at[view, half, k],
            device_id=address(to),
            device_id_type=MESH,
        )

    def each(self, view, act):
        for half in range(2):
            for k in (1, 3, 2):
                act(half, k)

    def begin(self, view):
        self.each(view, lambda half, k: self.copy(0, view, half, k, False).start())

    def pass_on(self, view):
        for half in range(2):
            for k in (1, 3, 2):
                self.copy(0, view, half, k, True).wait_recv()
            for k in (1, 3, 2):
                self.copy(1, view, half, k, False).start()

    def arrive(self, view):
        self.each(view, lambda half, k: self.copy(1, view, half, k, True).wait_recv())

    def drain(self):
        for view in range(len(self.views)):
            for turn in range(2):
                self.each(
                    view, lambda half, k: self.copy(turn, view, half, k, False).wait_send()
                )


class PlaneSums:
    def __init__(self, me, lines, got, middle_sums, got_last, first_send, first_recv, last_send, last_recv):
        self.me, self.lines, self.got, self.sums, self.got_last = me, lines, got, middle_sums, got_last
        self.sems = ((first_send, first_recv), (last_send, last_recv))

    def row(self, half, at):
        return (half, at) if half == 0 else (half, slice(None), at)

    def copy(self, turn, half, k):
        axis = "xy"[half] if turn == 0 else "yx"[half]
        to = shifted(self.me, (axis,), k, 1)
        if turn == 0:
            src, dst = self.lines.at[self.row(half, to[axis])], self.got.at[half, k]
        else:
            src, dst = self.sums.at[half, to[axis]], self.got_last.at[half, k]
        return pltpu.make_async_remote_copy(
            src_ref=src,
            dst_ref=dst,
            send_sem=self.sems[turn][0].at[half, k],
            recv_sem=self.sems[turn][1].at[half, k],
            device_id=address(to),
            device_id_type=MESH,
        )

    def begin(self):
        for half in range(2):
            for k in (1, 3, 2):
                self.copy(0, half, k).start()

    def pass_on(self):
        for half in range(2):
            total = self.lines[self.row(half, self.me["xy"[half]])].astype(F32)
            for k in (1, 3, 2):
                self.copy(0, half, k).wait_recv()
                total = total + self.got[half, k].astype(F32)
            self.sums[half] = total.astype(BF16)
            for k in (1, 3, 2):
                self.copy(1, half, k).start()

    def total(self, half):
        total = self.sums[half, self.me["yx"[half]]].astype(F32)
        for k in (1, 3, 2):
            self.copy(1, half, k).wait_recv()
            total = total + self.got_last[half, k].astype(F32)
        return total

    def drain(self):
        for turn in range(2):
            for half in range(2):
                for k in (1, 3, 2):
                    self.copy(turn, half, k).wait_send()


def start_kernel(
    sent_a,
    sent_b,
    tokens,
    output_rows,
    down_rows,
    frequency,
    q_mine,
    kv_mine,
    all_tokens,
    down_low,
    output_wide,
    gateup_low,
    extra_out,
    gains_out,
    qkv_part,
    projected,
    cosine,
    sine,
    head_gains,
    shares_a,
    shares_b,
    wide,
    blocks,
    queries,
    keyvals,
    a_send,
    a_recv,
    b_send,
    b_recv,
    w_send,
    w_recv,
    row_send,
    row_recv,
    near_send,
    near_recv,
    far_send,
    far_recv,
    q_send,
    q_recv,
    kv_send,
    kv_recv,
    relay_send,
    relay_recv,
    swap_sems,
    own_sems,
):
    me = where_am_i()
    x, y = me["x"], me["y"]
    rank, here = flat_index(me, COLUMN), flat_index(me, SURFACE)
    gathers = ColumnGathers(me, blocks, near_send, near_recv, far_send, far_recv)
    to_a = Exchange(
        me,
        COLUMN,
        lambda to: sent_a.at[flat_index(to, COLUMN)],
        lambda frm: shares_a.at[flat_index(frm, COLUMN)],
        a_send,
        a_recv,
    )
    to_b = Exchange(
        me,
        COLUMN,
        lambda to: sent_b.at[flat_index(to, COLUMN)],
        lambda frm: shares_b.at[flat_index(frm, COLUMN)],
        b_send,
        b_recv,
    )
    spread = PlaneGathers(
        me,
        (
            (
                lambda half, x, y: wide.at[half, x, y],
                lambda half, at: wide.at[0, :, at] if half == 0 else wide.at[1, at],
            ),
            (
                lambda half, x, y: output_wide.at[y, x, :, pl.ds(half * 512, 512)],
                lambda half, at: (
                    output_wide.at[at, :, :, pl.ds(0, 512)]
                    if half == 0
                    else output_wide.at[:, at, :, pl.ds(512, 512)]
                ),
            ),
        ),
        w_send,
        w_recv,
        row_send,
        row_recv,
    )
    output_swap = Swap(
        me, output_rows, output_wide.at[y, quarter(me)], output_wide.at[y, x], swap_sems.at[0]
    )
    down_swap = Swap(me, down_rows, down_low, down_low, swap_sems.at[1])
    own_a = pltpu.make_async_copy(sent_a.at[rank], shares_a.at[rank], own_sems.at[0])
    own_b = pltpu.make_async_copy(sent_b.at[rank], shares_b.at[rank], own_sems.at[1])
    own_a.start()
    own_b.start()
    greet_all(me, "all", "swap")
    to_a.begin()
    output_swap.begin()
    gathers.begin(0, tokens[...])
    down_swap.begin()
    to_b.begin()

    own_a.wait()
    to_a.arrive()
    wide[:, x, y] = shares_a[...].astype(BF16).reshape(2, 32, 640)
    spread.begin(0)
    output_swap.finish()
    extra_out[...] = shares_a[:, :, 512:]

    lanes = lax.broadcasted_iota(jnp.int32, (BLOCK, HD), 1)
    place = lax.broadcasted_iota(jnp.int32, (BLOCK, HD), 0).astype(F32)

    def tables(j, carry):
        for half in range(2):
            first = shares_a[j, 2 + half : 3 + half, 512:]
            angles = (first * float(BLOCK) + place) * frequency[...]
            at = pl.ds(pl.multiple_of(j * ROWS + half * BLOCK, BLOCK), BLOCK)
            cosine[at, :] = jnp.cos(angles)
            sines = jnp.sin(angles)
            sine[at, :] = jnp.where(lanes < HD // 2, -sines, sines)
        return carry

    lax.fori_loop(0, RANKS, tables, 0)
    spread.pass_on(0)
    spread.begin(1)
    own_b.wait()
    to_b.arrive()
    gateup_low[...] = shares_b[...].astype(BF16).reshape(2, 32, 768)

    spread.arrive(0)
    qkv_part[...] = wide[..., :512].reshape(D, 512)
    extra = wide[..., 512:].reshape(D, HD)
    gains_out[...] = extra
    entry = 2 * D + lax.broadcasted_iota(jnp.int32, (HD, 2 * HD), 1)
    pick = (lax.broadcasted_iota(jnp.int32, (HD, 2 * HD), 0) == lax.rem(entry, 18)).astype(BF16)
    entries = 2 * D + lax.broadcasted_iota(jnp.int32, (D, 2 * HD), 1)
    owned = lax.broadcasted_iota(jnp.int32, (D, 2 * HD), 0) == 8 * lax.div(entries, 18)
    gains = jnp.sum(jnp.where(owned, dot_nn(extra, pick), 0.0), axis=0, keepdims=True)
    head_gains[0:1, :] = gains[:, :HD]
    head_gains[1:2, :] = gains[:, HD:]

    def q_copy(row_zh, pack):
        return pltpu.make_async_remote_copy(
            src_ref=queries.at[row_zh, pack],
            dst_ref=q_mine.at[x, row_zh],
            send_sem=q_send.at[row_zh, pack],
            recv_sem=q_recv.at[row_zh, x],
            device_id=address(dict(me, x=pack)),
            device_id_type=MESH,
        )

    def kv_copy(row_zh, pack):
        return pltpu.make_async_remote_copy(
            src_ref=keyvals.at[row_zh, pack],
            dst_ref=kv_mine.at[here, row_zh],
            send_sem=kv_send.at[row_zh, pack],
            recv_sem=kv_recv.at[row_zh, x],
            device_id=address(dict(me, x=pack)),
            device_id_type=MESH,
        )

    def q_own(row_zh):
        return pltpu.make_async_copy(
            queries.at[row_zh, x], q_mine.at[x, row_zh], own_sems.at[2 + row_zh]
        )

    def kv_own(row_zh):
        return pltpu.make_async_copy(
            keyvals.at[row_zh, x], kv_mine.at[here, row_zh], own_sems.at[4 + row_zh]
        )

    def relay(row_zh, from_x, which, arriving):
        step = 1 if which in (1, 2) else 3
        back = (step if which in (1, 3) else 2 * step) if arriving else (0 if which in (1, 3) else step)
        block = kv_mine.at[from_x * 4 + lax.rem(y + 8 - back, 4), row_zh]
        if which == 2:
            block = block.at[pl.ds(0, BLOCK)]
        if which == 0:
            block = block.at[pl.ds(BLOCK, BLOCK)]
        return pltpu.make_async_remote_copy(
            src_ref=block,
            dst_ref=block,
            send_sem=relay_send.at[row_zh, from_x, which],
            recv_sem=relay_recv.at[row_zh, from_x, which],
            device_id=address(dict(me, y=lax.rem(y + step, 4))),
            device_id_type=MESH,
        )

    def project(i, carry):
        off, at_z = gathers.await_chip(0, i)
        at = pl.ds(pl.multiple_of(at_z * 2 * ROWS, 2 * ROWS), 2 * ROWS)
        both = dot_nn(blocks[0, pl.ds(at_z * 2, 2)].reshape(2 * ROWS, D), qkv_part[...])
        projected[at, :] = both[:, :384]
        row_zh, first = lax.div(at_z, 2), lax.rem(at_z, 2) * 2
        for head in range(3):
            values = both[:, head * HD : (head + 1) * HD]
            gain = head_gains[1:2, :] if head == 2 else head_gains[0:1, :]
            normed = values * norm_factor(values) * gain
            turned = (
                normed * cosine[at, :] + pltpu.roll(normed, HD // 2, 1) * sine[at, :]
            ).astype(BF16)
            turned = turned.reshape(2, ROWS, HD)
            for at_core in range(2):
                if head == 2:
                    keyvals[row_zh, first + at_core, :, :HD] = turned[at_core]
                else:
                    queries[row_zh, first + at_core, :, head * HD : (head + 1) * HD] = turned[
                        at_core
                    ]
        values = both[:, 384:].astype(BF16).reshape(2, ROWS, HD)
        for at_core in range(2):
            pack = first + at_core
            keyvals[row_zh, pack, :, HD:] = values[at_core]

            @pl.when(pack != x)
            def _():
                kv_copy(row_zh, pack).start()
                q_copy(row_zh, pack).start()

            @pl.when(pack == x)
            def _():
                kv_own(row_zh).start()
                q_own(row_zh).start()

        return carry

    gathers.pass_on(0)
    lax.fori_loop(0, 4, project, 0)
    spread.pass_on(1)
    for i in range(RANKS):
        slot = pltpu.make_async_copy(blocks.at[0, i], all_tokens.at[i], own_sems.at[6 + i])
        slot.start()
    for row_zh in range(2):
        kv_own(row_zh).wait()
        for which in (1, 3):
            relay(row_zh, x, which, False).start()
    for off in (1, 3, 2):
        from_x = lax.rem(x + 4 - off, 4)
        to_x = lax.rem(x + off, 4)
        for row_zh in range(2):
            pltpu.make_async_remote_copy(
                src_ref=keyvals.at[row_zh, to_x],
                dst_ref=kv_mine.at[from_x * 4 + y, row_zh],
                send_sem=kv_send.at[row_zh, to_x],
                recv_sem=kv_recv.at[row_zh, from_x],
                device_id=address(dict(me, x=to_x)),
                device_id_type=MESH,
            ).wait_recv()
            for which in (1, 3):
                relay(row_zh, from_x, which, False).start()

    def forward(j, carry):
        off, row_zh = lax.div(j, 2), lax.rem(j, 2)
        from_x = lax.rem(x + 4 - gray(off), 4)
        for which, by_way in ((1, 2), (3, 0)):
            relay(row_zh, from_x, which, True).wait_recv()
            relay(row_zh, from_x, by_way, False).start()
        return carry

    lax.fori_loop(0, 8, forward, 0)
    for off in (1, 3, 2):
        from_x = lax.rem(x + 4 - off, 4)
        to_x = lax.rem(x + off, 4)
        for row_zh in range(2):
            pltpu.make_async_remote_copy(
                src_ref=queries.at[row_zh, to_x],
                dst_ref=q_mine.at[from_x, row_zh],
                send_sem=q_send.at[row_zh, to_x],
                recv_sem=q_recv.at[row_zh, from_x],
                device_id=address(dict(me, x=to_x)),
                device_id_type=MESH,
            ).wait()
            kv_copy(row_zh, to_x).wait_send()
    for row_zh in range(2):
        q_own(row_zh).wait()

    def finish(j, carry):
        row_zh, from_x = lax.div(j, 4), lax.rem(j, 4)
        for which in range(4):
            relay(row_zh, from_x, which, False).wait_send()
        for which in (2, 0):
            relay(row_zh, from_x, which, True).wait_recv()
        return carry

    lax.fori_loop(0, 8, finish, 0)
    spread.arrive(1)
    down_swap.finish()
    for i in range(RANKS):
        pltpu.make_async_copy(blocks.at[0, i], all_tokens.at[i], own_sems.at[6 + i]).wait()
    for exchange in (to_a, to_b, spread):
        exchange.drain()
    gathers.drain(0)


def start(number, sent_a, sent_b, tokens, output_rows, down_rows, frequency):
    anywhere = pl.BlockSpec(memory_space=pl.ANY)
    vmem = pl.BlockSpec(memory_space=pltpu.VMEM)
    dma = pltpu.SemaphoreType.DMA
    struct = jax.ShapeDtypeStruct
    return pl.pallas_call(
        start_kernel,
        out_shape=(
            struct((4, 2, ROWS, 256), BF16),
            struct((PLANE, 2, ROWS, 256), BF16),
            struct((RANKS, ROWS, D), BF16),
            struct((48, 512), BF16),
            struct((4, 4, 16, D), BF16),
            struct((2, 32, 768), BF16),
            struct((RANKS, 8, HD), F32),
            struct((D, HD), BF16),
            struct((D, 512), BF16),
            struct((RANKS * ROWS, 384), F32),
            struct((RANKS * ROWS, HD), F32),
            struct((RANKS * ROWS, HD), F32),
            struct((2, HD), F32),
        ),
        in_specs=[anywhere, anywhere, vmem, anywhere, anywhere, vmem],
        out_specs=(anywhere,) * 4 + (vmem,) * 9,
        scratch_shapes=[
            pltpu.VMEM((RANKS, 8, 640), F32),
            pltpu.VMEM((RANKS, 8, 768), F32),
            pltpu.VMEM((2, 4, 4, 32, 640), BF16),
            pltpu.VMEM((1, RANKS, ROWS, D), BF16),
            pltpu.VMEM((2, 4, ROWS, 256), BF16),
            pltpu.VMEM((2, 4, ROWS, 256), BF16),
        ]
        + [dma((RANKS,))] * 4
        + [dma((2, 2, 4))] * 4
        + [dma((1, 4))] * 4
        + [dma((2, 4))] * 4
        + [dma((2, 4, 4)), dma((2, 4, 4)), dma((2, 2)), dma((6 + RANKS,))],
        compiler_params=pltpu.CompilerParams(
            collective_id=number, has_side_effects=True, vmem_limit_bytes=VMEM_LIMIT
        ),
        name="start",
    )(sent_a, sent_b, tokens, output_rows, down_rows, frequency)


def middle_kernel(
    out_mine,
    wo,
    gateup_low,
    down_rows,
    inputs,
    upstream,
    gains,
    result,
    grad_hidden,
    gains_grad,
    grad_mine,
    gateup_sum,
    down_parts,
    output_lines,
    attended,
    blocks,
    part,
    paired,
    sending,
    landed,
    gate_up,
    activated,
    grad_gate,
    grad_attended,
    gateup_lines,
    down_grad,
    down_lines,
    branch,
    hidden,
    wgu,
    wd,
    down_wide,
    got,
    plane_sums,
    got_last,
    near_send,
    near_recv,
    far_send,
    far_recv,
    gnear_send,
    gnear_recv,
    gfar_send,
    gfar_recv,
    att_send,
    att_recv,
    back_send,
    back_recv,
    plane_send,
    plane_recv,
    last_send,
    last_recv,
    w_send,
    w_recv,
    row_send,
    row_recv,
    down_send,
    down_recv,
    own_sems,
):
    me = where_am_i()
    x, here = me["x"], flat_index(me, SURFACE)
    z = me["zh"] * 2 + me["zl"]
    sums = ColumnSums(
        me, part, paired, sending, landed, near_send, near_recv, far_send, far_recv
    )
    gathers = ColumnGathers(me, blocks, gnear_send, gnear_recv, gfar_send, gfar_recv)
    own_wgu = pltpu.make_async_copy(gateup_low, wgu.at[:, x, me["y"]], own_sems.at[0])
    own_wgu.start()
    own_down = pltpu.make_async_copy(down_rows, down_wide.at[me["y"], x], own_sems.at[1])
    own_down.start()
    spread = PlaneGathers(
        me,
        (
            (
                lambda half, x, y: wgu.at[half, x, y],
                lambda half, at: wgu.at[0, :, at] if half == 0 else wgu.at[1, at],
            ),
            (
                lambda half, x, y: down_wide.at[y, x, :, pl.ds(half * 256, 256)],
                lambda half, at: (
                    down_wide.at[at, :, :, pl.ds(0, 256)]
                    if half == 0
                    else down_wide.at[:, at, :, pl.ds(256, 256)]
                ),
            ),
        ),
        w_send,
        w_recv,
        row_send,
        row_recv,
    )
    rows_back = RowCopies(me, down_lines, down_parts, down_send, down_recv, True)
    gateup_back = PlaneSums(
        me, gateup_lines, got, plane_sums, got_last, plane_send, plane_recv, last_send, last_recv
    )

    def half_rows(half):
        return pl.ds(half * BLOCK, BLOCK)

    def own_out(half):
        return pltpu.make_async_copy(
            out_mine.at[x, :, half_rows(half)], attended.at[half, :, x], own_sems.at[2 + half]
        )

    def attention_out(half, k, arriving):
        frm = shifted(me, ("x",), k, -1) if arriving else me
        to = shifted(me, ("x",), k, 1)
        return pltpu.make_async_remote_copy(
            src_ref=out_mine.at[to["x"], :, half_rows(half)],
            dst_ref=attended.at[half, :, frm["x"]],
            send_sem=att_send.at[half, k],
            recv_sem=att_recv.at[half, k],
            device_id=address(to),
            device_id_type=MESH,
        )

    for half in range(2):
        own_out(half).start()
    greet_all(me, "some", "own")
    for half in range(2):
        for k in (2, 1, 3):
            attention_out(half, k, False).start()
    own_wgu.wait()
    own_down.wait()
    spread.begin(0)
    spread.begin(1)

    def down_line_in(j, carry):
        at = pl.ds(pl.multiple_of(j * 48, 16), 48)
        pair = down_wide[lax.div(j, 2), pl.ds(lax.rem(j, 2) * 2, 2)].astype(F32)
        for side in range(2):
            rows = pair[:, side * 24 : side * 24 + 24].reshape(48, 512)
            wd[at, side * 512 : side * 512 + 512] = rows.astype(BF16)
        return carry

    def project_out(half):
        own_out(half).wait()
        for k in (1, 3, 2):
            attention_out(half, k, True).wait_recv()

        rows = attended[half].reshape(RANKS * BLOCK, 256)
        sums.put_all(half, dot_nn(rows, wo[...]))

    def block_rows(phase):
        return blocks[phase].reshape(RANKS * BLOCK, D)

    def at_half(half):
        return slice(half * RANKS * BLOCK, (half + 1) * RANKS * BLOCK)

    def attention_norm(half):
        at = half_rows(half)
        total = sums.total(half)
        branch[at, :] = total
        both = inputs[at, :].astype(F32) + total * norm_factor(total) * gains[0:1, :]
        hidden[at, :] = both
        gathers.begin(half, both.astype(BF16))

    def feed_forward(half):
        at = at_half(half)
        both = dot_nn(block_rows(half), wgu[...].reshape(D, 768))
        gate_up[at, :] = both
        gate, up = both[:, :384], both[:, 384:]
        acts = (gate * (1.0 / (1.0 + jnp.exp(-gate))) * up).astype(BF16)
        activated[at, :] = acts
        sums.put_all(2 + half, dot_nn(acts, wd[...]))

    def feed_forward_norm(half):
        at = half_rows(half)
        ffn_out = sums.total(2 + half)
        gain = gains[1:2, :]
        result[at, :] = (hidden[at, :] + ffn_out * norm_factor(ffn_out) * gain).astype(BF16)
        grad_ffn, grad_gain = norm_back(ffn_out, gain, upstream[at, :].astype(F32))
        gathers.begin(2 + half, grad_ffn.astype(BF16))
        return grad_gain

    def feed_forward_back(half):
        at = at_half(half)
        grad_act = dot_nt(block_rows(2 + half), wd[...])
        gate, up = gate_up[at, :384], gate_up[at, 384:]
        sig = 1.0 / (1.0 + jnp.exp(-gate))
        grad_gate[at, :384] = (grad_act * up * (sig * (1.0 + gate * (1.0 - sig)))).astype(BF16)
        grad_gate[at, 384:] = (grad_act * (gate * sig)).astype(BF16)
        sums.put_all(4 + half, dot_nt(grad_gate[at, :], wgu[...].reshape(D, 768)))

    def attention_norm_back(half):
        at = half_rows(half)
        total = upstream[at, :].astype(F32) + sums.total(4 + half)
        grad_hidden[at, :] = total
        grad_branch, grad_gain = norm_back(branch[at, :], gains[0:1, :], total)
        gathers.begin(4 + half, grad_branch.astype(BF16))
        return grad_gain

    def to_attention(half, row_zh, pack):
        return pltpu.make_async_remote_copy(
            src_ref=grad_attended.at[half, row_zh, pack],
            dst_ref=grad_mine.at[x, row_zh, half_rows(half)],
            send_sem=back_send.at[half, row_zh, pack],
            recv_sem=back_recv.at[half, row_zh, x],
            device_id=address(dict(me, x=pack)),
            device_id_type=MESH,
        )

    def own_attention(half, row_zh):
        return pltpu.make_async_copy(
            grad_attended.at[half, row_zh, x],
            grad_mine.at[x, row_zh, half_rows(half)],
            own_sems.at[4 + 2 * half + row_zh],
        )

    def project_out_back(half):
        grads = dot_nt(block_rows(4 + half), wo[...]).astype(BF16)
        grad_attended[half] = grads.reshape(2, 4, BLOCK, 256)
        for row_zh in range(2):
            own_attention(half, row_zh).start()
            for k in (1, 3, 2):
                to_attention(half, row_zh, lax.rem(x + k, 4)).start()

    def all_rows(phase):
        return blocks[phase : phase + 2].reshape(RANKS * ROWS, D)

    def down_line(s, carry):
        rows = down_grad[pl.ds(pl.multiple_of(s * 24, 8), 24), :].astype(BF16)
        down_lines[s, 0:24, :] = rows[:, :512]
        down_lines[s, 24:48, :] = rows[:, 512:]
        return carry

    def send_down():
        down_grad[...] = dot_tn(activated[...], all_rows(2))
        lax.fori_loop(0, PLANE, down_line, 0)
        rows_back.begin()

    def send_gateup():
        grads = dot_tn(all_rows(0), grad_gate[...])
        gateup_lines[...] = grads.astype(BF16).reshape(2, 4, 4, 32, 768)
        gateup_back.begin()

    works = (project_out, feed_forward, feed_forward_back, project_out_back)
    thens = (attention_norm, feed_forward_norm, attention_norm_back)
    gain_grads = [None, None, None]
    works[0](0)
    sums.first(0)
    works[0](1)
    spread.pass_on(0)
    spread.pass_on(1)
    sums.second(0)
    for stage in range(3):
        phase = 2 * stage
        if stage == 2:
            send_down()
        gain_grads[stage] = thens[stage](0)
        if stage > 0:
            works[stage](1)
        sums.first(phase + 1)
        gathers.pass_on(phase)
        sums.second(phase + 1)
        if stage == 2:
            send_gateup()
        gathers.await_all(phase)
        if stage == 0:
            spread.arrive(0)
            spread.arrive(1)
            lax.fori_loop(0, PLANE // 2, down_line_in, 0)
        works[stage + 1](0)
        other = thens[stage](1)
        if stage > 0:
            gains_grad[2 - stage : 3 - stage, :] = gain_grads[stage] + other
        if stage < 2:
            sums.first(phase + 2)
        gathers.pass_on(phase + 1)
        if stage < 2:
            sums.second(phase + 2)
        gathers.await_all(phase + 1)
    works[3](1)
    gateup_back.pass_on()
    grads = dot_tn(attended[...].reshape(RANKS * ROWS, 256), all_rows(4))
    output_lines[...] = grads.astype(BF16).reshape(PLANE, 16, D)

    for half in range(2):
        for k in (1, 3, 2):
            attention_out(half, k, False).wait_send()
            frm_x = lax.rem(x + 4 - k, 4)
            to_x = lax.rem(x + k, 4)
            for row_zh in range(2):
                to_attention(half, row_zh, to_x).wait_send()
                pltpu.make_async_remote_copy(
                    src_ref=grad_attended.at[half, row_zh, to_x],
                    dst_ref=grad_mine.at[frm_x, row_zh, half_rows(half)],
                    send_sem=back_send.at[half, row_zh, to_x],
                    recv_sem=back_recv.at[half, row_zh, frm_x],
                    device_id=address(dict(me, x=to_x)),
                    device_id_type=MESH,
                ).wait_recv()
        for row_zh in range(2):
            own_attention(half, row_zh).wait()
    for phase in range(6):
        sums.drain(phase)
        gathers.drain(phase)
    for half in range(2):
        gateup_sum[half] = gateup_back.total(half)
    rows_back.arrive()
    for exchange in (spread, gateup_back, rows_back):
        exchange.drain()


def middle(number, out_mine, wo, gateup_low, down_rows, inputs, upstream, gains):
    anywhere = pl.BlockSpec(memory_space=pl.ANY)
    vmem = pl.BlockSpec(memory_space=pltpu.VMEM)
    block, half = (ROWS, D), (BLOCK, D)
    dma = pltpu.SemaphoreType.DMA
    return pl.pallas_call(
        middle_kernel,
        out_shape=(
            jax.ShapeDtypeStruct(block, BF16),
            jax.ShapeDtypeStruct(block, F32),
            jax.ShapeDtypeStruct((2, D), F32),
            jax.ShapeDtypeStruct((4, 2, ROWS, 256), BF16),
            jax.ShapeDtypeStruct((2, 32, 768), F32),
            jax.ShapeDtypeStruct((PLANE, 48, 512), BF16),
            jax.ShapeDtypeStruct((PLANE, 16, D), BF16),
        ),
        in_specs=[anywhere, vmem, anywhere, anywhere, vmem, vmem, vmem],
        out_specs=(vmem, vmem, vmem, anywhere, vmem, anywhere, vmem),
        scratch_shapes=[
            pltpu.VMEM((2, 2, 4, BLOCK, 256), BF16),
            pltpu.VMEM((6, RANKS) + half, BF16),
            pltpu.VMEM((6, 4, 2) + half, BF16),
            pltpu.VMEM((6, 4) + half, BF16),
            pltpu.VMEM((6, 4) + half, BF16),
            pltpu.VMEM((6, 4) + half, BF16),
            pltpu.VMEM((RANKS * ROWS, 768), F32),
            pltpu.VMEM((RANKS * ROWS, 384), BF16),
            pltpu.VMEM((RANKS * ROWS, 768), BF16),
            pltpu.VMEM((2, 2, 4, BLOCK, 256), BF16),
            pltpu.VMEM((2, 4, 4, 32, 768), BF16),
            pltpu.VMEM((384, D), F32),
            pltpu.VMEM((PLANE, 48, 512), BF16),
            pltpu.VMEM(block, F32),
            pltpu.VMEM(block, F32),
            pltpu.VMEM((2, 4, 4, 32, 768), BF16),
            pltpu.VMEM((384, D), BF16),
            pltpu.VMEM((4, 4, 48, 512), BF16),
            pltpu.VMEM((2, 4, 4, 32, 768), BF16),
            pltpu.VMEM((2, 4, 32, 768), BF16),
            pltpu.VMEM((2, 4, 32, 768), BF16),
        ]
        + [dma((6, 4))] * 8
        + [dma((2, 4)), dma((2, 4)), dma((2, 2, 4)), dma((2, 2, 4))]
        + [dma((2, 4))] * 4
        + [dma((2, 2, 4))] * 4
        + [dma((PLANE,))] * 2
        + [dma((8,))],
        compiler_params=pltpu.CompilerParams(
            collective_id=number, has_side_effects=True, vmem_limit_bytes=VMEM_LIMIT
        ),
        name="middle",
    )(out_mine, wo, gateup_low, down_rows, inputs, upstream, gains)


def end_kernel(
    dq_mine,
    dkv_mine,
    projected,
    cosine,
    sine,
    head_gains,
    all_tokens,
    qkv_part,
    output_lines,
    column_b,
    grad_hidden,
    gains_grad,
    token_grad,
    summed_a,
    summed_b,
    output_parts,
    gains_sum,
    across,
    besides,
    landed_kv,
    passing,
    dq_all,
    dkv_all,
    grad_qkv,
    part,
    paired,
    sending,
    landed,
    qkv_lines,
    qkv_parts,
    column_a,
    gains_column,
    gains_plane,
    ring_send,
    ring_recv,
    kv_send,
    kv_recv,
    dq_send,
    dq_recv,
    near_send,
    near_recv,
    far_send,
    far_recv,
    plane_send,
    plane_recv,
    gplane_send,
    gplane_recv,
    row_send,
    row_recv,
    a_send,
    a_recv,
    b_send,
    b_recv,
    gcolumn_send,
    gcolumn_recv,
    own_sems,
):
    me = where_am_i()
    x, y, z = me["x"], me["y"], me["zh"] * 2 + me["zl"]
    rank, here = flat_index(me, COLUMN), flat_index(me, SURFACE)
    sums = ColumnSums(
        me, part, paired, sending, landed, near_send, near_recv, far_send, far_recv
    )

    def by_column(ref, out, send, recv):
        return Exchange(
            me,
            COLUMN,
            lambda to: ref.at[flat_index(to, COLUMN)],
            lambda frm: out.at[flat_index(frm, COLUMN)],
            send,
            recv,
        )

    to_a = by_column(column_a, summed_a, a_send, a_recv)
    to_b = by_column(column_b, summed_b, b_send, b_recv)
    gains_in = Exchange(
        me,
        COLUMN,
        lambda to: gains_column.at[rank],
        lambda frm: gains_column.at[flat_index(frm, COLUMN)],
        gcolumn_send,
        gcolumn_recv,
    )
    gains_over = Exchange(
        me,
        SURFACE,
        lambda to: gains_plane.at[here],
        lambda frm: gains_plane.at[flat_index(frm, SURFACE)],
        gplane_send,
        gplane_recv,
    )
    plane = Exchange(
        me,
        SURFACE,
        lambda to: qkv_lines.at[:, flat_index(to, SURFACE)],
        lambda frm: qkv_parts.at[flat_index(frm, SURFACE)],
        plane_send,
        plane_recv,
    )
    queries = Exchange(
        me,
        ("x",),
        lambda to: dq_mine.at[to["x"]],
        lambda frm: dq_all.at[:, frm["x"]],
        dq_send,
        dq_recv,
    )
    rows = RowCopies(me, output_lines, output_parts, row_send, row_recv, True)
    own_dq = pltpu.make_async_copy(dq_mine.at[x], dq_all.at[:, x], own_sems.at[4])
    own_plane = pltpu.make_async_copy(qkv_lines.at[:, here], qkv_parts.at[here], own_sems.at[5])
    own_a = pltpu.make_async_copy(column_a.at[rank], summed_a.at[rank], own_sems.at[6])
    own_b = pltpu.make_async_copy(column_b.at[rank], summed_b.at[rank], own_sems.at[7])

    def ring(j, which):
        to_x = lax.rem(x + j, 4)
        step = 1 if which in (1, 2) else 3
        if which in (1, 3):
            src, dst = besides.at[j, which // 2], landed_kv.at[j, which // 2]
        else:
            row_zh = 0 if which == 2 else 1
            src, dst = dkv_mine.at[to_x * 4 + lax.rem(y + 2, 4), row_zh], across.at[j, row_zh]
        return pltpu.make_async_remote_copy(
            src_ref=src,
            dst_ref=dst,
            send_sem=ring_send.at[j, which],
            recv_sem=ring_recv.at[j, which],
            device_id=address(dict(me, y=lax.rem(y + step, 4))),
            device_id_type=MESH,
        )

    def kv_copy(j, arriving):
        frm_x = lax.rem(x + 4 - j, 4) if arriving else x
        return pltpu.make_async_remote_copy(
            src_ref=passing.at[j],
            dst_ref=dkv_all.at[:, frm_x],
            send_sem=kv_send.at[j],
            recv_sem=kv_recv.at[j],
            device_id=address(dict(me, x=lax.rem(x + j, 4))),
            device_id_type=MESH,
        )

    own_dq.start()
    greet_all(me, "all", "own")
    for j in (2, 1, 3, 0):
        for which in (2, 0):
            ring(j, which).start()
    queries.begin()
    for j in (2, 1, 3, 0):
        to_x = lax.rem(x + j, 4)
        for which, by_way, step in ((1, 2, 1), (3, 0, 3)):
            row_zh, other = (0, 1) if by_way == 2 else (1, 0)
            own_block = to_x * 4 + lax.rem(y + step, 4)
            besides[j, which // 2, other] = dkv_mine[own_block, other]
            ring(j, by_way).wait_recv()
            both = dkv_mine[own_block, row_zh].astype(F32) + across[j, row_zh].astype(F32)
            besides[j, which // 2, row_zh] = both.astype(BF16)
            ring(j, which).start()

    own_b.start()
    to_b.begin()

    for j in (2, 1, 3, 0):
        total = dkv_mine[lax.rem(x + j, 4) * 4 + y].astype(F32)
        for which in (1, 3):
            ring(j, which).wait_recv()
            total = total + landed_kv[j, which // 2].astype(F32)
        if j:
            passing[j] = total.astype(BF16)
            kv_copy(j, False).start()
        else:
            dkv_all[:, x] = total.astype(BF16)
    rows.begin()
    own_dq.wait()
    queries.arrive()
    for j in (2, 1, 3):
        kv_copy(j, True).wait_recv()

    def project_back(i, carry):
        gain_q, gain_k = carry
        off = gray(3 - i)
        to_z = lax.rem(z + off, 4)
        at = pl.ds(pl.multiple_of(to_z * 2 * ROWS, 2 * ROWS), 2 * ROWS)
        row_zh, first = lax.div(to_z, 2), lax.rem(to_z, 2) * 2
        grad_q = dq_all[row_zh, pl.ds(first, 2)].reshape(2 * ROWS, 256).astype(F32)
        grad_kv = dkv_all[row_zh, pl.ds(first, 2)].reshape(2 * ROWS, 256)
        for head in range(3):
            if head == 2:
                grad, gain = grad_kv[:, :HD].astype(F32), head_gains[1:2, :]
            else:
                grad, gain = grad_q[:, head * HD : (head + 1) * HD], head_gains[0:1, :]
            turned = grad * cosine[at, :] - pltpu.roll(grad, HD // 2, 1) * sine[at, :]
            grad_in, grad_gain = norm_back(
                projected[at, head * HD : (head + 1) * HD], gain, turned
            )
            grad_qkv[at, head * HD : (head + 1) * HD] = grad_in.astype(BF16)
            if head == 2:
                gain_k = gain_k + grad_gain
            else:
                gain_q = gain_q + grad_gain
        grad_qkv[at, 384:] = grad_kv[:, HD:]
        sums.put(0, off, dot_nt(grad_qkv[at, :], qkv_part[...]))

        @pl.when(i == 1)
        def _():
            sums.first(0)

        return gain_q, gain_k

    nothing = jnp.zeros((1, HD), F32)
    gain_q, gain_k = lax.fori_loop(0, 4, project_back, (nothing, nothing))

    for j in range(16):
        gains_column[rank, j : j + 1, :] = gains_grad[
            j // 8 : j // 8 + 1, j % 8 * HD : (j % 8 + 1) * HD
        ]
    gains_column[rank, 16:17, :] = gain_q
    gains_column[rank, 17:18, :] = gain_k
    gains_column[rank, 18:24, :] = jnp.zeros((6, HD), F32)
    gains_in.begin()
    sums.second(0)

    def qkv_rows(j, carry):
        cols = pl.ds(pl.multiple_of(j * 256, 256), 256)
        grads = dot_tn(all_tokens[:, :, cols].reshape(RANKS * ROWS, 256), grad_qkv[...])
        qkv_lines[lax.div(j, 2), pl.ds(lax.rem(j, 2) * 8, 8)] = grads.astype(BF16).reshape(
            8, 32, 512
        )
        return carry

    lax.fori_loop(0, 4, qkv_rows, 0)
    own_plane.start()
    plane.begin()

    gains_in.arrive()
    gains_plane[here] = jnp.sum(gains_column[...], axis=0)
    gains_over.begin()
    token_grad[...] = grad_hidden[...] + sums.total(0)

    own_plane.wait()
    plane.arrive()
    for row_zh in range(2):

        def add_qkv(s, total):
            return total + qkv_parts[s, row_zh].astype(F32)

        total = lax.fori_loop(0, PLANE, add_qkv, jnp.zeros((32, 512), F32))
        column_a[pl.ds(row_zh * 4, 4)] = total.reshape(4, 8, 512)
    own_a.start()
    to_a.begin()
    gains_over.arrive()
    gains_sum[...] = jnp.sum(gains_plane[...], axis=0)
    to_b.arrive()
    rows.arrive()
    own_b.wait()
    for j in (2, 1, 3, 0):
        for which in range(4):
            ring(j, which).wait_send()
        if j:
            kv_copy(j, False).wait_send()
    sums.drain(0)
    for exchange in (queries, rows, to_b, gains_in, gains_over, plane):
        exchange.drain()
    own_a.wait()
    to_a.arrive()
    to_a.drain()


def end(number, *arrays):
    anywhere = pl.BlockSpec(memory_space=pl.ANY)
    vmem = pl.BlockSpec(memory_space=pltpu.VMEM)
    dma = pltpu.SemaphoreType.DMA
    struct = jax.ShapeDtypeStruct
    block = (ROWS, D)
    quarter_rows = (2, ROWS, 256)
    return pl.pallas_call(
        end_kernel,
        out_shape=(
            struct(block, F32),
            struct((RANKS, 8, 512), F32),
            struct((RANKS, 8, 768), F32),
            struct((PLANE, 16, D), BF16),
            struct((24, HD), F32),
        ),
        in_specs=[anywhere, vmem] + [vmem] * 6 + [anywhere, anywhere] + [vmem] * 2,
        out_specs=(vmem, anywhere, anywhere, anywhere, vmem),
        scratch_shapes=[
            pltpu.VMEM((4,) + quarter_rows, BF16),
            pltpu.VMEM((4, 2) + quarter_rows, BF16),
            pltpu.VMEM((4, 2) + quarter_rows, BF16),
            pltpu.VMEM((4,) + quarter_rows, BF16),
            pltpu.VMEM((2, 4, ROWS, 256), BF16),
            pltpu.VMEM((2, 4, ROWS, 256), BF16),
            pltpu.VMEM((RANKS * ROWS, 512), BF16),
            pltpu.VMEM((1, 4, 2) + block, BF16),
            pltpu.VMEM((1, 4) + block, BF16),
            pltpu.VMEM((1, 4) + block, BF16),
            pltpu.VMEM((1, 4) + block, BF16),
            pltpu.VMEM((2, PLANE, 32, 512), BF16),
            pltpu.VMEM((PLANE, 2, 32, 512), BF16),
            pltpu.VMEM((RANKS, 8, 512), F32),
            pltpu.VMEM((RANKS, 24, HD), F32),
            pltpu.VMEM((PLANE, 24, HD), F32),
        ]
        + [dma((4, 4))] * 2
        + [dma((4,))] * 4
        + [dma((1, 4))] * 4
        + [dma((PLANE,))] * 6
        + [dma((RANKS,))] * 6
        + [dma((8,))],
        compiler_params=pltpu.CompilerParams(
            collective_id=number, has_side_effects=True, vmem_limit_bytes=VMEM_LIMIT
        ),
        name="end",
    )(*arrays)


def adam_update(weight, gradient, mean_old, square_old, rate, decay):
    mean_new = BETA_ONE * mean_old + (1.0 - BETA_ONE) * gradient
    square_new = BETA_TWO * square_old + (1.0 - BETA_TWO) * gradient * gradient
    mean_hat = mean_new / (1.0 - BETA_ONE**STEP)
    square_hat = square_new / (1.0 - BETA_TWO**STEP)
    weight_new = weight - rate * (mean_hat / (jnp.sqrt(square_hat) + ADAM_EPS) + decay * weight)
    return (weight_new, mean_new, square_new)


def by_rank(array, width):
    return array.reshape(array.shape[0], RANKS, width)


def body(
    tokens,
    cotangent,
    positions,
    seq_ids,
    query_weight,
    keyval_weight,
    output_weight,
    gateup_weight,
    down_weight,
    norm_gains,
    query_mean,
    keyval_mean,
    output_mean,
    gateup_mean,
    down_mean,
    gains_mean,
    query_square,
    keyval_square,
    output_square,
    gateup_square,
    down_square,
    gains_square,
):
    inputs = tokens[0]
    at_x, at_y = lax.axis_index("x"), lax.axis_index("y")

    own_blocks = (positions[0] + LONG * seq_ids[0]).reshape(-1, BLOCK)[:, 0] // BLOCK
    own_pair = lax.dynamic_slice_in_dim(own_blocks, 2 * lax.axis_index(("zh", "x", "y")), 2)
    own_pair = jnp.where(own_pair >= LONG // BLOCK, own_pair - LONG // BLOCK, own_pair)
    extra = jnp.concatenate(
        [
            jnp.pad(norm_gains, (0, HD - norm_gains.shape[0]))[None],
            jnp.pad(own_blocks.astype(F32), (0, HD - BLOCK))[None],
            jnp.broadcast_to(own_pair.astype(F32)[:, None], (2, HD)),
            jnp.zeros((4, HD), F32),
        ]
    )
    sent_a = jnp.concatenate(
        [
            by_rank(query_weight, 256),
            by_rank(keyval_weight[:, :KV], 128),
            by_rank(keyval_weight[:, KV:], 128),
            jnp.broadcast_to(extra[:, None, :], (8, RANKS, HD)),
        ],
        axis=2,
    ).transpose(1, 0, 2)
    sent_b = jnp.concatenate(
        [by_rank(gateup_weight[:, :FF], 384), by_rank(gateup_weight[:, FF:], 384)], axis=2
    ).transpose(1, 0, 2)
    frequency = ROPE_BASE ** (-jnp.arange(HD // 2, dtype=F32) * 2.0 / HD)
    (
        q_mine,
        kv_mine,
        all_tokens,
        down_low,
        output_wide,
        gateup_low,
        extras,
        gains_low,
        qkv_part,
        projected,
        cosine,
        sine,
        head_gains,
    ) = start(
        1,
        sent_a,
        sent_b,
        inputs,
        output_weight.astype(BF16),
        jnp.concatenate([down_weight[:, :512], down_weight[:, 512:]], axis=0).astype(BF16),
        jnp.concatenate([frequency, frequency])[None],
    )
    gains_all = gains_low.reshape(-1, 8, HD)[:, 0, :18].reshape(-1).astype(F32)
    attn_gain = gains_all[:D]
    ffn_gain = gains_all[D : 2 * D]

    blocks = extras[:4, 1, :BLOCK].astype(jnp.int32).reshape(4, 2, 4, 4, 2)
    pack_blocks = lax.dynamic_index_in_dim(blocks, at_x, 0, keepdims=False)
    key_blocks = pack_blocks.transpose(1, 2, 0, 3).reshape(-1)
    query_blocks = (
        lax.dynamic_index_in_dim(pack_blocks, at_y, 2, keepdims=False).transpose(1, 0, 2).reshape(-1)
    )
    q_mine = q_mine.reshape(1024, 256)
    kv_mine = kv_mine.reshape(PACK_TOK, 256)
    out_mine, lse = attend(query_blocks, key_blocks, q_mine, kv_mine)

    def to_x(ref, to):
        return ref.at[to["x"]]

    def from_pack_x(ref, frm):
        return ref.at[:, frm["x"]]

    result, grad_hidden, gains_grad, grad_mine, gateup_sum, down_parts, output_lines = middle(
        2,
        out_mine.reshape(4, 2, ROWS, 256),
        output_wide.reshape(256, D),
        gateup_low,
        down_low,
        inputs,
        cotangent[0],
        jnp.stack([attn_gain, ffn_gain]),
    )
    dq_mine, dkv_mine = attend_back(
        query_blocks, key_blocks, q_mine, kv_mine, grad_mine.reshape(1024, 256), out_mine, lse
    )
    token_grad, summed_a, summed_b, output_parts, gains_total = end(
        3,
        dq_mine.reshape(4, 2, ROWS, 256),
        dkv_mine.reshape(PLANE, 2, ROWS, 256),
        projected,
        cosine,
        sine,
        head_gains,
        all_tokens,
        qkv_part,
        output_lines,
        gateup_sum.reshape(RANKS, 8, 768),
        grad_hidden,
        gains_grad,
    )
    gains_sum = lax.dynamic_slice_in_dim(
        gains_total.reshape(-1), lax.axis_index(AXES) * norm_gains.shape[0], norm_gains.shape[0]
    )
    output_sum = jnp.sum(output_parts.astype(F32), axis=0)
    down_sides = jnp.sum(down_parts.astype(F32), axis=0)
    down_sum = jnp.concatenate([down_sides[:24], down_sides[24:]], axis=1)
    wide_a, wide_b = summed_a.transpose(1, 0, 2), summed_b.transpose(1, 0, 2)
    query_sum = wide_a[:, :, :256].reshape(8, 2048)
    keyval_sum = jnp.concatenate(
        [wide_a[:, :, 256:384].reshape(8, KV), wide_a[:, :, 384:].reshape(8, KV)], axis=1
    )
    gateup_total = jnp.concatenate(
        [wide_b[:, :, :384].reshape(8, FF), wide_b[:, :, 384:].reshape(8, FF)], axis=1
    )

    query_new, query_mean_new, query_square_new = adam_update(
        query_weight, query_sum, query_mean, query_square, RATE_MATRIX, DECAY
    )
    keyval_new, keyval_mean_new, keyval_square_new = adam_update(
        keyval_weight, keyval_sum, keyval_mean, keyval_square, RATE_MATRIX, DECAY
    )
    output_new, output_mean_new, output_square_new = adam_update(
        output_weight, output_sum, output_mean, output_square, RATE_MATRIX, DECAY
    )
    gateup_new, gateup_mean_new, gateup_square_new = adam_update(
        gateup_weight, gateup_total, gateup_mean, gateup_square, RATE_MATRIX, DECAY
    )
    down_new, down_mean_new, down_square_new = adam_update(
        down_weight, down_sum, down_mean, down_square, RATE_MATRIX, DECAY
    )
    gains_new, gains_mean_new, gains_square_new = adam_update(
        norm_gains, gains_sum, gains_mean, gains_square, RATE_GAIN, 0.0
    )
    return (
        result[None],
        token_grad[None],
        query_sum,
        keyval_sum,
        output_sum,
        gateup_total,
        down_sum,
        gains_sum,
        query_new,
        keyval_new,
        output_new,
        gateup_new,
        down_new,
        gains_new,
        query_mean_new,
        keyval_mean_new,
        output_mean_new,
        gateup_mean_new,
        down_mean_new,
        gains_mean_new,
        query_square_new,
        keyval_square_new,
        output_square_new,
        gateup_square_new,
        down_square_new,
        gains_square_new,
    )


def solution(mesh):
    fine = Mesh(mesh.devices.reshape([SIZE[a] for a in AXES]), AXES)
    rows = P(("zl", "co"), ("zh", "x", "y"), None)
    packs = P(("zl", "co"), None)
    matrix = P(AXES, None)
    vector = P(AXES)
    params = [matrix] * 5 + [vector]
    return jax.shard_map(
        body,
        mesh=fine,
        in_specs=(rows, rows, packs, packs, *params, *params, *params),
        out_specs=(rows, rows, *params, *params, *params, *params),
        check_vma=False,
    )
```

```python
import functools
import math

import jax
import jax.numpy as jnp
from jax import lax
from jax.experimental import pallas as pl
from jax.experimental.pallas import tpu as pltpu
from jax.sharding import Mesh
from jax.sharding import PartitionSpec as P

D = 1024
H = 16
KVH = 8
HD = 128
FF = 3072
KV = 1024
STEP = 10
LONG = 3072
ROWS = 128
BLOCK = 64
CHUNK = 512
PACK_TOK = 4096
RANKS = 8
PLANE = 16


NORM_EPS = 1e-06
ROPE_BASE = 1000000.0
BETA_ONE = 0.9
BETA_TWO = 0.95
ADAM_EPS = 1e-08
DECAY = 0.1
RATE_MATRIX = 0.1
RATE_GAIN = 0.3

SCALE = HD**-0.5
LOG2E = math.log2(math.e)

AXES = ("zh", "x", "y", "zl", "co")
SIZE = {"zh": 2, "x": 4, "y": 4, "zl": 2, "co": 2}
COLUMN = ("zh", "zl", "co")
SURFACE = ("x", "y")
MESH = pl.DeviceIdType.MESH
F32 = jnp.float32
BF16 = jnp.bfloat16
VMEM_LIMIT = 50 * 1024 * 1024


def where_am_i():
    return {a: lax.axis_index(a) for a in AXES}


def address(place):
    return tuple(place[a] for a in AXES)


def flat_index(place, axes):
    at = 0
    for a in axes:
        at = at * SIZE[a] + place[a]
    return at


def shifted(place, axes, k, sign):
    to = dict(place)
    for a in reversed(axes):
        step = lax.rem(k, SIZE[a])
        k = lax.div(k, SIZE[a])
        to[a] = lax.rem(place[a] + sign * step + SIZE[a], SIZE[a])
    return to


def column_place(me, z, core):
    return dict(me, zh=lax.div(z, 2), zl=lax.rem(z, 2), co=core)


def dot_nn(a, b):
    return lax.dot_general(a, b, (((1,), (0,)), ((), ())), preferred_element_type=F32)


def dot_nt(a, b):
    return lax.dot_general(a, b, (((1,), (1,)), ((), ())), preferred_element_type=F32)


def dot_tn(a, b):
    return lax.dot_general(a, b, (((0,), (0,)), ((), ())), preferred_element_type=F32)


def stacked_heads(ref, tile):
    rows = ref[pl.ds(tile * BLOCK, BLOCK), :]
    return jnp.concatenate([rows[:, :HD], rows[:, HD:]], axis=0)


def allowed_keys(block, chunk):
    keys = chunk * CHUNK + lax.broadcasted_iota(jnp.int32, (CHUNK, 2 * BLOCK), 0)
    lanes = lax.broadcasted_iota(jnp.int32, (CHUNK, 2 * BLOCK), 1)
    return keys <= block * BLOCK + lax.rem(lanes, BLOCK)


def first_chunk(block):
    return jnp.where(block >= LONG // BLOCK, LONG // CHUNK, 0)


def attend_kernel(q_blocks, k_blocks, q_ref, kv_ref, out_ref, lse_ref, keys, values, values_t):
    def sort(i, carry):
        to = pl.multiple_of(k_blocks[i] * BLOCK, BLOCK)
        here = pl.multiple_of(i * BLOCK, BLOCK)
        keys[pl.ds(to, BLOCK), :] = kv_ref[pl.ds(here, BLOCK), :HD]
        values[pl.ds(to, BLOCK), :] = kv_ref[pl.ds(here, BLOCK), HD:]
        return carry

    lax.fori_loop(0, PACK_TOK // BLOCK, sort, 0)
    for c in range(PACK_TOK // CHUNK):
        part = values[c * CHUNK : (c + 1) * CHUNK, :].astype(F32)
        values_t[c] = part.T.astype(BF16)

    def one_tile(tile, carry):
        block = q_blocks[tile]
        query = stacked_heads(q_ref, tile)
        last = lax.div(block, CHUNK // BLOCK)

        def one_chunk(c, state, masked):
            total, mixed = state
            chunk_keys = keys[pl.ds(pl.multiple_of(c * CHUNK, CHUNK), CHUNK), :]
            weights = jnp.exp2(dot_nt(chunk_keys, query) * (SCALE * LOG2E))
            if masked:
                weights = jnp.where(allowed_keys(block, c), weights, 0.0)
            total = total + jnp.sum(weights, axis=0, keepdims=True)
            mixed = mixed + dot_nn(values_t[c], weights.astype(BF16))
            return total, mixed

        def two_chunks(j, state):
            c = first + 2 * j
            return one_chunk(c + 1, one_chunk(c, state, False), False)

        first = first_chunk(block)
        pairs = lax.div(last - first, 2)
        state = (jnp.zeros((1, 2 * BLOCK), F32), jnp.zeros((HD, 2 * BLOCK), F32))
        state = lax.fori_loop(0, pairs, two_chunks, state)
        state = lax.fori_loop(
            first + 2 * pairs, last, lambda c, s: one_chunk(c, s, False), state
        )
        total, mixed = one_chunk(last, state, True)
        result = (mixed / total).T.astype(BF16)
        rows = pl.ds(pl.multiple_of(tile * BLOCK, BLOCK), BLOCK)
        out_ref[rows, :HD] = result[:BLOCK]
        out_ref[rows, HD:] = result[BLOCK:]
        lse_ref[pl.ds(tile, 1), :] = jnp.log2(total)
        return carry

    lax.fori_loop(0, q_ref.shape[0] // BLOCK, one_tile, 0)


def attend(q_blocks, k_blocks, q, kv):
    smem = pl.BlockSpec(memory_space=pltpu.SMEM)
    vmem = pl.BlockSpec(memory_space=pltpu.VMEM)
    tiles = q.shape[0] // BLOCK
    return pl.pallas_call(
        attend_kernel,
        out_shape=(
            jax.ShapeDtypeStruct(q.shape, BF16),
            jax.ShapeDtypeStruct((tiles, 2 * BLOCK), F32),
        ),
        in_specs=[smem, smem, vmem, vmem],
        out_specs=(vmem, vmem),
        scratch_shapes=[
            pltpu.VMEM((PACK_TOK, HD), BF16),
            pltpu.VMEM((PACK_TOK, HD), BF16),
            pltpu.VMEM((PACK_TOK // CHUNK, HD, CHUNK), BF16),
        ],
        compiler_params=pltpu.CompilerParams(vmem_limit_bytes=VMEM_LIMIT),
        cost_estimate=pl.CostEstimate(
            flops=4 * 10**9, bytes_accessed=4 * 10**6, transcendentals=8 * 10**6
        ),
        name="attend",
    )(q_blocks, k_blocks, q, kv)


def attend_back_kernel(
    q_blocks,
    k_blocks,
    q_ref,
    kv_ref,
    grad_ref,
    out_ref,
    lse_ref,
    dq_ref,
    dkv_ref,
    keys,
    values,
    keys_t,
    dk,
    dv,
):
    def sort(i, carry):
        to = pl.multiple_of(k_blocks[i] * BLOCK, BLOCK)
        here = pl.multiple_of(i * BLOCK, BLOCK)
        keys[pl.ds(to, BLOCK), :] = kv_ref[pl.ds(here, BLOCK), :HD]
        values[pl.ds(to, BLOCK), :] = kv_ref[pl.ds(here, BLOCK), HD:]
        return carry

    lax.fori_loop(0, PACK_TOK // BLOCK, sort, 0)
    for c in range(PACK_TOK // CHUNK):
        part = keys[c * CHUNK : (c + 1) * CHUNK, :].astype(F32)
        keys_t[c] = part.T.astype(BF16)
    dk[...] = jnp.zeros_like(dk)
    dv[...] = jnp.zeros_like(dv)

    def one_tile(tile, carry):
        block = q_blocks[tile]
        query = stacked_heads(q_ref, tile)
        grad = stacked_heads(grad_ref, tile)
        out = stacked_heads(out_ref, tile)
        inner = jnp.sum((grad.astype(F32) * out.astype(F32)).T, axis=0, keepdims=True)
        lse = lse_ref[pl.ds(tile, 1), :]
        last = lax.div(block, CHUNK // BLOCK)

        def one_chunk(c, dq, masked):
            rows = pl.ds(pl.multiple_of(c * CHUNK, CHUNK), CHUNK)
            probs = jnp.exp2(dot_nt(keys[rows, :], query) * (SCALE * LOG2E) - lse)
            if masked:
                probs = jnp.where(allowed_keys(block, c), probs, 0.0)
            grad_probs = dot_nt(values[rows, :], grad)
            grad_scores = (probs * (grad_probs - inner)).astype(BF16)
            dv[rows, :] += dot_nn(probs.astype(BF16), grad)
            dk[rows, :] += dot_nn(grad_scores, query)
            return dq + dot_nn(keys_t[c], grad_scores)

        def two_chunks(j, dq):
            c = first + 2 * j
            return one_chunk(c + 1, one_chunk(c, dq, False), False)

        first = first_chunk(block)
        pairs = lax.div(last - first, 2)
        dq = lax.fori_loop(0, pairs, two_chunks, jnp.zeros((HD, 2 * BLOCK), F32))
        dq = lax.fori_loop(first + 2 * pairs, last, lambda c, s: one_chunk(c, s, False), dq)
        dq = (one_chunk(last, dq, True) * SCALE).T.astype(BF16)
        rows = pl.ds(pl.multiple_of(tile * BLOCK, BLOCK), BLOCK)
        dq_ref[rows, :HD] = dq[:BLOCK]
        dq_ref[rows, HD:] = dq[BLOCK:]
        return carry

    lax.fori_loop(0, q_ref.shape[0] // BLOCK, one_tile, 0)

    def unsort(i, carry):
        at = pl.multiple_of(k_blocks[i] * BLOCK, BLOCK)
        here = pl.multiple_of(i * BLOCK, BLOCK)
        dkv_ref[pl.ds(here, BLOCK), :HD] = (dk[pl.ds(at, BLOCK), :] * SCALE).astype(BF16)
        dkv_ref[pl.ds(here, BLOCK), HD:] = dv[pl.ds(at, BLOCK), :].astype(BF16)
        return carry

    lax.fori_loop(0, PACK_TOK // BLOCK, unsort, 0)


def attend_back(q_blocks, k_blocks, q, kv, grad, out, lse):
    smem = pl.BlockSpec(memory_space=pltpu.SMEM)
    vmem = pl.BlockSpec(memory_space=pltpu.VMEM)
    return pl.pallas_call(
        attend_back_kernel,
        out_shape=(
            jax.ShapeDtypeStruct(q.shape, BF16),
            jax.ShapeDtypeStruct(kv.shape, BF16),
        ),
        in_specs=[smem, smem] + [vmem] * 5,
        out_specs=(vmem, vmem),
        scratch_shapes=[
            pltpu.VMEM((PACK_TOK, HD), BF16),
            pltpu.VMEM((PACK_TOK, HD), BF16),
            pltpu.VMEM((PACK_TOK // CHUNK, HD, CHUNK), BF16),
            pltpu.VMEM((PACK_TOK, HD), F32),
            pltpu.VMEM((PACK_TOK, HD), F32),
        ],
        compiler_params=pltpu.CompilerParams(vmem_limit_bytes=VMEM_LIMIT),
        cost_estimate=pl.CostEstimate(
            flops=10**10, bytes_accessed=8 * 10**6, transcendentals=8 * 10**6
        ),
        name="attend_back",
    )(q_blocks, k_blocks, q, kv, grad, out, lse)


class ColumnSums:
    def __init__(self, me, part, paired, sending, landed, near_send, near_recv, far_send, far_recv):
        self.me, self.z, self.core = me, me["zh"] * 2 + me["zl"], me["co"]
        self.part, self.paired, self.sending, self.landed = part, paired, sending, landed
        self.near_sems, self.far_sems = (near_send, near_recv), (far_send, far_recv)
        self.rows = part.shape[-2]
        self.top, self.low = pl.ds(0, self.rows // 2), pl.ds(self.rows // 2, self.rows // 2)

    def near(self, phase, off):
        return pltpu.make_async_remote_copy(
            src_ref=self.part.at[phase, lax.rem(self.z + off, 4), 1 - self.core],
            dst_ref=self.paired.at[phase, off],
            send_sem=self.near_sems[0].at[phase, off],
            recv_sem=self.near_sems[1].at[phase, off],
            device_id=address(column_place(self.me, self.z, 1 - self.core)),
            device_id_type=MESH,
        )

    def far(self, phase, which):
        slot = which if which in (1, 3) else 2
        src, dst = self.sending.at[phase, slot], self.landed.at[phase, slot]
        if slot == 2:
            half = self.top if which == 2 else self.low
            src, dst = src.at[half], dst.at[half]
        step = 1 if which in (1, 2) else 3
        return pltpu.make_async_remote_copy(
            src_ref=src,
            dst_ref=dst,
            send_sem=self.far_sems[0].at[phase, which],
            recv_sem=self.far_sems[1].at[phase, which],
            device_id=address(column_place(self.me, lax.rem(self.z + step, 4), self.core)),
            device_id_type=MESH,
        )

    def put(self, phase, off, terms):
        self.part[phase, lax.rem(self.z + off, 4)] = terms.astype(BF16).reshape(2, self.rows, D)
        self.near(phase, off).start()

    def put_all(self, phase, terms):
        self.part[phase] = terms.astype(BF16).reshape(4, 2, self.rows, D)
        for off in (2, 1, 3, 0):
            self.near(phase, off).start()

    def chip_sum(self, phase, off):
        self.near(phase, off).wait_recv()
        mine = self.part[phase, lax.rem(self.z + off, 4), self.core].astype(F32)
        return mine + self.paired[phase, off].astype(F32)

    def first(self, phase):
        self.sending[phase, 2] = self.chip_sum(phase, 2).astype(BF16)
        self.far(phase, 2).start()
        self.far(phase, 0).start()

    def second(self, phase):
        for which, by_way, half in ((1, 2, self.top), (3, 0, self.low)):
            self.sending[phase, which] = self.chip_sum(phase, which).astype(BF16)
            self.far(phase, by_way).wait_recv()
            both = self.sending[phase, which, half].astype(F32)
            both = both + self.landed[phase, 2, half].astype(F32)
            self.sending[phase, which, half] = both.astype(BF16)
            self.far(phase, which).start()

    def total(self, phase):
        total = self.chip_sum(phase, 0)
        for which in (1, 3):
            self.far(phase, which).wait_recv()
            total = total + self.landed[phase, which].astype(F32)
        return total

    def drain(self, phase):
        for off in range(4):
            self.near(phase, off).wait_send()
            self.far(phase, off).wait_send()


class ColumnGathers:
    def __init__(self, me, blocks, near_send, near_recv, far_send, far_recv):
        self.me, self.z, self.core = me, me["zh"] * 2 + me["zl"], me["co"]
        self.blocks = blocks
        self.near_sems, self.far_sems = (near_send, near_recv), (far_send, far_recv)
        self.rows = blocks.shape[-2]

    def far(self, phase, which, arriving):
        step = 1 if which in (1, 2) else 3
        back = (step if which in (1, 3) else 2 * step) if arriving else (0 if which in (1, 3) else step)
        block = self.blocks.at[phase, lax.rem(self.z + 4 * 2 - back, 4) * 2 + self.core]
        if which == 2:
            block = block.at[pl.ds(0, self.rows // 2)]
        if which == 0:
            block = block.at[pl.ds(self.rows // 2, self.rows // 2)]
        return pltpu.make_async_remote_copy(
            src_ref=block,
            dst_ref=block,
            send_sem=self.far_sems[0].at[phase, which],
            recv_sem=self.far_sems[1].at[phase, which],
            device_id=address(column_place(self.me, lax.rem(self.z + step, 4), self.core)),
            device_id_type=MESH,
        )

    def near(self, phase, off, arriving):
        core = 1 - self.core if arriving else self.core
        block = self.blocks.at[phase, lax.rem(self.z + 4 - off, 4) * 2 + core]
        return pltpu.make_async_remote_copy(
            src_ref=block,
            dst_ref=block,
            send_sem=self.near_sems[0].at[phase, off],
            recv_sem=self.near_sems[1].at[phase, off],
            device_id=address(column_place(self.me, self.z, 1 - self.core)),
            device_id_type=MESH,
        )

    def begin(self, phase, rows):
        self.blocks[phase, self.z * 2 + self.core] = rows
        for off in (1, 3):
            self.far(phase, off, False).start()
        self.near(phase, 0, False).start()

    def pass_on(self, phase):
        for off, by_way in ((1, 2), (3, 0)):
            self.far(phase, off, True).wait_recv()
            self.far(phase, by_way, False).start()
            self.near(phase, off, False).start()

    def await_chip(self, phase, i):
        off = i + lax.div(i, 2) * (5 - 2 * i)

        @pl.when(i == 3)
        def _():
            for by_way in (2, 0):
                self.far(phase, by_way, True).wait_recv()
            self.near(phase, 2, False).start()

        self.near(phase, off, True).wait_recv()
        return off, lax.rem(self.z + 4 - off, 4)

    def await_all(self, phase):
        for by_way in (2, 0):
            self.far(phase, by_way, True).wait_recv()
        self.near(phase, 2, False).start()
        for off in range(4):
            self.near(phase, off, True).wait_recv()

    def drain(self, phase):
        for off in range(4):
            self.near(phase, off, False).wait_send()
            self.far(phase, off, False).wait_send()


def norm_factor(values):
    return lax.rsqrt(jnp.mean(values * values, axis=-1, keepdims=True) + NORM_EPS)


def norm_back(values, norm_gain, grad):
    factor = norm_factor(values)
    scaled = grad * norm_gain
    inner = jnp.mean(values * scaled, axis=-1, keepdims=True)
    grad_gain = jnp.sum(grad * values * factor, axis=0, keepdims=True)
    return factor * scaled - values * (factor * factor * factor * inner), grad_gain


def gray(i):
    return i + lax.div(i, 2) * (5 - 2 * i)


def quarter(place):
    return place["zl"] * 2 + place["co"]


def at_quarter(place, t):
    return dict(place, zl=lax.div(t, 2), co=lax.rem(t, 2))


def greet(barrier, place):
    pl.semaphore_signal(barrier, inc=1, device_id=address(place), device_id_type=MESH)


def greet_all(me, column, swap):
    barrier = pltpu.get_barrier_semaphore()

    def greet_surface(k, carry):
        greet(barrier, shifted(me, SURFACE, k, 1))
        return carry

    def greet_column_all(k, carry):
        greet(barrier, shifted(me, COLUMN, k, 1))
        return carry

    lax.fori_loop(1, PLANE, greet_surface, 0)
    expected = PLANE - 1
    if column == "all":
        lax.fori_loop(1, RANKS, greet_column_all, 0)
        expected = expected + RANKS - 1
    else:
        z = me["zh"] * 2 + me["zl"]
        for off in (1, 2, 3):
            greet(barrier, column_place(me, lax.rem(z + off, 4), me["co"]))
        greet(barrier, column_place(me, z, 1 - me["co"]))
        expected = expected + 4
    if swap:
        at_home = me["x"] == quarter(me)

        @pl.when(jnp.logical_not(at_home))
        def _():
            greet(barrier, swap_partner(me))

        expected = expected + 1 - jnp.where(at_home, 1, 0)
    pl.semaphore_wait(barrier, expected)


def swap_partner(me):
    return at_quarter(dict(me, x=quarter(me)), me["x"])


class Swap:
    def __init__(self, me, src, dst, own_dst, sems):
        self.at_home = me["x"] == quarter(me)
        self.remote = lambda: pltpu.make_async_remote_copy(
            src_ref=src,
            dst_ref=dst,
            send_sem=sems.at[0],
            recv_sem=sems.at[1],
            device_id=address(swap_partner(me)),
            device_id_type=MESH,
        )
        self.own = lambda: pltpu.make_async_copy(src, own_dst, sems.at[0])

    def either(self, remote, own):
        @pl.when(self.at_home)
        def _():
            own()

        @pl.when(jnp.logical_not(self.at_home))
        def _():
            remote()

    def begin(self):
        self.either(lambda: self.remote().start(), lambda: self.own().start())

    def finish(self):
        def both():
            copy = self.remote()
            copy.wait_recv()
            copy.wait_send()

        self.either(both, lambda: self.own().wait())


class Exchange:
    def __init__(self, me, axes, take, put, send, recv):
        self.me, self.axes, self.take, self.put, self.send, self.recv = me, axes, take, put, send, recv
        self.n = math.prod(SIZE[a] for a in axes)
        self.mix = {4: 1, 8: 3, 16: 7}[self.n]

    def copy(self, k, arriving):
        to = shifted(self.me, self.axes, k, 1)
        frm = shifted(self.me, self.axes, k, -1) if arriving else self.me
        return pltpu.make_async_remote_copy(
            src_ref=self.take(to),
            dst_ref=self.put(frm),
            send_sem=self.send.at[k],
            recv_sem=self.recv.at[k],
            device_id=address(to),
            device_id_type=MESH,
        )

    def each(self, act):
        def one(j, carry):
            act(lax.rem(j * self.mix, self.n))
            return carry

        lax.fori_loop(1, self.n, one, 0)

    def begin(self):
        self.each(lambda k: self.copy(k, False).start())

    def arrive(self):
        self.each(lambda k: self.copy(k, True).wait_recv())

    def drain(self):
        self.each(lambda k: self.copy(k, False).wait_send())


class PlaneGathers:
    def __init__(self, me, views, first_send, first_recv, second_send, second_recv):
        self.me, self.views = me, views
        self.sems = ((first_send, first_recv), (second_send, second_recv))

    def copy(self, turn, view, half, k, arriving):
        axis = "xy"[half] if turn == 0 else "yx"[half]
        to = shifted(self.me, (axis,), k, 1)
        frm = shifted(self.me, (axis,), k, -1) if arriving else self.me
        one, many = self.views[view]
        block = one(half, frm["x"], frm["y"]) if turn == 0 else many(half, frm["yx"[half]])
        return pltpu.make_async_remote_copy(
            src_ref=block,
            dst_ref=block,
            send_sem=self.sems[turn][0].at[view, half, k],
            recv_sem=self.sems[turn][1].at[view, half, k],
            device_id=address(to),
            device_id_type=MESH,
        )

    def each(self, view, act):
        for half in range(2):
            for k in (1, 3, 2):
                act(half, k)

    def begin(self, view):
        self.each(view, lambda half, k: self.copy(0, view, half, k, False).start())

    def pass_on(self, view):
        for half in range(2):
            for k in (1, 3, 2):
                self.copy(0, view, half, k, True).wait_recv()
            for k in (1, 3, 2):
                self.copy(1, view, half, k, False).start()

    def arrive(self, view):
        self.each(view, lambda half, k: self.copy(1, view, half, k, True).wait_recv())

    def drain(self):
        for view in range(len(self.views)):
            for turn in range(2):
                self.each(
                    view, lambda half, k: self.copy(turn, view, half, k, False).wait_send()
                )


class PlaneSums:
    def __init__(self, me, lines, got, middle_sums, got_last, first_send, first_recv, last_send, last_recv):
        self.me, self.lines, self.got, self.sums, self.got_last = me, lines, got, middle_sums, got_last
        self.sems = ((first_send, first_recv), (last_send, last_recv))

    def row(self, half, at):
        return (half, at) if half == 0 else (half, slice(None), at)

    def copy(self, turn, half, k):
        axis = "xy"[half] if turn == 0 else "yx"[half]
        to = shifted(self.me, (axis,), k, 1)
        if turn == 0:
            src, dst = self.lines.at[self.row(half, to[axis])], self.got.at[half, k]
        else:
            src, dst = self.sums.at[half, to[axis]], self.got_last.at[half, k]
        return pltpu.make_async_remote_copy(
            src_ref=src,
            dst_ref=dst,
            send_sem=self.sems[turn][0].at[half, k],
            recv_sem=self.sems[turn][1].at[half, k],
            device_id=address(to),
            device_id_type=MESH,
        )

    def begin(self):
        for half in range(2):
            for k in (1, 3, 2):
                self.copy(0, half, k).start()

    def pass_on(self):
        for half in range(2):
            total = self.lines[self.row(half, self.me["xy"[half]])].astype(F32)
            for k in (1, 3, 2):
                self.copy(0, half, k).wait_recv()
                total = total + self.got[half, k].astype(F32)
            self.sums[half] = total.astype(BF16)
            for k in (1, 3, 2):
                self.copy(1, half, k).start()

    def total(self, half):
        total = self.sums[half, self.me["yx"[half]]].astype(F32)
        for k in (1, 3, 2):
            self.copy(1, half, k).wait_recv()
            total = total + self.got_last[half, k].astype(F32)
        return total

    def drain(self):
        for turn in range(2):
            for half in range(2):
                for k in (1, 3, 2):
                    self.copy(turn, half, k).wait_send()


def start_kernel(
    sent_a,
    sent_b,
    tokens,
    output_rows,
    down_rows,
    frequency,
    q_mine,
    kv_mine,
    all_tokens,
    down_low,
    output_wide,
    gateup_low,
    extra_out,
    gains_out,
    qkv_part,
    projected,
    cosine,
    sine,
    head_gains,
    shares_a,
    shares_b,
    wide,
    blocks,
    queries,
    keyvals,
    a_send,
    a_recv,
    b_send,
    b_recv,
    w_send,
    w_recv,
    row_send,
    row_recv,
    near_send,
    near_recv,
    far_send,
    far_recv,
    q_send,
    q_recv,
    kv_send,
    kv_recv,
    relay_send,
    relay_recv,
    swap_sems,
    own_sems,
):
    me = where_am_i()
    x, y = me["x"], me["y"]
    rank, here = flat_index(me, COLUMN), flat_index(me, SURFACE)
    gathers = ColumnGathers(me, blocks, near_send, near_recv, far_send, far_recv)
    to_a = Exchange(
        me,
        COLUMN,
        lambda to: sent_a.at[flat_index(to, COLUMN)],
        lambda frm: shares_a.at[flat_index(frm, COLUMN)],
        a_send,
        a_recv,
    )
    to_b = Exchange(
        me,
        COLUMN,
        lambda to: sent_b.at[flat_index(to, COLUMN)],
        lambda frm: shares_b.at[flat_index(frm, COLUMN)],
        b_send,
        b_recv,
    )
    spread = PlaneGathers(
        me,
        (
            (
                lambda half, x, y: wide.at[half, x, y],
                lambda half, at: wide.at[0, :, at] if half == 0 else wide.at[1, at],
            ),
            (
                lambda half, x, y: output_wide.at[y, x, :, pl.ds(half * 512, 512)],
                lambda half, at: (
                    output_wide.at[at, :, :, pl.ds(0, 512)]
                    if half == 0
                    else output_wide.at[:, at, :, pl.ds(512, 512)]
                ),
            ),
        ),
        w_send,
        w_recv,
        row_send,
        row_recv,
    )
    output_swap = Swap(
        me, output_rows, output_wide.at[y, quarter(me)], output_wide.at[y, x], swap_sems.at[0]
    )
    down_swap = Swap(me, down_rows, down_low, down_low, swap_sems.at[1])
    own_a = pltpu.make_async_copy(sent_a.at[rank], shares_a.at[rank], own_sems.at[0])
    own_b = pltpu.make_async_copy(sent_b.at[rank], shares_b.at[rank], own_sems.at[1])
    own_a.start()
    own_b.start()
    greet_all(me, "all", True)
    to_a.begin()
    output_swap.begin()
    gathers.begin(0, tokens[...])
    down_swap.begin()
    to_b.begin()

    own_a.wait()
    to_a.arrive()
    wide[:, x, y] = shares_a[...].astype(BF16).reshape(2, 32, 640)
    spread.begin(0)
    output_swap.finish()
    extra_out[...] = shares_a[:, :, 512:]

    lanes = lax.broadcasted_iota(jnp.int32, (BLOCK, HD), 1)
    place = lax.broadcasted_iota(jnp.int32, (BLOCK, HD), 0).astype(F32)

    def tables(j, carry):
        for half in range(2):
            first = shares_a[j, 2 + half : 3 + half, 512:]
            angles = (first * float(BLOCK) + place) * frequency[...]
            at = pl.ds(pl.multiple_of(j * ROWS + half * BLOCK, BLOCK), BLOCK)
            cosine[at, :] = jnp.cos(angles)
            sines = jnp.sin(angles)
            sine[at, :] = jnp.where(lanes < HD // 2, -sines, sines)
        return carry

    lax.fori_loop(0, RANKS, tables, 0)
    spread.pass_on(0)
    spread.begin(1)
    own_b.wait()
    to_b.arrive()
    gateup_low[...] = shares_b[...].astype(BF16).reshape(2, 32, 768)

    spread.arrive(0)
    qkv_part[...] = wide[..., :512].reshape(D, 512)
    extra = wide[..., 512:].reshape(D, HD)
    gains_out[...] = extra
    entry = 2 * D + lax.broadcasted_iota(jnp.int32, (HD, 2 * HD), 1)
    pick = (lax.broadcasted_iota(jnp.int32, (HD, 2 * HD), 0) == lax.rem(entry, 18)).astype(BF16)
    entries = 2 * D + lax.broadcasted_iota(jnp.int32, (D, 2 * HD), 1)
    owned = lax.broadcasted_iota(jnp.int32, (D, 2 * HD), 0) == 8 * lax.div(entries, 18)
    gains = jnp.sum(jnp.where(owned, dot_nn(extra, pick), 0.0), axis=0, keepdims=True)
    head_gains[0:1, :] = gains[:, :HD]
    head_gains[1:2, :] = gains[:, HD:]

    def q_copy(row_zh, pack):
        return pltpu.make_async_remote_copy(
            src_ref=queries.at[row_zh, pack],
            dst_ref=q_mine.at[x, row_zh],
            send_sem=q_send.at[row_zh, pack],
            recv_sem=q_recv.at[row_zh, x],
            device_id=address(dict(me, x=pack)),
            device_id_type=MESH,
        )

    def kv_copy(row_zh, pack):
        return pltpu.make_async_remote_copy(
            src_ref=keyvals.at[row_zh, pack],
            dst_ref=kv_mine.at[here, row_zh],
            send_sem=kv_send.at[row_zh, pack],
            recv_sem=kv_recv.at[row_zh, x],
            device_id=address(dict(me, x=pack)),
            device_id_type=MESH,
        )

    def q_own(row_zh):
        return pltpu.make_async_copy(
            queries.at[row_zh, x], q_mine.at[x, row_zh], own_sems.at[2 + row_zh]
        )

    def kv_own(row_zh):
        return pltpu.make_async_copy(
            keyvals.at[row_zh, x], kv_mine.at[here, row_zh], own_sems.at[4 + row_zh]
        )

    def relay(row_zh, from_x, which, arriving):
        step = 1 if which in (1, 2) else 3
        back = (step if which in (1, 3) else 2 * step) if arriving else (0 if which in (1, 3) else step)
        block = kv_mine.at[from_x * 4 + lax.rem(y + 8 - back, 4), row_zh]
        if which == 2:
            block = block.at[pl.ds(0, BLOCK)]
        if which == 0:
            block = block.at[pl.ds(BLOCK, BLOCK)]
        return pltpu.make_async_remote_copy(
            src_ref=block,
            dst_ref=block,
            send_sem=relay_send.at[row_zh, from_x, which],
            recv_sem=relay_recv.at[row_zh, from_x, which],
            device_id=address(dict(me, y=lax.rem(y + step, 4))),
            device_id_type=MESH,
        )

    def project(i, carry):
        off, at_z = gathers.await_chip(0, i)
        at = pl.ds(pl.multiple_of(at_z * 2 * ROWS, 2 * ROWS), 2 * ROWS)
        both = dot_nn(blocks[0, pl.ds(at_z * 2, 2)].reshape(2 * ROWS, D), qkv_part[...])
        projected[at, :] = both[:, :384]
        row_zh, first = lax.div(at_z, 2), lax.rem(at_z, 2) * 2
        for head in range(3):
            values = both[:, head * HD : (head + 1) * HD]
            gain = head_gains[1:2, :] if head == 2 else head_gains[0:1, :]
            normed = values * norm_factor(values) * gain
            turned = (
                normed * cosine[at, :] + pltpu.roll(normed, HD // 2, 1) * sine[at, :]
            ).astype(BF16)
            turned = turned.reshape(2, ROWS, HD)
            for at_core in range(2):
                if head == 2:
                    keyvals[row_zh, first + at_core, :, :HD] = turned[at_core]
                else:
                    queries[row_zh, first + at_core, :, head * HD : (head + 1) * HD] = turned[
                        at_core
                    ]
        values = both[:, 384:].astype(BF16).reshape(2, ROWS, HD)
        for at_core in range(2):
            pack = first + at_core
            keyvals[row_zh, pack, :, HD:] = values[at_core]

            @pl.when(pack != x)
            def _():
                kv_copy(row_zh, pack).start()
                q_copy(row_zh, pack).start()

            @pl.when(pack == x)
            def _():
                kv_own(row_zh).start()
                q_own(row_zh).start()

        return carry

    gathers.pass_on(0)
    lax.fori_loop(0, 4, project, 0)
    spread.pass_on(1)
    for i in range(RANKS):
        slot = pltpu.make_async_copy(blocks.at[0, i], all_tokens.at[i], own_sems.at[6 + i])
        slot.start()
    for row_zh in range(2):
        kv_own(row_zh).wait()
        for which in (1, 3):
            relay(row_zh, x, which, False).start()
    for off in (1, 3, 2):
        from_x = lax.rem(x + 4 - off, 4)
        to_x = lax.rem(x + off, 4)
        for row_zh in range(2):
            pltpu.make_async_remote_copy(
                src_ref=keyvals.at[row_zh, to_x],
                dst_ref=kv_mine.at[from_x * 4 + y, row_zh],
                send_sem=kv_send.at[row_zh, to_x],
                recv_sem=kv_recv.at[row_zh, from_x],
                device_id=address(dict(me, x=to_x)),
                device_id_type=MESH,
            ).wait_recv()
            for which in (1, 3):
                relay(row_zh, from_x, which, False).start()

    def forward(j, carry):
        off, row_zh = lax.div(j, 2), lax.rem(j, 2)
        from_x = lax.rem(x + 4 - gray(off), 4)
        for which, by_way in ((1, 2), (3, 0)):
            relay(row_zh, from_x, which, True).wait_recv()
            relay(row_zh, from_x, by_way, False).start()
        return carry

    lax.fori_loop(0, 8, forward, 0)
    for off in (1, 3, 2):
        from_x = lax.rem(x + 4 - off, 4)
        to_x = lax.rem(x + off, 4)
        for row_zh in range(2):
            pltpu.make_async_remote_copy(
                src_ref=queries.at[row_zh, to_x],
                dst_ref=q_mine.at[from_x, row_zh],
                send_sem=q_send.at[row_zh, to_x],
                recv_sem=q_recv.at[row_zh, from_x],
                device_id=address(dict(me, x=to_x)),
                device_id_type=MESH,
            ).wait()
            kv_copy(row_zh, to_x).wait_send()
    for row_zh in range(2):
        q_own(row_zh).wait()

    def finish(j, carry):
        row_zh, from_x = lax.div(j, 4), lax.rem(j, 4)
        for which in range(4):
            relay(row_zh, from_x, which, False).wait_send()
        for which in (2, 0):
            relay(row_zh, from_x, which, True).wait_recv()
        return carry

    lax.fori_loop(0, 8, finish, 0)
    spread.arrive(1)
    down_swap.finish()
    for i in range(RANKS):
        pltpu.make_async_copy(blocks.at[0, i], all_tokens.at[i], own_sems.at[6 + i]).wait()
    for exchange in (to_a, to_b, spread):
        exchange.drain()
    gathers.drain(0)


def start(number, sent_a, sent_b, tokens, output_rows, down_rows, frequency):
    anywhere = pl.BlockSpec(memory_space=pl.ANY)
    vmem = pl.BlockSpec(memory_space=pltpu.VMEM)
    dma = pltpu.SemaphoreType.DMA
    struct = jax.ShapeDtypeStruct
    return pl.pallas_call(
        start_kernel,
        out_shape=(
            struct((4, 2, ROWS, 256), BF16),
            struct((PLANE, 2, ROWS, 256), BF16),
            struct((RANKS, ROWS, D), BF16),
            struct((48, 512), BF16),
            struct((4, 4, 16, D), BF16),
            struct((2, 32, 768), BF16),
            struct((RANKS, 8, HD), F32),
            struct((D, HD), BF16),
            struct((D, 512), BF16),
            struct((RANKS * ROWS, 384), F32),
            struct((RANKS * ROWS, HD), F32),
            struct((RANKS * ROWS, HD), F32),
            struct((2, HD), F32),
        ),
        in_specs=[anywhere, anywhere, vmem, anywhere, anywhere, vmem],
        out_specs=(anywhere,) * 4 + (vmem,) * 9,
        scratch_shapes=[
            pltpu.VMEM((RANKS, 8, 640), F32),
            pltpu.VMEM((RANKS, 8, 768), F32),
            pltpu.VMEM((2, 4, 4, 32, 640), BF16),
            pltpu.VMEM((1, RANKS, ROWS, D), BF16),
            pltpu.VMEM((2, 4, ROWS, 256), BF16),
            pltpu.VMEM((2, 4, ROWS, 256), BF16),
        ]
        + [dma((RANKS,))] * 4
        + [dma((2, 2, 4))] * 4
        + [dma((1, 4))] * 4
        + [dma((2, 4))] * 4
        + [dma((2, 4, 4)), dma((2, 4, 4)), dma((2, 2)), dma((6 + RANKS,))],
        compiler_params=pltpu.CompilerParams(
            collective_id=number, has_side_effects=True, vmem_limit_bytes=VMEM_LIMIT
        ),
        name="start",
    )(sent_a, sent_b, tokens, output_rows, down_rows, frequency)


def middle_kernel(
    out_mine,
    wo,
    gateup_low,
    down_rows,
    inputs,
    upstream,
    gains,
    result,
    grad_hidden,
    gains_grad,
    grad_mine,
    gateup_sum,
    down_sum,
    output_lines,
    attended,
    blocks,
    part,
    paired,
    sending,
    landed,
    gate_up,
    activated,
    grad_gate,
    grad_attended,
    gateup_lines,
    down_grad,
    down_lines,
    branch,
    hidden,
    wgu,
    wd,
    down_wide,
    got,
    plane_sums,
    got_last,
    d_got,
    d_sums,
    d_got_last,
    near_send,
    near_recv,
    far_send,
    far_recv,
    gnear_send,
    gnear_recv,
    gfar_send,
    gfar_recv,
    att_send,
    att_recv,
    back_send,
    back_recv,
    plane_send,
    plane_recv,
    last_send,
    last_recv,
    w_send,
    w_recv,
    row_send,
    row_recv,
    down_send,
    down_recv,
    dlast_send,
    dlast_recv,
    own_sems,
):
    me = where_am_i()
    x = me["x"]
    z = me["zh"] * 2 + me["zl"]
    sums = ColumnSums(
        me, part, paired, sending, landed, near_send, near_recv, far_send, far_recv
    )
    gathers = ColumnGathers(me, blocks, gnear_send, gnear_recv, gfar_send, gfar_recv)
    own_wgu = pltpu.make_async_copy(gateup_low, wgu.at[:, x, me["y"]], own_sems.at[0])
    own_wgu.start()
    own_down = pltpu.make_async_copy(down_rows, down_wide.at[me["y"], x], own_sems.at[1])
    own_down.start()
    spread = PlaneGathers(
        me,
        (
            (
                lambda half, x, y: wgu.at[half, x, y],
                lambda half, at: wgu.at[0, :, at] if half == 0 else wgu.at[1, at],
            ),
            (
                lambda half, x, y: down_wide.at[y, x, :, pl.ds(half * 256, 256)],
                lambda half, at: (
                    down_wide.at[at, :, :, pl.ds(0, 256)]
                    if half == 0
                    else down_wide.at[:, at, :, pl.ds(256, 256)]
                ),
            ),
        ),
        w_send,
        w_recv,
        row_send,
        row_recv,
    )
    down_back = PlaneSums(
        me, down_lines, d_got, d_sums, d_got_last, down_send, down_recv, dlast_send, dlast_recv
    )
    gateup_back = PlaneSums(
        me, gateup_lines, got, plane_sums, got_last, plane_send, plane_recv, last_send, last_recv
    )

    def half_rows(half):
        return pl.ds(half * BLOCK, BLOCK)

    def own_out(half):
        return pltpu.make_async_copy(
            out_mine.at[x, :, half_rows(half)], attended.at[half, :, x], own_sems.at[2 + half]
        )

    def attention_out(half, k, arriving):
        frm = shifted(me, ("x",), k, -1) if arriving else me
        to = shifted(me, ("x",), k, 1)
        return pltpu.make_async_remote_copy(
            src_ref=out_mine.at[to["x"], :, half_rows(half)],
            dst_ref=attended.at[half, :, frm["x"]],
            send_sem=att_send.at[half, k],
            recv_sem=att_recv.at[half, k],
            device_id=address(to),
            device_id_type=MESH,
        )

    for half in range(2):
        own_out(half).start()
    greet_all(me, "some", False)
    for half in range(2):
        for k in (2, 1, 3):
            attention_out(half, k, False).start()
    own_wgu.wait()
    own_down.wait()
    spread.begin(0)
    spread.begin(1)

    def down_line_in(j, carry):
        at = pl.ds(pl.multiple_of(j * 48, 16), 48)
        pair = down_wide[lax.div(j, 2), pl.ds(lax.rem(j, 2) * 2, 2)].astype(F32)
        for side in range(2):
            rows = pair[:, side * 24 : side * 24 + 24].reshape(48, 512)
            wd[at, side * 512 : side * 512 + 512] = rows.astype(BF16)
        return carry

    def project_out(half):
        own_out(half).wait()
        for k in (1, 3, 2):
            attention_out(half, k, True).wait_recv()

        rows = attended[half].reshape(RANKS * BLOCK, 256)
        sums.put_all(half, dot_nn(rows, wo[...]))

    def block_rows(phase):
        return blocks[phase].reshape(RANKS * BLOCK, D)

    def at_half(half):
        return slice(half * RANKS * BLOCK, (half + 1) * RANKS * BLOCK)

    def attention_norm(half):
        at = half_rows(half)
        total = sums.total(half)
        branch[at, :] = total
        both = inputs[at, :].astype(F32) + total * norm_factor(total) * gains[0:1, :]
        hidden[at, :] = both
        gathers.begin(half, both.astype(BF16))

    def feed_forward(half):
        at = at_half(half)
        both = dot_nn(block_rows(half), wgu[...].reshape(D, 768))
        gate_up[at, :] = both
        gate, up = both[:, :384], both[:, 384:]
        acts = (gate * (1.0 / (1.0 + jnp.exp(-gate))) * up).astype(BF16)
        activated[at, :] = acts
        sums.put_all(2 + half, dot_nn(acts, wd[...]))

    def feed_forward_norm(half):
        at = half_rows(half)
        ffn_out = sums.total(2 + half)
        gain = gains[1:2, :]
        result[at, :] = (hidden[at, :] + ffn_out * norm_factor(ffn_out) * gain).astype(BF16)
        grad_ffn, grad_gain = norm_back(ffn_out, gain, upstream[at, :].astype(F32))
        gathers.begin(2 + half, grad_ffn.astype(BF16))
        return grad_gain

    def feed_forward_back(half):
        at = at_half(half)
        grad_act = dot_nt(block_rows(2 + half), wd[...])
        gate, up = gate_up[at, :384], gate_up[at, 384:]
        sig = 1.0 / (1.0 + jnp.exp(-gate))
        grad_gate[at, :384] = (grad_act * up * (sig * (1.0 + gate * (1.0 - sig)))).astype(BF16)
        grad_gate[at, 384:] = (grad_act * (gate * sig)).astype(BF16)
        sums.put_all(4 + half, dot_nt(grad_gate[at, :], wgu[...].reshape(D, 768)))

    def attention_norm_back(half):
        at = half_rows(half)
        total = upstream[at, :].astype(F32) + sums.total(4 + half)
        grad_hidden[at, :] = total
        grad_branch, grad_gain = norm_back(branch[at, :], gains[0:1, :], total)
        gathers.begin(4 + half, grad_branch.astype(BF16))
        return grad_gain

    def to_attention(half, row_zh, pack):
        return pltpu.make_async_remote_copy(
            src_ref=grad_attended.at[half, row_zh, pack],
            dst_ref=grad_mine.at[x, row_zh, half_rows(half)],
            send_sem=back_send.at[half, row_zh, pack],
            recv_sem=back_recv.at[half, row_zh, x],
            device_id=address(dict(me, x=pack)),
            device_id_type=MESH,
        )

    def own_attention(half, row_zh):
        return pltpu.make_async_copy(
            grad_attended.at[half, row_zh, x],
            grad_mine.at[x, row_zh, half_rows(half)],
            own_sems.at[4 + 2 * half + row_zh],
        )

    def project_out_back(half):
        grads = dot_nt(block_rows(4 + half), wo[...]).astype(BF16)
        grad_attended[half] = grads.reshape(2, 4, BLOCK, 256)
        for row_zh in range(2):
            own_attention(half, row_zh).start()
            for k in (1, 3, 2):
                to_attention(half, row_zh, lax.rem(x + k, 4)).start()

    def all_rows(phase):
        return blocks[phase : phase + 2].reshape(RANKS * ROWS, D)

    def down_line(s, carry):
        rows = down_grad[pl.ds(pl.multiple_of(s * 24, 8), 24), :].astype(BF16)
        at_y, at_x = lax.div(s, 4), lax.rem(s, 4)
        for half in range(2):
            for side in range(2):
                cols = slice(side * 512 + half * 256, side * 512 + half * 256 + 256)
                down_lines[half, at_x, at_y, side * 24 : side * 24 + 24, :] = rows[:, cols]
        return carry

    def send_down():
        down_grad[...] = dot_tn(activated[...], all_rows(2))
        lax.fori_loop(0, PLANE, down_line, 0)
        down_back.begin()

    def send_gateup():
        grads = dot_tn(all_rows(0), grad_gate[...])
        gateup_lines[...] = grads.astype(BF16).reshape(2, 4, 4, 32, 768)
        gateup_back.begin()

    works = (project_out, feed_forward, feed_forward_back, project_out_back)
    thens = (attention_norm, feed_forward_norm, attention_norm_back)
    gain_grads = [None, None, None]
    works[0](0)
    sums.first(0)
    works[0](1)
    spread.pass_on(0)
    spread.pass_on(1)
    sums.second(0)
    for stage in range(3):
        phase = 2 * stage
        if stage == 2:
            send_down()
        gain_grads[stage] = thens[stage](0)
        if stage > 0:
            works[stage](1)
        sums.first(phase + 1)
        gathers.pass_on(phase)
        sums.second(phase + 1)
        if stage == 2:
            down_back.pass_on()
            send_gateup()
        gathers.await_all(phase)
        if stage == 0:
            spread.arrive(0)
            spread.arrive(1)
            lax.fori_loop(0, PLANE // 2, down_line_in, 0)
        works[stage + 1](0)
        other = thens[stage](1)
        if stage > 0:
            gains_grad[2 - stage : 3 - stage, :] = gain_grads[stage] + other
        if stage < 2:
            sums.first(phase + 2)
        gathers.pass_on(phase + 1)
        if stage < 2:
            sums.second(phase + 2)
        if stage == 2:
            gateup_back.pass_on()
        gathers.await_all(phase + 1)
    works[3](1)
    grads = dot_tn(attended[...].reshape(RANKS * ROWS, 256), all_rows(4))
    for line in range(PLANE):
        rows = grads[line * 16 : line * 16 + 16].astype(BF16)
        for half in range(2):
            output_lines[half, line % 4, line // 4] = rows[:, half * 512 : half * 512 + 512]

    for half in range(2):
        for k in (1, 3, 2):
            attention_out(half, k, False).wait_send()
            frm_x = lax.rem(x + 4 - k, 4)
            to_x = lax.rem(x + k, 4)
            for row_zh in range(2):
                to_attention(half, row_zh, to_x).wait_send()
                pltpu.make_async_remote_copy(
                    src_ref=grad_attended.at[half, row_zh, to_x],
                    dst_ref=grad_mine.at[frm_x, row_zh, half_rows(half)],
                    send_sem=back_send.at[half, row_zh, to_x],
                    recv_sem=back_recv.at[half, row_zh, frm_x],
                    device_id=address(dict(me, x=to_x)),
                    device_id_type=MESH,
                ).wait_recv()
        for row_zh in range(2):
            own_attention(half, row_zh).wait()
    for phase in range(6):
        sums.drain(phase)
        gathers.drain(phase)
    for half in range(2):
        down_sum[:, half * 256 : half * 256 + 256] = down_back.total(half)
        gateup_sum[half] = gateup_back.total(half)
    for exchange in (spread, gateup_back, down_back):
        exchange.drain()


def middle(number, out_mine, wo, gateup_low, down_rows, inputs, upstream, gains):
    anywhere = pl.BlockSpec(memory_space=pl.ANY)
    vmem = pl.BlockSpec(memory_space=pltpu.VMEM)
    block, half = (ROWS, D), (BLOCK, D)
    dma = pltpu.SemaphoreType.DMA
    return pl.pallas_call(
        middle_kernel,
        out_shape=(
            jax.ShapeDtypeStruct(block, BF16),
            jax.ShapeDtypeStruct(block, F32),
            jax.ShapeDtypeStruct((2, D), F32),
            jax.ShapeDtypeStruct((4, 2, ROWS, 256), BF16),
            jax.ShapeDtypeStruct((2, 32, 768), F32),
            jax.ShapeDtypeStruct((48, 512), F32),
            jax.ShapeDtypeStruct((2, 4, 4, 16, 512), BF16),
        ),
        in_specs=[anywhere, vmem, anywhere, anywhere, vmem, vmem, vmem],
        out_specs=(vmem, vmem, vmem, anywhere, vmem, vmem, vmem),
        scratch_shapes=[
            pltpu.VMEM((2, 2, 4, BLOCK, 256), BF16),
            pltpu.VMEM((6, RANKS) + half, BF16),
            pltpu.VMEM((6, 4, 2) + half, BF16),
            pltpu.VMEM((6, 4) + half, BF16),
            pltpu.VMEM((6, 4) + half, BF16),
            pltpu.VMEM((6, 4) + half, BF16),
            pltpu.VMEM((RANKS * ROWS, 768), F32),
            pltpu.VMEM((RANKS * ROWS, 384), BF16),
            pltpu.VMEM((RANKS * ROWS, 768), BF16),
            pltpu.VMEM((2, 2, 4, BLOCK, 256), BF16),
            pltpu.VMEM((2, 4, 4, 32, 768), BF16),
            pltpu.VMEM((384, D), F32),
            pltpu.VMEM((2, 4, 4, 48, 256), BF16),
            pltpu.VMEM(block, F32),
            pltpu.VMEM(block, F32),
            pltpu.VMEM((2, 4, 4, 32, 768), BF16),
            pltpu.VMEM((384, D), BF16),
            pltpu.VMEM((4, 4, 48, 512), BF16),
            pltpu.VMEM((2, 4, 4, 32, 768), BF16),
            pltpu.VMEM((2, 4, 32, 768), BF16),
            pltpu.VMEM((2, 4, 32, 768), BF16),
            pltpu.VMEM((2, 4, 4, 48, 256), BF16),
            pltpu.VMEM((2, 4, 48, 256), BF16),
            pltpu.VMEM((2, 4, 48, 256), BF16),
        ]
        + [dma((6, 4))] * 8
        + [dma((2, 4)), dma((2, 4)), dma((2, 2, 4)), dma((2, 2, 4))]
        + [dma((2, 4))] * 4
        + [dma((2, 2, 4))] * 4
        + [dma((2, 4))] * 4
        + [dma((8,))],
        compiler_params=pltpu.CompilerParams(
            collective_id=number, has_side_effects=True, vmem_limit_bytes=VMEM_LIMIT
        ),
        name="middle",
    )(out_mine, wo, gateup_low, down_rows, inputs, upstream, gains)


def end_kernel(
    dq_mine,
    dkv_mine,
    projected,
    cosine,
    sine,
    head_gains,
    all_tokens,
    qkv_part,
    output_lines,
    down_total,
    column_b,
    grad_hidden,
    gains_grad,
    token_grad,
    summed_a,
    summed_b,
    output_sum,
    down_sum,
    gains_sum,
    across,
    besides,
    landed_kv,
    passing,
    dq_all,
    dkv_all,
    grad_qkv,
    part,
    paired,
    sending,
    landed,
    qkv_lines,
    q_got,
    q_sums,
    q_got_last,
    o_got,
    o_sums,
    o_got_last,
    output_total,
    column_a,
    gains_column,
    gains_plane,
    ring_send,
    ring_recv,
    kv_send,
    kv_recv,
    dq_send,
    dq_recv,
    near_send,
    near_recv,
    far_send,
    far_recv,
    plane_send,
    plane_recv,
    qlast_send,
    qlast_recv,
    row_send,
    row_recv,
    olast_send,
    olast_recv,
    gplane_send,
    gplane_recv,
    swap_sems,
    a_send,
    a_recv,
    b_send,
    b_recv,
    gcolumn_send,
    gcolumn_recv,
    own_sems,
):
    me = where_am_i()
    x, y, z = me["x"], me["y"], me["zh"] * 2 + me["zl"]
    rank, here = flat_index(me, COLUMN), flat_index(me, SURFACE)
    sums = ColumnSums(
        me, part, paired, sending, landed, near_send, near_recv, far_send, far_recv
    )

    def by_column(ref, out, send, recv):
        return Exchange(
            me,
            COLUMN,
            lambda to: ref.at[flat_index(to, COLUMN)],
            lambda frm: out.at[flat_index(frm, COLUMN)],
            send,
            recv,
        )

    to_a = by_column(column_a, summed_a, a_send, a_recv)
    to_b = by_column(column_b, summed_b, b_send, b_recv)
    gains_in = Exchange(
        me,
        COLUMN,
        lambda to: gains_column.at[rank],
        lambda frm: gains_column.at[flat_index(frm, COLUMN)],
        gcolumn_send,
        gcolumn_recv,
    )
    gains_over = Exchange(
        me,
        SURFACE,
        lambda to: gains_plane.at[here],
        lambda frm: gains_plane.at[flat_index(frm, SURFACE)],
        gplane_send,
        gplane_recv,
    )
    qkv_back = PlaneSums(
        me, qkv_lines, q_got, q_sums, q_got_last, plane_send, plane_recv, qlast_send, qlast_recv
    )
    queries = Exchange(
        me,
        ("x",),
        lambda to: dq_mine.at[to["x"]],
        lambda frm: dq_all.at[:, frm["x"]],
        dq_send,
        dq_recv,
    )
    output_back = PlaneSums(
        me, output_lines, o_got, o_sums, o_got_last, row_send, row_recv, olast_send, olast_recv
    )
    output_swap = Swap(me, output_total, output_sum, output_sum, swap_sems.at[0])
    down_swap = Swap(me, down_total, down_sum, down_sum, swap_sems.at[1])
    own_dq = pltpu.make_async_copy(dq_mine.at[x], dq_all.at[:, x], own_sems.at[4])
    own_a = pltpu.make_async_copy(column_a.at[rank], summed_a.at[rank], own_sems.at[6])
    own_b = pltpu.make_async_copy(column_b.at[rank], summed_b.at[rank], own_sems.at[7])

    def ring(j, which):
        to_x = lax.rem(x + j, 4)
        step = 1 if which in (1, 2) else 3
        if which in (1, 3):
            src, dst = besides.at[j, which // 2], landed_kv.at[j, which // 2]
        else:
            row_zh = 0 if which == 2 else 1
            src, dst = dkv_mine.at[to_x * 4 + lax.rem(y + 2, 4), row_zh], across.at[j, row_zh]
        return pltpu.make_async_remote_copy(
            src_ref=src,
            dst_ref=dst,
            send_sem=ring_send.at[j, which],
            recv_sem=ring_recv.at[j, which],
            device_id=address(dict(me, y=lax.rem(y + step, 4))),
            device_id_type=MESH,
        )

    def kv_copy(j, arriving):
        frm_x = lax.rem(x + 4 - j, 4) if arriving else x
        return pltpu.make_async_remote_copy(
            src_ref=passing.at[j],
            dst_ref=dkv_all.at[:, frm_x],
            send_sem=kv_send.at[j],
            recv_sem=kv_recv.at[j],
            device_id=address(dict(me, x=lax.rem(x + j, 4))),
            device_id_type=MESH,
        )

    own_dq.start()
    greet_all(me, "all", True)
    for j in (2, 1, 3, 0):
        for which in (2, 0):
            ring(j, which).start()
    queries.begin()
    down_swap.begin()
    for j in (2, 1, 3, 0):
        to_x = lax.rem(x + j, 4)
        for which, by_way, step in ((1, 2, 1), (3, 0, 3)):
            row_zh, other = (0, 1) if by_way == 2 else (1, 0)
            own_block = to_x * 4 + lax.rem(y + step, 4)
            besides[j, which // 2, other] = dkv_mine[own_block, other]
            ring(j, by_way).wait_recv()
            both = dkv_mine[own_block, row_zh].astype(F32) + across[j, row_zh].astype(F32)
            besides[j, which // 2, row_zh] = both.astype(BF16)
            ring(j, which).start()

    own_b.start()
    to_b.begin()

    for j in (2, 1, 3, 0):
        total = dkv_mine[lax.rem(x + j, 4) * 4 + y].astype(F32)
        for which in (1, 3):
            ring(j, which).wait_recv()
            total = total + landed_kv[j, which // 2].astype(F32)
        if j:
            passing[j] = total.astype(BF16)
            kv_copy(j, False).start()
        else:
            dkv_all[:, x] = total.astype(BF16)
    output_back.begin()
    own_dq.wait()
    queries.arrive()
    for j in (2, 1, 3):
        kv_copy(j, True).wait_recv()

    def project_back(i, carry):
        gain_q, gain_k = carry
        off = gray(3 - i)
        to_z = lax.rem(z + off, 4)
        at = pl.ds(pl.multiple_of(to_z * 2 * ROWS, 2 * ROWS), 2 * ROWS)
        row_zh, first = lax.div(to_z, 2), lax.rem(to_z, 2) * 2
        grad_q = dq_all[row_zh, pl.ds(first, 2)].reshape(2 * ROWS, 256).astype(F32)
        grad_kv = dkv_all[row_zh, pl.ds(first, 2)].reshape(2 * ROWS, 256)
        for head in range(3):
            if head == 2:
                grad, gain = grad_kv[:, :HD].astype(F32), head_gains[1:2, :]
            else:
                grad, gain = grad_q[:, head * HD : (head + 1) * HD], head_gains[0:1, :]
            turned = grad * cosine[at, :] - pltpu.roll(grad, HD // 2, 1) * sine[at, :]
            grad_in, grad_gain = norm_back(
                projected[at, head * HD : (head + 1) * HD], gain, turned
            )
            grad_qkv[at, head * HD : (head + 1) * HD] = grad_in.astype(BF16)
            if head == 2:
                gain_k = gain_k + grad_gain
            else:
                gain_q = gain_q + grad_gain
        grad_qkv[at, 384:] = grad_kv[:, HD:]
        sums.put(0, off, dot_nt(grad_qkv[at, :], qkv_part[...]))

        @pl.when(i == 1)
        def _():
            sums.first(0)

        return gain_q, gain_k

    nothing = jnp.zeros((1, HD), F32)
    gain_q, gain_k = lax.fori_loop(0, 4, project_back, (nothing, nothing))

    for j in range(16):
        gains_column[rank, j : j + 1, :] = gains_grad[
            j // 8 : j // 8 + 1, j % 8 * HD : (j % 8 + 1) * HD
        ]
    gains_column[rank, 16:17, :] = gain_q
    gains_column[rank, 17:18, :] = gain_k
    gains_column[rank, 18:24, :] = jnp.zeros((6, HD), F32)
    gains_in.begin()
    sums.second(0)
    output_back.pass_on()

    def qkv_rows(j, carry):
        cols = pl.ds(pl.multiple_of(j * 256, 256), 256)
        grads = dot_tn(all_tokens[:, :, cols].reshape(RANKS * ROWS, 256), grad_qkv[...])
        qkv_lines[lax.div(j, 2), pl.ds(lax.rem(j, 2) * 2, 2)] = grads.astype(BF16).reshape(
            2, 4, 32, 512
        )
        return carry

    lax.fori_loop(0, 4, qkv_rows, 0)
    qkv_back.begin()

    gains_in.arrive()
    gains_plane[here] = jnp.sum(gains_column[...], axis=0)
    gains_over.begin()
    token_grad[...] = grad_hidden[...] + sums.total(0)
    qkv_back.pass_on()
    for half in range(2):
        output_total[:, half * 512 : half * 512 + 512] = output_back.total(half)
    output_swap.begin()

    for half in range(2):
        column_a[pl.ds(half * 4, 4)] = qkv_back.total(half).reshape(4, 8, 512)
    own_a.start()
    to_a.begin()
    gains_over.arrive()
    gains_sum[...] = jnp.sum(gains_plane[...], axis=0)
    to_b.arrive()
    output_swap.finish()
    down_swap.finish()
    own_b.wait()
    for j in (2, 1, 3, 0):
        for which in range(4):
            ring(j, which).wait_send()
        if j:
            kv_copy(j, False).wait_send()
    sums.drain(0)
    for exchange in (queries, output_back, to_b, gains_in, gains_over, qkv_back):
        exchange.drain()
    own_a.wait()
    to_a.arrive()
    to_a.drain()


def end(number, *arrays):
    anywhere = pl.BlockSpec(memory_space=pl.ANY)
    vmem = pl.BlockSpec(memory_space=pltpu.VMEM)
    dma = pltpu.SemaphoreType.DMA
    struct = jax.ShapeDtypeStruct
    block = (ROWS, D)
    quarter_rows = (2, ROWS, 256)
    return pl.pallas_call(
        end_kernel,
        out_shape=(
            struct(block, F32),
            struct((RANKS, 8, 512), F32),
            struct((RANKS, 8, 768), F32),
            struct((16, D), F32),
            struct((48, 512), F32),
            struct((24, HD), F32),
        ),
        in_specs=[anywhere, vmem] + [vmem] * 6 + [vmem, anywhere, anywhere] + [vmem] * 2,
        out_specs=(vmem, anywhere, anywhere, anywhere, anywhere, vmem),
        scratch_shapes=[
            pltpu.VMEM((4,) + quarter_rows, BF16),
            pltpu.VMEM((4, 2) + quarter_rows, BF16),
            pltpu.VMEM((4, 2) + quarter_rows, BF16),
            pltpu.VMEM((4,) + quarter_rows, BF16),
            pltpu.VMEM((2, 4, ROWS, 256), BF16),
            pltpu.VMEM((2, 4, ROWS, 256), BF16),
            pltpu.VMEM((RANKS * ROWS, 512), BF16),
            pltpu.VMEM((1, 4, 2) + block, BF16),
            pltpu.VMEM((1, 4) + block, BF16),
            pltpu.VMEM((1, 4) + block, BF16),
            pltpu.VMEM((1, 4) + block, BF16),
            pltpu.VMEM((2, 4, 4, 32, 512), BF16),
            pltpu.VMEM((2, 4, 4, 32, 512), BF16),
            pltpu.VMEM((2, 4, 32, 512), BF16),
            pltpu.VMEM((2, 4, 32, 512), BF16),
            pltpu.VMEM((2, 4, 4, 16, 512), BF16),
            pltpu.VMEM((2, 4, 16, 512), BF16),
            pltpu.VMEM((2, 4, 16, 512), BF16),
            pltpu.VMEM((16, D), F32),
            pltpu.VMEM((RANKS, 8, 512), F32),
            pltpu.VMEM((RANKS, 24, HD), F32),
            pltpu.VMEM((PLANE, 24, HD), F32),
        ]
        + [dma((4, 4))] * 2
        + [dma((4,))] * 4
        + [dma((1, 4))] * 4
        + [dma((2, 4))] * 8
        + [dma((PLANE,))] * 2
        + [dma((2, 2))]
        + [dma((RANKS,))] * 6
        + [dma((8,))],
        compiler_params=pltpu.CompilerParams(
            collective_id=number, has_side_effects=True, vmem_limit_bytes=VMEM_LIMIT
        ),
        name="end",
    )(*arrays)


def adam_update(weight, gradient, mean_old, square_old, rate, decay):
    mean_new = BETA_ONE * mean_old + (1.0 - BETA_ONE) * gradient
    square_new = BETA_TWO * square_old + (1.0 - BETA_TWO) * gradient * gradient
    mean_hat = mean_new / (1.0 - BETA_ONE**STEP)
    square_hat = square_new / (1.0 - BETA_TWO**STEP)
    weight_new = weight - rate * (mean_hat / (jnp.sqrt(square_hat) + ADAM_EPS) + decay * weight)
    return (weight_new, mean_new, square_new)


def by_rank(array, width):
    return array.reshape(array.shape[0], RANKS, width)


def body(
    tokens,
    cotangent,
    positions,
    seq_ids,
    query_weight,
    keyval_weight,
    output_weight,
    gateup_weight,
    down_weight,
    norm_gains,
    query_mean,
    keyval_mean,
    output_mean,
    gateup_mean,
    down_mean,
    gains_mean,
    query_square,
    keyval_square,
    output_square,
    gateup_square,
    down_square,
    gains_square,
):
    inputs = tokens[0]
    at_x, at_y = lax.axis_index("x"), lax.axis_index("y")

    own_blocks = (positions[0] + LONG * seq_ids[0]).reshape(-1, BLOCK)[:, 0] // BLOCK
    own_pair = lax.dynamic_slice_in_dim(own_blocks, 2 * lax.axis_index(("zh", "x", "y")), 2)
    own_pair = jnp.where(own_pair >= LONG // BLOCK, own_pair - LONG // BLOCK, own_pair)
    extra = jnp.concatenate(
        [
            jnp.pad(norm_gains, (0, HD - norm_gains.shape[0]))[None],
            jnp.pad(own_blocks.astype(F32), (0, HD - BLOCK))[None],
            jnp.broadcast_to(own_pair.astype(F32)[:, None], (2, HD)),
            jnp.zeros((4, HD), F32),
        ]
    )
    sent_a = jnp.concatenate(
        [
            by_rank(query_weight, 256),
            by_rank(keyval_weight[:, :KV], 128),
            by_rank(keyval_weight[:, KV:], 128),
            jnp.broadcast_to(extra[:, None, :], (8, RANKS, HD)),
        ],
        axis=2,
    ).transpose(1, 0, 2)
    sent_b = jnp.concatenate(
        [by_rank(gateup_weight[:, :FF], 384), by_rank(gateup_weight[:, FF:], 384)], axis=2
    ).transpose(1, 0, 2)
    frequency = ROPE_BASE ** (-jnp.arange(HD // 2, dtype=F32) * 2.0 / HD)
    (
        q_mine,
        kv_mine,
        all_tokens,
        down_low,
        output_wide,
        gateup_low,
        extras,
        gains_low,
        qkv_part,
        projected,
        cosine,
        sine,
        head_gains,
    ) = start(
        1,
        sent_a,
        sent_b,
        inputs,
        output_weight.astype(BF16),
        jnp.concatenate([down_weight[:, :512], down_weight[:, 512:]], axis=0).astype(BF16),
        jnp.concatenate([frequency, frequency])[None],
    )
    gains_all = gains_low.reshape(-1, 8, HD)[:, 0, :18].reshape(-1).astype(F32)
    attn_gain = gains_all[:D]
    ffn_gain = gains_all[D : 2 * D]

    blocks = extras[:4, 1, :BLOCK].astype(jnp.int32).reshape(4, 2, 4, 4, 2)
    pack_blocks = lax.dynamic_index_in_dim(blocks, at_x, 0, keepdims=False)
    key_blocks = pack_blocks.transpose(1, 2, 0, 3).reshape(-1)
    query_blocks = (
        lax.dynamic_index_in_dim(pack_blocks, at_y, 2, keepdims=False).transpose(1, 0, 2).reshape(-1)
    )
    q_mine = q_mine.reshape(1024, 256)
    kv_mine = kv_mine.reshape(PACK_TOK, 256)
    out_mine, lse = attend(query_blocks, key_blocks, q_mine, kv_mine)

    def to_x(ref, to):
        return ref.at[to["x"]]

    def from_pack_x(ref, frm):
        return ref.at[:, frm["x"]]

    result, grad_hidden, gains_grad, grad_mine, gateup_sum, down_total, output_lines = middle(
        2,
        out_mine.reshape(4, 2, ROWS, 256),
        output_wide.reshape(256, D),
        gateup_low,
        down_low,
        inputs,
        cotangent[0],
        jnp.stack([attn_gain, ffn_gain]),
    )
    dq_mine, dkv_mine = attend_back(
        query_blocks, key_blocks, q_mine, kv_mine, grad_mine.reshape(1024, 256), out_mine, lse
    )
    token_grad, summed_a, summed_b, output_sum, down_sides, gains_total = end(
        3,
        dq_mine.reshape(4, 2, ROWS, 256),
        dkv_mine.reshape(PLANE, 2, ROWS, 256),
        projected,
        cosine,
        sine,
        head_gains,
        all_tokens,
        qkv_part,
        output_lines,
        down_total,
        gateup_sum.reshape(RANKS, 8, 768),
        grad_hidden,
        gains_grad,
    )
    gains_sum = lax.dynamic_slice_in_dim(
        gains_total.reshape(-1), lax.axis_index(AXES) * norm_gains.shape[0], norm_gains.shape[0]
    )
    down_sum = jnp.concatenate([down_sides[:24], down_sides[24:]], axis=1)
    wide_a, wide_b = summed_a.transpose(1, 0, 2), summed_b.transpose(1, 0, 2)
    query_sum = wide_a[:, :, :256].reshape(8, 2048)
    keyval_sum = jnp.concatenate(
        [wide_a[:, :, 256:384].reshape(8, KV), wide_a[:, :, 384:].reshape(8, KV)], axis=1
    )
    gateup_total = jnp.concatenate(
        [wide_b[:, :, :384].reshape(8, FF), wide_b[:, :, 384:].reshape(8, FF)], axis=1
    )

    query_new, query_mean_new, query_square_new = adam_update(
        query_weight, query_sum, query_mean, query_square, RATE_MATRIX, DECAY
    )
    keyval_new, keyval_mean_new, keyval_square_new = adam_update(
        keyval_weight, keyval_sum, keyval_mean, keyval_square, RATE_MATRIX, DECAY
    )
    output_new, output_mean_new, output_square_new = adam_update(
        output_weight, output_sum, output_mean, output_square, RATE_MATRIX, DECAY
    )
    gateup_new, gateup_mean_new, gateup_square_new = adam_update(
        gateup_weight, gateup_total, gateup_mean, gateup_square, RATE_MATRIX, DECAY
    )
    down_new, down_mean_new, down_square_new = adam_update(
        down_weight, down_sum, down_mean, down_square, RATE_MATRIX, DECAY
    )
    gains_new, gains_mean_new, gains_square_new = adam_update(
        norm_gains, gains_sum, gains_mean, gains_square, RATE_GAIN, 0.0
    )
    return (
        result[None],
        token_grad[None],
        query_sum,
        keyval_sum,
        output_sum,
        gateup_total,
        down_sum,
        gains_sum,
        query_new,
        keyval_new,
        output_new,
        gateup_new,
        down_new,
        gains_new,
        query_mean_new,
        keyval_mean_new,
        output_mean_new,
        gateup_mean_new,
        down_mean_new,
        gains_mean_new,
        query_square_new,
        keyval_square_new,
        output_square_new,
        gateup_square_new,
        down_square_new,
        gains_square_new,
    )


def solution(mesh):
    fine = Mesh(mesh.devices.reshape([SIZE[a] for a in AXES]), AXES)
    rows = P(("zl", "co"), ("zh", "x", "y"), None)
    packs = P(("zl", "co"), None)
    matrix = P(AXES, None)
    vector = P(AXES)
    params = [matrix] * 5 + [vector]
    return jax.shard_map(
        body,
        mesh=fine,
        in_specs=(rows, rows, packs, packs, *params, *params, *params),
        out_specs=(rows, rows, *params, *params, *params, *params),
        check_vma=False,
    )
```

```python
import functools
import math

import jax
import jax.numpy as jnp
from jax import lax
from jax.experimental import pallas as pl
from jax.experimental.pallas import tpu as pltpu
from jax.sharding import Mesh
from jax.sharding import PartitionSpec as P

D = 1024
H = 16
KVH = 8
HD = 128
FF = 3072
KV = 1024
STEP = 10
LONG = 3072
ROWS = 128
BLOCK = 64
CHUNK = 1024
TOGETHER = 4
PACK_TOK = 4096
RANKS = 8
PLANE = 16


NORM_EPS = 1e-06
ROPE_BASE = 1000000.0
BETA_ONE = 0.9
BETA_TWO = 0.95
ADAM_EPS = 1e-08
DECAY = 0.1
RATE_MATRIX = 0.1
RATE_GAIN = 0.3

SCALE = HD**-0.5
LOG2E = math.log2(math.e)

AXES = ("zh", "x", "y", "zl", "co")
SIZE = {"zh": 2, "x": 4, "y": 4, "zl": 2, "co": 2}
COLUMN = ("zh", "zl", "co")
SURFACE = ("x", "y")
MESH = pl.DeviceIdType.MESH
F32 = jnp.float32
BF16 = jnp.bfloat16
VMEM_LIMIT = 50 * 1024 * 1024


def where_am_i():
    return {a: lax.axis_index(a) for a in AXES}


def address(place):
    return tuple(place[a] for a in AXES)


def flat_index(place, axes):
    at = 0
    for a in axes:
        at = at * SIZE[a] + place[a]
    return at


def shifted(place, axes, k, sign):
    to = dict(place)
    for a in reversed(axes):
        step = lax.rem(k, SIZE[a])
        k = lax.div(k, SIZE[a])
        to[a] = lax.rem(place[a] + sign * step + SIZE[a], SIZE[a])
    return to


def column_place(me, z, core):
    return dict(me, zh=lax.div(z, 2), zl=lax.rem(z, 2), co=core)


def dot_nn(a, b):
    return lax.dot_general(a, b, (((1,), (0,)), ((), ())), preferred_element_type=F32)


def dot_nt(a, b):
    return lax.dot_general(a, b, (((1,), (1,)), ((), ())), preferred_element_type=F32)


def dot_tn(a, b):
    return lax.dot_general(a, b, (((0,), (0,)), ((), ())), preferred_element_type=F32)


def stacked_heads(ref, tile):
    rows = ref[pl.ds(tile * BLOCK, BLOCK), :]
    return jnp.concatenate([rows[:, :HD], rows[:, HD:]], axis=0)


def allowed_keys(block, chunk):
    keys = chunk * CHUNK + lax.broadcasted_iota(jnp.int32, (CHUNK, 2 * BLOCK), 0)
    lanes = lax.broadcasted_iota(jnp.int32, (CHUNK, 2 * BLOCK), 1)
    return keys <= block * BLOCK + lax.rem(lanes, BLOCK)


def first_chunk(block):
    return jnp.where(block >= LONG // BLOCK, LONG // CHUNK, 0)


def attend_kernel(q_blocks, k_blocks, q_ref, kv_ref, out_ref, lse_ref, keys, values, values_t):
    def sort(i, carry):
        to = pl.multiple_of(k_blocks[i] * BLOCK, BLOCK)
        here = pl.multiple_of(i * BLOCK, BLOCK)
        keys[pl.ds(to, BLOCK), :] = kv_ref[pl.ds(here, BLOCK), :HD]
        values[pl.ds(to, BLOCK), :] = kv_ref[pl.ds(here, BLOCK), HD:]
        return carry

    lax.fori_loop(0, PACK_TOK // BLOCK, sort, 0)
    for c in range(PACK_TOK // CHUNK):
        part = values[c * CHUNK : (c + 1) * CHUNK, :].astype(F32)
        values_t[c] = part.T.astype(BF16)

    def one_chunk(query, block, c, state, masked):
        total, mixed = state
        chunk_keys = keys[pl.ds(pl.multiple_of(c * CHUNK, CHUNK), CHUNK), :]
        weights = jnp.exp2(dot_nt(chunk_keys, query) * (SCALE * LOG2E))
        if masked:
            weights = jnp.where(allowed_keys(block, c), weights, 0.0)
        total = total + jnp.sum(weights, axis=0, keepdims=True)
        mixed = mixed + dot_nn(values_t[c], weights.astype(BF16))
        return total, mixed

    def some_tiles(group, carry):
        tiles = [TOGETHER * group + u for u in range(TOGETHER)]
        blocks = [q_blocks[tile] for tile in tiles]
        queries = [stacked_heads(q_ref, tile) for tile in tiles]
        firsts = [first_chunk(block) for block in blocks]
        lasts = [lax.div(block, CHUNK // BLOCK) for block in blocks]
        full = [last - first for first, last in zip(firsts, lasts)]
        common = functools.reduce(jnp.minimum, full)

        def step(u, j, state):
            return one_chunk(queries[u], blocks[u], firsts[u] + j, state, False)

        empty = (jnp.zeros((1, 2 * BLOCK), F32), jnp.zeros((HD, 2 * BLOCK), F32))
        states = lax.fori_loop(
            0,
            common,
            lambda j, s: tuple(step(u, j, s[u]) for u in range(TOGETHER)),
            (empty,) * TOGETHER,
        )
        states = [
            lax.fori_loop(common, full[u], functools.partial(step, u), states[u]) for u in range(TOGETHER)
        ]
        states = [
            one_chunk(queries[u], blocks[u], lasts[u], states[u], True) for u in range(TOGETHER)
        ]
        for tile, (total, mixed) in zip(tiles, states):
            result = (mixed / total).T.astype(BF16)
            rows = pl.ds(pl.multiple_of(tile * BLOCK, BLOCK), BLOCK)
            out_ref[rows, :HD] = result[:BLOCK]
            out_ref[rows, HD:] = result[BLOCK:]
            lse_ref[pl.ds(tile, 1), :] = jnp.log2(total)
        return carry

    lax.fori_loop(0, q_ref.shape[0] // BLOCK // TOGETHER, some_tiles, 0)


def attend(q_blocks, k_blocks, q, kv):
    smem = pl.BlockSpec(memory_space=pltpu.SMEM)
    vmem = pl.BlockSpec(memory_space=pltpu.VMEM)
    tiles = q.shape[0] // BLOCK
    return pl.pallas_call(
        attend_kernel,
        out_shape=(
            jax.ShapeDtypeStruct(q.shape, BF16),
            jax.ShapeDtypeStruct((tiles, 2 * BLOCK), F32),
        ),
        in_specs=[smem, smem, vmem, vmem],
        out_specs=(vmem, vmem),
        scratch_shapes=[
            pltpu.VMEM((PACK_TOK, HD), BF16),
            pltpu.VMEM((PACK_TOK, HD), BF16),
            pltpu.VMEM((PACK_TOK // CHUNK, HD, CHUNK), BF16),
        ],
        compiler_params=pltpu.CompilerParams(vmem_limit_bytes=VMEM_LIMIT),
        cost_estimate=pl.CostEstimate(
            flops=4 * 10**9, bytes_accessed=4 * 10**6, transcendentals=8 * 10**6
        ),
        name="attend",
    )(q_blocks, k_blocks, q, kv)


def attend_back_kernel(
    q_blocks,
    k_blocks,
    q_ref,
    kv_ref,
    grad_ref,
    out_ref,
    lse_ref,
    dq_ref,
    dkv_ref,
    keys,
    values,
    keys_t,
    dk,
    dv,
):
    def sort(i, carry):
        to = pl.multiple_of(k_blocks[i] * BLOCK, BLOCK)
        here = pl.multiple_of(i * BLOCK, BLOCK)
        keys[pl.ds(to, BLOCK), :] = kv_ref[pl.ds(here, BLOCK), :HD]
        values[pl.ds(to, BLOCK), :] = kv_ref[pl.ds(here, BLOCK), HD:]
        return carry

    lax.fori_loop(0, PACK_TOK // BLOCK, sort, 0)
    for c in range(PACK_TOK // CHUNK):
        part = keys[c * CHUNK : (c + 1) * CHUNK, :].astype(F32)
        keys_t[c] = part.T.astype(BF16)
    dk[...] = jnp.zeros_like(dk)
    dv[...] = jnp.zeros_like(dv)

    def one_chunk(given, block, c, dq, masked):
        query, grad, inner, lse = given
        rows = pl.ds(pl.multiple_of(c * CHUNK, CHUNK), CHUNK)
        probs = jnp.exp2(dot_nt(keys[rows, :], query) * (SCALE * LOG2E) - lse)
        if masked:
            probs = jnp.where(allowed_keys(block, c), probs, 0.0)
        grad_probs = dot_nt(values[rows, :], grad)
        grad_scores = (probs * (grad_probs - inner)).astype(BF16)
        dv[rows, :] += dot_nn(probs.astype(BF16), grad)
        dk[rows, :] += dot_nn(grad_scores, query)
        return dq + dot_nn(keys_t[c], grad_scores)

    def some_tiles(group, carry):
        tiles = [TOGETHER * group + u for u in range(TOGETHER)]
        blocks = [q_blocks[tile] for tile in tiles]
        given = []
        for tile in tiles:
            query, grad = stacked_heads(q_ref, tile), stacked_heads(grad_ref, tile)
            out = stacked_heads(out_ref, tile)
            inner = jnp.sum((grad.astype(F32) * out.astype(F32)).T, axis=0, keepdims=True)
            given.append((query, grad, inner, lse_ref[pl.ds(tile, 1), :]))
        firsts = [first_chunk(block) for block in blocks]
        lasts = [lax.div(block, CHUNK // BLOCK) for block in blocks]
        full = [last - first for first, last in zip(firsts, lasts)]
        common = functools.reduce(jnp.minimum, full)

        def step(u, j, dq):
            return one_chunk(given[u], blocks[u], firsts[u] + j, dq, False)

        empty = jnp.zeros((HD, 2 * BLOCK), F32)
        dqs = lax.fori_loop(
            0,
            common,
            lambda j, s: tuple(step(u, j, s[u]) for u in range(TOGETHER)),
            (empty,) * TOGETHER,
        )
        dqs = [
            lax.fori_loop(common, full[u], functools.partial(step, u), dqs[u]) for u in range(TOGETHER)
        ]
        dqs = [
            one_chunk(given[u], blocks[u], lasts[u], dqs[u], True) for u in range(TOGETHER)
        ]
        for tile, dq in zip(tiles, dqs):
            dq = (dq * SCALE).T.astype(BF16)
            rows = pl.ds(pl.multiple_of(tile * BLOCK, BLOCK), BLOCK)
            dq_ref[rows, :HD] = dq[:BLOCK]
            dq_ref[rows, HD:] = dq[BLOCK:]
        return carry

    lax.fori_loop(0, q_ref.shape[0] // BLOCK // TOGETHER, some_tiles, 0)

    def unsort(i, carry):
        at = pl.multiple_of(k_blocks[i] * BLOCK, BLOCK)
        here = pl.multiple_of(i * BLOCK, BLOCK)
        dkv_ref[pl.ds(here, BLOCK), :HD] = (dk[pl.ds(at, BLOCK), :] * SCALE).astype(BF16)
        dkv_ref[pl.ds(here, BLOCK), HD:] = dv[pl.ds(at, BLOCK), :].astype(BF16)
        return carry

    lax.fori_loop(0, PACK_TOK // BLOCK, unsort, 0)


def attend_back(q_blocks, k_blocks, q, kv, grad, out, lse):
    smem = pl.BlockSpec(memory_space=pltpu.SMEM)
    vmem = pl.BlockSpec(memory_space=pltpu.VMEM)
    return pl.pallas_call(
        attend_back_kernel,
        out_shape=(
            jax.ShapeDtypeStruct(q.shape, BF16),
            jax.ShapeDtypeStruct(kv.shape, BF16),
        ),
        in_specs=[smem, smem] + [vmem] * 5,
        out_specs=(vmem, vmem),
        scratch_shapes=[
            pltpu.VMEM((PACK_TOK, HD), BF16),
            pltpu.VMEM((PACK_TOK, HD), BF16),
            pltpu.VMEM((PACK_TOK // CHUNK, HD, CHUNK), BF16),
            pltpu.VMEM((PACK_TOK, HD), F32),
            pltpu.VMEM((PACK_TOK, HD), F32),
        ],
        compiler_params=pltpu.CompilerParams(vmem_limit_bytes=VMEM_LIMIT),
        cost_estimate=pl.CostEstimate(
            flops=10**10, bytes_accessed=8 * 10**6, transcendentals=8 * 10**6
        ),
        name="attend_back",
    )(q_blocks, k_blocks, q, kv, grad, out, lse)


class ColumnSums:
    def __init__(self, me, part, paired, sending, landed, near_send, near_recv, far_send, far_recv):
        self.me, self.z, self.core = me, me["zh"] * 2 + me["zl"], me["co"]
        self.part, self.paired, self.sending, self.landed = part, paired, sending, landed
        self.near_sems, self.far_sems = (near_send, near_recv), (far_send, far_recv)
        self.rows = part.shape[-2]
        self.top, self.low = pl.ds(0, self.rows // 2), pl.ds(self.rows // 2, self.rows // 2)

    def near(self, phase, off):
        return pltpu.make_async_remote_copy(
            src_ref=self.part.at[phase, lax.rem(self.z + off, 4), 1 - self.core],
            dst_ref=self.paired.at[phase, off],
            send_sem=self.near_sems[0].at[phase, off],
            recv_sem=self.near_sems[1].at[phase, off],
            device_id=address(column_place(self.me, self.z, 1 - self.core)),
            device_id_type=MESH,
        )

    def far(self, phase, which):
        slot = which if which in (1, 3) else 2
        src, dst = self.sending.at[phase, slot], self.landed.at[phase, slot]
        if slot == 2:
            half = self.top if which == 2 else self.low
            src, dst = src.at[half], dst.at[half]
        step = 1 if which in (1, 2) else 3
        return pltpu.make_async_remote_copy(
            src_ref=src,
            dst_ref=dst,
            send_sem=self.far_sems[0].at[phase, which],
            recv_sem=self.far_sems[1].at[phase, which],
            device_id=address(column_place(self.me, lax.rem(self.z + step, 4), self.core)),
            device_id_type=MESH,
        )

    def put(self, phase, off, terms):
        self.part[phase, lax.rem(self.z + off, 4)] = terms.astype(BF16).reshape(2, self.rows, D)
        self.near(phase, off).start()

    def put_all(self, phase, terms):
        self.part[phase] = terms.astype(BF16).reshape(4, 2, self.rows, D)
        for off in (2, 1, 3, 0):
            self.near(phase, off).start()

    def chip_sum(self, phase, off):
        self.near(phase, off).wait_recv()
        mine = self.part[phase, lax.rem(self.z + off, 4), self.core].astype(F32)
        return mine + self.paired[phase, off].astype(F32)

    def first(self, phase):
        self.sending[phase, 2] = self.chip_sum(phase, 2).astype(BF16)
        self.far(phase, 2).start()
        self.far(phase, 0).start()

    def second(self, phase):
        for which, by_way, half in ((1, 2, self.top), (3, 0, self.low)):
            self.sending[phase, which] = self.chip_sum(phase, which).astype(BF16)
            self.far(phase, by_way).wait_recv()
            both = self.sending[phase, which, half].astype(F32)
            both = both + self.landed[phase, 2, half].astype(F32)
            self.sending[phase, which, half] = both.astype(BF16)
            self.far(phase, which).start()

    def total(self, phase):
        total = self.chip_sum(phase, 0)
        for which in (1, 3):
            self.far(phase, which).wait_recv()
            total = total + self.landed[phase, which].astype(F32)
        return total

    def drain(self, phase):
        for off in range(4):
            self.near(phase, off).wait_send()
            self.far(phase, off).wait_send()


class ColumnGathers:
    def __init__(self, me, blocks, near_send, near_recv, far_send, far_recv):
        self.me, self.z, self.core = me, me["zh"] * 2 + me["zl"], me["co"]
        self.blocks = blocks
        self.near_sems, self.far_sems = (near_send, near_recv), (far_send, far_recv)
        self.rows = blocks.shape[-2]

    def far(self, phase, which, arriving):
        step = 1 if which in (1, 2) else 3
        back = (step if which in (1, 3) else 2 * step) if arriving else (0 if which in (1, 3) else step)
        block = self.blocks.at[phase, lax.rem(self.z + 4 * 2 - back, 4) * 2 + self.core]
        if which == 2:
            block = block.at[pl.ds(0, self.rows // 2)]
        if which == 0:
            block = block.at[pl.ds(self.rows // 2, self.rows // 2)]
        return pltpu.make_async_remote_copy(
            src_ref=block,
            dst_ref=block,
            send_sem=self.far_sems[0].at[phase, which],
            recv_sem=self.far_sems[1].at[phase, which],
            device_id=address(column_place(self.me, lax.rem(self.z + step, 4), self.core)),
            device_id_type=MESH,
        )

    def near(self, phase, off, arriving):
        core = 1 - self.core if arriving else self.core
        block = self.blocks.at[phase, lax.rem(self.z + 4 - off, 4) * 2 + core]
        return pltpu.make_async_remote_copy(
            src_ref=block,
            dst_ref=block,
            send_sem=self.near_sems[0].at[phase, off],
            recv_sem=self.near_sems[1].at[phase, off],
            device_id=address(column_place(self.me, self.z, 1 - self.core)),
            device_id_type=MESH,
        )

    def begin(self, phase, rows):
        self.blocks[phase, self.z * 2 + self.core] = rows
        for off in (1, 3):
            self.far(phase, off, False).start()
        self.near(phase, 0, False).start()

    def pass_on(self, phase):
        for off, by_way in ((1, 2), (3, 0)):
            self.far(phase, off, True).wait_recv()
            self.far(phase, by_way, False).start()
            self.near(phase, off, False).start()

    def await_chip(self, phase, i):
        off = i + lax.div(i, 2) * (5 - 2 * i)

        @pl.when(i == 3)
        def _():
            for by_way in (2, 0):
                self.far(phase, by_way, True).wait_recv()
            self.near(phase, 2, False).start()

        self.near(phase, off, True).wait_recv()
        return off, lax.rem(self.z + 4 - off, 4)

    def await_all(self, phase):
        for by_way in (2, 0):
            self.far(phase, by_way, True).wait_recv()
        self.near(phase, 2, False).start()
        for off in range(4):
            self.near(phase, off, True).wait_recv()

    def drain(self, phase):
        for off in range(4):
            self.near(phase, off, False).wait_send()
            self.far(phase, off, False).wait_send()


def norm_factor(values):
    return lax.rsqrt(jnp.mean(values * values, axis=-1, keepdims=True) + NORM_EPS)


def norm_back(values, norm_gain, grad):
    factor = norm_factor(values)
    scaled = grad * norm_gain
    inner = jnp.mean(values * scaled, axis=-1, keepdims=True)
    grad_gain = jnp.sum(grad * values * factor, axis=0, keepdims=True)
    return factor * scaled - values * (factor * factor * factor * inner), grad_gain


def gray(i):
    return i + lax.div(i, 2) * (5 - 2 * i)


def quarter(place):
    return place["zl"] * 2 + place["co"]


def at_quarter(place, t):
    return dict(place, zl=lax.div(t, 2), co=lax.rem(t, 2))


def greet(barrier, place):
    pl.semaphore_signal(barrier, inc=1, device_id=address(place), device_id_type=MESH)


def greet_all(me, column, swap):
    barrier = pltpu.get_barrier_semaphore()

    def greet_surface(k, carry):
        greet(barrier, shifted(me, SURFACE, k, 1))
        return carry

    def greet_column_all(k, carry):
        greet(barrier, shifted(me, COLUMN, k, 1))
        return carry

    lax.fori_loop(1, PLANE, greet_surface, 0)
    expected = PLANE - 1
    if column == "all":
        lax.fori_loop(1, RANKS, greet_column_all, 0)
        expected = expected + RANKS - 1
    else:
        z = me["zh"] * 2 + me["zl"]
        for off in (1, 2, 3):
            greet(barrier, column_place(me, lax.rem(z + off, 4), me["co"]))
        greet(barrier, column_place(me, z, 1 - me["co"]))
        expected = expected + 4
    if swap:
        at_home = me["x"] == quarter(me)

        @pl.when(jnp.logical_not(at_home))
        def _():
            greet(barrier, swap_partner(me))

        expected = expected + 1 - jnp.where(at_home, 1, 0)
    pl.semaphore_wait(barrier, expected)


def swap_partner(me):
    return at_quarter(dict(me, x=quarter(me)), me["x"])


class Swap:
    def __init__(self, me, src, dst, own_dst, sems):
        self.at_home = me["x"] == quarter(me)
        self.remote = lambda: pltpu.make_async_remote_copy(
            src_ref=src,
            dst_ref=dst,
            send_sem=sems.at[0],
            recv_sem=sems.at[1],
            device_id=address(swap_partner(me)),
            device_id_type=MESH,
        )
        self.own = lambda: pltpu.make_async_copy(src, own_dst, sems.at[0])

    def either(self, remote, own):
        @pl.when(self.at_home)
        def _():
            own()

        @pl.when(jnp.logical_not(self.at_home))
        def _():
            remote()

    def begin(self):
        self.either(lambda: self.remote().start(), lambda: self.own().start())

    def finish(self):
        def both():
            copy = self.remote()
            copy.wait_recv()
            copy.wait_send()

        self.either(both, lambda: self.own().wait())


class Exchange:
    def __init__(self, me, axes, take, put, send, recv):
        self.me, self.axes, self.take, self.put, self.send, self.recv = me, axes, take, put, send, recv
        self.n = math.prod(SIZE[a] for a in axes)
        self.mix = {4: 1, 8: 3, 16: 7}[self.n]

    def copy(self, k, arriving):
        to = shifted(self.me, self.axes, k, 1)
        frm = shifted(self.me, self.axes, k, -1) if arriving else self.me
        return pltpu.make_async_remote_copy(
            src_ref=self.take(to),
            dst_ref=self.put(frm),
            send_sem=self.send.at[k],
            recv_sem=self.recv.at[k],
            device_id=address(to),
            device_id_type=MESH,
        )

    def each(self, act):
        def one(j, carry):
            act(lax.rem(j * self.mix, self.n))
            return carry

        lax.fori_loop(1, self.n, one, 0)

    def begin(self):
        self.each(lambda k: self.copy(k, False).start())

    def arrive(self):
        self.each(lambda k: self.copy(k, True).wait_recv())

    def drain(self):
        self.each(lambda k: self.copy(k, False).wait_send())


class PlaneGathers:
    def __init__(self, me, views, first_send, first_recv, second_send, second_recv):
        self.me, self.views = me, views
        self.sems = ((first_send, first_recv), (second_send, second_recv))

    def copy(self, turn, view, half, k, arriving):
        axis = "xy"[half] if turn == 0 else "yx"[half]
        to = shifted(self.me, (axis,), k, 1)
        frm = shifted(self.me, (axis,), k, -1) if arriving else self.me
        one, many = self.views[view]
        block = one(half, frm["x"], frm["y"]) if turn == 0 else many(half, frm["yx"[half]])
        return pltpu.make_async_remote_copy(
            src_ref=block,
            dst_ref=block,
            send_sem=self.sems[turn][0].at[view, half, k],
            recv_sem=self.sems[turn][1].at[view, half, k],
            device_id=address(to),
            device_id_type=MESH,
        )

    def each(self, view, act):
        for half in range(2):
            for k in (1, 3, 2):
                act(half, k)

    def begin(self, view):
        self.each(view, lambda half, k: self.copy(0, view, half, k, False).start())

    def pass_on(self, view):
        for half in range(2):
            for k in (1, 3, 2):
                self.copy(0, view, half, k, True).wait_recv()
            for k in (1, 3, 2):
                self.copy(1, view, half, k, False).start()

    def arrive(self, view):
        self.each(view, lambda half, k: self.copy(1, view, half, k, True).wait_recv())

    def drain(self):
        for view in range(len(self.views)):
            for turn in range(2):
                self.each(
                    view, lambda half, k: self.copy(turn, view, half, k, False).wait_send()
                )


class PlaneSums:
    def __init__(self, me, lines, got, middle_sums, got_last, first_send, first_recv, last_send, last_recv):
        self.me, self.lines, self.got, self.sums, self.got_last = me, lines, got, middle_sums, got_last
        self.sems = ((first_send, first_recv), (last_send, last_recv))

    def row(self, half, at):
        return (half, at) if half == 0 else (half, slice(None), at)

    def copy(self, turn, half, k):
        axis = "xy"[half] if turn == 0 else "yx"[half]
        to = shifted(self.me, (axis,), k, 1)
        if turn == 0:
            src, dst = self.lines.at[self.row(half, to[axis])], self.got.at[half, k]
        else:
            src, dst = self.sums.at[half, to[axis]], self.got_last.at[half, k]
        return pltpu.make_async_remote_copy(
            src_ref=src,
            dst_ref=dst,
            send_sem=self.sems[turn][0].at[half, k],
            recv_sem=self.sems[turn][1].at[half, k],
            device_id=address(to),
            device_id_type=MESH,
        )

    def begin(self):
        for half in range(2):
            for k in (1, 3, 2):
                self.copy(0, half, k).start()

    def pass_on(self):
        for half in range(2):
            total = self.lines[self.row(half, self.me["xy"[half]])].astype(F32)
            for k in (1, 3, 2):
                self.copy(0, half, k).wait_recv()
                total = total + self.got[half, k].astype(F32)
            self.sums[half] = total.astype(BF16)
            for k in (1, 3, 2):
                self.copy(1, half, k).start()

    def total(self, half):
        total = self.sums[half, self.me["yx"[half]]].astype(F32)
        for k in (1, 3, 2):
            self.copy(1, half, k).wait_recv()
            total = total + self.got_last[half, k].astype(F32)
        return total

    def drain(self):
        for turn in range(2):
            for half in range(2):
                for k in (1, 3, 2):
                    self.copy(turn, half, k).wait_send()


def start_kernel(
    sent_a,
    sent_b,
    tokens,
    output_rows,
    down_rows,
    frequency,
    q_mine,
    kv_mine,
    all_tokens,
    down_low,
    output_wide,
    gateup_low,
    extra_out,
    gains_out,
    qkv_part,
    projected,
    cosine,
    sine,
    head_gains,
    shares_a,
    shares_b,
    wide,
    blocks,
    queries,
    keyvals,
    a_send,
    a_recv,
    b_send,
    b_recv,
    w_send,
    w_recv,
    row_send,
    row_recv,
    near_send,
    near_recv,
    far_send,
    far_recv,
    q_send,
    q_recv,
    kv_send,
    kv_recv,
    relay_send,
    relay_recv,
    swap_sems,
    own_sems,
):
    me = where_am_i()
    x, y = me["x"], me["y"]
    rank, here = flat_index(me, COLUMN), flat_index(me, SURFACE)
    gathers = ColumnGathers(me, blocks, near_send, near_recv, far_send, far_recv)
    to_a = Exchange(
        me,
        COLUMN,
        lambda to: sent_a.at[flat_index(to, COLUMN)],
        lambda frm: shares_a.at[flat_index(frm, COLUMN)],
        a_send,
        a_recv,
    )
    to_b = Exchange(
        me,
        COLUMN,
        lambda to: sent_b.at[flat_index(to, COLUMN)],
        lambda frm: shares_b.at[flat_index(frm, COLUMN)],
        b_send,
        b_recv,
    )
    spread = PlaneGathers(
        me,
        (
            (
                lambda half, x, y: wide.at[half, x, y],
                lambda half, at: wide.at[0, :, at] if half == 0 else wide.at[1, at],
            ),
            (
                lambda half, x, y: output_wide.at[y, x, :, pl.ds(half * 512, 512)],
                lambda half, at: (
                    output_wide.at[at, :, :, pl.ds(0, 512)]
                    if half == 0
                    else output_wide.at[:, at, :, pl.ds(512, 512)]
                ),
            ),
        ),
        w_send,
        w_recv,
        row_send,
        row_recv,
    )
    output_swap = Swap(
        me, output_rows, output_wide.at[y, quarter(me)], output_wide.at[y, x], swap_sems.at[0]
    )
    down_swap = Swap(me, down_rows, down_low, down_low, swap_sems.at[1])
    own_a = pltpu.make_async_copy(sent_a.at[rank], shares_a.at[rank], own_sems.at[0])
    own_b = pltpu.make_async_copy(sent_b.at[rank], shares_b.at[rank], own_sems.at[1])
    own_a.start()
    own_b.start()
    greet_all(me, "all", True)
    to_a.begin()
    output_swap.begin()
    gathers.begin(0, tokens[...])
    down_swap.begin()
    to_b.begin()

    own_a.wait()
    to_a.arrive()
    wide[:, x, y] = shares_a[...].astype(BF16).reshape(2, 32, 640)
    spread.begin(0)
    output_swap.finish()
    extra_out[...] = shares_a[:, :, 512:]

    lanes = lax.broadcasted_iota(jnp.int32, (BLOCK, HD), 1)
    place = lax.broadcasted_iota(jnp.int32, (BLOCK, HD), 0).astype(F32)

    def tables(j, carry):
        for half in range(2):
            first = shares_a[j, 2 + half : 3 + half, 512:]
            angles = (first * float(BLOCK) + place) * frequency[...]
            at = pl.ds(pl.multiple_of(j * ROWS + half * BLOCK, BLOCK), BLOCK)
            cosine[at, :] = jnp.cos(angles)
            sines = jnp.sin(angles)
            sine[at, :] = jnp.where(lanes < HD // 2, -sines, sines)
        return carry

    lax.fori_loop(0, RANKS, tables, 0)
    spread.pass_on(0)
    spread.begin(1)
    own_b.wait()
    to_b.arrive()
    gateup_low[...] = shares_b[...].astype(BF16).reshape(2, 32, 768)

    spread.arrive(0)
    qkv_part[...] = wide[..., :512].reshape(D, 512)
    extra = wide[..., 512:].reshape(D, HD)
    gains_out[...] = extra
    entry = 2 * D + lax.broadcasted_iota(jnp.int32, (HD, 2 * HD), 1)
    pick = (lax.broadcasted_iota(jnp.int32, (HD, 2 * HD), 0) == lax.rem(entry, 18)).astype(BF16)
    entries = 2 * D + lax.broadcasted_iota(jnp.int32, (D, 2 * HD), 1)
    owned = lax.broadcasted_iota(jnp.int32, (D, 2 * HD), 0) == 8 * lax.div(entries, 18)
    gains = jnp.sum(jnp.where(owned, dot_nn(extra, pick), 0.0), axis=0, keepdims=True)
    head_gains[0:1, :] = gains[:, :HD]
    head_gains[1:2, :] = gains[:, HD:]

    def q_copy(row_zh, pack):
        return pltpu.make_async_remote_copy(
            src_ref=queries.at[row_zh, pack],
            dst_ref=q_mine.at[x, row_zh],
            send_sem=q_send.at[row_zh, pack],
            recv_sem=q_recv.at[row_zh, x],
            device_id=address(dict(me, x=pack)),
            device_id_type=MESH,
        )

    def kv_copy(row_zh, pack):
        return pltpu.make_async_remote_copy(
            src_ref=keyvals.at[row_zh, pack],
            dst_ref=kv_mine.at[here, row_zh],
            send_sem=kv_send.at[row_zh, pack],
            recv_sem=kv_recv.at[row_zh, x],
            device_id=address(dict(me, x=pack)),
            device_id_type=MESH,
        )

    def q_own(row_zh):
        return pltpu.make_async_copy(
            queries.at[row_zh, x], q_mine.at[x, row_zh], own_sems.at[2 + row_zh]
        )

    def kv_own(row_zh):
        return pltpu.make_async_copy(
            keyvals.at[row_zh, x], kv_mine.at[here, row_zh], own_sems.at[4 + row_zh]
        )

    def relay(row_zh, from_x, which, arriving):
        step = 1 if which in (1, 2) else 3
        back = (step if which in (1, 3) else 2 * step) if arriving else (0 if which in (1, 3) else step)
        block = kv_mine.at[from_x * 4 + lax.rem(y + 8 - back, 4), row_zh]
        if which == 2:
            block = block.at[pl.ds(0, BLOCK)]
        if which == 0:
            block = block.at[pl.ds(BLOCK, BLOCK)]
        return pltpu.make_async_remote_copy(
            src_ref=block,
            dst_ref=block,
            send_sem=relay_send.at[row_zh, from_x, which],
            recv_sem=relay_recv.at[row_zh, from_x, which],
            device_id=address(dict(me, y=lax.rem(y + step, 4))),
            device_id_type=MESH,
        )

    def project(i, carry):
        off, at_z = gathers.await_chip(0, i)
        at = pl.ds(pl.multiple_of(at_z * 2 * ROWS, 2 * ROWS), 2 * ROWS)
        both = dot_nn(blocks[0, pl.ds(at_z * 2, 2)].reshape(2 * ROWS, D), qkv_part[...])
        projected[at, :] = both[:, :384]
        row_zh, first = lax.div(at_z, 2), lax.rem(at_z, 2) * 2
        for head in range(3):
            values = both[:, head * HD : (head + 1) * HD]
            gain = head_gains[1:2, :] if head == 2 else head_gains[0:1, :]
            normed = values * norm_factor(values) * gain
            turned = (
                normed * cosine[at, :] + pltpu.roll(normed, HD // 2, 1) * sine[at, :]
            ).astype(BF16)
            turned = turned.reshape(2, ROWS, HD)
            for at_core in range(2):
                if head == 2:
                    keyvals[row_zh, first + at_core, :, :HD] = turned[at_core]
                else:
                    queries[row_zh, first + at_core, :, head * HD : (head + 1) * HD] = turned[
                        at_core
                    ]
        values = both[:, 384:].astype(BF16).reshape(2, ROWS, HD)
        for at_core in range(2):
            pack = first + at_core
            keyvals[row_zh, pack, :, HD:] = values[at_core]

            @pl.when(pack != x)
            def _():
                kv_copy(row_zh, pack).start()
                q_copy(row_zh, pack).start()

            @pl.when(pack == x)
            def _():
                kv_own(row_zh).start()
                q_own(row_zh).start()

        return carry

    gathers.pass_on(0)
    lax.fori_loop(0, 4, project, 0)
    spread.pass_on(1)
    for i in range(RANKS):
        slot = pltpu.make_async_copy(blocks.at[0, i], all_tokens.at[i], own_sems.at[6 + i])
        slot.start()
    for row_zh in range(2):
        kv_own(row_zh).wait()
        for which in (1, 3):
            relay(row_zh, x, which, False).start()
    for off in (1, 3, 2):
        from_x = lax.rem(x + 4 - off, 4)
        to_x = lax.rem(x + off, 4)
        for row_zh in range(2):
            pltpu.make_async_remote_copy(
                src_ref=keyvals.at[row_zh, to_x],
                dst_ref=kv_mine.at[from_x * 4 + y, row_zh],
                send_sem=kv_send.at[row_zh, to_x],
                recv_sem=kv_recv.at[row_zh, from_x],
                device_id=address(dict(me, x=to_x)),
                device_id_type=MESH,
            ).wait_recv()
            for which in (1, 3):
                relay(row_zh, from_x, which, False).start()

    def forward(j, carry):
        off, row_zh = lax.div(j, 2), lax.rem(j, 2)
        from_x = lax.rem(x + 4 - gray(off), 4)
        for which, by_way in ((1, 2), (3, 0)):
            relay(row_zh, from_x, which, True).wait_recv()
            relay(row_zh, from_x, by_way, False).start()
        return carry

    lax.fori_loop(0, 8, forward, 0)
    for off in (1, 3, 2):
        from_x = lax.rem(x + 4 - off, 4)
        to_x = lax.rem(x + off, 4)
        for row_zh in range(2):
            pltpu.make_async_remote_copy(
                src_ref=queries.at[row_zh, to_x],
                dst_ref=q_mine.at[from_x, row_zh],
                send_sem=q_send.at[row_zh, to_x],
                recv_sem=q_recv.at[row_zh, from_x],
                device_id=address(dict(me, x=to_x)),
                device_id_type=MESH,
            ).wait()
            kv_copy(row_zh, to_x).wait_send()
    for row_zh in range(2):
        q_own(row_zh).wait()

    def finish(j, carry):
        row_zh, from_x = lax.div(j, 4), lax.rem(j, 4)
        for which in range(4):
            relay(row_zh, from_x, which, False).wait_send()
        for which in (2, 0):
            relay(row_zh, from_x, which, True).wait_recv()
        return carry

    lax.fori_loop(0, 8, finish, 0)
    spread.arrive(1)
    down_swap.finish()
    for i in range(RANKS):
        pltpu.make_async_copy(blocks.at[0, i], all_tokens.at[i], own_sems.at[6 + i]).wait()
    for exchange in (to_a, to_b, spread):
        exchange.drain()
    gathers.drain(0)


def start(number, sent_a, sent_b, tokens, output_rows, down_rows, frequency):
    anywhere = pl.BlockSpec(memory_space=pl.ANY)
    vmem = pl.BlockSpec(memory_space=pltpu.VMEM)
    dma = pltpu.SemaphoreType.DMA
    struct = jax.ShapeDtypeStruct
    return pl.pallas_call(
        start_kernel,
        out_shape=(
            struct((4, 2, ROWS, 256), BF16),
            struct((PLANE, 2, ROWS, 256), BF16),
            struct((RANKS, ROWS, D), BF16),
            struct((48, 512), BF16),
            struct((4, 4, 16, D), BF16),
            struct((2, 32, 768), BF16),
            struct((RANKS, 8, HD), F32),
            struct((D, HD), BF16),
            struct((D, 512), BF16),
            struct((RANKS * ROWS, 384), F32),
            struct((RANKS * ROWS, HD), F32),
            struct((RANKS * ROWS, HD), F32),
            struct((2, HD), F32),
        ),
        in_specs=[anywhere, anywhere, vmem, anywhere, anywhere, vmem],
        out_specs=(anywhere,) * 4 + (vmem,) * 9,
        scratch_shapes=[
            pltpu.VMEM((RANKS, 8, 640), F32),
            pltpu.VMEM((RANKS, 8, 768), F32),
            pltpu.VMEM((2, 4, 4, 32, 640), BF16),
            pltpu.VMEM((1, RANKS, ROWS, D), BF16),
            pltpu.VMEM((2, 4, ROWS, 256), BF16),
            pltpu.VMEM((2, 4, ROWS, 256), BF16),
        ]
        + [dma((RANKS,))] * 4
        + [dma((2, 2, 4))] * 4
        + [dma((1, 4))] * 4
        + [dma((2, 4))] * 4
        + [dma((2, 4, 4)), dma((2, 4, 4)), dma((2, 2)), dma((6 + RANKS,))],
        compiler_params=pltpu.CompilerParams(
            collective_id=number, has_side_effects=True, vmem_limit_bytes=VMEM_LIMIT
        ),
        name="start",
    )(sent_a, sent_b, tokens, output_rows, down_rows, frequency)


def middle_kernel(
    out_mine,
    wo,
    gateup_low,
    down_rows,
    inputs,
    upstream,
    gains,
    result,
    grad_hidden,
    gains_grad,
    grad_mine,
    gateup_sum,
    down_sum,
    output_lines,
    attended,
    blocks,
    part,
    paired,
    sending,
    landed,
    gate_up,
    activated,
    grad_gate,
    grad_attended,
    gateup_lines,
    down_grad,
    down_lines,
    branch,
    hidden,
    wgu,
    wd,
    down_wide,
    got,
    plane_sums,
    got_last,
    d_got,
    d_sums,
    d_got_last,
    near_send,
    near_recv,
    far_send,
    far_recv,
    gnear_send,
    gnear_recv,
    gfar_send,
    gfar_recv,
    att_send,
    att_recv,
    back_send,
    back_recv,
    plane_send,
    plane_recv,
    last_send,
    last_recv,
    w_send,
    w_recv,
    row_send,
    row_recv,
    down_send,
    down_recv,
    dlast_send,
    dlast_recv,
    own_sems,
):
    me = where_am_i()
    x = me["x"]
    z = me["zh"] * 2 + me["zl"]
    sums = ColumnSums(
        me, part, paired, sending, landed, near_send, near_recv, far_send, far_recv
    )
    gathers = ColumnGathers(me, blocks, gnear_send, gnear_recv, gfar_send, gfar_recv)
    own_wgu = pltpu.make_async_copy(gateup_low, wgu.at[:, x, me["y"]], own_sems.at[0])
    own_wgu.start()
    own_down = pltpu.make_async_copy(down_rows, down_wide.at[me["y"], x], own_sems.at[1])
    own_down.start()
    spread = PlaneGathers(
        me,
        (
            (
                lambda half, x, y: wgu.at[half, x, y],
                lambda half, at: wgu.at[0, :, at] if half == 0 else wgu.at[1, at],
            ),
            (
                lambda half, x, y: down_wide.at[y, x, :, pl.ds(half * 256, 256)],
                lambda half, at: (
                    down_wide.at[at, :, :, pl.ds(0, 256)]
                    if half == 0
                    else down_wide.at[:, at, :, pl.ds(256, 256)]
                ),
            ),
        ),
        w_send,
        w_recv,
        row_send,
        row_recv,
    )
    down_back = PlaneSums(
        me, down_lines, d_got, d_sums, d_got_last, down_send, down_recv, dlast_send, dlast_recv
    )
    gateup_back = PlaneSums(
        me, gateup_lines, got, plane_sums, got_last, plane_send, plane_recv, last_send, last_recv
    )

    def half_rows(half):
        return pl.ds(half * BLOCK, BLOCK)

    def own_out(half):
        return pltpu.make_async_copy(
            out_mine.at[x, :, half_rows(half)], attended.at[half, :, x], own_sems.at[2 + half]
        )

    def attention_out(half, k, arriving):
        frm = shifted(me, ("x",), k, -1) if arriving else me
        to = shifted(me, ("x",), k, 1)
        return pltpu.make_async_remote_copy(
            src_ref=out_mine.at[to["x"], :, half_rows(half)],
            dst_ref=attended.at[half, :, frm["x"]],
            send_sem=att_send.at[half, k],
            recv_sem=att_recv.at[half, k],
            device_id=address(to),
            device_id_type=MESH,
        )

    for half in range(2):
        own_out(half).start()
    greet_all(me, "some", False)
    for half in range(2):
        for k in (2, 1, 3):
            attention_out(half, k, False).start()
    own_wgu.wait()
    own_down.wait()
    spread.begin(0)
    spread.begin(1)

    def down_line_in(j, carry):
        at = pl.ds(pl.multiple_of(j * 48, 16), 48)
        pair = down_wide[lax.div(j, 2), pl.ds(lax.rem(j, 2) * 2, 2)].astype(F32)
        for side in range(2):
            rows = pair[:, side * 24 : side * 24 + 24].reshape(48, 512)
            wd[at, side * 512 : side * 512 + 512] = rows.astype(BF16)
        return carry

    def project_out(half):
        own_out(half).wait()
        for k in (1, 3, 2):
            attention_out(half, k, True).wait_recv()

        rows = attended[half].reshape(RANKS * BLOCK, 256)
        sums.put_all(half, dot_nn(rows, wo[...]))

    def block_rows(phase):
        return blocks[phase].reshape(RANKS * BLOCK, D)

    def at_half(half):
        return slice(half * RANKS * BLOCK, (half + 1) * RANKS * BLOCK)

    def attention_norm(half):
        at = half_rows(half)
        total = sums.total(half)
        branch[at, :] = total
        both = inputs[at, :].astype(F32) + total * norm_factor(total) * gains[0:1, :]
        hidden[at, :] = both
        gathers.begin(half, both.astype(BF16))

    def feed_forward(half):
        at = at_half(half)
        both = dot_nn(block_rows(half), wgu[...].reshape(D, 768))
        gate_up[at, :] = both
        gate, up = both[:, :384], both[:, 384:]
        acts = (gate * (1.0 / (1.0 + jnp.exp(-gate))) * up).astype(BF16)
        activated[at, :] = acts
        sums.put_all(2 + half, dot_nn(acts, wd[...]))

    def feed_forward_norm(half):
        at = half_rows(half)
        ffn_out = sums.total(2 + half)
        gain = gains[1:2, :]
        result[at, :] = (hidden[at, :] + ffn_out * norm_factor(ffn_out) * gain).astype(BF16)
        grad_ffn, grad_gain = norm_back(ffn_out, gain, upstream[at, :].astype(F32))
        gathers.begin(2 + half, grad_ffn.astype(BF16))
        return grad_gain

    def feed_forward_back(half):
        at = at_half(half)
        grad_act = dot_nt(block_rows(2 + half), wd[...])
        gate, up = gate_up[at, :384], gate_up[at, 384:]
        sig = 1.0 / (1.0 + jnp.exp(-gate))
        grad_gate[at, :384] = (grad_act * up * (sig * (1.0 + gate * (1.0 - sig)))).astype(BF16)
        grad_gate[at, 384:] = (grad_act * (gate * sig)).astype(BF16)
        sums.put_all(4 + half, dot_nt(grad_gate[at, :], wgu[...].reshape(D, 768)))

    def attention_norm_back(half):
        at = half_rows(half)
        total = upstream[at, :].astype(F32) + sums.total(4 + half)
        grad_hidden[at, :] = total
        grad_branch, grad_gain = norm_back(branch[at, :], gains[0:1, :], total)
        gathers.begin(4 + half, grad_branch.astype(BF16))
        return grad_gain

    def to_attention(half, row_zh, pack):
        return pltpu.make_async_remote_copy(
            src_ref=grad_attended.at[half, row_zh, pack],
            dst_ref=grad_mine.at[x, row_zh, half_rows(half)],
            send_sem=back_send.at[half, row_zh, pack],
            recv_sem=back_recv.at[half, row_zh, x],
            device_id=address(dict(me, x=pack)),
            device_id_type=MESH,
        )

    def own_attention(half, row_zh):
        return pltpu.make_async_copy(
            grad_attended.at[half, row_zh, x],
            grad_mine.at[x, row_zh, half_rows(half)],
            own_sems.at[4 + 2 * half + row_zh],
        )

    def project_out_back(half):
        grads = dot_nt(block_rows(4 + half), wo[...]).astype(BF16)
        grad_attended[half] = grads.reshape(2, 4, BLOCK, 256)
        for row_zh in range(2):
            own_attention(half, row_zh).start()
            for k in (1, 3, 2):
                to_attention(half, row_zh, lax.rem(x + k, 4)).start()

    def all_rows(phase):
        return blocks[phase : phase + 2].reshape(RANKS * ROWS, D)

    def down_line(s, carry):
        rows = down_grad[pl.ds(pl.multiple_of(s * 24, 8), 24), :].astype(BF16)
        at_y, at_x = lax.div(s, 4), lax.rem(s, 4)
        for half in range(2):
            for side in range(2):
                cols = slice(side * 512 + half * 256, side * 512 + half * 256 + 256)
                down_lines[half, at_x, at_y, side * 24 : side * 24 + 24, :] = rows[:, cols]
        return carry

    def send_down():
        down_grad[...] = dot_tn(activated[...], all_rows(2))
        lax.fori_loop(0, PLANE, down_line, 0)
        down_back.begin()

    def send_gateup():
        grads = dot_tn(all_rows(0), grad_gate[...])
        gateup_lines[...] = grads.astype(BF16).reshape(2, 4, 4, 32, 768)
        gateup_back.begin()

    works = (project_out, feed_forward, feed_forward_back, project_out_back)
    thens = (attention_norm, feed_forward_norm, attention_norm_back)
    gain_grads = [None, None, None]
    works[0](0)
    sums.first(0)
    works[0](1)
    spread.pass_on(0)
    spread.pass_on(1)
    sums.second(0)
    for stage in range(3):
        phase = 2 * stage
        if stage == 2:
            send_down()
        gain_grads[stage] = thens[stage](0)
        if stage > 0:
            works[stage](1)
        sums.first(phase + 1)
        gathers.pass_on(phase)
        sums.second(phase + 1)
        if stage == 2:
            down_back.pass_on()
            send_gateup()
        gathers.await_all(phase)
        if stage == 0:
            spread.arrive(0)
            spread.arrive(1)
            lax.fori_loop(0, PLANE // 2, down_line_in, 0)
        works[stage + 1](0)
        other = thens[stage](1)
        if stage > 0:
            gains_grad[2 - stage : 3 - stage, :] = gain_grads[stage] + other
        if stage < 2:
            sums.first(phase + 2)
        gathers.pass_on(phase + 1)
        if stage < 2:
            sums.second(phase + 2)
        if stage == 2:
            gateup_back.pass_on()
        gathers.await_all(phase + 1)
    works[3](1)
    grads = dot_tn(attended[...].reshape(RANKS * ROWS, 256), all_rows(4))
    for line in range(PLANE):
        rows = grads[line * 16 : line * 16 + 16].astype(BF16)
        for half in range(2):
            output_lines[half, line % 4, line // 4] = rows[:, half * 512 : half * 512 + 512]

    for half in range(2):
        for k in (1, 3, 2):
            attention_out(half, k, False).wait_send()
            frm_x = lax.rem(x + 4 - k, 4)
            to_x = lax.rem(x + k, 4)
            for row_zh in range(2):
                to_attention(half, row_zh, to_x).wait_send()
                pltpu.make_async_remote_copy(
                    src_ref=grad_attended.at[half, row_zh, to_x],
                    dst_ref=grad_mine.at[frm_x, row_zh, half_rows(half)],
                    send_sem=back_send.at[half, row_zh, to_x],
                    recv_sem=back_recv.at[half, row_zh, frm_x],
                    device_id=address(dict(me, x=to_x)),
                    device_id_type=MESH,
                ).wait_recv()
        for row_zh in range(2):
            own_attention(half, row_zh).wait()
    for phase in range(6):
        sums.drain(phase)
        gathers.drain(phase)
    for half in range(2):
        down_sum[:, half * 256 : half * 256 + 256] = down_back.total(half)
        gateup_sum[half] = gateup_back.total(half)
    for exchange in (spread, gateup_back, down_back):
        exchange.drain()


def middle(number, out_mine, wo, gateup_low, down_rows, inputs, upstream, gains):
    anywhere = pl.BlockSpec(memory_space=pl.ANY)
    vmem = pl.BlockSpec(memory_space=pltpu.VMEM)
    block, half = (ROWS, D), (BLOCK, D)
    dma = pltpu.SemaphoreType.DMA
    return pl.pallas_call(
        middle_kernel,
        out_shape=(
            jax.ShapeDtypeStruct(block, BF16),
            jax.ShapeDtypeStruct(block, F32),
            jax.ShapeDtypeStruct((2, D), F32),
            jax.ShapeDtypeStruct((4, 2, ROWS, 256), BF16),
            jax.ShapeDtypeStruct((2, 32, 768), F32),
            jax.ShapeDtypeStruct((48, 512), F32),
            jax.ShapeDtypeStruct((2, 4, 4, 16, 512), BF16),
        ),
        in_specs=[anywhere, vmem, anywhere, anywhere, vmem, vmem, vmem],
        out_specs=(vmem, vmem, vmem, anywhere, vmem, vmem, vmem),
        scratch_shapes=[
            pltpu.VMEM((2, 2, 4, BLOCK, 256), BF16),
            pltpu.VMEM((6, RANKS) + half, BF16),
            pltpu.VMEM((6, 4, 2) + half, BF16),
            pltpu.VMEM((6, 4) + half, BF16),
            pltpu.VMEM((6, 4) + half, BF16),
            pltpu.VMEM((6, 4) + half, BF16),
            pltpu.VMEM((RANKS * ROWS, 768), F32),
            pltpu.VMEM((RANKS * ROWS, 384), BF16),
            pltpu.VMEM((RANKS * ROWS, 768), BF16),
            pltpu.VMEM((2, 2, 4, BLOCK, 256), BF16),
            pltpu.VMEM((2, 4, 4, 32, 768), BF16),
            pltpu.VMEM((384, D), F32),
            pltpu.VMEM((2, 4, 4, 48, 256), BF16),
            pltpu.VMEM(block, F32),
            pltpu.VMEM(block, F32),
            pltpu.VMEM((2, 4, 4, 32, 768), BF16),
            pltpu.VMEM((384, D), BF16),
            pltpu.VMEM((4, 4, 48, 512), BF16),
            pltpu.VMEM((2, 4, 4, 32, 768), BF16),
            pltpu.VMEM((2, 4, 32, 768), BF16),
            pltpu.VMEM((2, 4, 32, 768), BF16),
            pltpu.VMEM((2, 4, 4, 48, 256), BF16),
            pltpu.VMEM((2, 4, 48, 256), BF16),
            pltpu.VMEM((2, 4, 48, 256), BF16),
        ]
        + [dma((6, 4))] * 8
        + [dma((2, 4)), dma((2, 4)), dma((2, 2, 4)), dma((2, 2, 4))]
        + [dma((2, 4))] * 4
        + [dma((2, 2, 4))] * 4
        + [dma((2, 4))] * 4
        + [dma((8,))],
        compiler_params=pltpu.CompilerParams(
            collective_id=number, has_side_effects=True, vmem_limit_bytes=VMEM_LIMIT
        ),
        name="middle",
    )(out_mine, wo, gateup_low, down_rows, inputs, upstream, gains)


def end_kernel(
    dq_mine,
    dkv_mine,
    projected,
    cosine,
    sine,
    head_gains,
    all_tokens,
    qkv_part,
    output_lines,
    down_total,
    column_b,
    grad_hidden,
    gains_grad,
    token_grad,
    summed_a,
    summed_b,
    output_sum,
    down_sum,
    gains_sum,
    across,
    besides,
    landed_kv,
    passing,
    dq_all,
    dkv_all,
    grad_qkv,
    part,
    paired,
    sending,
    landed,
    qkv_lines,
    q_got,
    q_sums,
    q_got_last,
    o_got,
    o_sums,
    o_got_last,
    output_total,
    column_a,
    gains_column,
    gains_plane,
    ring_send,
    ring_recv,
    kv_send,
    kv_recv,
    dq_send,
    dq_recv,
    near_send,
    near_recv,
    far_send,
    far_recv,
    plane_send,
    plane_recv,
    qlast_send,
    qlast_recv,
    row_send,
    row_recv,
    olast_send,
    olast_recv,
    gplane_send,
    gplane_recv,
    swap_sems,
    a_send,
    a_recv,
    b_send,
    b_recv,
    gcolumn_send,
    gcolumn_recv,
    own_sems,
):
    me = where_am_i()
    x, y, z = me["x"], me["y"], me["zh"] * 2 + me["zl"]
    rank, here = flat_index(me, COLUMN), flat_index(me, SURFACE)
    sums = ColumnSums(
        me, part, paired, sending, landed, near_send, near_recv, far_send, far_recv
    )

    def by_column(ref, out, send, recv):
        return Exchange(
            me,
            COLUMN,
            lambda to: ref.at[flat_index(to, COLUMN)],
            lambda frm: out.at[flat_index(frm, COLUMN)],
            send,
            recv,
        )

    to_a = by_column(column_a, summed_a, a_send, a_recv)
    to_b = by_column(column_b, summed_b, b_send, b_recv)
    gains_in = Exchange(
        me,
        COLUMN,
        lambda to: gains_column.at[rank],
        lambda frm: gains_column.at[flat_index(frm, COLUMN)],
        gcolumn_send,
        gcolumn_recv,
    )
    gains_over = Exchange(
        me,
        SURFACE,
        lambda to: gains_plane.at[here],
        lambda frm: gains_plane.at[flat_index(frm, SURFACE)],
        gplane_send,
        gplane_recv,
    )
    qkv_back = PlaneSums(
        me, qkv_lines, q_got, q_sums, q_got_last, plane_send, plane_recv, qlast_send, qlast_recv
    )
    queries = Exchange(
        me,
        ("x",),
        lambda to: dq_mine.at[to["x"]],
        lambda frm: dq_all.at[:, frm["x"]],
        dq_send,
        dq_recv,
    )
    output_back = PlaneSums(
        me, output_lines, o_got, o_sums, o_got_last, row_send, row_recv, olast_send, olast_recv
    )
    output_swap = Swap(me, output_total, output_sum, output_sum, swap_sems.at[0])
    down_swap = Swap(me, down_total, down_sum, down_sum, swap_sems.at[1])
    own_dq = pltpu.make_async_copy(dq_mine.at[x], dq_all.at[:, x], own_sems.at[4])
    own_a = pltpu.make_async_copy(column_a.at[rank], summed_a.at[rank], own_sems.at[6])
    own_b = pltpu.make_async_copy(column_b.at[rank], summed_b.at[rank], own_sems.at[7])

    def ring(j, which):
        to_x = lax.rem(x + j, 4)
        step = 1 if which in (1, 2) else 3
        if which in (1, 3):
            src, dst = besides.at[j, which // 2], landed_kv.at[j, which // 2]
        else:
            row_zh = 0 if which == 2 else 1
            src, dst = dkv_mine.at[to_x * 4 + lax.rem(y + 2, 4), row_zh], across.at[j, row_zh]
        return pltpu.make_async_remote_copy(
            src_ref=src,
            dst_ref=dst,
            send_sem=ring_send.at[j, which],
            recv_sem=ring_recv.at[j, which],
            device_id=address(dict(me, y=lax.rem(y + step, 4))),
            device_id_type=MESH,
        )

    def kv_copy(j, arriving):
        frm_x = lax.rem(x + 4 - j, 4) if arriving else x
        return pltpu.make_async_remote_copy(
            src_ref=passing.at[j],
            dst_ref=dkv_all.at[:, frm_x],
            send_sem=kv_send.at[j],
            recv_sem=kv_recv.at[j],
            device_id=address(dict(me, x=lax.rem(x + j, 4))),
            device_id_type=MESH,
        )

    own_dq.start()
    greet_all(me, "all", True)
    for j in (2, 1, 3, 0):
        for which in (2, 0):
            ring(j, which).start()
    queries.begin()
    down_swap.begin()
    for j in (2, 1, 3, 0):
        to_x = lax.rem(x + j, 4)
        for which, by_way, step in ((1, 2, 1), (3, 0, 3)):
            row_zh, other = (0, 1) if by_way == 2 else (1, 0)
            own_block = to_x * 4 + lax.rem(y + step, 4)
            besides[j, which // 2, other] = dkv_mine[own_block, other]
            ring(j, by_way).wait_recv()
            both = dkv_mine[own_block, row_zh].astype(F32) + across[j, row_zh].astype(F32)
            besides[j, which // 2, row_zh] = both.astype(BF16)
            ring(j, which).start()

    own_b.start()
    to_b.begin()

    for j in (2, 1, 3, 0):
        total = dkv_mine[lax.rem(x + j, 4) * 4 + y].astype(F32)
        for which in (1, 3):
            ring(j, which).wait_recv()
            total = total + landed_kv[j, which // 2].astype(F32)
        if j:
            passing[j] = total.astype(BF16)
            kv_copy(j, False).start()
        else:
            dkv_all[:, x] = total.astype(BF16)
    output_back.begin()
    own_dq.wait()
    queries.arrive()
    for j in (2, 1, 3):
        kv_copy(j, True).wait_recv()

    def project_back(i, carry):
        gain_q, gain_k = carry
        off = gray(3 - i)
        to_z = lax.rem(z + off, 4)
        at = pl.ds(pl.multiple_of(to_z * 2 * ROWS, 2 * ROWS), 2 * ROWS)
        row_zh, first = lax.div(to_z, 2), lax.rem(to_z, 2) * 2
        grad_q = dq_all[row_zh, pl.ds(first, 2)].reshape(2 * ROWS, 256).astype(F32)
        grad_kv = dkv_all[row_zh, pl.ds(first, 2)].reshape(2 * ROWS, 256)
        for head in range(3):
            if head == 2:
                grad, gain = grad_kv[:, :HD].astype(F32), head_gains[1:2, :]
            else:
                grad, gain = grad_q[:, head * HD : (head + 1) * HD], head_gains[0:1, :]
            turned = grad * cosine[at, :] - pltpu.roll(grad, HD // 2, 1) * sine[at, :]
            grad_in, grad_gain = norm_back(
                projected[at, head * HD : (head + 1) * HD], gain, turned
            )
            grad_qkv[at, head * HD : (head + 1) * HD] = grad_in.astype(BF16)
            if head == 2:
                gain_k = gain_k + grad_gain
            else:
                gain_q = gain_q + grad_gain
        grad_qkv[at, 384:] = grad_kv[:, HD:]
        sums.put(0, off, dot_nt(grad_qkv[at, :], qkv_part[...]))

        @pl.when(i == 1)
        def _():
            sums.first(0)

        return gain_q, gain_k

    nothing = jnp.zeros((1, HD), F32)
    gain_q, gain_k = lax.fori_loop(0, 4, project_back, (nothing, nothing))

    for j in range(16):
        gains_column[rank, j : j + 1, :] = gains_grad[
            j // 8 : j // 8 + 1, j % 8 * HD : (j % 8 + 1) * HD
        ]
    gains_column[rank, 16:17, :] = gain_q
    gains_column[rank, 17:18, :] = gain_k
    gains_column[rank, 18:24, :] = jnp.zeros((6, HD), F32)
    gains_in.begin()
    sums.second(0)
    output_back.pass_on()

    def qkv_rows(j, carry):
        cols = pl.ds(pl.multiple_of(j * 256, 256), 256)
        grads = dot_tn(all_tokens[:, :, cols].reshape(RANKS * ROWS, 256), grad_qkv[...])
        qkv_lines[lax.div(j, 2), pl.ds(lax.rem(j, 2) * 2, 2)] = grads.astype(BF16).reshape(
            2, 4, 32, 512
        )
        return carry

    lax.fori_loop(0, 4, qkv_rows, 0)
    qkv_back.begin()

    gains_in.arrive()
    gains_plane[here] = jnp.sum(gains_column[...], axis=0)
    gains_over.begin()
    token_grad[...] = grad_hidden[...] + sums.total(0)
    qkv_back.pass_on()
    for half in range(2):
        output_total[:, half * 512 : half * 512 + 512] = output_back.total(half)
    output_swap.begin()

    for half in range(2):
        column_a[pl.ds(half * 4, 4)] = qkv_back.total(half).reshape(4, 8, 512)
    own_a.start()
    to_a.begin()
    gains_over.arrive()
    gains_sum[...] = jnp.sum(gains_plane[...], axis=0)
    to_b.arrive()
    output_swap.finish()
    down_swap.finish()
    own_b.wait()
    for j in (2, 1, 3, 0):
        for which in range(4):
            ring(j, which).wait_send()
        if j:
            kv_copy(j, False).wait_send()
    sums.drain(0)
    for exchange in (queries, output_back, to_b, gains_in, gains_over, qkv_back):
        exchange.drain()
    own_a.wait()
    to_a.arrive()
    to_a.drain()


def end(number, *arrays):
    anywhere = pl.BlockSpec(memory_space=pl.ANY)
    vmem = pl.BlockSpec(memory_space=pltpu.VMEM)
    dma = pltpu.SemaphoreType.DMA
    struct = jax.ShapeDtypeStruct
    block = (ROWS, D)
    quarter_rows = (2, ROWS, 256)
    return pl.pallas_call(
        end_kernel,
        out_shape=(
            struct(block, F32),
            struct((RANKS, 8, 512), F32),
            struct((RANKS, 8, 768), F32),
            struct((16, D), F32),
            struct((48, 512), F32),
            struct((24, HD), F32),
        ),
        in_specs=[anywhere, vmem] + [vmem] * 6 + [vmem, anywhere, anywhere] + [vmem] * 2,
        out_specs=(vmem, anywhere, anywhere, anywhere, anywhere, vmem),
        scratch_shapes=[
            pltpu.VMEM((4,) + quarter_rows, BF16),
            pltpu.VMEM((4, 2) + quarter_rows, BF16),
            pltpu.VMEM((4, 2) + quarter_rows, BF16),
            pltpu.VMEM((4,) + quarter_rows, BF16),
            pltpu.VMEM((2, 4, ROWS, 256), BF16),
            pltpu.VMEM((2, 4, ROWS, 256), BF16),
            pltpu.VMEM((RANKS * ROWS, 512), BF16),
            pltpu.VMEM((1, 4, 2) + block, BF16),
            pltpu.VMEM((1, 4) + block, BF16),
            pltpu.VMEM((1, 4) + block, BF16),
            pltpu.VMEM((1, 4) + block, BF16),
            pltpu.VMEM((2, 4, 4, 32, 512), BF16),
            pltpu.VMEM((2, 4, 4, 32, 512), BF16),
            pltpu.VMEM((2, 4, 32, 512), BF16),
            pltpu.VMEM((2, 4, 32, 512), BF16),
            pltpu.VMEM((2, 4, 4, 16, 512), BF16),
            pltpu.VMEM((2, 4, 16, 512), BF16),
            pltpu.VMEM((2, 4, 16, 512), BF16),
            pltpu.VMEM((16, D), F32),
            pltpu.VMEM((RANKS, 8, 512), F32),
            pltpu.VMEM((RANKS, 24, HD), F32),
            pltpu.VMEM((PLANE, 24, HD), F32),
        ]
        + [dma((4, 4))] * 2
        + [dma((4,))] * 4
        + [dma((1, 4))] * 4
        + [dma((2, 4))] * 8
        + [dma((PLANE,))] * 2
        + [dma((2, 2))]
        + [dma((RANKS,))] * 6
        + [dma((8,))],
        compiler_params=pltpu.CompilerParams(
            collective_id=number, has_side_effects=True, vmem_limit_bytes=VMEM_LIMIT
        ),
        name="end",
    )(*arrays)


def adam_update(weight, gradient, mean_old, square_old, rate, decay):
    mean_new = BETA_ONE * mean_old + (1.0 - BETA_ONE) * gradient
    square_new = BETA_TWO * square_old + (1.0 - BETA_TWO) * gradient * gradient
    mean_hat = mean_new / (1.0 - BETA_ONE**STEP)
    square_hat = square_new / (1.0 - BETA_TWO**STEP)
    weight_new = weight - rate * (mean_hat / (jnp.sqrt(square_hat) + ADAM_EPS) + decay * weight)
    return (weight_new, mean_new, square_new)


def by_rank(array, width):
    return array.reshape(array.shape[0], RANKS, width)


def body(
    tokens,
    cotangent,
    positions,
    seq_ids,
    query_weight,
    keyval_weight,
    output_weight,
    gateup_weight,
    down_weight,
    norm_gains,
    query_mean,
    keyval_mean,
    output_mean,
    gateup_mean,
    down_mean,
    gains_mean,
    query_square,
    keyval_square,
    output_square,
    gateup_square,
    down_square,
    gains_square,
):
    inputs = tokens[0]
    at_x, at_y = lax.axis_index("x"), lax.axis_index("y")

    own_blocks = (positions[0] + LONG * seq_ids[0]).reshape(-1, BLOCK)[:, 0] // BLOCK
    own_pair = lax.dynamic_slice_in_dim(own_blocks, 2 * lax.axis_index(("zh", "x", "y")), 2)
    own_pair = jnp.where(own_pair >= LONG // BLOCK, own_pair - LONG // BLOCK, own_pair)
    extra = jnp.concatenate(
        [
            jnp.pad(norm_gains, (0, HD - norm_gains.shape[0]))[None],
            jnp.pad(own_blocks.astype(F32), (0, HD - BLOCK))[None],
            jnp.broadcast_to(own_pair.astype(F32)[:, None], (2, HD)),
            jnp.zeros((4, HD), F32),
        ]
    )
    sent_a = jnp.concatenate(
        [
            by_rank(query_weight, 256),
            by_rank(keyval_weight[:, :KV], 128),
            by_rank(keyval_weight[:, KV:], 128),
            jnp.broadcast_to(extra[:, None, :], (8, RANKS, HD)),
        ],
        axis=2,
    ).transpose(1, 0, 2)
    sent_b = jnp.concatenate(
        [by_rank(gateup_weight[:, :FF], 384), by_rank(gateup_weight[:, FF:], 384)], axis=2
    ).transpose(1, 0, 2)
    frequency = ROPE_BASE ** (-jnp.arange(HD // 2, dtype=F32) * 2.0 / HD)
    (
        q_mine,
        kv_mine,
        all_tokens,
        down_low,
        output_wide,
        gateup_low,
        extras,
        gains_low,
        qkv_part,
        projected,
        cosine,
        sine,
        head_gains,
    ) = start(
        1,
        sent_a,
        sent_b,
        inputs,
        output_weight.astype(BF16),
        jnp.concatenate([down_weight[:, :512], down_weight[:, 512:]], axis=0).astype(BF16),
        jnp.concatenate([frequency, frequency])[None],
    )
    gains_all = gains_low.reshape(-1, 8, HD)[:, 0, :18].reshape(-1).astype(F32)
    attn_gain = gains_all[:D]
    ffn_gain = gains_all[D : 2 * D]

    blocks = extras[:4, 1, :BLOCK].astype(jnp.int32).reshape(4, 2, 4, 4, 2)
    pack_blocks = lax.dynamic_index_in_dim(blocks, at_x, 0, keepdims=False)
    key_blocks = pack_blocks.transpose(1, 2, 0, 3).reshape(-1)
    query_blocks = (
        lax.dynamic_index_in_dim(pack_blocks, at_y, 2, keepdims=False).transpose(1, 0, 2).reshape(-1)
    )
    q_mine = q_mine.reshape(1024, 256)
    kv_mine = kv_mine.reshape(PACK_TOK, 256)
    out_mine, lse = attend(query_blocks, key_blocks, q_mine, kv_mine)

    def to_x(ref, to):
        return ref.at[to["x"]]

    def from_pack_x(ref, frm):
        return ref.at[:, frm["x"]]

    result, grad_hidden, gains_grad, grad_mine, gateup_sum, down_total, output_lines = middle(
        2,
        out_mine.reshape(4, 2, ROWS, 256),
        output_wide.reshape(256, D),
        gateup_low,
        down_low,
        inputs,
        cotangent[0],
        jnp.stack([attn_gain, ffn_gain]),
    )
    dq_mine, dkv_mine = attend_back(
        query_blocks, key_blocks, q_mine, kv_mine, grad_mine.reshape(1024, 256), out_mine, lse
    )
    token_grad, summed_a, summed_b, output_sum, down_sides, gains_total = end(
        3,
        dq_mine.reshape(4, 2, ROWS, 256),
        dkv_mine.reshape(PLANE, 2, ROWS, 256),
        projected,
        cosine,
        sine,
        head_gains,
        all_tokens,
        qkv_part,
        output_lines,
        down_total,
        gateup_sum.reshape(RANKS, 8, 768),
        grad_hidden,
        gains_grad,
    )
    gains_sum = lax.dynamic_slice_in_dim(
        gains_total.reshape(-1), lax.axis_index(AXES) * norm_gains.shape[0], norm_gains.shape[0]
    )
    down_sum = jnp.concatenate([down_sides[:24], down_sides[24:]], axis=1)
    wide_a, wide_b = summed_a.transpose(1, 0, 2), summed_b.transpose(1, 0, 2)
    query_sum = wide_a[:, :, :256].reshape(8, 2048)
    keyval_sum = jnp.concatenate(
        [wide_a[:, :, 256:384].reshape(8, KV), wide_a[:, :, 384:].reshape(8, KV)], axis=1
    )
    gateup_total = jnp.concatenate(
        [wide_b[:, :, :384].reshape(8, FF), wide_b[:, :, 384:].reshape(8, FF)], axis=1
    )

    query_new, query_mean_new, query_square_new = adam_update(
        query_weight, query_sum, query_mean, query_square, RATE_MATRIX, DECAY
    )
    keyval_new, keyval_mean_new, keyval_square_new = adam_update(
        keyval_weight, keyval_sum, keyval_mean, keyval_square, RATE_MATRIX, DECAY
    )
    output_new, output_mean_new, output_square_new = adam_update(
        output_weight, output_sum, output_mean, output_square, RATE_MATRIX, DECAY
    )
    gateup_new, gateup_mean_new, gateup_square_new = adam_update(
        gateup_weight, gateup_total, gateup_mean, gateup_square, RATE_MATRIX, DECAY
    )
    down_new, down_mean_new, down_square_new = adam_update(
        down_weight, down_sum, down_mean, down_square, RATE_MATRIX, DECAY
    )
    gains_new, gains_mean_new, gains_square_new = adam_update(
        norm_gains, gains_sum, gains_mean, gains_square, RATE_GAIN, 0.0
    )
    return (
        result[None],
        token_grad[None],
        query_sum,
        keyval_sum,
        output_sum,
        gateup_total,
        down_sum,
        gains_sum,
        query_new,
        keyval_new,
        output_new,
        gateup_new,
        down_new,
        gains_new,
        query_mean_new,
        keyval_mean_new,
        output_mean_new,
        gateup_mean_new,
        down_mean_new,
        gains_mean_new,
        query_square_new,
        keyval_square_new,
        output_square_new,
        gateup_square_new,
        down_square_new,
        gains_square_new,
    )


def solution(mesh):
    fine = Mesh(mesh.devices.reshape([SIZE[a] for a in AXES]), AXES)
    rows = P(("zl", "co"), ("zh", "x", "y"), None)
    packs = P(("zl", "co"), None)
    matrix = P(AXES, None)
    vector = P(AXES)
    params = [matrix] * 5 + [vector]
    return jax.shard_map(
        body,
        mesh=fine,
        in_specs=(rows, rows, packs, packs, *params, *params, *params),
        out_specs=(rows, rows, *params, *params, *params, *params),
        check_vma=False,
    )
```

```python
import functools
import math

import jax
import jax.numpy as jnp
from jax import lax
from jax.experimental import pallas as pl
from jax.experimental.pallas import tpu as pltpu
from jax.sharding import Mesh
from jax.sharding import PartitionSpec as P

D = 1024
H = 16
KVH = 8
HD = 128
FF = 3072
KV = 1024
STEP = 10
LONG = 3072
ROWS = 128
BLOCK = 64
CHUNK = 1024
TOGETHER = 4
PACK_TOK = 4096
RANKS = 8
PLANE = 16


NORM_EPS = 1e-06
ROPE_BASE = 1000000.0
BETA_ONE = 0.9
BETA_TWO = 0.95
ADAM_EPS = 1e-08
DECAY = 0.1
RATE_MATRIX = 0.1
RATE_GAIN = 0.3

SCALE = HD**-0.5
LOG2E = math.log2(math.e)

AXES = ("zh", "x", "y", "zl", "co")
SIZE = {"zh": 2, "x": 4, "y": 4, "zl": 2, "co": 2}
COLUMN = ("zh", "zl", "co")
SURFACE = ("x", "y")
MESH = pl.DeviceIdType.MESH
F32 = jnp.float32
BF16 = jnp.bfloat16
VMEM_LIMIT = 50 * 1024 * 1024


def where_am_i():
    return {a: lax.axis_index(a) for a in AXES}


def address(place):
    return tuple(place[a] for a in AXES)


def flat_index(place, axes):
    at = 0
    for a in axes:
        at = at * SIZE[a] + place[a]
    return at


def shifted(place, axes, k, sign):
    to = dict(place)
    for a in reversed(axes):
        step = lax.rem(k, SIZE[a])
        k = lax.div(k, SIZE[a])
        to[a] = lax.rem(place[a] + sign * step + SIZE[a], SIZE[a])
    return to


def column_place(me, z, core):
    return dict(me, zh=lax.div(z, 2), zl=lax.rem(z, 2), co=core)


def dot_nn(a, b):
    return lax.dot_general(a, b, (((1,), (0,)), ((), ())), preferred_element_type=F32)


def dot_nt(a, b):
    return lax.dot_general(a, b, (((1,), (1,)), ((), ())), preferred_element_type=F32)


def dot_tn(a, b):
    return lax.dot_general(a, b, (((0,), (0,)), ((), ())), preferred_element_type=F32)


def stacked_heads(ref, tile):
    rows = ref[pl.ds(tile * BLOCK, BLOCK), :]
    return jnp.concatenate([rows[:, :HD], rows[:, HD:]], axis=0)


def allowed_keys(block, chunk):
    keys = chunk * CHUNK + lax.broadcasted_iota(jnp.int32, (CHUNK, 2 * BLOCK), 0)
    lanes = lax.broadcasted_iota(jnp.int32, (CHUNK, 2 * BLOCK), 1)
    return keys <= block * BLOCK + lax.rem(lanes, BLOCK)


def first_chunk(block):
    return jnp.where(block >= LONG // BLOCK, LONG // CHUNK, 0)


def attend_kernel(q_blocks, k_blocks, q_ref, kv_ref, out_ref, lse_ref, keys, values, values_t):
    def sort(i, carry):
        to = pl.multiple_of(k_blocks[i] * BLOCK, BLOCK)
        here = pl.multiple_of(i * BLOCK, BLOCK)
        keys[pl.ds(to, BLOCK), :] = kv_ref[pl.ds(here, BLOCK), :HD]
        values[pl.ds(to, BLOCK), :] = kv_ref[pl.ds(here, BLOCK), HD:]
        return carry

    lax.fori_loop(0, PACK_TOK // BLOCK, sort, 0)
    for c in range(PACK_TOK // CHUNK):
        part = values[c * CHUNK : (c + 1) * CHUNK, :].astype(F32)
        values_t[c] = part.T.astype(BF16)

    def one_chunk(query, block, c, state, masked):
        total, mixed = state
        chunk_keys = keys[pl.ds(pl.multiple_of(c * CHUNK, CHUNK), CHUNK), :]
        weights = jnp.exp2(dot_nt(chunk_keys, query) * (SCALE * LOG2E))
        if masked:
            weights = jnp.where(allowed_keys(block, c), weights, 0.0)
        total = total + jnp.sum(weights, axis=0, keepdims=True)
        mixed = mixed + dot_nn(values_t[c], weights.astype(BF16))
        return total, mixed

    def some_tiles(group, carry):
        tiles = [TOGETHER * group + u for u in range(TOGETHER)]
        blocks = [q_blocks[tile] for tile in tiles]
        queries = [stacked_heads(q_ref, tile) for tile in tiles]
        firsts = [first_chunk(block) for block in blocks]
        lasts = [lax.div(block, CHUNK // BLOCK) for block in blocks]
        full = [last - first for first, last in zip(firsts, lasts)]
        common = functools.reduce(jnp.minimum, full)

        def step(u, j, state):
            return one_chunk(queries[u], blocks[u], firsts[u] + j, state, False)

        empty = (jnp.zeros((1, 2 * BLOCK), F32), jnp.zeros((HD, 2 * BLOCK), F32))
        states = lax.fori_loop(
            0,
            common,
            lambda j, s: tuple(step(u, j, s[u]) for u in range(TOGETHER)),
            (empty,) * TOGETHER,
        )
        states = [
            lax.fori_loop(common, full[u], functools.partial(step, u), states[u]) for u in range(TOGETHER)
        ]
        states = [
            one_chunk(queries[u], blocks[u], lasts[u], states[u], True) for u in range(TOGETHER)
        ]
        for tile, (total, mixed) in zip(tiles, states):
            result = (mixed / total).T.astype(BF16)
            rows = pl.ds(pl.multiple_of(tile * BLOCK, BLOCK), BLOCK)
            out_ref[rows, :HD] = result[:BLOCK]
            out_ref[rows, HD:] = result[BLOCK:]
            lse_ref[pl.ds(tile, 1), :] = jnp.log2(total)
        return carry

    lax.fori_loop(0, q_ref.shape[0] // BLOCK // TOGETHER, some_tiles, 0)


def attend(q_blocks, k_blocks, q, kv):
    smem = pl.BlockSpec(memory_space=pltpu.SMEM)
    vmem = pl.BlockSpec(memory_space=pltpu.VMEM)
    tiles = q.shape[0] // BLOCK
    return pl.pallas_call(
        attend_kernel,
        out_shape=(
            jax.ShapeDtypeStruct(q.shape, BF16),
            jax.ShapeDtypeStruct((tiles, 2 * BLOCK), F32),
        ),
        in_specs=[smem, smem, vmem, vmem],
        out_specs=(vmem, vmem),
        scratch_shapes=[
            pltpu.VMEM((PACK_TOK, HD), BF16),
            pltpu.VMEM((PACK_TOK, HD), BF16),
            pltpu.VMEM((PACK_TOK // CHUNK, HD, CHUNK), BF16),
        ],
        compiler_params=pltpu.CompilerParams(vmem_limit_bytes=VMEM_LIMIT),
        cost_estimate=pl.CostEstimate(
            flops=4 * 10**9, bytes_accessed=4 * 10**6, transcendentals=8 * 10**6
        ),
        name="attend",
    )(q_blocks, k_blocks, q, kv)


def attend_back_kernel(
    q_blocks,
    k_blocks,
    q_ref,
    kv_ref,
    grad_ref,
    out_ref,
    lse_ref,
    dq_ref,
    dkv_ref,
    keys,
    values,
    keys_t,
    dk,
    dv,
):
    def sort(i, carry):
        to = pl.multiple_of(k_blocks[i] * BLOCK, BLOCK)
        here = pl.multiple_of(i * BLOCK, BLOCK)
        keys[pl.ds(to, BLOCK), :] = kv_ref[pl.ds(here, BLOCK), :HD]
        values[pl.ds(to, BLOCK), :] = kv_ref[pl.ds(here, BLOCK), HD:]
        return carry

    lax.fori_loop(0, PACK_TOK // BLOCK, sort, 0)
    for c in range(PACK_TOK // CHUNK):
        part = keys[c * CHUNK : (c + 1) * CHUNK, :].astype(F32)
        keys_t[c] = part.T.astype(BF16)
    dk[...] = jnp.zeros_like(dk)
    dv[...] = jnp.zeros_like(dv)

    def one_chunk(given, block, c, dq, masked):
        query, grad, inner, lse = given
        rows = pl.ds(pl.multiple_of(c * CHUNK, CHUNK), CHUNK)
        probs = jnp.exp2(dot_nt(keys[rows, :], query) * (SCALE * LOG2E) - lse)
        if masked:
            probs = jnp.where(allowed_keys(block, c), probs, 0.0)
        grad_probs = dot_nt(values[rows, :], grad)
        grad_scores = (probs * (grad_probs - inner)).astype(BF16)
        dv[rows, :] += dot_nn(probs.astype(BF16), grad)
        dk[rows, :] += dot_nn(grad_scores, query)
        return dq + dot_nn(keys_t[c], grad_scores)

    def some_tiles(group, carry):
        tiles = [TOGETHER * group + u for u in range(TOGETHER)]
        blocks = [q_blocks[tile] for tile in tiles]
        given = []
        for tile in tiles:
            query, grad = stacked_heads(q_ref, tile), stacked_heads(grad_ref, tile)
            out = stacked_heads(out_ref, tile)
            inner = jnp.sum((grad.astype(F32) * out.astype(F32)).T, axis=0, keepdims=True)
            given.append((query, grad, inner, lse_ref[pl.ds(tile, 1), :]))
        firsts = [first_chunk(block) for block in blocks]
        lasts = [lax.div(block, CHUNK // BLOCK) for block in blocks]
        full = [last - first for first, last in zip(firsts, lasts)]
        common = functools.reduce(jnp.minimum, full)

        def step(u, j, dq):
            return one_chunk(given[u], blocks[u], firsts[u] + j, dq, False)

        empty = jnp.zeros((HD, 2 * BLOCK), F32)
        dqs = lax.fori_loop(
            0,
            common,
            lambda j, s: tuple(step(u, j, s[u]) for u in range(TOGETHER)),
            (empty,) * TOGETHER,
        )
        dqs = [
            lax.fori_loop(common, full[u], functools.partial(step, u), dqs[u]) for u in range(TOGETHER)
        ]
        dqs = [
            one_chunk(given[u], blocks[u], lasts[u], dqs[u], True) for u in range(TOGETHER)
        ]
        for tile, dq in zip(tiles, dqs):
            dq = (dq * SCALE).T.astype(BF16)
            rows = pl.ds(pl.multiple_of(tile * BLOCK, BLOCK), BLOCK)
            dq_ref[rows, :HD] = dq[:BLOCK]
            dq_ref[rows, HD:] = dq[BLOCK:]
        return carry

    lax.fori_loop(0, q_ref.shape[0] // BLOCK // TOGETHER, some_tiles, 0)

    def unsort(i, carry):
        at = pl.multiple_of(k_blocks[i] * BLOCK, BLOCK)
        here = pl.multiple_of(i * BLOCK, BLOCK)
        dkv_ref[pl.ds(here, BLOCK), :HD] = (dk[pl.ds(at, BLOCK), :] * SCALE).astype(BF16)
        dkv_ref[pl.ds(here, BLOCK), HD:] = dv[pl.ds(at, BLOCK), :].astype(BF16)
        return carry

    lax.fori_loop(0, PACK_TOK // BLOCK, unsort, 0)


def attend_back(q_blocks, k_blocks, q, kv, grad, out, lse):
    smem = pl.BlockSpec(memory_space=pltpu.SMEM)
    vmem = pl.BlockSpec(memory_space=pltpu.VMEM)
    return pl.pallas_call(
        attend_back_kernel,
        out_shape=(
            jax.ShapeDtypeStruct(q.shape, BF16),
            jax.ShapeDtypeStruct(kv.shape, BF16),
        ),
        in_specs=[smem, smem] + [vmem] * 5,
        out_specs=(vmem, vmem),
        scratch_shapes=[
            pltpu.VMEM((PACK_TOK, HD), BF16),
            pltpu.VMEM((PACK_TOK, HD), BF16),
            pltpu.VMEM((PACK_TOK // CHUNK, HD, CHUNK), BF16),
            pltpu.VMEM((PACK_TOK, HD), F32),
            pltpu.VMEM((PACK_TOK, HD), F32),
        ],
        compiler_params=pltpu.CompilerParams(vmem_limit_bytes=VMEM_LIMIT),
        cost_estimate=pl.CostEstimate(
            flops=10**10, bytes_accessed=8 * 10**6, transcendentals=8 * 10**6
        ),
        name="attend_back",
    )(q_blocks, k_blocks, q, kv, grad, out, lse)


class ColumnSums:
    def __init__(self, me, part, paired, sending, landed, near_send, near_recv, far_send, far_recv):
        self.me, self.z, self.core = me, me["zh"] * 2 + me["zl"], me["co"]
        self.part, self.paired, self.sending, self.landed = part, paired, sending, landed
        self.near_sems, self.far_sems = (near_send, near_recv), (far_send, far_recv)
        self.rows = part.shape[-2]
        self.top, self.low = pl.ds(0, self.rows // 2), pl.ds(self.rows // 2, self.rows // 2)

    def near(self, phase, off):
        return pltpu.make_async_remote_copy(
            src_ref=self.part.at[phase, lax.rem(self.z + off, 4), 1 - self.core],
            dst_ref=self.paired.at[phase, off],
            send_sem=self.near_sems[0].at[phase, off],
            recv_sem=self.near_sems[1].at[phase, off],
            device_id=address(column_place(self.me, self.z, 1 - self.core)),
            device_id_type=MESH,
        )

    def far(self, phase, which):
        slot = which if which in (1, 3) else 2
        src, dst = self.sending.at[phase, slot], self.landed.at[phase, slot]
        if slot == 2:
            half = self.top if which == 2 else self.low
            src, dst = src.at[half], dst.at[half]
        step = 1 if which in (1, 2) else 3
        return pltpu.make_async_remote_copy(
            src_ref=src,
            dst_ref=dst,
            send_sem=self.far_sems[0].at[phase, which],
            recv_sem=self.far_sems[1].at[phase, which],
            device_id=address(column_place(self.me, lax.rem(self.z + step, 4), self.core)),
            device_id_type=MESH,
        )

    def put(self, phase, off, terms):
        self.part[phase, lax.rem(self.z + off, 4)] = terms.astype(BF16).reshape(2, self.rows, D)
        self.near(phase, off).start()

    def put_all(self, phase, terms):
        self.part[phase] = terms.astype(BF16).reshape(4, 2, self.rows, D)
        for off in (2, 1, 3, 0):
            self.near(phase, off).start()

    def chip_sum(self, phase, off):
        self.near(phase, off).wait_recv()
        mine = self.part[phase, lax.rem(self.z + off, 4), self.core].astype(F32)
        return mine + self.paired[phase, off].astype(F32)

    def first(self, phase):
        self.sending[phase, 2] = self.chip_sum(phase, 2).astype(BF16)
        self.far(phase, 2).start()
        self.far(phase, 0).start()

    def second(self, phase):
        for which, by_way, half in ((1, 2, self.top), (3, 0, self.low)):
            self.sending[phase, which] = self.chip_sum(phase, which).astype(BF16)
            self.far(phase, by_way).wait_recv()
            both = self.sending[phase, which, half].astype(F32)
            both = both + self.landed[phase, 2, half].astype(F32)
            self.sending[phase, which, half] = both.astype(BF16)
            self.far(phase, which).start()

    def total(self, phase):
        total = self.chip_sum(phase, 0)
        for which in (1, 3):
            self.far(phase, which).wait_recv()
            total = total + self.landed[phase, which].astype(F32)
        return total

    def drain(self, phase):
        for off in range(4):
            self.near(phase, off).wait_send()
            self.far(phase, off).wait_send()


class ColumnGathers:
    def __init__(self, me, blocks, near_send, near_recv, far_send, far_recv):
        self.me, self.z, self.core = me, me["zh"] * 2 + me["zl"], me["co"]
        self.blocks = blocks
        self.near_sems, self.far_sems = (near_send, near_recv), (far_send, far_recv)
        self.rows = blocks.shape[-2]

    def far(self, phase, which, arriving):
        step = 1 if which in (1, 2) else 3
        back = (step if which in (1, 3) else 2 * step) if arriving else (0 if which in (1, 3) else step)
        block = self.blocks.at[phase, lax.rem(self.z + 4 * 2 - back, 4) * 2 + self.core]
        if which == 2:
            block = block.at[pl.ds(0, self.rows // 2)]
        if which == 0:
            block = block.at[pl.ds(self.rows // 2, self.rows // 2)]
        return pltpu.make_async_remote_copy(
            src_ref=block,
            dst_ref=block,
            send_sem=self.far_sems[0].at[phase, which],
            recv_sem=self.far_sems[1].at[phase, which],
            device_id=address(column_place(self.me, lax.rem(self.z + step, 4), self.core)),
            device_id_type=MESH,
        )

    def near(self, phase, off, arriving):
        core = 1 - self.core if arriving else self.core
        block = self.blocks.at[phase, lax.rem(self.z + 4 - off, 4) * 2 + core]
        return pltpu.make_async_remote_copy(
            src_ref=block,
            dst_ref=block,
            send_sem=self.near_sems[0].at[phase, off],
            recv_sem=self.near_sems[1].at[phase, off],
            device_id=address(column_place(self.me, self.z, 1 - self.core)),
            device_id_type=MESH,
        )

    def begin(self, phase, rows):
        self.blocks[phase, self.z * 2 + self.core] = rows
        for off in (1, 3):
            self.far(phase, off, False).start()
        self.near(phase, 0, False).start()

    def pass_on(self, phase):
        for off, by_way in ((1, 2), (3, 0)):
            self.far(phase, off, True).wait_recv()
            self.far(phase, by_way, False).start()
            self.near(phase, off, False).start()

    def await_chip(self, phase, i):
        off = i + lax.div(i, 2) * (5 - 2 * i)

        @pl.when(i == 3)
        def _():
            for by_way in (2, 0):
                self.far(phase, by_way, True).wait_recv()
            self.near(phase, 2, False).start()

        self.near(phase, off, True).wait_recv()
        return off, lax.rem(self.z + 4 - off, 4)

    def await_all(self, phase):
        for by_way in (2, 0):
            self.far(phase, by_way, True).wait_recv()
        self.near(phase, 2, False).start()
        for off in range(4):
            self.near(phase, off, True).wait_recv()

    def drain(self, phase):
        for off in range(4):
            self.near(phase, off, False).wait_send()
            self.far(phase, off, False).wait_send()


def norm_factor(values):
    return lax.rsqrt(jnp.mean(values * values, axis=-1, keepdims=True) + NORM_EPS)


def norm_back(values, norm_gain, grad):
    factor = norm_factor(values)
    scaled = grad * norm_gain
    inner = jnp.mean(values * scaled, axis=-1, keepdims=True)
    grad_gain = jnp.sum(grad * values * factor, axis=0, keepdims=True)
    return factor * scaled - values * (factor * factor * factor * inner), grad_gain


def gray(i):
    return i + lax.div(i, 2) * (5 - 2 * i)


def quarter(place):
    return place["zl"] * 2 + place["co"]


def at_quarter(place, t):
    return dict(place, zl=lax.div(t, 2), co=lax.rem(t, 2))


def greet(barrier, place):
    pl.semaphore_signal(barrier, inc=1, device_id=address(place), device_id_type=MESH)


def greet_all(me, column, swap):
    barrier = pltpu.get_barrier_semaphore()

    def greet_surface(k, carry):
        greet(barrier, shifted(me, SURFACE, k, 1))
        return carry

    def greet_column_all(k, carry):
        greet(barrier, shifted(me, COLUMN, k, 1))
        return carry

    lax.fori_loop(1, PLANE, greet_surface, 0)
    expected = PLANE - 1
    if column == "all":
        lax.fori_loop(1, RANKS, greet_column_all, 0)
        expected = expected + RANKS - 1
    else:
        z = me["zh"] * 2 + me["zl"]
        for off in (1, 2, 3):
            greet(barrier, column_place(me, lax.rem(z + off, 4), me["co"]))
        greet(barrier, column_place(me, z, 1 - me["co"]))
        expected = expected + 4
    if swap:
        at_home = me["x"] == quarter(me)

        @pl.when(jnp.logical_not(at_home))
        def _():
            greet(barrier, swap_partner(me))

        expected = expected + 1 - jnp.where(at_home, 1, 0)
    pl.semaphore_wait(barrier, expected)


def swap_partner(me):
    return at_quarter(dict(me, x=quarter(me)), me["x"])


class Swap:
    def __init__(self, me, src, dst, own_dst, sems):
        self.at_home = me["x"] == quarter(me)
        self.remote = lambda: pltpu.make_async_remote_copy(
            src_ref=src,
            dst_ref=dst,
            send_sem=sems.at[0],
            recv_sem=sems.at[1],
            device_id=address(swap_partner(me)),
            device_id_type=MESH,
        )
        self.own = lambda: pltpu.make_async_copy(src, own_dst, sems.at[0])

    def either(self, remote, own):
        @pl.when(self.at_home)
        def _():
            own()

        @pl.when(jnp.logical_not(self.at_home))
        def _():
            remote()

    def begin(self):
        self.either(lambda: self.remote().start(), lambda: self.own().start())

    def finish(self):
        def both():
            copy = self.remote()
            copy.wait_recv()
            copy.wait_send()

        self.either(both, lambda: self.own().wait())


class Exchange:
    def __init__(self, me, axes, take, put, send, recv):
        self.me, self.axes, self.take, self.put, self.send, self.recv = me, axes, take, put, send, recv
        self.n = math.prod(SIZE[a] for a in axes)
        self.mix = {4: 1, 8: 3, 16: 7}[self.n]

    def copy(self, k, arriving):
        to = shifted(self.me, self.axes, k, 1)
        frm = shifted(self.me, self.axes, k, -1) if arriving else self.me
        return pltpu.make_async_remote_copy(
            src_ref=self.take(to),
            dst_ref=self.put(frm),
            send_sem=self.send.at[k],
            recv_sem=self.recv.at[k],
            device_id=address(to),
            device_id_type=MESH,
        )

    def each(self, act):
        def one(j, carry):
            act(lax.rem(j * self.mix, self.n))
            return carry

        lax.fori_loop(1, self.n, one, 0)

    def begin(self):
        self.each(lambda k: self.copy(k, False).start())

    def arrive(self):
        self.each(lambda k: self.copy(k, True).wait_recv())

    def drain(self):
        self.each(lambda k: self.copy(k, False).wait_send())


class PlaneGathers:
    def __init__(self, me, views, first_send, first_recv, second_send, second_recv):
        self.me, self.views = me, views
        self.sems = ((first_send, first_recv), (second_send, second_recv))

    def copy(self, turn, view, half, k, arriving):
        axis = "xy"[half] if turn == 0 else "yx"[half]
        to = shifted(self.me, (axis,), k, 1)
        frm = shifted(self.me, (axis,), k, -1) if arriving else self.me
        one, many = self.views[view]
        block = one(half, frm["x"], frm["y"]) if turn == 0 else many(half, frm["yx"[half]])
        return pltpu.make_async_remote_copy(
            src_ref=block,
            dst_ref=block,
            send_sem=self.sems[turn][0].at[view, half, k],
            recv_sem=self.sems[turn][1].at[view, half, k],
            device_id=address(to),
            device_id_type=MESH,
        )

    def each(self, view, act):
        for half in range(2):
            for k in (1, 3, 2):
                act(half, k)

    def begin(self, view):
        self.each(view, lambda half, k: self.copy(0, view, half, k, False).start())

    def pass_on(self, view):
        for half in range(2):
            for k in (1, 3, 2):
                self.copy(0, view, half, k, True).wait_recv()
            for k in (1, 3, 2):
                self.copy(1, view, half, k, False).start()

    def arrive(self, view):
        self.each(view, lambda half, k: self.copy(1, view, half, k, True).wait_recv())

    def drain(self):
        for view in range(len(self.views)):
            for turn in range(2):
                self.each(
                    view, lambda half, k: self.copy(turn, view, half, k, False).wait_send()
                )


class PlaneSums:
    def __init__(self, me, lines, got, middle_sums, got_last, first_send, first_recv, last_send, last_recv):
        self.me, self.lines, self.got, self.sums, self.got_last = me, lines, got, middle_sums, got_last
        self.sems = ((first_send, first_recv), (last_send, last_recv))

    def row(self, half, at):
        return (half, at) if half == 0 else (half, slice(None), at)

    def copy(self, turn, half, k):
        axis = "xy"[half] if turn == 0 else "yx"[half]
        to = shifted(self.me, (axis,), k, 1)
        if turn == 0:
            src, dst = self.lines.at[self.row(half, to[axis])], self.got.at[half, k]
        else:
            src, dst = self.sums.at[half, to[axis]], self.got_last.at[half, k]
        return pltpu.make_async_remote_copy(
            src_ref=src,
            dst_ref=dst,
            send_sem=self.sems[turn][0].at[half, k],
            recv_sem=self.sems[turn][1].at[half, k],
            device_id=address(to),
            device_id_type=MESH,
        )

    def begin(self):
        for half in range(2):
            for k in (1, 3, 2):
                self.copy(0, half, k).start()

    def pass_on(self):
        for half in range(2):
            total = self.lines[self.row(half, self.me["xy"[half]])].astype(F32)
            for k in (1, 3, 2):
                self.copy(0, half, k).wait_recv()
                total = total + self.got[half, k].astype(F32)
            self.sums[half] = total.astype(BF16)
            for k in (1, 3, 2):
                self.copy(1, half, k).start()

    def total(self, half):
        total = self.sums[half, self.me["yx"[half]]].astype(F32)
        for k in (1, 3, 2):
            self.copy(1, half, k).wait_recv()
            total = total + self.got_last[half, k].astype(F32)
        return total

    def drain(self):
        for turn in range(2):
            for half in range(2):
                for k in (1, 3, 2):
                    self.copy(turn, half, k).wait_send()


def start_kernel(
    sent_a,
    sent_b,
    tokens,
    output_rows,
    down_rows,
    frequency,
    q_mine,
    kv_mine,
    all_tokens,
    down_low,
    output_wide,
    gateup_low,
    extra_out,
    gains_out,
    qkv_part,
    projected,
    cosine,
    sine,
    head_gains,
    shares_a,
    shares_b,
    wide,
    blocks,
    queries,
    keyvals,
    a_send,
    a_recv,
    b_send,
    b_recv,
    w_send,
    w_recv,
    row_send,
    row_recv,
    near_send,
    near_recv,
    far_send,
    far_recv,
    q_send,
    q_recv,
    kv_send,
    kv_recv,
    relay_send,
    relay_recv,
    swap_sems,
    own_sems,
):
    me = where_am_i()
    x, y = me["x"], me["y"]
    rank, here = flat_index(me, COLUMN), flat_index(me, SURFACE)
    gathers = ColumnGathers(me, blocks, near_send, near_recv, far_send, far_recv)
    to_a = Exchange(
        me,
        COLUMN,
        lambda to: sent_a.at[flat_index(to, COLUMN)],
        lambda frm: shares_a.at[flat_index(frm, COLUMN)],
        a_send,
        a_recv,
    )
    to_b = Exchange(
        me,
        COLUMN,
        lambda to: sent_b.at[flat_index(to, COLUMN)],
        lambda frm: shares_b.at[flat_index(frm, COLUMN)],
        b_send,
        b_recv,
    )
    spread = PlaneGathers(
        me,
        (
            (
                lambda half, x, y: wide.at[half, x, y],
                lambda half, at: wide.at[0, :, at] if half == 0 else wide.at[1, at],
            ),
            (
                lambda half, x, y: output_wide.at[y, x, :, pl.ds(half * 512, 512)],
                lambda half, at: (
                    output_wide.at[at, :, :, pl.ds(0, 512)]
                    if half == 0
                    else output_wide.at[:, at, :, pl.ds(512, 512)]
                ),
            ),
        ),
        w_send,
        w_recv,
        row_send,
        row_recv,
    )
    output_swap = Swap(
        me, output_rows, output_wide.at[y, quarter(me)], output_wide.at[y, x], swap_sems.at[0]
    )
    down_swap = Swap(me, down_rows, down_low, down_low, swap_sems.at[1])
    own_a = pltpu.make_async_copy(sent_a.at[rank], shares_a.at[rank], own_sems.at[0])
    own_b = pltpu.make_async_copy(sent_b.at[rank], shares_b.at[rank], own_sems.at[1])
    own_a.start()
    own_b.start()
    greet_all(me, "all", True)
    to_a.begin()
    output_swap.begin()
    gathers.begin(0, tokens[...])
    down_swap.begin()
    to_b.begin()

    own_a.wait()
    to_a.arrive()
    wide[:, x, y] = shares_a[...].astype(BF16).reshape(2, 32, 640)
    spread.begin(0)
    output_swap.finish()
    extra_out[...] = shares_a[:, :, 512:]

    lanes = lax.broadcasted_iota(jnp.int32, (BLOCK, HD), 1)
    place = lax.broadcasted_iota(jnp.int32, (BLOCK, HD), 0).astype(F32)

    def tables(j, carry):
        for half in range(2):
            first = shares_a[j, 2 + half : 3 + half, 512:]
            angles = (first * float(BLOCK) + place) * frequency[...]
            at = pl.ds(pl.multiple_of(j * ROWS + half * BLOCK, BLOCK), BLOCK)
            cosine[at, :] = jnp.cos(angles)
            sines = jnp.sin(angles)
            sine[at, :] = jnp.where(lanes < HD // 2, -sines, sines)
        return carry

    lax.fori_loop(0, RANKS, tables, 0)
    spread.pass_on(0)
    spread.begin(1)
    own_b.wait()
    to_b.arrive()
    gateup_low[...] = shares_b[...].astype(BF16).reshape(2, 32, 768)

    spread.arrive(0)
    qkv_part[...] = wide[..., :512].reshape(D, 512)
    extra = wide[..., 512:].reshape(D, HD)
    gains_out[...] = extra
    entry = 2 * D + lax.broadcasted_iota(jnp.int32, (HD, 2 * HD), 1)
    pick = (lax.broadcasted_iota(jnp.int32, (HD, 2 * HD), 0) == lax.rem(entry, 18)).astype(BF16)
    entries = 2 * D + lax.broadcasted_iota(jnp.int32, (D, 2 * HD), 1)
    owned = lax.broadcasted_iota(jnp.int32, (D, 2 * HD), 0) == 8 * lax.div(entries, 18)
    gains = jnp.sum(jnp.where(owned, dot_nn(extra, pick), 0.0), axis=0, keepdims=True)
    head_gains[0:1, :] = gains[:, :HD]
    head_gains[1:2, :] = gains[:, HD:]

    def q_copy(row_zh, pack):
        return pltpu.make_async_remote_copy(
            src_ref=queries.at[row_zh, pack],
            dst_ref=q_mine.at[x, row_zh],
            send_sem=q_send.at[row_zh, pack],
            recv_sem=q_recv.at[row_zh, x],
            device_id=address(dict(me, x=pack)),
            device_id_type=MESH,
        )

    def kv_copy(row_zh, pack):
        return pltpu.make_async_remote_copy(
            src_ref=keyvals.at[row_zh, pack],
            dst_ref=kv_mine.at[here, row_zh],
            send_sem=kv_send.at[row_zh, pack],
            recv_sem=kv_recv.at[row_zh, x],
            device_id=address(dict(me, x=pack)),
            device_id_type=MESH,
        )

    def q_own(row_zh):
        return pltpu.make_async_copy(
            queries.at[row_zh, x], q_mine.at[x, row_zh], own_sems.at[2 + row_zh]
        )

    def kv_own(row_zh):
        return pltpu.make_async_copy(
            keyvals.at[row_zh, x], kv_mine.at[here, row_zh], own_sems.at[4 + row_zh]
        )

    def relay(row_zh, from_x, which, arriving):
        step = 1 if which in (1, 2) else 3
        back = (step if which in (1, 3) else 2 * step) if arriving else (0 if which in (1, 3) else step)
        block = kv_mine.at[from_x * 4 + lax.rem(y + 8 - back, 4), row_zh]
        if which == 2:
            block = block.at[pl.ds(0, BLOCK)]
        if which == 0:
            block = block.at[pl.ds(BLOCK, BLOCK)]
        return pltpu.make_async_remote_copy(
            src_ref=block,
            dst_ref=block,
            send_sem=relay_send.at[row_zh, from_x, which],
            recv_sem=relay_recv.at[row_zh, from_x, which],
            device_id=address(dict(me, y=lax.rem(y + step, 4))),
            device_id_type=MESH,
        )

    def project(i, carry):
        off, at_z = gathers.await_chip(0, i)
        at = pl.ds(pl.multiple_of(at_z * 2 * ROWS, 2 * ROWS), 2 * ROWS)
        both = dot_nn(blocks[0, pl.ds(at_z * 2, 2)].reshape(2 * ROWS, D), qkv_part[...])
        projected[at, :] = both[:, :384]
        row_zh, first = lax.div(at_z, 2), lax.rem(at_z, 2) * 2
        for head in range(3):
            values = both[:, head * HD : (head + 1) * HD]
            gain = head_gains[1:2, :] if head == 2 else head_gains[0:1, :]
            normed = values * norm_factor(values) * gain
            turned = (
                normed * cosine[at, :] + pltpu.roll(normed, HD // 2, 1) * sine[at, :]
            ).astype(BF16)
            turned = turned.reshape(2, ROWS, HD)
            for at_core in range(2):
                if head == 2:
                    keyvals[row_zh, first + at_core, :, :HD] = turned[at_core]
                else:
                    queries[row_zh, first + at_core, :, head * HD : (head + 1) * HD] = turned[
                        at_core
                    ]
        values = both[:, 384:].astype(BF16).reshape(2, ROWS, HD)
        for at_core in range(2):
            pack = first + at_core
            keyvals[row_zh, pack, :, HD:] = values[at_core]

            @pl.when(pack != x)
            def _():
                kv_copy(row_zh, pack).start()
                q_copy(row_zh, pack).start()

            @pl.when(pack == x)
            def _():
                kv_own(row_zh).start()
                q_own(row_zh).start()

        return carry

    gathers.pass_on(0)
    lax.fori_loop(0, 4, project, 0)
    spread.pass_on(1)
    for i in range(RANKS):
        slot = pltpu.make_async_copy(blocks.at[0, i], all_tokens.at[i], own_sems.at[6 + i])
        slot.start()
    for row_zh in range(2):
        kv_own(row_zh).wait()
        for which in (1, 3):
            relay(row_zh, x, which, False).start()
    for off in (1, 3, 2):
        from_x = lax.rem(x + 4 - off, 4)
        to_x = lax.rem(x + off, 4)
        for row_zh in range(2):
            pltpu.make_async_remote_copy(
                src_ref=keyvals.at[row_zh, to_x],
                dst_ref=kv_mine.at[from_x * 4 + y, row_zh],
                send_sem=kv_send.at[row_zh, to_x],
                recv_sem=kv_recv.at[row_zh, from_x],
                device_id=address(dict(me, x=to_x)),
                device_id_type=MESH,
            ).wait_recv()
            for which in (1, 3):
                relay(row_zh, from_x, which, False).start()

    def forward(j, carry):
        off, row_zh = lax.div(j, 2), lax.rem(j, 2)
        from_x = lax.rem(x + 4 - gray(off), 4)
        for which, by_way in ((1, 2), (3, 0)):
            relay(row_zh, from_x, which, True).wait_recv()
            relay(row_zh, from_x, by_way, False).start()
        return carry

    lax.fori_loop(0, 8, forward, 0)
    for off in (1, 3, 2):
        from_x = lax.rem(x + 4 - off, 4)
        to_x = lax.rem(x + off, 4)
        for row_zh in range(2):
            pltpu.make_async_remote_copy(
                src_ref=queries.at[row_zh, to_x],
                dst_ref=q_mine.at[from_x, row_zh],
                send_sem=q_send.at[row_zh, to_x],
                recv_sem=q_recv.at[row_zh, from_x],
                device_id=address(dict(me, x=to_x)),
                device_id_type=MESH,
            ).wait()
            kv_copy(row_zh, to_x).wait_send()
    for row_zh in range(2):
        q_own(row_zh).wait()

    def finish(j, carry):
        row_zh, from_x = lax.div(j, 4), lax.rem(j, 4)
        for which in range(4):
            relay(row_zh, from_x, which, False).wait_send()
        for which in (2, 0):
            relay(row_zh, from_x, which, True).wait_recv()
        return carry

    lax.fori_loop(0, 8, finish, 0)
    spread.arrive(1)
    down_swap.finish()
    for i in range(RANKS):
        pltpu.make_async_copy(blocks.at[0, i], all_tokens.at[i], own_sems.at[6 + i]).wait()
    for exchange in (to_a, to_b, spread):
        exchange.drain()
    gathers.drain(0)


def start(number, sent_a, sent_b, tokens, output_rows, down_rows, frequency):
    anywhere = pl.BlockSpec(memory_space=pl.ANY)
    vmem = pl.BlockSpec(memory_space=pltpu.VMEM)
    dma = pltpu.SemaphoreType.DMA
    struct = jax.ShapeDtypeStruct
    return pl.pallas_call(
        start_kernel,
        out_shape=(
            struct((4, 2, ROWS, 256), BF16),
            struct((PLANE, 2, ROWS, 256), BF16),
            struct((RANKS, ROWS, D), BF16),
            struct((48, 512), BF16),
            struct((4, 4, 16, D), BF16),
            struct((2, 32, 768), BF16),
            struct((RANKS, 8, HD), F32),
            struct((D, HD), BF16),
            struct((D, 512), BF16),
            struct((RANKS * ROWS, 384), F32),
            struct((RANKS * ROWS, HD), F32),
            struct((RANKS * ROWS, HD), F32),
            struct((2, HD), F32),
        ),
        in_specs=[anywhere, anywhere, vmem, anywhere, anywhere, vmem],
        out_specs=(anywhere,) * 4 + (vmem,) * 9,
        scratch_shapes=[
            pltpu.VMEM((RANKS, 8, 640), F32),
            pltpu.VMEM((RANKS, 8, 768), F32),
            pltpu.VMEM((2, 4, 4, 32, 640), BF16),
            pltpu.VMEM((1, RANKS, ROWS, D), BF16),
            pltpu.VMEM((2, 4, ROWS, 256), BF16),
            pltpu.VMEM((2, 4, ROWS, 256), BF16),
        ]
        + [dma((RANKS,))] * 4
        + [dma((2, 2, 4))] * 4
        + [dma((1, 4))] * 4
        + [dma((2, 4))] * 4
        + [dma((2, 4, 4)), dma((2, 4, 4)), dma((2, 2)), dma((6 + RANKS,))],
        compiler_params=pltpu.CompilerParams(
            collective_id=number, has_side_effects=True, vmem_limit_bytes=VMEM_LIMIT
        ),
        name="start",
    )(sent_a, sent_b, tokens, output_rows, down_rows, frequency)


def middle_kernel(
    out_mine,
    wo,
    gateup_low,
    down_rows,
    inputs,
    upstream,
    gains,
    result,
    grad_hidden,
    gains_grad,
    grad_mine,
    gateup_sum,
    down_sum,
    output_lines,
    attended,
    blocks,
    part,
    paired,
    sending,
    landed,
    gate_up,
    activated,
    grad_gate,
    grad_attended,
    gateup_lines,
    down_grad,
    down_lines,
    branch,
    hidden,
    wgu,
    wd,
    down_wide,
    got,
    plane_sums,
    got_last,
    d_got,
    d_sums,
    d_got_last,
    near_send,
    near_recv,
    far_send,
    far_recv,
    gnear_send,
    gnear_recv,
    gfar_send,
    gfar_recv,
    att_send,
    att_recv,
    back_send,
    back_recv,
    plane_send,
    plane_recv,
    last_send,
    last_recv,
    w_send,
    w_recv,
    row_send,
    row_recv,
    down_send,
    down_recv,
    dlast_send,
    dlast_recv,
    own_sems,
):
    me = where_am_i()
    x = me["x"]
    z = me["zh"] * 2 + me["zl"]
    sums = ColumnSums(
        me, part, paired, sending, landed, near_send, near_recv, far_send, far_recv
    )
    gathers = ColumnGathers(me, blocks, gnear_send, gnear_recv, gfar_send, gfar_recv)
    own_wgu = pltpu.make_async_copy(gateup_low, wgu.at[:, x, me["y"]], own_sems.at[0])
    own_wgu.start()
    own_down = pltpu.make_async_copy(down_rows, down_wide.at[me["y"], x], own_sems.at[1])
    own_down.start()
    spread = PlaneGathers(
        me,
        (
            (
                lambda half, x, y: wgu.at[half, x, y],
                lambda half, at: wgu.at[0, :, at] if half == 0 else wgu.at[1, at],
            ),
            (
                lambda half, x, y: down_wide.at[y, x, :, pl.ds(half * 256, 256)],
                lambda half, at: (
                    down_wide.at[at, :, :, pl.ds(0, 256)]
                    if half == 0
                    else down_wide.at[:, at, :, pl.ds(256, 256)]
                ),
            ),
        ),
        w_send,
        w_recv,
        row_send,
        row_recv,
    )
    down_back = PlaneSums(
        me, down_lines, d_got, d_sums, d_got_last, down_send, down_recv, dlast_send, dlast_recv
    )
    gateup_back = PlaneSums(
        me, gateup_lines, got, plane_sums, got_last, plane_send, plane_recv, last_send, last_recv
    )

    def half_rows(half):
        return pl.ds(half * BLOCK, BLOCK)

    def own_out(half):
        return pltpu.make_async_copy(
            out_mine.at[x, :, half_rows(half)], attended.at[half, :, x], own_sems.at[2 + half]
        )

    def attention_out(half, k, arriving):
        frm = shifted(me, ("x",), k, -1) if arriving else me
        to = shifted(me, ("x",), k, 1)
        return pltpu.make_async_remote_copy(
            src_ref=out_mine.at[to["x"], :, half_rows(half)],
            dst_ref=attended.at[half, :, frm["x"]],
            send_sem=att_send.at[half, k],
            recv_sem=att_recv.at[half, k],
            device_id=address(to),
            device_id_type=MESH,
        )

    for half in range(2):
        own_out(half).start()
    greet_all(me, "some", False)
    for half in range(2):
        for k in (2, 1, 3):
            attention_out(half, k, False).start()
    own_wgu.wait()
    own_down.wait()
    spread.begin(0)
    spread.begin(1)

    def down_line_in(j, carry):
        at = pl.ds(pl.multiple_of(j * 48, 16), 48)
        pair = down_wide[lax.div(j, 2), pl.ds(lax.rem(j, 2) * 2, 2)].astype(F32)
        for side in range(2):
            rows = pair[:, side * 24 : side * 24 + 24].reshape(48, 512)
            wd[at, side * 512 : side * 512 + 512] = rows.astype(BF16)
        return carry

    def project_out(half):
        own_out(half).wait()
        for k in (1, 3, 2):
            attention_out(half, k, True).wait_recv()

        rows = attended[half].reshape(RANKS * BLOCK, 256)
        sums.put_all(half, dot_nn(rows, wo[...]))

    def block_rows(phase):
        return blocks[phase].reshape(RANKS * BLOCK, D)

    def at_half(half):
        return slice(half * RANKS * BLOCK, (half + 1) * RANKS * BLOCK)

    def attention_norm(half):
        at = half_rows(half)
        total = sums.total(half)
        branch[at, :] = total
        both = inputs[at, :].astype(F32) + total * norm_factor(total) * gains[0:1, :]
        hidden[at, :] = both
        gathers.begin(half, both.astype(BF16))

    def feed_forward(half):
        at = at_half(half)
        both = dot_nn(block_rows(half), wgu[...].reshape(D, 768))
        gate_up[at, :] = both
        gate, up = both[:, :384], both[:, 384:]
        acts = (gate * (1.0 / (1.0 + jnp.exp(-gate))) * up).astype(BF16)
        activated[at, :] = acts
        sums.put_all(2 + half, dot_nn(acts, wd[...]))

    def feed_forward_norm(half):
        at = half_rows(half)
        ffn_out = sums.total(2 + half)
        gain = gains[1:2, :]
        result[at, :] = (hidden[at, :] + ffn_out * norm_factor(ffn_out) * gain).astype(BF16)
        grad_ffn, grad_gain = norm_back(ffn_out, gain, upstream[at, :].astype(F32))
        gathers.begin(2 + half, grad_ffn.astype(BF16))
        return grad_gain

    def feed_forward_back(half):
        at = at_half(half)
        grad_act = dot_nt(block_rows(2 + half), wd[...])
        gate, up = gate_up[at, :384], gate_up[at, 384:]
        sig = 1.0 / (1.0 + jnp.exp(-gate))
        grad_gate[at, :384] = (grad_act * up * (sig * (1.0 + gate * (1.0 - sig)))).astype(BF16)
        grad_gate[at, 384:] = (grad_act * (gate * sig)).astype(BF16)
        sums.put_all(4 + half, dot_nt(grad_gate[at, :], wgu[...].reshape(D, 768)))

    def attention_norm_back(half):
        at = half_rows(half)
        total = upstream[at, :].astype(F32) + sums.total(4 + half)
        grad_hidden[at, :] = total
        grad_branch, grad_gain = norm_back(branch[at, :], gains[0:1, :], total)
        gathers.begin(4 + half, grad_branch.astype(BF16))
        return grad_gain

    def to_attention(half, row_zh, pack):
        return pltpu.make_async_remote_copy(
            src_ref=grad_attended.at[half, row_zh, pack],
            dst_ref=grad_mine.at[x, row_zh, half_rows(half)],
            send_sem=back_send.at[half, row_zh, pack],
            recv_sem=back_recv.at[half, row_zh, x],
            device_id=address(dict(me, x=pack)),
            device_id_type=MESH,
        )

    def own_attention(half, row_zh):
        return pltpu.make_async_copy(
            grad_attended.at[half, row_zh, x],
            grad_mine.at[x, row_zh, half_rows(half)],
            own_sems.at[4 + 2 * half + row_zh],
        )

    def project_out_back(half):
        grads = dot_nt(block_rows(4 + half), wo[...]).astype(BF16)
        grad_attended[half] = grads.reshape(2, 4, BLOCK, 256)
        for row_zh in range(2):
            own_attention(half, row_zh).start()
            for k in (1, 3, 2):
                to_attention(half, row_zh, lax.rem(x + k, 4)).start()

    def all_rows(phase):
        return blocks[phase : phase + 2].reshape(RANKS * ROWS, D)

    def down_line(s, carry):
        rows = down_grad[pl.ds(pl.multiple_of(s * 24, 8), 24), :].astype(BF16)
        at_y, at_x = lax.div(s, 4), lax.rem(s, 4)
        for half in range(2):
            for side in range(2):
                cols = slice(side * 512 + half * 256, side * 512 + half * 256 + 256)
                down_lines[half, at_x, at_y, side * 24 : side * 24 + 24, :] = rows[:, cols]
        return carry

    def send_down():
        down_grad[...] = dot_tn(activated[...], all_rows(2))
        lax.fori_loop(0, PLANE, down_line, 0)
        down_back.begin()

    def send_gateup():
        grads = dot_tn(all_rows(0), grad_gate[...])
        gateup_lines[...] = grads.astype(BF16).reshape(2, 4, 4, 32, 768)
        gateup_back.begin()

    works = (project_out, feed_forward, feed_forward_back, project_out_back)
    thens = (attention_norm, feed_forward_norm, attention_norm_back)
    gain_grads = [None, None, None]
    works[0](0)
    sums.first(0)
    works[0](1)
    spread.pass_on(0)
    spread.pass_on(1)
    sums.second(0)
    for stage in range(3):
        phase = 2 * stage
        if stage == 2:
            send_down()
        gain_grads[stage] = thens[stage](0)
        if stage > 0:
            works[stage](1)
        sums.first(phase + 1)
        gathers.pass_on(phase)
        sums.second(phase + 1)
        if stage == 2:
            down_back.pass_on()
            send_gateup()
        gathers.await_all(phase)
        if stage == 0:
            spread.arrive(0)
            spread.arrive(1)
            lax.fori_loop(0, PLANE // 2, down_line_in, 0)
        works[stage + 1](0)
        other = thens[stage](1)
        if stage > 0:
            gains_grad[2 - stage : 3 - stage, :] = gain_grads[stage] + other
        if stage < 2:
            sums.first(phase + 2)
        gathers.pass_on(phase + 1)
        if stage < 2:
            sums.second(phase + 2)
        if stage == 2:
            gateup_back.pass_on()
        gathers.await_all(phase + 1)
    works[3](1)
    grads = dot_tn(attended[...].reshape(RANKS * ROWS, 256), all_rows(4))
    for line in range(PLANE):
        rows = grads[line * 16 : line * 16 + 16].astype(BF16)
        for half in range(2):
            output_lines[half, line % 4, line // 4] = rows[:, half * 512 : half * 512 + 512]

    for half in range(2):
        for k in (1, 3, 2):
            attention_out(half, k, False).wait_send()
            frm_x = lax.rem(x + 4 - k, 4)
            to_x = lax.rem(x + k, 4)
            for row_zh in range(2):
                to_attention(half, row_zh, to_x).wait_send()
                pltpu.make_async_remote_copy(
                    src_ref=grad_attended.at[half, row_zh, to_x],
                    dst_ref=grad_mine.at[frm_x, row_zh, half_rows(half)],
                    send_sem=back_send.at[half, row_zh, to_x],
                    recv_sem=back_recv.at[half, row_zh, frm_x],
                    device_id=address(dict(me, x=to_x)),
                    device_id_type=MESH,
                ).wait_recv()
        for row_zh in range(2):
            own_attention(half, row_zh).wait()
    for phase in range(6):
        sums.drain(phase)
        gathers.drain(phase)
    for half in range(2):
        down_sum[:, half * 256 : half * 256 + 256] = down_back.total(half)
        gateup_sum[half] = gateup_back.total(half)
    for exchange in (spread, gateup_back, down_back):
        exchange.drain()


def middle(number, out_mine, wo, gateup_low, down_rows, inputs, upstream, gains):
    anywhere = pl.BlockSpec(memory_space=pl.ANY)
    vmem = pl.BlockSpec(memory_space=pltpu.VMEM)
    block, half = (ROWS, D), (BLOCK, D)
    dma = pltpu.SemaphoreType.DMA
    return pl.pallas_call(
        middle_kernel,
        out_shape=(
            jax.ShapeDtypeStruct(block, BF16),
            jax.ShapeDtypeStruct(block, F32),
            jax.ShapeDtypeStruct((2, D), F32),
            jax.ShapeDtypeStruct((4, 2, ROWS, 256), BF16),
            jax.ShapeDtypeStruct((2, 32, 768), F32),
            jax.ShapeDtypeStruct((48, 512), F32),
            jax.ShapeDtypeStruct((2, 4, 4, 16, 512), BF16),
        ),
        in_specs=[anywhere, vmem, anywhere, anywhere, vmem, vmem, vmem],
        out_specs=(vmem, vmem, vmem, anywhere, vmem, vmem, vmem),
        scratch_shapes=[
            pltpu.VMEM((2, 2, 4, BLOCK, 256), BF16),
            pltpu.VMEM((6, RANKS) + half, BF16),
            pltpu.VMEM((6, 4, 2) + half, BF16),
            pltpu.VMEM((6, 4) + half, BF16),
            pltpu.VMEM((6, 4) + half, BF16),
            pltpu.VMEM((6, 4) + half, BF16),
            pltpu.VMEM((RANKS * ROWS, 768), F32),
            pltpu.VMEM((RANKS * ROWS, 384), BF16),
            pltpu.VMEM((RANKS * ROWS, 768), BF16),
            pltpu.VMEM((2, 2, 4, BLOCK, 256), BF16),
            pltpu.VMEM((2, 4, 4, 32, 768), BF16),
            pltpu.VMEM((384, D), F32),
            pltpu.VMEM((2, 4, 4, 48, 256), BF16),
            pltpu.VMEM(block, F32),
            pltpu.VMEM(block, F32),
            pltpu.VMEM((2, 4, 4, 32, 768), BF16),
            pltpu.VMEM((384, D), BF16),
            pltpu.VMEM((4, 4, 48, 512), BF16),
            pltpu.VMEM((2, 4, 4, 32, 768), BF16),
            pltpu.VMEM((2, 4, 32, 768), BF16),
            pltpu.VMEM((2, 4, 32, 768), BF16),
            pltpu.VMEM((2, 4, 4, 48, 256), BF16),
            pltpu.VMEM((2, 4, 48, 256), BF16),
            pltpu.VMEM((2, 4, 48, 256), BF16),
        ]
        + [dma((6, 4))] * 8
        + [dma((2, 4)), dma((2, 4)), dma((2, 2, 4)), dma((2, 2, 4))]
        + [dma((2, 4))] * 4
        + [dma((2, 2, 4))] * 4
        + [dma((2, 4))] * 4
        + [dma((8,))],
        compiler_params=pltpu.CompilerParams(
            collective_id=number, has_side_effects=True, vmem_limit_bytes=VMEM_LIMIT
        ),
        name="middle",
    )(out_mine, wo, gateup_low, down_rows, inputs, upstream, gains)


def end_kernel(
    dq_mine,
    dkv_mine,
    projected,
    cosine,
    sine,
    head_gains,
    all_tokens,
    qkv_part,
    output_lines,
    down_total,
    column_b,
    grad_hidden,
    gains_grad,
    token_grad,
    summed_a,
    summed_b,
    output_sum,
    down_sum,
    gains_sum,
    across,
    besides,
    landed_kv,
    passing,
    dq_all,
    dkv_all,
    grad_qkv,
    part,
    paired,
    sending,
    landed,
    qkv_lines,
    q_got,
    q_sums,
    q_got_last,
    o_got,
    o_sums,
    o_got_last,
    output_total,
    column_a,
    gains_column,
    gains_plane,
    ring_send,
    ring_recv,
    kv_send,
    kv_recv,
    dq_send,
    dq_recv,
    near_send,
    near_recv,
    far_send,
    far_recv,
    plane_send,
    plane_recv,
    qlast_send,
    qlast_recv,
    row_send,
    row_recv,
    olast_send,
    olast_recv,
    gplane_send,
    gplane_recv,
    swap_sems,
    a_send,
    a_recv,
    b_send,
    b_recv,
    gcolumn_send,
    gcolumn_recv,
    own_sems,
):
    me = where_am_i()
    x, y, z = me["x"], me["y"], me["zh"] * 2 + me["zl"]
    rank, here = flat_index(me, COLUMN), flat_index(me, SURFACE)
    sums = ColumnSums(
        me, part, paired, sending, landed, near_send, near_recv, far_send, far_recv
    )

    def by_column(ref, out, send, recv):
        return Exchange(
            me,
            COLUMN,
            lambda to: ref.at[flat_index(to, COLUMN)],
            lambda frm: out.at[flat_index(frm, COLUMN)],
            send,
            recv,
        )

    to_a = by_column(column_a, summed_a, a_send, a_recv)
    to_b = by_column(column_b, summed_b, b_send, b_recv)
    gains_in = Exchange(
        me,
        COLUMN,
        lambda to: gains_column.at[rank],
        lambda frm: gains_column.at[flat_index(frm, COLUMN)],
        gcolumn_send,
        gcolumn_recv,
    )
    gains_over = Exchange(
        me,
        SURFACE,
        lambda to: gains_plane.at[here],
        lambda frm: gains_plane.at[flat_index(frm, SURFACE)],
        gplane_send,
        gplane_recv,
    )
    qkv_back = PlaneSums(
        me, qkv_lines, q_got, q_sums, q_got_last, plane_send, plane_recv, qlast_send, qlast_recv
    )
    queries = Exchange(
        me,
        ("x",),
        lambda to: dq_mine.at[to["x"]],
        lambda frm: dq_all.at[:, frm["x"]],
        dq_send,
        dq_recv,
    )
    output_back = PlaneSums(
        me, output_lines, o_got, o_sums, o_got_last, row_send, row_recv, olast_send, olast_recv
    )
    output_swap = Swap(me, output_total, output_sum, output_sum, swap_sems.at[0])
    down_swap = Swap(me, down_total, down_sum, down_sum, swap_sems.at[1])
    own_dq = pltpu.make_async_copy(dq_mine.at[x], dq_all.at[:, x], own_sems.at[4])
    own_a = pltpu.make_async_copy(column_a.at[rank], summed_a.at[rank], own_sems.at[6])
    own_b = pltpu.make_async_copy(column_b.at[rank], summed_b.at[rank], own_sems.at[7])

    def ring(j, which):
        to_x = lax.rem(x + j, 4)
        step = 1 if which in (1, 2) else 3
        if which in (1, 3):
            src, dst = besides.at[j, which // 2], landed_kv.at[j, which // 2]
        else:
            row_zh = 0 if which == 2 else 1
            src, dst = dkv_mine.at[to_x * 4 + lax.rem(y + 2, 4), row_zh], across.at[j, row_zh]
        return pltpu.make_async_remote_copy(
            src_ref=src,
            dst_ref=dst,
            send_sem=ring_send.at[j, which],
            recv_sem=ring_recv.at[j, which],
            device_id=address(dict(me, y=lax.rem(y + step, 4))),
            device_id_type=MESH,
        )

    def kv_copy(j, arriving):
        frm_x = lax.rem(x + 4 - j, 4) if arriving else x
        return pltpu.make_async_remote_copy(
            src_ref=passing.at[j],
            dst_ref=dkv_all.at[:, frm_x],
            send_sem=kv_send.at[j],
            recv_sem=kv_recv.at[j],
            device_id=address(dict(me, x=lax.rem(x + j, 4))),
            device_id_type=MESH,
        )

    own_dq.start()
    greet_all(me, "all", True)
    for j in (2, 1, 3, 0):
        for which in (2, 0):
            ring(j, which).start()
    queries.begin()
    down_swap.begin()
    for j in (2, 1, 3, 0):
        to_x = lax.rem(x + j, 4)
        for which, by_way, step in ((1, 2, 1), (3, 0, 3)):
            row_zh, other = (0, 1) if by_way == 2 else (1, 0)
            own_block = to_x * 4 + lax.rem(y + step, 4)
            besides[j, which // 2, other] = dkv_mine[own_block, other]
            ring(j, by_way).wait_recv()
            both = dkv_mine[own_block, row_zh].astype(F32) + across[j, row_zh].astype(F32)
            besides[j, which // 2, row_zh] = both.astype(BF16)
            ring(j, which).start()

    own_b.start()
    to_b.begin()

    for j in (2, 1, 3, 0):
        total = dkv_mine[lax.rem(x + j, 4) * 4 + y].astype(F32)
        for which in (1, 3):
            ring(j, which).wait_recv()
            total = total + landed_kv[j, which // 2].astype(F32)
        if j:
            passing[j] = total.astype(BF16)
            kv_copy(j, False).start()
        else:
            dkv_all[:, x] = total.astype(BF16)
    output_back.begin()
    own_dq.wait()
    queries.arrive()
    for j in (2, 1, 3):
        kv_copy(j, True).wait_recv()

    def project_back(i, carry):
        gain_q, gain_k = carry
        off = gray(3 - i)
        to_z = lax.rem(z + off, 4)
        at = pl.ds(pl.multiple_of(to_z * 2 * ROWS, 2 * ROWS), 2 * ROWS)
        row_zh, first = lax.div(to_z, 2), lax.rem(to_z, 2) * 2
        grad_q = dq_all[row_zh, pl.ds(first, 2)].reshape(2 * ROWS, 256).astype(F32)
        grad_kv = dkv_all[row_zh, pl.ds(first, 2)].reshape(2 * ROWS, 256)
        for head in range(3):
            if head == 2:
                grad, gain = grad_kv[:, :HD].astype(F32), head_gains[1:2, :]
            else:
                grad, gain = grad_q[:, head * HD : (head + 1) * HD], head_gains[0:1, :]
            turned = grad * cosine[at, :] - pltpu.roll(grad, HD // 2, 1) * sine[at, :]
            grad_in, grad_gain = norm_back(
                projected[at, head * HD : (head + 1) * HD], gain, turned
            )
            grad_qkv[at, head * HD : (head + 1) * HD] = grad_in.astype(BF16)
            if head == 2:
                gain_k = gain_k + grad_gain
            else:
                gain_q = gain_q + grad_gain
        grad_qkv[at, 384:] = grad_kv[:, HD:]
        return gain_q, gain_k

    nothing = jnp.zeros((1, HD), F32)
    gain_q, gain_k = lax.fori_loop(0, 4, project_back, (nothing, nothing))

    def qkv_rows(j, carry):
        cols = pl.ds(pl.multiple_of(j * 256, 256), 256)
        grads = dot_tn(all_tokens[:, :, cols].reshape(RANKS * ROWS, 256), grad_qkv[...])
        qkv_lines[lax.div(j, 2), pl.ds(lax.rem(j, 2) * 2, 2)] = grads.astype(BF16).reshape(
            2, 4, 32, 512
        )
        return carry

    lax.fori_loop(0, 4, qkv_rows, 0)
    qkv_back.begin()

    def put_tokens(i, carry):
        off = gray(3 - i)
        to_z = lax.rem(z + off, 4)
        at = pl.ds(pl.multiple_of(to_z * 2 * ROWS, 2 * ROWS), 2 * ROWS)
        sums.put(0, off, dot_nt(grad_qkv[at, :], qkv_part[...]))

        @pl.when(i == 1)
        def _():
            sums.first(0)

        return carry

    lax.fori_loop(0, 4, put_tokens, 0)
    for j in range(16):
        gains_column[rank, j : j + 1, :] = gains_grad[
            j // 8 : j // 8 + 1, j % 8 * HD : (j % 8 + 1) * HD
        ]
    gains_column[rank, 16:17, :] = gain_q
    gains_column[rank, 17:18, :] = gain_k
    gains_column[rank, 18:24, :] = jnp.zeros((6, HD), F32)
    gains_in.begin()
    sums.second(0)
    qkv_back.pass_on()
    output_back.pass_on()
    gains_in.arrive()
    gains_plane[here] = jnp.sum(gains_column[...], axis=0)
    gains_over.begin()
    token_grad[...] = grad_hidden[...] + sums.total(0)

    for half in range(2):
        column_a[pl.ds(half * 4, 4)] = qkv_back.total(half).reshape(4, 8, 512)
    own_a.start()
    to_a.begin()
    for half in range(2):
        output_total[:, half * 512 : half * 512 + 512] = output_back.total(half)
    output_swap.begin()
    gains_over.arrive()
    gains_sum[...] = jnp.sum(gains_plane[...], axis=0)
    to_b.arrive()
    output_swap.finish()
    down_swap.finish()
    own_b.wait()
    for j in (2, 1, 3, 0):
        for which in range(4):
            ring(j, which).wait_send()
        if j:
            kv_copy(j, False).wait_send()
    sums.drain(0)
    for exchange in (queries, output_back, to_b, gains_in, gains_over, qkv_back):
        exchange.drain()
    own_a.wait()
    to_a.arrive()
    to_a.drain()


def end(number, *arrays):
    anywhere = pl.BlockSpec(memory_space=pl.ANY)
    vmem = pl.BlockSpec(memory_space=pltpu.VMEM)
    dma = pltpu.SemaphoreType.DMA
    struct = jax.ShapeDtypeStruct
    block = (ROWS, D)
    quarter_rows = (2, ROWS, 256)
    return pl.pallas_call(
        end_kernel,
        out_shape=(
            struct(block, F32),
            struct((RANKS, 8, 512), F32),
            struct((RANKS, 8, 768), F32),
            struct((16, D), F32),
            struct((48, 512), F32),
            struct((24, HD), F32),
        ),
        in_specs=[anywhere, vmem] + [vmem] * 6 + [vmem, anywhere, anywhere] + [vmem] * 2,
        out_specs=(vmem, anywhere, anywhere, anywhere, anywhere, vmem),
        scratch_shapes=[
            pltpu.VMEM((4,) + quarter_rows, BF16),
            pltpu.VMEM((4, 2) + quarter_rows, BF16),
            pltpu.VMEM((4, 2) + quarter_rows, BF16),
            pltpu.VMEM((4,) + quarter_rows, BF16),
            pltpu.VMEM((2, 4, ROWS, 256), BF16),
            pltpu.VMEM((2, 4, ROWS, 256), BF16),
            pltpu.VMEM((RANKS * ROWS, 512), BF16),
            pltpu.VMEM((1, 4, 2) + block, BF16),
            pltpu.VMEM((1, 4) + block, BF16),
            pltpu.VMEM((1, 4) + block, BF16),
            pltpu.VMEM((1, 4) + block, BF16),
            pltpu.VMEM((2, 4, 4, 32, 512), BF16),
            pltpu.VMEM((2, 4, 4, 32, 512), BF16),
            pltpu.VMEM((2, 4, 32, 512), BF16),
            pltpu.VMEM((2, 4, 32, 512), BF16),
            pltpu.VMEM((2, 4, 4, 16, 512), BF16),
            pltpu.VMEM((2, 4, 16, 512), BF16),
            pltpu.VMEM((2, 4, 16, 512), BF16),
            pltpu.VMEM((16, D), F32),
            pltpu.VMEM((RANKS, 8, 512), F32),
            pltpu.VMEM((RANKS, 24, HD), F32),
            pltpu.VMEM((PLANE, 24, HD), F32),
        ]
        + [dma((4, 4))] * 2
        + [dma((4,))] * 4
        + [dma((1, 4))] * 4
        + [dma((2, 4))] * 8
        + [dma((PLANE,))] * 2
        + [dma((2, 2))]
        + [dma((RANKS,))] * 6
        + [dma((8,))],
        compiler_params=pltpu.CompilerParams(
            collective_id=number, has_side_effects=True, vmem_limit_bytes=VMEM_LIMIT
        ),
        name="end",
    )(*arrays)


def adam_update(weight, gradient, mean_old, square_old, rate, decay):
    mean_new = BETA_ONE * mean_old + (1.0 - BETA_ONE) * gradient
    square_new = BETA_TWO * square_old + (1.0 - BETA_TWO) * gradient * gradient
    mean_hat = mean_new / (1.0 - BETA_ONE**STEP)
    square_hat = square_new / (1.0 - BETA_TWO**STEP)
    weight_new = weight - rate * (mean_hat / (jnp.sqrt(square_hat) + ADAM_EPS) + decay * weight)
    return (weight_new, mean_new, square_new)


def by_rank(array, width):
    return array.reshape(array.shape[0], RANKS, width)


def body(
    tokens,
    cotangent,
    positions,
    seq_ids,
    query_weight,
    keyval_weight,
    output_weight,
    gateup_weight,
    down_weight,
    norm_gains,
    query_mean,
    keyval_mean,
    output_mean,
    gateup_mean,
    down_mean,
    gains_mean,
    query_square,
    keyval_square,
    output_square,
    gateup_square,
    down_square,
    gains_square,
):
    inputs = tokens[0]
    at_x, at_y = lax.axis_index("x"), lax.axis_index("y")

    own_blocks = (positions[0] + LONG * seq_ids[0]).reshape(-1, BLOCK)[:, 0] // BLOCK
    own_pair = lax.dynamic_slice_in_dim(own_blocks, 2 * lax.axis_index(("zh", "x", "y")), 2)
    own_pair = jnp.where(own_pair >= LONG // BLOCK, own_pair - LONG // BLOCK, own_pair)
    extra = jnp.concatenate(
        [
            jnp.pad(norm_gains, (0, HD - norm_gains.shape[0]))[None],
            jnp.pad(own_blocks.astype(F32), (0, HD - BLOCK))[None],
            jnp.broadcast_to(own_pair.astype(F32)[:, None], (2, HD)),
            jnp.zeros((4, HD), F32),
        ]
    )
    sent_a = jnp.concatenate(
        [
            by_rank(query_weight, 256),
            by_rank(keyval_weight[:, :KV], 128),
            by_rank(keyval_weight[:, KV:], 128),
            jnp.broadcast_to(extra[:, None, :], (8, RANKS, HD)),
        ],
        axis=2,
    ).transpose(1, 0, 2)
    sent_b = jnp.concatenate(
        [by_rank(gateup_weight[:, :FF], 384), by_rank(gateup_weight[:, FF:], 384)], axis=2
    ).transpose(1, 0, 2)
    frequency = ROPE_BASE ** (-jnp.arange(HD // 2, dtype=F32) * 2.0 / HD)
    (
        q_mine,
        kv_mine,
        all_tokens,
        down_low,
        output_wide,
        gateup_low,
        extras,
        gains_low,
        qkv_part,
        projected,
        cosine,
        sine,
        head_gains,
    ) = start(
        1,
        sent_a,
        sent_b,
        inputs,
        output_weight.astype(BF16),
        jnp.concatenate([down_weight[:, :512], down_weight[:, 512:]], axis=0).astype(BF16),
        jnp.concatenate([frequency, frequency])[None],
    )
    gains_all = gains_low.reshape(-1, 8, HD)[:, 0, :18].reshape(-1).astype(F32)
    attn_gain = gains_all[:D]
    ffn_gain = gains_all[D : 2 * D]

    blocks = extras[:4, 1, :BLOCK].astype(jnp.int32).reshape(4, 2, 4, 4, 2)
    pack_blocks = lax.dynamic_index_in_dim(blocks, at_x, 0, keepdims=False)
    key_blocks = pack_blocks.transpose(1, 2, 0, 3).reshape(-1)
    query_blocks = (
        lax.dynamic_index_in_dim(pack_blocks, at_y, 2, keepdims=False).transpose(1, 0, 2).reshape(-1)
    )
    q_mine = q_mine.reshape(1024, 256)
    kv_mine = kv_mine.reshape(PACK_TOK, 256)
    out_mine, lse = attend(query_blocks, key_blocks, q_mine, kv_mine)

    def to_x(ref, to):
        return ref.at[to["x"]]

    def from_pack_x(ref, frm):
        return ref.at[:, frm["x"]]

    result, grad_hidden, gains_grad, grad_mine, gateup_sum, down_total, output_lines = middle(
        2,
        out_mine.reshape(4, 2, ROWS, 256),
        output_wide.reshape(256, D),
        gateup_low,
        down_low,
        inputs,
        cotangent[0],
        jnp.stack([attn_gain, ffn_gain]),
    )
    dq_mine, dkv_mine = attend_back(
        query_blocks, key_blocks, q_mine, kv_mine, grad_mine.reshape(1024, 256), out_mine, lse
    )
    token_grad, summed_a, summed_b, output_sum, down_sides, gains_total = end(
        3,
        dq_mine.reshape(4, 2, ROWS, 256),
        dkv_mine.reshape(PLANE, 2, ROWS, 256),
        projected,
        cosine,
        sine,
        head_gains,
        all_tokens,
        qkv_part,
        output_lines,
        down_total,
        gateup_sum.reshape(RANKS, 8, 768),
        grad_hidden,
        gains_grad,
    )
    gains_sum = lax.dynamic_slice_in_dim(
        gains_total.reshape(-1), lax.axis_index(AXES) * norm_gains.shape[0], norm_gains.shape[0]
    )
    down_sum = jnp.concatenate([down_sides[:24], down_sides[24:]], axis=1)
    wide_a, wide_b = summed_a.transpose(1, 0, 2), summed_b.transpose(1, 0, 2)
    query_sum = wide_a[:, :, :256].reshape(8, 2048)
    keyval_sum = jnp.concatenate(
        [wide_a[:, :, 256:384].reshape(8, KV), wide_a[:, :, 384:].reshape(8, KV)], axis=1
    )
    gateup_total = jnp.concatenate(
        [wide_b[:, :, :384].reshape(8, FF), wide_b[:, :, 384:].reshape(8, FF)], axis=1
    )

    query_new, query_mean_new, query_square_new = adam_update(
        query_weight, query_sum, query_mean, query_square, RATE_MATRIX, DECAY
    )
    keyval_new, keyval_mean_new, keyval_square_new = adam_update(
        keyval_weight, keyval_sum, keyval_mean, keyval_square, RATE_MATRIX, DECAY
    )
    output_new, output_mean_new, output_square_new = adam_update(
        output_weight, output_sum, output_mean, output_square, RATE_MATRIX, DECAY
    )
    gateup_new, gateup_mean_new, gateup_square_new = adam_update(
        gateup_weight, gateup_total, gateup_mean, gateup_square, RATE_MATRIX, DECAY
    )
    down_new, down_mean_new, down_square_new = adam_update(
        down_weight, down_sum, down_mean, down_square, RATE_MATRIX, DECAY
    )
    gains_new, gains_mean_new, gains_square_new = adam_update(
        norm_gains, gains_sum, gains_mean, gains_square, RATE_GAIN, 0.0
    )
    return (
        result[None],
        token_grad[None],
        query_sum,
        keyval_sum,
        output_sum,
        gateup_total,
        down_sum,
        gains_sum,
        query_new,
        keyval_new,
        output_new,
        gateup_new,
        down_new,
        gains_new,
        query_mean_new,
        keyval_mean_new,
        output_mean_new,
        gateup_mean_new,
        down_mean_new,
        gains_mean_new,
        query_square_new,
        keyval_square_new,
        output_square_new,
        gateup_square_new,
        down_square_new,
        gains_square_new,
    )


def solution(mesh):
    fine = Mesh(mesh.devices.reshape([SIZE[a] for a in AXES]), AXES)
    rows = P(("zl", "co"), ("zh", "x", "y"), None)
    packs = P(("zl", "co"), None)
    matrix = P(AXES, None)
    vector = P(AXES)
    params = [matrix] * 5 + [vector]
    return jax.shard_map(
        body,
        mesh=fine,
        in_specs=(rows, rows, packs, packs, *params, *params, *params),
        out_specs=(rows, rows, *params, *params, *params, *params),
        check_vma=False,
    )
```
